32 devices in a mesh: dp: 8 (over y, x, core), tensor: 4 (over z).
Axes of the slice: x: 2, y: 2, z: 4, core: 2. Of those that a mesh axis runs over, the one named last changes fastest.
Arguments:
- query: bfloat16 [8192, 2048], P('dp', 'tensor'), may hold values from -26.25 to 26.25
- key: bfloat16 [8192, 512], P('dp'), may hold values from -26.25 to 26.25
- value: bfloat16 [8192, 512], P('dp'), may hold values from -6 to 6
- grad_out: bfloat16 [8192, 3584], P('dp'), may hold values from -12 to 12
- out_weight: bfloat16 [3584, 2048], P(None, 'tensor'), may hold values from -0.125 to 0.125
- plan: int32 [64], replicated, may hold values from 0 to 63, as said below
- segments: int32 [8192], P('dp'), may hold values from 0 to 1023, as said below
Outputs:
- grad_query: bfloat16 [8192, 2048], P('dp', 'tensor')
- grad_key: bfloat16 [8192, 512], P('dp')
- grad_value: bfloat16 [8192, 512], P('dp')
- grad_out_weight: float32 [3584, 2048], P('dp', 'tensor')
The draws below stay inside these ranges and needn't reach their ends.
Inputs may be any that keep to these rules, and one draw needn't show every extreme that they name: plan is a permutation of the blocks; the 8 blocks that one index of dp holds go to 8 different indices of dp, at most one to each. `segments`: within each aligned block of 1024 rows of one index of dp the ids start at 0 and never fall; ids may skip values.
All inputs are finite; a program needn't handle non-finite values.
Results may differ from the reference program's by a relative error of at most 0.034.
The reference program's roundings to bfloat16 on the way count: a program that leaves them out, or rounds other values in their place, can miss the bound.
Values may be sent and summed in bfloat16 or wider, within the bound.
No kernel may reach another device: no remote copies, remote signals or barrier semaphores. Data moves between devices by JAX's collectives and lax.ppermute only.
A program may use at most 128 MiB of HBM per device.

```python
import math
import jax
import jax.numpy as jnp
from jax import lax

D = 3584
KV = 4
HD = 128
HEADS = 16
ROWBLK = 128
TOK_DEV = 1024
HEADS_DEV = 4
BLK_DEV = 8
BLOCKS = 64
TOKENS = 8192
REPLICAS = 8
N_DP = 8


def drawn_pair(key):
    base = jax.random.fold_in(key, 7001)
    subkeys = jax.random.split(base, 2)
    group = HEADS // KV
    key_rows = jnp.clip(jax.random.normal(subkeys[0], (TOKENS, KV, HD), jnp.float32), -5.0, 5.0)
    query_rows = jnp.clip(jax.random.normal(subkeys[1], (TOKENS, KV, group, HD), jnp.float32), -5.0, 5.0)
    return (query_rows.reshape(TOKENS, HEADS * HD), key_rows.reshape(TOKENS, KV * HD))


def draw_query(key, part):
    return drawn_pair(key)[0].astype(jnp.bfloat16)


def draw_key(key, part):
    return drawn_pair(key)[1].astype(jnp.bfloat16)


def draw_segments(key, part):
    base = jax.random.fold_in(key, 5003)
    subkeys = jax.random.split(base, 3)
    spacing = jnp.array([24, 96, 384, 1536, 1000000], dtype=jnp.int32)
    picked = jax.random.randint(subkeys[0], (REPLICAS, 1), 0, 5)
    row_limit = jnp.take(spacing, picked)
    rolled = jax.random.randint(subkeys[1], (REPLICAS, TOK_DEV), 0, 1000000)
    boundary = rolled % row_limit == 0
    boundary = boundary.at[:, 0].set(False)
    marked = jax.random.randint(subkeys[2], (), 0, REPLICAS)
    replica_index = jnp.arange(REPLICAS, dtype=jnp.int32)[:, None]
    row_index = jnp.arange(TOK_DEV, dtype=jnp.int32)[None, :]
    forced = (replica_index == marked) & (row_index == TOK_DEV // 2)
    boundary = boundary | forced
    counted = jnp.cumsum(boundary.astype(jnp.int32), axis=1).astype(jnp.int32)
    last_id = counted[:, -1:]
    lifted = (replica_index == marked) & (counted == last_id)
    return jnp.where(lifted, TOK_DEV - 1, counted).astype(jnp.int32).reshape(TOKENS)


def draw_plan(key, part):
    base = jax.random.fold_in(key, 9001)
    subkeys = jax.random.split(base, 5)
    outer_perm = jax.random.permutation(subkeys[0], REPLICAS)
    rounds = jax.random.permutation(subkeys[1], REPLICAS)[:BLK_DEV]
    inner_perm = jax.random.permutation(subkeys[2], REPLICAS)
    local_order = jax.vmap(lambda subkey: jax.random.permutation(subkey, BLK_DEV))(jax.random.split(subkeys[3], REPLICAS))
    slot_order = jax.vmap(lambda subkey: jax.random.permutation(subkey, BLK_DEV))(jax.random.split(subkeys[4], REPLICAS))
    sender = jnp.arange(REPLICAS)[:, None]
    round_index = jnp.arange(BLK_DEV)[None, :]
    target = outer_perm[(rounds[round_index] + inner_perm[sender]) % REPLICAS]
    target_slot = slot_order[target, round_index]
    destination = (target * BLK_DEV + target_slot).reshape(-1)
    from_block = (sender * BLK_DEV + local_order).reshape(-1)
    return jnp.zeros((BLOCKS,), jnp.int32).at[destination].set(from_block.astype(jnp.int32))


def with_spikes(entries, stream_key, source, target, blocks, factor):
    def block_of(position):
        return (jnp.arange(entries.shape[position]) // (entries.shape[position] // blocks)).reshape((-1,) + (1,) * (entries.ndim - 1 - position))

    one_side = jax.random.permutation(stream_key, blocks)[block_of(target)]
    far = (block_of(target) + blocks // 2) % blocks
    return jnp.where((block_of(source) == one_side) | (block_of(source) == far), factor * entries, entries)


def levels(key, extent, pieces, low, largest):
    factor_of, own = 1.0, jax.random.fold_in(key, 6)
    for dim, parts in pieces:
        draws = jnp.exp(jax.random.uniform(jax.random.fold_in(own, dim), (parts,), jnp.float32, low / len(pieces), largest / len(pieces)))
        factor_of = factor_of * jnp.repeat(draws, extent[dim] // parts).reshape([-1 if axis == dim else 1 for axis in range(len(extent))])
    return factor_of


def scatter_about(key, extent, spread, bound, pieces=(), kind=jnp.bfloat16):
    gain = levels(key, extent, pieces, -0.22, 0.18) if pieces else 1.0
    values = jax.random.normal(key, extent, jnp.float32) * spread * gain
    return jnp.minimum(jnp.maximum(values, -bound), bound).astype(kind)


def heavy_noise(stream_key, shape, deviation, limit, shards, heavy, kind=jnp.bfloat16):
    entries = deviation * jax.random.normal(stream_key, shape, jnp.float32)
    if shards:
        entries = entries * levels(stream_key, shape, shards, -0.22, 0.18)
    return jnp.clip(with_spikes(entries, jax.random.fold_in(stream_key, 3), *heavy), -limit, limit).astype(kind)


def setup_inputs(seed: int = 0) -> dict:
    arg_keys = jax.random.split(jax.random.key(seed), 8)
    query = draw_query(jax.random.fold_in(arg_keys[7], 71), 0)
    key = draw_key(jax.random.fold_in(arg_keys[7], 71), 0)
    value = scatter_about(arg_keys[2], (TOKENS, KV * HD), 1.0, 6.0, ((0, 8),))
    grad_out = heavy_noise(arg_keys[3], (TOKENS, D), 2.0, 12.0, ((0, 8),), (0, 1, 8, 2.0))
    out_weight = scatter_about(arg_keys[4], (D, HEADS * HD), (HEADS * HD) ** -0.5, 0.125, ((1, 4),))
    plan = draw_plan(jax.random.fold_in(arg_keys[7], 71), 0)
    segments = draw_segments(jax.random.fold_in(arg_keys[7], 71), 0)
    return {"query": query, "key": key, "value": value, "grad_out": grad_out, "out_weight": out_weight, "plan": plan, "segments": segments}


rope_base = 1000000.0
yarn_factor = 4.0
yarn_context = 32768.0
beta_fast = 32.0
beta_slow = 1.0
masked_score = -1e+30

def yarn_frequencies(head_size):
    half_size = head_size // 2

    def correction(rotations):
        return head_size * math.log(yarn_context / (rotations * 2.0 * math.pi)) / (2.0 * math.log(rope_base))
    lower_bound = max(math.floor(correction(beta_fast)), 0)
    upper_bound = min(math.ceil(correction(beta_slow)), head_size - 1)
    ramp_span = max(upper_bound - lower_bound, 0.001)
    row_index = jnp.arange(half_size).astype(jnp.float32)
    extrap_freq = rope_base ** (-2.0 * row_index / head_size)
    interp_freq = extrap_freq / yarn_factor
    ramp_weight = jnp.clip((row_index - lower_bound) / ramp_span, 0.0, 1.0)
    return interp_freq * ramp_weight + extrap_freq * (1.0 - ramp_weight)

def positions_of(segments):
    row_count = segments.shape[-1]
    row_index = jnp.arange(row_count, dtype=jnp.int32)
    is_start = jnp.concatenate([jnp.ones(segments.shape[:-1] + (1,), dtype=jnp.bool_), segments[..., 1:] != segments[..., :-1]], axis=-1)
    seg_start = lax.cummax(jnp.where(is_start, row_index, 0).astype(jnp.int32), axis=segments.ndim - 1)
    return row_index - seg_start

def rotate(values, cosine, sine):
    half_size = values.shape[-1] // 2
    first_half = values[..., :half_size]
    second_half = values[..., half_size:]
    return jnp.concatenate([first_half * cosine - second_half * sine, second_half * cosine + first_half * sine], axis=-1)

def unrotate(grads, cosine, sine):
    half_size = grads.shape[-1] // 2
    first_half = grads[..., :half_size]
    second_half = grads[..., half_size:]
    return jnp.concatenate([first_half * cosine + second_half * sine, second_half * cosine - first_half * sine], axis=-1)

def reference(query, key, value, grad_out, out_weight, plan, segments):
    group = HEADS // KV
    inv_scale = 1.0 / math.sqrt(HD)
    factor = 0.1 * math.log(yarn_factor) + 1.0

    def to_dest(array):
        blocked = array.reshape((BLOCKS, ROWBLK) + array.shape[1:])
        return jnp.take(blocked, plan, axis=0).reshape(array.shape)

    def to_source(array):
        blocked = array.reshape((BLOCKS, ROWBLK) + array.shape[1:])
        return jnp.zeros_like(blocked).at[plan].set(blocked).reshape(array.shape)
    moved_query = to_dest(query)
    moved_key = to_dest(key)
    moved_value = to_dest(value)
    moved_grad = to_dest(grad_out)
    places = positions_of(segments.reshape(N_DP, TOK_DEV)).reshape(TOKENS)
    angles = places.astype(jnp.float32)[:, None] * yarn_frequencies(HD)[None, :]
    cosine = jnp.cos(angles) * factor
    sine = jnp.sin(angles) * factor
    rot_query = rotate(moved_query.astype(jnp.float32).reshape(TOKENS, HEADS, HD), cosine[:, None, :], sine[:, None, :]).astype(jnp.bfloat16)
    rot_key = rotate(moved_key.astype(jnp.float32).reshape(TOKENS, KV, HD), cosine[:, None, :], sine[:, None, :]).astype(jnp.bfloat16)
    grad_attn = jnp.dot(moved_grad, out_weight, preferred_element_type=jnp.float32).astype(jnp.bfloat16)
    row_index = jnp.arange(TOK_DEV, dtype=jnp.int32)
    causal = row_index[None, :] <= row_index[:, None]

    def one_replica(items):
        query_rows, key_rows, value_rows, grad_rows, seg_rows = items
        query_f = query_rows.astype(jnp.float32)
        key_f = jnp.repeat(key_rows.astype(jnp.float32), group, axis=1)
        value_f = jnp.repeat(value_rows.astype(jnp.float32), group, axis=1)
        grad_f = grad_rows.astype(jnp.float32).reshape(TOK_DEV, HEADS, HD)
        allowed = (seg_rows[:, None] == seg_rows[None, :]) & causal
        scores = jnp.einsum('qhd,khd->hqk', query_f, key_f) * inv_scale
        scores = jnp.where(allowed[None], scores, masked_score)
        row_peak = lax.optimization_barrier(jnp.max(scores, axis=2, keepdims=True))
        exp_scores = jnp.exp(scores - row_peak)
        prob_full = exp_scores / lax.optimization_barrier(jnp.sum(exp_scores, axis=2, keepdims=True))
        prob_bf = lax.optimization_barrier(prob_full.astype(jnp.bfloat16))
        prob_f = prob_bf.astype(jnp.float32)
        head_out = jnp.einsum('hqk,khd->qhd', prob_f, value_f).astype(jnp.bfloat16)
        grad_prob = jnp.einsum('qhd,khd->hqk', grad_f, value_f)
        row_delta = lax.optimization_barrier(jnp.sum(grad_f * head_out.astype(jnp.float32), axis=2))
        grad_bf = lax.optimization_barrier((prob_full * (grad_prob - jnp.transpose(row_delta)[:, :, None])).astype(jnp.bfloat16))
        grad_score = grad_bf.astype(jnp.float32)
        grad_rot_query = jnp.einsum('hqk,khd->qhd', grad_score, key_f) * inv_scale
        grad_rot_key = jnp.einsum('hqk,qhd->khd', grad_score, query_f) * inv_scale
        grad_value_heads = jnp.einsum('hqk,qhd->khd', prob_f, grad_f)
        return (head_out, grad_rot_query, grad_rot_key, grad_value_heads)
    stacked = (rot_query.reshape(N_DP, TOK_DEV, HEADS, HD), rot_key.reshape(N_DP, TOK_DEV, KV, HD), moved_value.reshape(N_DP, TOK_DEV, KV, HD), grad_attn.reshape(N_DP, TOK_DEV, HEADS * HD), segments.reshape(N_DP, TOK_DEV))
    head_out, grad_rot_query, grad_rot_key, grad_value_heads = lax.map(one_replica, stacked)
    head_out = head_out.reshape(TOKENS, HEADS * HD)
    grad_query = unrotate(grad_rot_query.reshape(TOKENS, HEADS, HD), cosine[:, None, :], sine[:, None, :]).astype(jnp.bfloat16).reshape(TOKENS, HEADS * HD)
    head_runs = HEADS // HEADS_DEV
    key_sum = grad_rot_key.reshape(TOKENS, head_runs, HEADS_DEV, HD).sum(axis=2)
    key_partial = lax.optimization_barrier(unrotate(key_sum, cosine[:, None, :], sine[:, None, :]).astype(jnp.bfloat16))
    value_partial = lax.optimization_barrier(grad_value_heads.reshape(TOKENS, head_runs, HEADS_DEV, HD).sum(axis=2).astype(jnp.bfloat16))
    runs_per_key = group // HEADS_DEV
    grad_key = key_partial.astype(jnp.float32).reshape(TOKENS, KV, runs_per_key, HD).sum(axis=2).astype(jnp.bfloat16).reshape(TOKENS, KV * HD)
    grad_value = value_partial.astype(jnp.float32).reshape(TOKENS, KV, runs_per_key, HD).sum(axis=2).astype(jnp.bfloat16).reshape(TOKENS, KV * HD)
    grad_out_weight = jnp.dot(moved_grad.T, head_out, preferred_element_type=jnp.float32) * (1.0 / N_DP)
    return (to_source(grad_query), to_source(grad_key), to_source(grad_value), grad_out_weight)
```

```python
from functools import partial
import math

import jax
import jax.numpy as jnp
from jax import lax
from jax.experimental import pallas as pl
from jax.experimental.pallas import tpu as pltpu
from jax.sharding import PartitionSpec as P

KV = 4
HD = 128
HEADS = 16
ROWBLK = 128
RUN_BLOCKS = 8


rope_base = 1000000.0
yarn_factor = 4.0
yarn_context = 32768.0
beta_fast = 32.0
beta_slow = 1.0
masked_score = -1e30


def yarn_frequencies(head_size):
    half_size = head_size // 2

    def correction(rotations):
        return (
            head_size
            * math.log(yarn_context / (rotations * 2.0 * math.pi))
            / (2.0 * math.log(rope_base))
        )

    lower_bound = max(math.floor(correction(beta_fast)), 0)
    upper_bound = min(math.ceil(correction(beta_slow)), head_size - 1)
    ramp_span = max(upper_bound - lower_bound, 0.001)
    row_index = jnp.arange(half_size).astype(jnp.float32)
    extrap_freq = rope_base ** (-2.0 * row_index / head_size)
    interp_freq = extrap_freq / yarn_factor
    ramp_weight = jnp.clip((row_index - lower_bound) / ramp_span, 0.0, 1.0)
    return interp_freq * ramp_weight + extrap_freq * (1.0 - ramp_weight)


def positions_of(segments):
    row_count = segments.shape[-1]
    row_index = jnp.arange(row_count, dtype=jnp.int32)
    is_start = jnp.concatenate(
        [
            jnp.ones(segments.shape[:-1] + (1,), dtype=jnp.bool_),
            segments[..., 1:] != segments[..., :-1],
        ],
        axis=-1,
    )
    seg_start = lax.cummax(jnp.where(is_start, row_index, 0), axis=segments.ndim - 1)
    return row_index - seg_start


def rope_tables(places, head_size):
    angles = places.astype(jnp.float32)[:, None] * yarn_frequencies(head_size)[None, :]
    factor = 0.1 * math.log(yarn_factor) + 1.0
    cosine = jnp.cos(angles) * factor
    sine = jnp.sin(angles) * factor
    return (
        jnp.concatenate([cosine, cosine], axis=1),
        jnp.concatenate([-sine, sine], axis=1),
    )


def swap_halves(values):
    half = values.shape[-1] // 2
    return jnp.concatenate([values[..., half:], values[..., :half]], axis=-1)


NT = (((1,), (1,)), ((), ()))
TN = (((0,), (0,)), ((), ()))


def attend_kernel(
    heads,
    plan_ref,
    run_ref,
    slot_ref,
    need_ref,
    query_ref,
    up_ref,
    cos_ref,
    sin_ref,
    key_ref,
    value_ref,
    place_ref,
    gquery_ref,
    out_ref,
    gkv_ref,
    key_win,
    value_win,
):
    scale = 1.0 / math.sqrt(HD)
    to_exp2 = scale * math.log2(math.e)
    wide = min(2, heads)
    cols = wide * ROWBLK
    gkv_ref[...] = jnp.zeros_like(gkv_ref)

    def window(count, block):
        slot = slot_ref[block]
        run = run_ref[block]
        first = jnp.maximum(slot + 1 - count, 0)
        rows = count * ROWBLK
        for step in range(count):
            source = plan_ref[run * RUN_BLOCKS + first + step]
            start = pl.multiple_of(source * ROWBLK, ROWBLK)
            key_win[pl.ds(step * ROWBLK, ROWBLK), :] = key_ref[pl.ds(start, ROWBLK), :]
            value_win[pl.ds(step * ROWBLK, ROWBLK), :] = value_ref[pl.ds(start, ROWBLK), :]
        base = pl.multiple_of(block * ROWBLK, ROWBLK)
        cosine = cos_ref[pl.ds(base, ROWBLK), :]
        sine = sin_ref[pl.ds(base, ROWBLK), :]
        place = place_ref[pl.ds(block, 1), :]
        lane = lax.broadcasted_iota(jnp.int32, (1, ROWBLK), 1)
        last = (slot - first) * ROWBLK + lane
        last_all = jnp.concatenate([last] * wide, axis=1)
        start_all = jnp.concatenate([last - place] * wide, axis=1)
        key_index = lax.broadcasted_iota(jnp.int32, (rows, cols), 0)
        allowed = (key_index >= start_all) & (key_index <= last_all)
        keys = key_win[pl.ds(0, rows), :]
        values = value_win[pl.ds(0, rows), :]
        gkey = jnp.zeros((rows, HD), jnp.float32)
        gvalue = jnp.zeros((rows, HD), jnp.float32)
        for group in range(heads // wide):
            queries = []
            ups = []
            for item in range(wide):
                at = (group * wide + item) * HD
                raw = query_ref[pl.ds(base, ROWBLK), pl.ds(at, HD)].astype(jnp.float32)
                turned = raw * cosine + pltpu.roll(raw, HD // 2, 1) * sine
                queries.append(turned.astype(jnp.bfloat16))
                ups.append(up_ref[pl.ds(base, ROWBLK), pl.ds(at, HD)])
            query = jnp.concatenate(queries, axis=0)
            up = jnp.concatenate(ups, axis=0)
            up_t = jnp.concatenate([u.astype(jnp.float32).T for u in ups], axis=1)
            score = lax.dot_general(keys, query, NT, preferred_element_type=jnp.float32)
            score = jnp.where(allowed, score, masked_score)
            peak = jnp.max(score, axis=0, keepdims=True)
            raised = jnp.exp2((score - peak) * to_exp2)
            total = jnp.sum(raised, axis=0, keepdims=True)
            prob = raised * (1.0 / total)
            prob_b = prob.astype(jnp.bfloat16)
            out_t = lax.dot_general(values, prob_b, TN, preferred_element_type=jnp.float32)
            out_r = out_t.astype(jnp.bfloat16).astype(jnp.float32)
            delta = jnp.sum(up_t * out_r, axis=0, keepdims=True)
            gprob = lax.dot_general(values, up, NT, preferred_element_type=jnp.float32)
            gscore = (prob * (gprob - delta)).astype(jnp.bfloat16)
            gquery_t = lax.dot_general(keys, gscore, TN, preferred_element_type=jnp.float32)
            gkey = gkey + jnp.dot(gscore, query, preferred_element_type=jnp.float32)
            gvalue = gvalue + jnp.dot(prob_b, up, preferred_element_type=jnp.float32)
            for item in range(wide):
                at = (group * wide + item) * HD
                part = slice(item * ROWBLK, (item + 1) * ROWBLK)
                out_ref[pl.ds(base, ROWBLK), pl.ds(at, HD)] = out_r[:, part].T.astype(jnp.bfloat16)
                grad = gquery_t[:, part].T * scale
                back = grad * cosine - pltpu.roll(grad, HD // 2, 1) * sine
                gquery_ref[pl.ds(base, ROWBLK), pl.ds(at, HD)] = back.astype(jnp.bfloat16)
        gkey = (gkey * scale).astype(jnp.bfloat16)
        gvalue = gvalue.astype(jnp.bfloat16)
        for step in range(count):
            source = plan_ref[run * RUN_BLOCKS + first + step]
            start = pl.multiple_of(source * ROWBLK, ROWBLK)
            part = slice(step * ROWBLK, (step + 1) * ROWBLK)
            gkv_ref[pl.ds(start, ROWBLK), pl.ds(0, HD)] = gkey[part]
            gkv_ref[pl.ds(start, ROWBLK), pl.ds(HD, HD)] = gvalue[part]

    def body(block, carry):
        need = need_ref[block]
        sizes = (1, 2, 4, 8)
        floor = 0
        for size in sizes:
            pl.when((need > floor) & (need <= size))(partial(window, size, block))
            floor = size
        return carry

    lax.fori_loop(0, query_ref.shape[0] // ROWBLK, body, 0)


def attend(plan, run, slot, need, query, up, cosine, sine, keys, values, places):
    rows, width = query.shape
    heads = width // HD
    every = keys.shape[0]
    smem = pl.BlockSpec(memory_space=pltpu.SMEM)
    vmem = pl.BlockSpec(memory_space=pltpu.VMEM)
    pairs = rows * RUN_BLOCKS * ROWBLK * heads
    return pl.pallas_call(
        partial(attend_kernel, heads),
        out_shape=(
            jax.ShapeDtypeStruct((rows, width), jnp.bfloat16),
            jax.ShapeDtypeStruct((rows, width), jnp.bfloat16),
            jax.ShapeDtypeStruct((every, 2 * HD), jnp.bfloat16),
        ),
        in_specs=[smem] * 4 + [vmem] * 7,
        out_specs=(vmem, vmem, vmem),
        scratch_shapes=[
            pltpu.VMEM((RUN_BLOCKS * ROWBLK, HD), jnp.bfloat16),
            pltpu.VMEM((RUN_BLOCKS * ROWBLK, HD), jnp.bfloat16),
        ],
        compiler_params=pltpu.CompilerParams(vmem_limit_bytes=48 * 1024 * 1024),
        cost_estimate=pl.CostEstimate(
            flops=10 * pairs * HD, bytes_accessed=16 * 1024 * 1024, transcendentals=pairs
        ),
    )(plan, run, slot, need, query, up, cosine, sine, keys, values, places)


def local(query, key, value, grad_out, out_weight, plan, segments):
    rank_count = lax.axis_size("dp")
    my_rank = lax.axis_index("dp")
    my_lane = lax.axis_index("tensor")
    row_count = query.shape[0]
    block_count = row_count // ROWBLK
    local_heads = query.shape[1] // HD
    group = HEADS // KV
    kv_head = my_lane * local_heads // group
    own_key = lax.dynamic_slice_in_dim(key, kv_head * HD, HD, 1)
    own_value = lax.dynamic_slice_in_dim(value, kv_head * HD, HD, 1)

    places_all = lax.all_gather(positions_of(segments), "dp", axis=0, tiled=True)
    values = lax.all_gather(own_value, "dp", axis=0, tiled=True)
    up = jnp.dot(grad_out, out_weight, preferred_element_type=jnp.float32).astype(jnp.bfloat16)

    mine = my_rank * block_count + jnp.arange(block_count, dtype=jnp.int32)
    hit = plan[None, :] == mine[:, None]
    dest = jnp.sum(
        jnp.where(hit, jnp.arange(plan.shape[0], dtype=jnp.int32)[None, :], 0), axis=1
    )
    run = dest // RUN_BLOCKS
    slot = dest % RUN_BLOCKS
    places = jnp.take(places_all.reshape(-1, ROWBLK), dest, axis=0)
    need = slot - (slot * ROWBLK - places[:, 0]) // ROWBLK + 1
    cosine, sine = rope_tables(places.reshape(row_count), HD)
    key_f = own_key.astype(jnp.float32)
    rot_key = (key_f * cosine + swap_halves(key_f) * sine).astype(jnp.bfloat16)
    keys = lax.all_gather(rot_key, "dp", axis=0, tiled=True)

    grad_query, attn_out, gkv = attend(
        plan, run, slot, need, query, up, cosine, sine, keys, values, places
    )
    gkv_sum = lax.psum_scatter(gkv, "dp", scatter_dimension=0, tiled=True)
    gkey = gkv_sum[:, :HD].astype(jnp.float32)
    key_partial = (gkey * cosine - swap_halves(gkey) * sine).astype(jnp.bfloat16)
    value_partial = gkv_sum[:, HD:]
    key_all = lax.all_gather(key_partial, "tensor", axis=1, tiled=True)
    value_all = lax.all_gather(value_partial, "tensor", axis=1, tiled=True)

    weight_term = jnp.dot(
        grad_out.T, attn_out, preferred_element_type=jnp.float32
    ).astype(jnp.bfloat16)
    weight_grad = lax.psum_scatter(
        weight_term, "dp", scatter_dimension=0, tiled=True
    ).astype(jnp.float32)

    lanes_per_key = group // local_heads

    def combine(gathered):
        if lanes_per_key == 1:
            return gathered
        merged = (
            gathered.astype(jnp.float32).reshape(row_count, KV, lanes_per_key, HD).sum(axis=2)
        )
        return merged.astype(jnp.bfloat16).reshape(row_count, KV * HD)

    return (grad_query, combine(key_all), combine(value_all), weight_grad * (1.0 / rank_count))


def solution(mesh):
    in_specs = (
        P("dp", "tensor"),
        P("dp", None),
        P("dp", None),
        P("dp", None),
        P(None, "tensor"),
        P(),
        P("dp"),
    )
    out_specs = (P("dp", "tensor"), P("dp", None), P("dp", None), P("dp", "tensor"))
    return jax.shard_map(local, mesh=mesh, in_specs=in_specs, out_specs=out_specs, check_vma=False)
```

```python
from functools import partial
import math

import jax
import jax.numpy as jnp
from jax import lax
from jax.experimental import pallas as pl
from jax.experimental.pallas import tpu as pltpu
from jax.sharding import PartitionSpec as P

KV = 4
HD = 128
HEADS = 16
ROWBLK = 128
RUN_BLOCKS = 8


rope_base = 1000000.0
yarn_factor = 4.0
yarn_context = 32768.0
beta_fast = 32.0
beta_slow = 1.0
masked_score = -1e30


def yarn_frequencies(head_size):
    half_size = head_size // 2

    def correction(rotations):
        return (
            head_size
            * math.log(yarn_context / (rotations * 2.0 * math.pi))
            / (2.0 * math.log(rope_base))
        )

    lower_bound = max(math.floor(correction(beta_fast)), 0)
    upper_bound = min(math.ceil(correction(beta_slow)), head_size - 1)
    ramp_span = max(upper_bound - lower_bound, 0.001)
    row_index = jnp.arange(half_size).astype(jnp.float32)
    extrap_freq = rope_base ** (-2.0 * row_index / head_size)
    interp_freq = extrap_freq / yarn_factor
    ramp_weight = jnp.clip((row_index - lower_bound) / ramp_span, 0.0, 1.0)
    return interp_freq * ramp_weight + extrap_freq * (1.0 - ramp_weight)


def positions_of(segments):
    row_count = segments.shape[-1]
    row_index = jnp.arange(row_count, dtype=jnp.int32)
    is_start = jnp.concatenate(
        [
            jnp.ones(segments.shape[:-1] + (1,), dtype=jnp.bool_),
            segments[..., 1:] != segments[..., :-1],
        ],
        axis=-1,
    )
    seg_start = lax.cummax(jnp.where(is_start, row_index, 0), axis=segments.ndim - 1)
    return row_index - seg_start


def rope_tables(places, head_size):
    angles = places.astype(jnp.float32)[:, None] * yarn_frequencies(head_size)[None, :]
    factor = 0.1 * math.log(yarn_factor) + 1.0
    cosine = jnp.cos(angles) * factor
    sine = jnp.sin(angles) * factor
    return (
        jnp.concatenate([cosine, cosine], axis=1),
        jnp.concatenate([-sine, sine], axis=1),
    )


def swap_halves(values):
    half = values.shape[-1] // 2
    return jnp.concatenate([values[..., half:], values[..., :half]], axis=-1)


NT = (((1,), (1,)), ((), ()))
TN = (((0,), (0,)), ((), ()))


def attend_kernel(
    heads,
    ranks,
    key_at_ref,
    value_at_ref,
    source_ref,
    run_ref,
    slot_ref,
    need_ref,
    query_ref,
    up_ref,
    cos_ref,
    sin_ref,
    place_ref,
    *refs,
):
    key_parts, refs = refs[:ranks], refs[ranks:]
    value_parts, refs = refs[:ranks], refs[ranks:]
    gquery_ref, out_ref, gkey_keep, gkey_send, gvalue_keep, gvalue_send = refs[:6]
    key_ref, value_ref, gkey_ref, gvalue_ref, key_win, value_win, sems = refs[6:]
    rows_each = query_ref.shape[0]
    scale = 1.0 / math.sqrt(HD)
    to_exp2 = scale * math.log2(math.e)
    wide = min(2, heads)
    cols = wide * ROWBLK

    loads = []
    for item, (parts, whole) in enumerate(((key_parts, key_ref), (value_parts, value_ref))):
        for rank in range(ranks):
            copy = pltpu.make_async_copy(
                parts[rank], whole.at[pl.ds(rank * rows_each, rows_each)], sems.at[item, rank]
            )
            copy.start()
            loads.append(copy)
    gkey_ref[...] = jnp.zeros_like(gkey_ref)
    gvalue_ref[...] = jnp.zeros_like(gvalue_ref)
    for copy in loads:
        copy.wait()

    def window(count, block):
        slot = slot_ref[block]
        run = run_ref[block]
        first = jnp.maximum(slot + 1 - count, 0)
        rows = count * ROWBLK
        for step in range(count):
            source = source_ref[run * RUN_BLOCKS + first + step]
            start = pl.multiple_of(source * ROWBLK, ROWBLK)
            key_win[pl.ds(step * ROWBLK, ROWBLK), :] = key_ref[pl.ds(start, ROWBLK), :]
            value_win[pl.ds(step * ROWBLK, ROWBLK), :] = value_ref[pl.ds(start, ROWBLK), :]
        base = pl.multiple_of(block * ROWBLK, ROWBLK)
        cosine = cos_ref[pl.ds(base, ROWBLK), :]
        sine = sin_ref[pl.ds(base, ROWBLK), :]
        place = place_ref[pl.ds(block, 1), :]
        lane = lax.broadcasted_iota(jnp.int32, (1, ROWBLK), 1)
        last = (slot - first) * ROWBLK + lane
        last_all = jnp.concatenate([last] * wide, axis=1)
        start_all = jnp.concatenate([last - place] * wide, axis=1)
        key_index = lax.broadcasted_iota(jnp.int32, (rows, cols), 0)
        allowed = (key_index >= start_all) & (key_index <= last_all)
        keys = key_win[pl.ds(0, rows), :]
        values = value_win[pl.ds(0, rows), :]
        gkey = jnp.zeros((rows, HD), jnp.float32)
        gvalue = jnp.zeros((rows, HD), jnp.float32)
        for group in range(heads // wide):
            queries = []
            ups = []
            for item in range(wide):
                at = (group * wide + item) * HD
                raw = query_ref[pl.ds(base, ROWBLK), pl.ds(at, HD)].astype(jnp.float32)
                turned = raw * cosine + pltpu.roll(raw, HD // 2, 1) * sine
                queries.append(turned.astype(jnp.bfloat16))
                ups.append(up_ref[pl.ds(base, ROWBLK), pl.ds(at, HD)])
            query = jnp.concatenate(queries, axis=0)
            up = jnp.concatenate(ups, axis=0)
            up_t = jnp.concatenate([u.astype(jnp.float32).T for u in ups], axis=1)
            score = lax.dot_general(keys, query, NT, preferred_element_type=jnp.float32)
            score = jnp.where(allowed, score, masked_score)
            peak = jnp.max(score, axis=0, keepdims=True)
            raised = jnp.exp2((score - peak) * to_exp2)
            total = jnp.sum(raised, axis=0, keepdims=True)
            prob = raised * (1.0 / total)
            prob_b = prob.astype(jnp.bfloat16)
            out_t = lax.dot_general(values, prob_b, TN, preferred_element_type=jnp.float32)
            out_b = out_t.astype(jnp.bfloat16)
            delta = jnp.sum(up_t * out_b.astype(jnp.float32), axis=0, keepdims=True)
            gprob = lax.dot_general(values, up, NT, preferred_element_type=jnp.float32)
            gscore = (prob * (gprob - delta)).astype(jnp.bfloat16)
            gquery_t = lax.dot_general(keys, gscore, TN, preferred_element_type=jnp.float32)
            gkey = gkey + jnp.dot(gscore, query, preferred_element_type=jnp.float32)
            gvalue = gvalue + jnp.dot(prob_b, up, preferred_element_type=jnp.float32)
            for item in range(wide):
                at = (group * wide + item) * HD
                part = slice(item * ROWBLK, (item + 1) * ROWBLK)
                out_ref[pl.ds(at, HD), pl.ds(base, ROWBLK)] = out_b[:, part]
                grad = gquery_t[:, part].T * scale
                back = grad * cosine - pltpu.roll(grad, HD // 2, 1) * sine
                gquery_ref[pl.ds(base, ROWBLK), pl.ds(at, HD)] = back.astype(jnp.bfloat16)
        gkey = (gkey * scale).astype(jnp.bfloat16)
        gvalue = gvalue.astype(jnp.bfloat16)
        for step in range(count):
            block_id = run * RUN_BLOCKS + first + step
            part = slice(step * ROWBLK, (step + 1) * ROWBLK)
            key_start = pl.multiple_of(key_at_ref[block_id] * ROWBLK, ROWBLK)
            value_start = pl.multiple_of(value_at_ref[block_id] * ROWBLK, ROWBLK)
            gkey_ref[pl.ds(key_start, ROWBLK), :] = gkey[part]
            gvalue_ref[pl.ds(value_start, ROWBLK), :] = gvalue[part]

    def body(block, carry):
        need = need_ref[block]
        floor = 0
        for size in (1, 2, 4, 8):
            pl.when((need > floor) & (need <= size))(partial(window, size, block))
            floor = size
        return carry

    lax.fori_loop(0, rows_each // ROWBLK, body, 0)
    half = ranks * rows_each // 2
    stores = []
    for item, (whole, keep, send) in enumerate(
        ((gkey_ref, gkey_keep, gkey_send), (gvalue_ref, gvalue_keep, gvalue_send))
    ):
        for place, target in enumerate((keep, send)):
            copy = pltpu.make_async_copy(
                whole.at[pl.ds(place * half, half)], target, sems.at[item, place]
            )
            copy.start()
            stores.append(copy)
    for copy in stores:
        copy.wait()


def attend(tables, query, up, cosine, sine, places, keys, values):
    rows, width = query.shape
    heads = width // HD
    ranks = len(keys)
    every = rows * ranks
    smem = pl.BlockSpec(memory_space=pltpu.SMEM)
    vmem = pl.BlockSpec(memory_space=pltpu.VMEM)
    hbm = pl.BlockSpec(memory_space=pl.ANY)
    pairs = rows * RUN_BLOCKS * ROWBLK * heads
    half = jax.ShapeDtypeStruct((every // 2, HD), jnp.bfloat16)
    return pl.pallas_call(
        partial(attend_kernel, heads, ranks),
        out_shape=(
            jax.ShapeDtypeStruct((rows, width), jnp.bfloat16),
            jax.ShapeDtypeStruct((width, rows), jnp.bfloat16),
            half,
            half,
            half,
            half,
        ),
        in_specs=[smem] * 6 + [vmem] * 5 + [hbm] * (2 * ranks),
        out_specs=(vmem, vmem, hbm, hbm, hbm, hbm),
        scratch_shapes=[pltpu.VMEM((every, HD), jnp.bfloat16)] * 4
        + [pltpu.VMEM((RUN_BLOCKS * ROWBLK, HD), jnp.bfloat16)] * 2
        + [pltpu.SemaphoreType.DMA((2, ranks))],
        compiler_params=pltpu.CompilerParams(vmem_limit_bytes=48 * 1024 * 1024),
        cost_estimate=pl.CostEstimate(
            flops=10 * pairs * HD, bytes_accessed=16 * 1024 * 1024, transcendentals=pairs
        ),
    )(*tables, query, up, cosine, sine, places, *keys, *values)


def assemble_kernel(lanes, order_ref, *refs):
    sources, outs, sems = refs[: 2 * lanes], refs[2 * lanes : 2 * lanes + 2], refs[-1]
    copies = []
    for index, source in enumerate(sources):
        column = pl.multiple_of(order_ref[index] * HD, HD)
        target = outs[index // lanes].at[:, pl.ds(column, HD)]
        copy = pltpu.make_async_copy(source, target, sems.at[index])
        copy.start()
        copies.append(copy)
    for copy in copies:
        copy.wait()


def assemble(order, pieces):
    lanes = len(pieces) // 2
    hbm = pl.BlockSpec(memory_space=pl.ANY)
    whole = jax.ShapeDtypeStruct((pieces[0].shape[0], lanes * HD), pieces[0].dtype)
    return pl.pallas_call(
        partial(assemble_kernel, lanes),
        out_shape=(whole, whole),
        in_specs=[pl.BlockSpec(memory_space=pltpu.SMEM)] + [hbm] * len(pieces),
        out_specs=(hbm, hbm),
        scratch_shapes=[pltpu.SemaphoreType.DMA((len(pieces),))],
    )(order, *pieces)


def swap(array, bit):
    ranks = lax.axis_size("dp")
    return lax.ppermute(array, "dp", [(rank, rank ^ bit) for rank in range(ranks)])


def spread(array, bits):
    found = {0: array}
    for bit in bits:
        found.update({place | bit: swap(item, bit) for place, item in list(found.items())})
    return [found[place] for place in range(len(found))]


def added(left, right):
    return left.astype(jnp.float32) + right.astype(jnp.float32)


def halve(keep, send, bits):
    received = swap(send, bits[0])
    for bit in bits[1:]:
        half = keep.shape[0] // 2
        send = added(keep[half:], received[half:]).astype(keep.dtype)
        keep = added(keep[:half], received[:half]).astype(keep.dtype)
        received = swap(send, bit)
    return added(keep, received)


def place_of(distance, bits):
    place = jnp.zeros_like(distance)
    for bit in bits:
        place = place * 2 + (distance & bit) // bit
    return place


def weight_sum(attn_t, grad_out, my_rank, bits):
    width = attn_t.shape[0]
    odd = my_rank & 1
    halves = attn_t.reshape(2, width // 2, attn_t.shape[1])

    def product(which):
        picked = lax.dynamic_index_in_dim(halves, which, 0, keepdims=False)
        return jnp.dot(picked, grad_out, preferred_element_type=jnp.float32)

    received = swap(product(1 - odd).astype(jnp.bfloat16), 1)
    total = product(odd) + received.astype(jnp.float32)
    pair_count = lax.axis_size("dp") // 2
    pair_rows = grad_out.shape[1] // pair_count
    sums = []
    for part, order in enumerate((bits[1:], bits[1:][::-1])):
        rows = total[part * width // 4 : (part + 1) * width // 4]
        pieces = {
            2 * pair: rows[:, pair * pair_rows : (pair + 1) * pair_rows]
            for pair in range(pair_count)
        }
        for bit in order:
            high = (my_rank & bit) > 0
            lows = [rank for rank in sorted(pieces) if not rank & bit]
            send = jnp.concatenate(
                [jnp.where(high, pieces[rank], pieces[rank | bit]) for rank in lows], axis=1
            )
            back = swap(send.astype(jnp.bfloat16), bit).astype(jnp.float32)
            pieces = {
                rank: jnp.where(high, pieces[rank | bit], pieces[rank])
                + back[:, at * pair_rows : (at + 1) * pair_rows]
                for at, rank in enumerate(lows)
            }
        sums.append(pieces[0])
    total = jnp.concatenate(sums, axis=0)
    first, second = total[:, : pair_rows // 2], total[:, pair_rows // 2 :]
    is_odd = odd > 0
    other = swap(jnp.where(is_odd, first, second).astype(jnp.bfloat16), 1).astype(jnp.float32)
    mine = jnp.where(is_odd, second, first)
    return jnp.concatenate(
        [jnp.where(is_odd, other, mine), jnp.where(is_odd, mine, other)], axis=0
    )


def local(query, key, value, grad_out, out_weight, plan, segments):
    rank_count = lax.axis_size("dp")
    lane_count = lax.axis_size("tensor")
    my_rank = lax.axis_index("dp")
    my_lane = lax.axis_index("tensor")
    row_count = query.shape[0]
    block_count = row_count // ROWBLK
    local_heads = query.shape[1] // HD
    group = HEADS // KV
    bits = [1 << at for at in range(rank_count.bit_length() - 1)]
    kv_head = my_lane * local_heads // group
    own_key = lax.dynamic_slice_in_dim(key, kv_head * HD, HD, 1)
    own_value = lax.dynamic_slice_in_dim(value, kv_head * HD, HD, 1)

    own_places = positions_of(segments).reshape(block_count, ROWBLK)
    places_all = jnp.concatenate(
        [own_places] + [swap(own_places, step) for step in range(1, rank_count)], axis=0
    )
    values = spread(own_value, bits[1:] + bits[:1])
    up = jnp.dot(grad_out, out_weight, preferred_element_type=jnp.float32).astype(jnp.bfloat16)

    mine = my_rank * block_count + jnp.arange(block_count, dtype=jnp.int32)
    hit = plan[None, :] == mine[:, None]
    dest = jnp.sum(
        jnp.where(hit, jnp.arange(plan.shape[0], dtype=jnp.int32)[None, :], 0), axis=1
    )
    run = dest // RUN_BLOCKS
    slot = dest % RUN_BLOCKS
    places = jnp.take(places_all, (run ^ my_rank) * RUN_BLOCKS + slot, axis=0)
    need = slot - (slot * ROWBLK - places[:, 0]) // ROWBLK + 1
    cosine, sine = rope_tables(places.reshape(row_count), HD)
    key_f = own_key.astype(jnp.float32)
    rot_key = (key_f * cosine + swap_halves(key_f) * sine).astype(jnp.bfloat16)
    keys = spread(rot_key, bits[:0:-1] + bits[:1])

    distance = (plan // block_count) ^ my_rank
    within = plan % block_count
    key_bits = bits[:1] + bits[:0:-1]
    tables = (
        place_of(distance, key_bits) * block_count + within,
        place_of(distance, bits) * block_count + within,
        distance * block_count + within,
        run,
        slot,
        need,
    )
    grad_query, attn_t, gkey_keep, gkey_send, gvalue_keep, gvalue_send = attend(
        tables, query, up, cosine, sine, places, keys, values
    )
    value_partial = halve(gvalue_keep, gvalue_send, bits).astype(jnp.bfloat16)
    gkey = halve(gkey_keep, gkey_send, key_bits)
    key_partial = (gkey * cosine - swap_halves(gkey) * sine).astype(jnp.bfloat16)

    key_ring = [key_partial]
    value_ring = [value_partial]
    down = [(lane, (lane - 1) % lane_count) for lane in range(lane_count)]
    above = [(lane, (lane + 1) % lane_count) for lane in range(lane_count)]
    for unused in range(lane_count - 1):
        value_ring.append(lax.ppermute(value_ring[-1], "tensor", above))
        key_ring.append(lax.ppermute(key_ring[-1], "tensor", down))
    step = jnp.arange(lane_count, dtype=jnp.int32)
    order = jnp.concatenate([(my_lane + step) % lane_count, (my_lane - step) % lane_count])
    key_all, value_all = assemble(order, key_ring + value_ring)

    weight_grad = weight_sum(attn_t, grad_out, my_rank, bits).T
    lanes_per_key = group // local_heads

    def combine(gathered):
        if lanes_per_key == 1:
            return gathered
        merged = (
            gathered.astype(jnp.float32).reshape(row_count, KV, lanes_per_key, HD).sum(axis=2)
        )
        return merged.astype(jnp.bfloat16).reshape(row_count, KV * HD)

    return (grad_query, combine(key_all), combine(value_all), weight_grad * (1.0 / rank_count))


def solution(mesh):
    in_specs = (
        P("dp", "tensor"),
        P("dp", None),
        P("dp", None),
        P("dp", None),
        P(None, "tensor"),
        P(),
        P("dp"),
    )
    out_specs = (P("dp", "tensor"), P("dp", None), P("dp", None), P("dp", "tensor"))
    return jax.shard_map(local, mesh=mesh, in_specs=in_specs, out_specs=out_specs, check_vma=False)
```

```python
from functools import partial
import math

import jax
import jax.numpy as jnp
from jax import lax
from jax.experimental import pallas as pl
from jax.experimental.pallas import tpu as pltpu
from jax.sharding import PartitionSpec as P

KV = 4
HD = 128
HEADS = 16
ROWBLK = 128
RUN_BLOCKS = 8


rope_base = 1000000.0
yarn_factor = 4.0
yarn_context = 32768.0
beta_fast = 32.0
beta_slow = 1.0
masked_score = -1e30


def yarn_frequencies(head_size):
    half_size = head_size // 2

    def correction(rotations):
        return (
            head_size
            * math.log(yarn_context / (rotations * 2.0 * math.pi))
            / (2.0 * math.log(rope_base))
        )

    lower_bound = max(math.floor(correction(beta_fast)), 0)
    upper_bound = min(math.ceil(correction(beta_slow)), head_size - 1)
    ramp_span = max(upper_bound - lower_bound, 0.001)
    row_index = jnp.arange(half_size).astype(jnp.float32)
    extrap_freq = rope_base ** (-2.0 * row_index / head_size)
    interp_freq = extrap_freq / yarn_factor
    ramp_weight = jnp.clip((row_index - lower_bound) / ramp_span, 0.0, 1.0)
    return interp_freq * ramp_weight + extrap_freq * (1.0 - ramp_weight)


def positions_of(segments):
    row_count = segments.shape[-1]
    row_index = jnp.arange(row_count, dtype=jnp.int32)
    is_start = jnp.concatenate(
        [
            jnp.ones(segments.shape[:-1] + (1,), dtype=jnp.bool_),
            segments[..., 1:] != segments[..., :-1],
        ],
        axis=-1,
    )
    seg_start = lax.cummax(jnp.where(is_start, row_index, 0), axis=segments.ndim - 1)
    return row_index - seg_start


def rope_tables(places, head_size):
    angles = places.astype(jnp.float32)[:, None] * yarn_frequencies(head_size)[None, :]
    factor = 0.1 * math.log(yarn_factor) + 1.0
    cosine = jnp.cos(angles) * factor
    sine = jnp.sin(angles) * factor
    return (
        jnp.concatenate([cosine, cosine], axis=1),
        jnp.concatenate([-sine, sine], axis=1),
    )


def swap_halves(values):
    half = values.shape[-1] // 2
    return jnp.concatenate([values[..., half:], values[..., :half]], axis=-1)


NT = (((1,), (1,)), ((), ()))
TN = (((0,), (0,)), ((), ()))


def attend_kernel(
    heads,
    ranks,
    key_at_ref,
    value_at_ref,
    source_ref,
    run_ref,
    slot_ref,
    need_ref,
    query_ref,
    up_ref,
    cos_ref,
    sin_ref,
    place_ref,
    *refs,
):
    key_parts, refs = refs[:ranks], refs[ranks:]
    value_parts, refs = refs[:ranks], refs[ranks:]
    gquery_ref, out_ref, gkey_keep, gkey_send, gvalue_keep, gvalue_send = refs[:6]
    key_ref, value_ref, gkey_ref, gvalue_ref, key_win, value_win, sems = refs[6:]
    rows_each = query_ref.shape[0]
    scale = 1.0 / math.sqrt(HD)
    to_exp2 = scale * math.log2(math.e)
    wide = min(2, heads)
    cols = wide * ROWBLK

    loads = []
    for item, (parts, whole) in enumerate(((key_parts, key_ref), (value_parts, value_ref))):
        for rank in range(ranks):
            copy = pltpu.make_async_copy(
                parts[rank], whole.at[pl.ds(rank * rows_each, rows_each)], sems.at[item, rank]
            )
            copy.start()
            loads.append(copy)
    gkey_ref[...] = jnp.zeros_like(gkey_ref)
    gvalue_ref[...] = jnp.zeros_like(gvalue_ref)
    for copy in loads:
        copy.wait()

    def window(count, block):
        slot = slot_ref[block]
        run = run_ref[block]
        first = jnp.maximum(slot + 1 - count, 0)
        rows = count * ROWBLK
        for step in range(count):
            source = source_ref[run * RUN_BLOCKS + first + step]
            start = pl.multiple_of(source * ROWBLK, ROWBLK)
            key_win[pl.ds(step * ROWBLK, ROWBLK), :] = key_ref[pl.ds(start, ROWBLK), :]
            value_win[pl.ds(step * ROWBLK, ROWBLK), :] = value_ref[pl.ds(start, ROWBLK), :]
        base = pl.multiple_of(block * ROWBLK, ROWBLK)
        cosine = cos_ref[pl.ds(base, ROWBLK), :]
        sine = sin_ref[pl.ds(base, ROWBLK), :]
        place = place_ref[pl.ds(block, 1), :]
        lane = lax.broadcasted_iota(jnp.int32, (1, ROWBLK), 1)
        last = (slot - first) * ROWBLK + lane
        last_all = jnp.concatenate([last] * wide, axis=1)
        start_all = jnp.concatenate([last - place] * wide, axis=1)
        key_index = lax.broadcasted_iota(jnp.int32, (rows, cols), 0)
        allowed = (key_index >= start_all) & (key_index <= last_all)
        keys = key_win[pl.ds(0, rows), :]
        values = value_win[pl.ds(0, rows), :]
        gkey = jnp.zeros((rows, HD), jnp.float32)
        gvalue = jnp.zeros((rows, HD), jnp.float32)
        for group in range(heads // wide):
            queries = []
            ups = []
            for item in range(wide):
                at = (group * wide + item) * HD
                raw = query_ref[pl.ds(base, ROWBLK), pl.ds(at, HD)].astype(jnp.float32)
                turned = raw * cosine + pltpu.roll(raw, HD // 2, 1) * sine
                queries.append(turned.astype(jnp.bfloat16))
                ups.append(up_ref[pl.ds(base, ROWBLK), pl.ds(at, HD)])
            query = jnp.concatenate(queries, axis=0)
            up = jnp.concatenate(ups, axis=0)
            up_t = jnp.concatenate([u.astype(jnp.float32).T for u in ups], axis=1)
            score = lax.dot_general(keys, query, NT, preferred_element_type=jnp.float32)
            score = jnp.where(allowed, score, masked_score)
            peak = jnp.max(score, axis=0, keepdims=True)
            raised = jnp.exp2((score - peak) * to_exp2)
            total = jnp.sum(raised, axis=0, keepdims=True)
            prob = raised * (1.0 / total)
            prob_b = prob.astype(jnp.bfloat16)
            out_t = lax.dot_general(values, prob_b, TN, preferred_element_type=jnp.float32)
            out_b = out_t.astype(jnp.bfloat16)
            delta = jnp.sum(up_t * out_b.astype(jnp.float32), axis=0, keepdims=True)
            gprob = lax.dot_general(values, up, NT, preferred_element_type=jnp.float32)
            gscore = (prob * (gprob - delta)).astype(jnp.bfloat16)
            gquery_t = lax.dot_general(keys, gscore, TN, preferred_element_type=jnp.float32)
            gkey = gkey + jnp.dot(gscore, query, preferred_element_type=jnp.float32)
            gvalue = gvalue + jnp.dot(prob_b, up, preferred_element_type=jnp.float32)
            for item in range(wide):
                at = (group * wide + item) * HD
                part = slice(item * ROWBLK, (item + 1) * ROWBLK)
                out_ref[pl.ds(at, HD), pl.ds(base, ROWBLK)] = out_b[:, part]
                grad = gquery_t[:, part].T * scale
                back = grad * cosine - pltpu.roll(grad, HD // 2, 1) * sine
                gquery_ref[pl.ds(base, ROWBLK), pl.ds(at, HD)] = back.astype(jnp.bfloat16)
        gkey = (gkey * scale).astype(jnp.bfloat16)
        gvalue = gvalue.astype(jnp.bfloat16)
        for step in range(count):
            block_id = run * RUN_BLOCKS + first + step
            part = slice(step * ROWBLK, (step + 1) * ROWBLK)
            key_start = pl.multiple_of(key_at_ref[block_id] * ROWBLK, ROWBLK)
            value_start = pl.multiple_of(value_at_ref[block_id] * ROWBLK, ROWBLK)
            gkey_ref[pl.ds(key_start, ROWBLK), :] = gkey[part]
            gvalue_ref[pl.ds(value_start, ROWBLK), :] = gvalue[part]

    def body(block, carry):
        need = need_ref[block]
        floor = 0
        for size in (1, 2, 3, 4, 6, 8):
            pl.when((need > floor) & (need <= size))(partial(window, size, block))
            floor = size
        return carry

    lax.fori_loop(0, rows_each // ROWBLK, body, 0)
    half = ranks * rows_each // 2
    stores = []
    for item, (whole, keep, send) in enumerate(
        ((gkey_ref, gkey_keep, gkey_send), (gvalue_ref, gvalue_keep, gvalue_send))
    ):
        for place, target in enumerate((keep, send)):
            copy = pltpu.make_async_copy(
                whole.at[pl.ds(place * half, half)], target, sems.at[item, place]
            )
            copy.start()
            stores.append(copy)
    for copy in stores:
        copy.wait()


def attend(tables, query, up, cosine, sine, places, keys, values):
    rows, width = query.shape
    heads = width // HD
    ranks = len(keys)
    every = rows * ranks
    smem = pl.BlockSpec(memory_space=pltpu.SMEM)
    vmem = pl.BlockSpec(memory_space=pltpu.VMEM)
    hbm = pl.BlockSpec(memory_space=pl.ANY)
    pairs = rows * RUN_BLOCKS * ROWBLK * heads
    half = jax.ShapeDtypeStruct((every // 2, HD), jnp.bfloat16)
    return pl.pallas_call(
        partial(attend_kernel, heads, ranks),
        out_shape=(
            jax.ShapeDtypeStruct((rows, width), jnp.bfloat16),
            jax.ShapeDtypeStruct((width, rows), jnp.bfloat16),
            half,
            half,
            half,
            half,
        ),
        in_specs=[smem] * 6 + [vmem] * 5 + [hbm] * (2 * ranks),
        out_specs=(vmem, vmem, hbm, hbm, hbm, hbm),
        scratch_shapes=[pltpu.VMEM((every, HD), jnp.bfloat16)] * 4
        + [pltpu.VMEM((RUN_BLOCKS * ROWBLK, HD), jnp.bfloat16)] * 2
        + [pltpu.SemaphoreType.DMA((2, ranks))],
        compiler_params=pltpu.CompilerParams(vmem_limit_bytes=48 * 1024 * 1024),
        cost_estimate=pl.CostEstimate(
            flops=10 * pairs * HD, bytes_accessed=16 * 1024 * 1024, transcendentals=pairs
        ),
    )(*tables, query, up, cosine, sine, places, *keys, *values)


def assemble_kernel(count, column_ref, active_ref, *refs):
    out_ref = refs[count]
    for index in range(count):

        @pl.when(active_ref[index] > 0)
        def store():
            column = pl.multiple_of(column_ref[index] * HD, HD)
            out_ref[:, pl.ds(column, HD)] = refs[index][...]


def assemble(columns, active, pieces, lanes):
    rows = pieces[0].shape[0]
    steps = 4
    smem = pl.BlockSpec(memory_space=pltpu.SMEM)
    return pl.pallas_call(
        partial(assemble_kernel, len(pieces)),
        grid=(steps,),
        out_shape=jax.ShapeDtypeStruct((rows, lanes * HD), pieces[0].dtype),
        in_specs=[smem, smem]
        + [pl.BlockSpec((rows // steps, HD), lambda step: (step, 0))] * len(pieces),
        out_specs=pl.BlockSpec((rows // steps, lanes * HD), lambda step: (step, 0)),
        cost_estimate=pl.CostEstimate(
            flops=0, bytes_accessed=4 * rows * lanes * HD, transcendentals=0
        ),
    )(columns, active, *pieces)


def lane_gather(array, my_lane):
    lanes = lax.axis_size("tensor")

    def send(item, pairs):
        return lax.ppermute(item, "tensor", pairs)

    if lanes == 4:
        second = send(array, [(0, 2), (2, 0), (1, 3), (3, 1)])
        first = send(array, [(0, 1), (1, 0), (2, 3), (3, 2)])
        inner = send(array, [(1, 2), (2, 1)])
        outer = send(second, [(1, 0), (2, 3)])
        middle = (my_lane == 1) | (my_lane == 2)
        pieces = [array, first, second, inner, outer]
        columns = my_lane ^ jnp.array([0, 1, 2, 3, 3], jnp.int32)
        always = jnp.array([True, True, True, False, False])
        at_inner = jnp.array([False, False, False, True, False])
        active = always | (at_inner & middle) | (~always & ~at_inner & ~middle)
    else:
        pieces = [array]
        for unused in range(lanes - 1):
            pieces.append(send(pieces[-1], [(lane, (lane + 1) % lanes) for lane in range(lanes)]))
        columns = (my_lane - jnp.arange(lanes, dtype=jnp.int32)) % lanes
        active = jnp.ones((lanes,), jnp.bool_)
    return assemble(columns, active.astype(jnp.int32), pieces, lanes)


def swap(array, bit):
    ranks = lax.axis_size("dp")
    return lax.ppermute(array, "dp", [(rank, rank ^ bit) for rank in range(ranks)])


def spread(array, bits):
    found = {0: array}
    for bit in bits:
        found.update({place | bit: swap(item, bit) for place, item in list(found.items())})
    return [found[place] for place in range(len(found))]


def added(left, right):
    return left.astype(jnp.float32) + right.astype(jnp.float32)


def halve(keep, send, bits):
    received = swap(send, bits[0])
    for bit in bits[1:]:
        half = keep.shape[0] // 2
        send = added(keep[half:], received[half:]).astype(keep.dtype)
        keep = added(keep[:half], received[:half]).astype(keep.dtype)
        received = swap(send, bit)
    return added(keep, received)


def place_of(distance, bits):
    place = jnp.zeros_like(distance)
    for bit in bits:
        place = place * 2 + (distance & bit) // bit
    return place


def weight_sum(attn_t, grad_out, my_rank, bits):
    width = attn_t.shape[0]
    odd = my_rank & 1
    halves = attn_t.reshape(2, width // 2, attn_t.shape[1])

    def product(which):
        picked = lax.dynamic_index_in_dim(halves, which, 0, keepdims=False)
        return jnp.dot(picked, grad_out, preferred_element_type=jnp.float32)

    received = swap(product(1 - odd).astype(jnp.bfloat16), 1)
    total = product(odd) + received.astype(jnp.float32)
    pair_count = lax.axis_size("dp") // 2
    pair_rows = grad_out.shape[1] // pair_count
    sums = []
    for part, order in enumerate((bits[1:], bits[1:][::-1])):
        rows = total[part * width // 4 : (part + 1) * width // 4]
        pieces = {
            2 * pair: rows[:, pair * pair_rows : (pair + 1) * pair_rows]
            for pair in range(pair_count)
        }
        for bit in order:
            high = (my_rank & bit) > 0
            lows = [rank for rank in sorted(pieces) if not rank & bit]
            send = jnp.concatenate(
                [jnp.where(high, pieces[rank], pieces[rank | bit]) for rank in lows], axis=1
            )
            back = swap(send.astype(jnp.bfloat16), bit).astype(jnp.float32)
            pieces = {
                rank: jnp.where(high, pieces[rank | bit], pieces[rank])
                + back[:, at * pair_rows : (at + 1) * pair_rows]
                for at, rank in enumerate(lows)
            }
        sums.append(pieces[0])
    total = jnp.concatenate(sums, axis=0)
    first, second = total[:, : pair_rows // 2], total[:, pair_rows // 2 :]
    is_odd = odd > 0
    other = swap(jnp.where(is_odd, first, second).astype(jnp.bfloat16), 1).astype(jnp.float32)
    mine = jnp.where(is_odd, second, first)
    return jnp.concatenate(
        [jnp.where(is_odd, other, mine), jnp.where(is_odd, mine, other)], axis=0
    )


def local(query, key, value, grad_out, out_weight, plan, segments):
    rank_count = lax.axis_size("dp")
    my_rank = lax.axis_index("dp")
    my_lane = lax.axis_index("tensor")
    row_count = query.shape[0]
    block_count = row_count // ROWBLK
    local_heads = query.shape[1] // HD
    group = HEADS // KV
    bits = [1 << at for at in range(rank_count.bit_length() - 1)]
    kv_head = my_lane * local_heads // group
    own_key = lax.dynamic_slice_in_dim(key, kv_head * HD, HD, 1)
    own_value = lax.dynamic_slice_in_dim(value, kv_head * HD, HD, 1)

    own_places = positions_of(segments).reshape(block_count, ROWBLK)
    places_all = own_places
    for bit in bits:
        places_all = jnp.concatenate([places_all, swap(places_all, bit)], axis=0)
    values = spread(own_value, bits[1:] + bits[:1])
    up = jnp.dot(grad_out, out_weight, preferred_element_type=jnp.float32).astype(jnp.bfloat16)

    mine = my_rank * block_count + jnp.arange(block_count, dtype=jnp.int32)
    hit = plan[None, :] == mine[:, None]
    dest = jnp.sum(
        jnp.where(hit, jnp.arange(plan.shape[0], dtype=jnp.int32)[None, :], 0), axis=1
    )
    run = dest // RUN_BLOCKS
    slot = dest % RUN_BLOCKS
    places = jnp.take(places_all, (run ^ my_rank) * RUN_BLOCKS + slot, axis=0)
    need = slot - (slot * ROWBLK - places[:, 0]) // ROWBLK + 1
    cosine, sine = rope_tables(places.reshape(row_count), HD)
    key_f = own_key.astype(jnp.float32)
    rot_key = (key_f * cosine + swap_halves(key_f) * sine).astype(jnp.bfloat16)
    keys = spread(rot_key, bits[:0:-1] + bits[:1])

    distance = (plan // block_count) ^ my_rank
    within = plan % block_count
    key_bits = bits[:1] + bits[:0:-1]
    tables = (
        place_of(distance, key_bits) * block_count + within,
        place_of(distance, bits) * block_count + within,
        distance * block_count + within,
        run,
        slot,
        need,
    )
    grad_query, attn_t, gkey_keep, gkey_send, gvalue_keep, gvalue_send = attend(
        tables, query, up, cosine, sine, places, keys, values
    )
    value_partial = halve(gvalue_keep, gvalue_send, bits).astype(jnp.bfloat16)
    gkey = halve(gkey_keep, gkey_send, key_bits)
    key_partial = (gkey * cosine - swap_halves(gkey) * sine).astype(jnp.bfloat16)

    value_all = lane_gather(value_partial, my_lane)
    key_all = lane_gather(key_partial, my_lane)

    attn_t = lax.optimization_barrier((attn_t, key_partial, value_partial))[0]
    weight_grad = weight_sum(attn_t, grad_out, my_rank, bits).T
    lanes_per_key = group // local_heads

    def combine(gathered):
        if lanes_per_key == 1:
            return gathered
        merged = (
            gathered.astype(jnp.float32).reshape(row_count, KV, lanes_per_key, HD).sum(axis=2)
        )
        return merged.astype(jnp.bfloat16).reshape(row_count, KV * HD)

    return (grad_query, combine(key_all), combine(value_all), weight_grad * (1.0 / rank_count))


def solution(mesh):
    in_specs = (
        P("dp", "tensor"),
        P("dp", None),
        P("dp", None),
        P("dp", None),
        P(None, "tensor"),
        P(),
        P("dp"),
    )
    out_specs = (P("dp", "tensor"), P("dp", None), P("dp", None), P("dp", "tensor"))
    return jax.shard_map(local, mesh=mesh, in_specs=in_specs, out_specs=out_specs, check_vma=False)
```

```python
from functools import partial
import math

import jax
import jax.numpy as jnp
from jax import lax
from jax.experimental import pallas as pl
from jax.experimental.pallas import tpu as pltpu
from jax.sharding import PartitionSpec as P

KV = 4
HD = 128
HEADS = 16
ROWBLK = 128
RUN_BLOCKS = 8


rope_base = 1000000.0
yarn_factor = 4.0
yarn_context = 32768.0
beta_fast = 32.0
beta_slow = 1.0
masked_score = -1e30


def yarn_frequencies(head_size):
    half_size = head_size // 2

    def correction(rotations):
        return (
            head_size
            * math.log(yarn_context / (rotations * 2.0 * math.pi))
            / (2.0 * math.log(rope_base))
        )

    lower_bound = max(math.floor(correction(beta_fast)), 0)
    upper_bound = min(math.ceil(correction(beta_slow)), head_size - 1)
    ramp_span = max(upper_bound - lower_bound, 0.001)
    row_index = jnp.arange(half_size).astype(jnp.float32)
    extrap_freq = rope_base ** (-2.0 * row_index / head_size)
    interp_freq = extrap_freq / yarn_factor
    ramp_weight = jnp.clip((row_index - lower_bound) / ramp_span, 0.0, 1.0)
    return interp_freq * ramp_weight + extrap_freq * (1.0 - ramp_weight)


def positions_of(segments):
    row_count = segments.shape[-1]
    row_index = jnp.arange(row_count, dtype=jnp.int32)
    is_start = jnp.concatenate(
        [
            jnp.ones(segments.shape[:-1] + (1,), dtype=jnp.bool_),
            segments[..., 1:] != segments[..., :-1],
        ],
        axis=-1,
    )
    seg_start = lax.cummax(jnp.where(is_start, row_index, 0), axis=segments.ndim - 1)
    return row_index - seg_start


def rope_tables(places, head_size):
    angles = places.astype(jnp.float32)[:, None] * yarn_frequencies(head_size)[None, :]
    factor = 0.1 * math.log(yarn_factor) + 1.0
    cosine = jnp.cos(angles) * factor
    sine = jnp.sin(angles) * factor
    return (
        jnp.concatenate([cosine, cosine], axis=1),
        jnp.concatenate([-sine, sine], axis=1),
    )


def swap_halves(values):
    half = values.shape[-1] // 2
    return jnp.concatenate([values[..., half:], values[..., :half]], axis=-1)


NT = (((1,), (1,)), ((), ()))
TN = (((0,), (0,)), ((), ()))


def attend_kernel(
    heads,
    ranks,
    target_ref,
    source_ref,
    run_ref,
    slot_ref,
    need_ref,
    query_ref,
    up_ref,
    cos_ref,
    sin_ref,
    place_ref,
    *refs,
):
    key_parts, refs = refs[:ranks], refs[ranks:]
    value_parts, refs = refs[:ranks], refs[ranks:]
    gquery_ref, out_ref, gkey_keep, gkey_send, gvalue_keep, gvalue_send = refs[:6]
    key_ref, value_ref, gkey_ref, gvalue_ref, key_win, value_win, sems = refs[6:]
    rows_each = query_ref.shape[0]
    scale = 1.0 / math.sqrt(HD)
    to_exp2 = scale * math.log2(math.e)
    wide = min(2, heads)
    cols = wide * ROWBLK

    loads = []
    for item, (parts, whole) in enumerate(((key_parts, key_ref), (value_parts, value_ref))):
        for rank in range(ranks):
            copy = pltpu.make_async_copy(
                parts[rank], whole.at[pl.ds(rank * rows_each, rows_each)], sems.at[item, rank]
            )
            copy.start()
            loads.append(copy)
    gkey_ref[...] = jnp.zeros_like(gkey_ref)
    gvalue_ref[...] = jnp.zeros_like(gvalue_ref)
    for copy in loads:
        copy.wait()

    def window(count, block):
        slot = slot_ref[block]
        run = run_ref[block]
        first = jnp.maximum(slot + 1 - count, 0)
        rows = count * ROWBLK
        for step in range(count):
            source = source_ref[run * RUN_BLOCKS + first + step]
            start = pl.multiple_of(source * ROWBLK, ROWBLK)
            key_win[pl.ds(step * ROWBLK, ROWBLK), :] = key_ref[pl.ds(start, ROWBLK), :]
            value_win[pl.ds(step * ROWBLK, ROWBLK), :] = value_ref[pl.ds(start, ROWBLK), :]
        base = pl.multiple_of(block * ROWBLK, ROWBLK)
        cosine = cos_ref[pl.ds(base, ROWBLK), :]
        sine = sin_ref[pl.ds(base, ROWBLK), :]
        place = place_ref[pl.ds(block, 1), :]
        lane = lax.broadcasted_iota(jnp.int32, (1, ROWBLK), 1)
        last = (slot - first) * ROWBLK + lane
        last_all = jnp.concatenate([last] * wide, axis=1)
        start_all = jnp.concatenate([last - place] * wide, axis=1)
        key_index = lax.broadcasted_iota(jnp.int32, (rows, cols), 0)
        allowed = (key_index >= start_all) & (key_index <= last_all)
        keys = key_win[pl.ds(0, rows), :]
        values = value_win[pl.ds(0, rows), :]
        gkey = jnp.zeros((rows, HD), jnp.float32)
        gvalue = jnp.zeros((rows, HD), jnp.float32)
        for group in range(heads // wide):
            queries = []
            ups = []
            for item in range(wide):
                at = (group * wide + item) * HD
                raw = query_ref[pl.ds(base, ROWBLK), pl.ds(at, HD)].astype(jnp.float32)
                turned = raw * cosine + pltpu.roll(raw, HD // 2, 1) * sine
                queries.append(turned.astype(jnp.bfloat16))
                ups.append(up_ref[pl.ds(base, ROWBLK), pl.ds(at, HD)])
            query = jnp.concatenate(queries, axis=0)
            up = jnp.concatenate(ups, axis=0)
            up_t = jnp.concatenate([u.astype(jnp.float32).T for u in ups], axis=1)
            score = lax.dot_general(keys, query, NT, preferred_element_type=jnp.float32)
            score = jnp.where(allowed, score, masked_score)
            peak = jnp.max(score, axis=0, keepdims=True)
            raised = jnp.exp2((score - peak) * to_exp2)
            total = jnp.sum(raised, axis=0, keepdims=True)
            prob = raised * (1.0 / total)
            prob_b = prob.astype(jnp.bfloat16)
            out_t = lax.dot_general(values, prob_b, TN, preferred_element_type=jnp.float32)
            out_b = out_t.astype(jnp.bfloat16)
            delta = jnp.sum(up_t * out_b.astype(jnp.float32), axis=0, keepdims=True)
            gprob = lax.dot_general(values, up, NT, preferred_element_type=jnp.float32)
            gscore = (prob * (gprob - delta)).astype(jnp.bfloat16)
            gquery_t = lax.dot_general(keys, gscore, TN, preferred_element_type=jnp.float32)
            gkey = gkey + jnp.dot(gscore, query, preferred_element_type=jnp.float32)
            gvalue = gvalue + jnp.dot(prob_b, up, preferred_element_type=jnp.float32)
            for item in range(wide):
                at = (group * wide + item) * HD
                part = slice(item * ROWBLK, (item + 1) * ROWBLK)
                out_ref[pl.ds(at, HD), pl.ds(base, ROWBLK)] = out_b[:, part]
                grad = gquery_t[:, part].T * scale
                back = grad * cosine - pltpu.roll(grad, HD // 2, 1) * sine
                gquery_ref[pl.ds(base, ROWBLK), pl.ds(at, HD)] = back.astype(jnp.bfloat16)
        gkey = (gkey * scale).astype(jnp.bfloat16)
        gvalue = gvalue.astype(jnp.bfloat16)
        for step in range(count):
            block_id = run * RUN_BLOCKS + first + step
            part = slice(step * ROWBLK, (step + 1) * ROWBLK)
            start = pl.multiple_of(target_ref[block_id] * ROWBLK, ROWBLK)
            gkey_ref[pl.ds(start, ROWBLK), :] = gkey[part]
            gvalue_ref[pl.ds(start, ROWBLK), :] = gvalue[part]

    def body(block, carry):
        need = need_ref[block]
        floor = 0
        for size in (1, 2, 3, 4, 6, 8):
            pl.when((need > floor) & (need <= size))(partial(window, size, block))
            floor = size
        return carry

    lax.fori_loop(0, rows_each // ROWBLK, body, 0)
    half = ranks * rows_each // 2
    stores = []
    for item, (whole, keep, send) in enumerate(
        ((gkey_ref, gkey_keep, gkey_send), (gvalue_ref, gvalue_keep, gvalue_send))
    ):
        for place, target in enumerate((keep, send)):
            copy = pltpu.make_async_copy(
                whole.at[pl.ds(place * half, half)], target, sems.at[item, place]
            )
            copy.start()
            stores.append(copy)
    for copy in stores:
        copy.wait()


def attend(tables, query, up, cosine, sine, places, keys, values):
    rows, width = query.shape
    heads = width // HD
    ranks = len(keys)
    every = rows * ranks
    smem = pl.BlockSpec(memory_space=pltpu.SMEM)
    vmem = pl.BlockSpec(memory_space=pltpu.VMEM)
    hbm = pl.BlockSpec(memory_space=pl.ANY)
    pairs = rows * RUN_BLOCKS * ROWBLK * heads
    half = jax.ShapeDtypeStruct((every // 2, HD), jnp.bfloat16)
    return pl.pallas_call(
        partial(attend_kernel, heads, ranks),
        out_shape=(
            jax.ShapeDtypeStruct((rows, width), jnp.bfloat16),
            jax.ShapeDtypeStruct((width, rows), jnp.bfloat16),
            half,
            half,
            half,
            half,
        ),
        in_specs=[smem] * 5 + [vmem] * 5 + [hbm] * (2 * ranks),
        out_specs=(vmem, vmem, hbm, hbm, hbm, hbm),
        scratch_shapes=[pltpu.VMEM((every, HD), jnp.bfloat16)] * 4
        + [pltpu.VMEM((RUN_BLOCKS * ROWBLK, HD), jnp.bfloat16)] * 2
        + [pltpu.SemaphoreType.DMA((2, ranks))],
        compiler_params=pltpu.CompilerParams(vmem_limit_bytes=48 * 1024 * 1024),
        cost_estimate=pl.CostEstimate(
            flops=10 * pairs * HD, bytes_accessed=16 * 1024 * 1024, transcendentals=pairs
        ),
    )(*tables, query, up, cosine, sine, places, *keys, *values)


def assemble_kernel(count, column_ref, active_ref, *refs):
    out_ref, sems = refs[count:]

    def copy_of(index):
        column = pl.multiple_of(column_ref[index] * HD, HD)
        return pltpu.make_async_copy(
            refs[index], out_ref.at[:, pl.ds(column, HD)], sems.at[index]
        )

    for index in range(count):
        pl.when(active_ref[index] > 0)(lambda index=index: copy_of(index).start())
    for index in range(count):
        pl.when(active_ref[index] > 0)(lambda index=index: copy_of(index).wait())


def assemble(columns, active, pieces, lanes):
    rows = pieces[0].shape[0]
    smem = pl.BlockSpec(memory_space=pltpu.SMEM)
    vmem = pl.BlockSpec(memory_space=pltpu.VMEM)
    return pl.pallas_call(
        partial(assemble_kernel, len(pieces)),
        out_shape=jax.ShapeDtypeStruct((rows, lanes * HD), pieces[0].dtype),
        in_specs=[smem, smem] + [vmem] * len(pieces),
        out_specs=pl.BlockSpec(memory_space=pl.ANY),
        scratch_shapes=[pltpu.SemaphoreType.DMA((len(pieces),))],
        cost_estimate=pl.CostEstimate(
            flops=0, bytes_accessed=4 * rows * lanes * HD, transcendentals=0
        ),
    )(columns, active, *pieces)


def lane_gather(array, my_lane):
    lanes = lax.axis_size("tensor")

    def send(item, pairs):
        return lax.ppermute(item, "tensor", pairs)

    if lanes == 4:
        second = send(array, [(0, 2), (2, 0), (1, 3), (3, 1)])
        first = send(array, [(0, 1), (1, 0), (2, 3), (3, 2)])
        inner = send(array, [(1, 2), (2, 1)])
        outer = send(second, [(1, 0), (2, 3)])
        middle = (my_lane == 1) | (my_lane == 2)
        pieces = [array, first, second, inner, outer]
        columns = my_lane ^ jnp.array([0, 1, 2, 3, 3], jnp.int32)
        always = jnp.array([True, True, True, False, False])
        at_inner = jnp.array([False, False, False, True, False])
        active = always | (at_inner & middle) | (~always & ~at_inner & ~middle)
    else:
        pieces = [array]
        for unused in range(lanes - 1):
            pieces.append(send(pieces[-1], [(lane, (lane + 1) % lanes) for lane in range(lanes)]))
        columns = (my_lane - jnp.arange(lanes, dtype=jnp.int32)) % lanes
        active = jnp.ones((lanes,), jnp.bool_)
    return assemble(columns, active.astype(jnp.int32), pieces, lanes), pieces[1:]


def swap(array, bit):
    ranks = lax.axis_size("dp")
    return lax.ppermute(array, "dp", [(rank, rank ^ bit) for rank in range(ranks)])


def spread(array):
    found = [array, swap(array, 1)]
    others = [swap(array, step) for step in range(2, lax.axis_size("dp"), 2)]
    for other in others:
        found += [other, swap(other, 1)]
    return found


def added(left, right):
    return left.astype(jnp.float32) + right.astype(jnp.float32)


def chip_sum(keep, send):
    received = swap(send, 1)
    count = lax.axis_size("dp") // 2
    rows = keep.shape[0] // count
    total = [
        added(keep[at * rows : (at + 1) * rows], received[at * rows : (at + 1) * rows])
        for at in range(count)
    ]
    return total[0], [item.astype(keep.dtype) for item in total[1:]]


def exchange(sends):
    return [swap(item, 2 * at + 2) for at, item in enumerate(sends)]


def final_kernel(count, rotary, *refs):
    total = refs[0][...].astype(jnp.float32)
    for ref in refs[1 : 1 + count]:
        total = total + ref[...].astype(jnp.float32)
    if rotary:
        total = total * refs[1 + count][...] - pltpu.roll(total, HD // 2, 1) * refs[2 + count][...]
    out_ref = refs[-1]
    out_ref[...] = total.astype(out_ref.dtype)


def final_sum(keep, received, tables, after):
    vmem = pl.BlockSpec(memory_space=pltpu.VMEM)
    hbm = pl.BlockSpec(memory_space=pl.ANY)
    parts = [keep, *received, *tables]
    return pl.pallas_call(
        partial(final_kernel, len(received), len(tables) > 0),
        out_shape=jax.ShapeDtypeStruct(keep.shape, jnp.bfloat16),
        in_specs=[vmem] * len(parts) + [hbm] * len(after),
        out_specs=vmem,
        cost_estimate=pl.CostEstimate(
            flops=8 * keep.size, bytes_accessed=12 * keep.size, transcendentals=0
        ),
    )(*parts, *after)


def product_kernel(my_ref, left_ref, right_ref, *refs):
    total = jnp.dot(left_ref[...], right_ref[...], preferred_element_type=jnp.float32)
    refs[-1][0] = total.astype(refs[-1].dtype)


def product_sum_kernel(count, my_ref, left_ref, right_ref, base_ref, *refs):
    total = jnp.dot(left_ref[...], right_ref[...], preferred_element_type=jnp.float32)
    total = total + base_ref[0].astype(jnp.float32)
    for at, out_ref in enumerate(refs[-count:]):

        @pl.when(pl.program_id(0) == at)
        def store():
            out_ref[...] = total.astype(out_ref.dtype)


def product(mine, left, right, base, after):
    count = lax.axis_size("dp") // 2
    rows = left.shape[0]
    cols = right.shape[1] // count
    if cols % 128:
        total = jnp.dot(left, right, preferred_element_type=jnp.float32)
        pieces = jnp.moveaxis(total.reshape(rows, count, cols), 1, 0)
        pieces = jnp.take(pieces, jnp.arange(count, dtype=jnp.int32) ^ mine, axis=0)
        if base is None:
            return pieces.astype(jnp.bfloat16)
        pieces = pieces + base.astype(jnp.float32)
        return [pieces[0]] + [pieces[at].astype(jnp.bfloat16) for at in range(1, count)]
    stacked = pl.BlockSpec((1, rows, cols), lambda step, my_ref: (step, 0, 0))
    if base is None:
        body = product_kernel
        bases = []
        out_specs = stacked
        out_shape = jax.ShapeDtypeStruct((count, rows, cols), jnp.bfloat16)
    else:
        body = partial(product_sum_kernel, count)
        bases = [base]
        out_specs = [pl.BlockSpec((rows, cols), lambda step, my_ref: (0, 0))] * count
        out_shape = [
            jax.ShapeDtypeStruct((rows, cols), jnp.bfloat16 if at else jnp.float32)
            for at in range(count)
        ]
    return pl.pallas_call(
        body,
        grid_spec=pltpu.PrefetchScalarGridSpec(
            num_scalar_prefetch=1,
            grid=(count,),
            in_specs=[
                pl.BlockSpec(left.shape, lambda step, my_ref: (0, 0)),
                pl.BlockSpec((right.shape[0], cols), lambda step, my_ref: (0, step ^ my_ref[0])),
            ]
            + [stacked] * len(bases)
            + [pl.BlockSpec(memory_space=pl.ANY)] * len(after),
            out_specs=out_specs,
        ),
        out_shape=out_shape,
        compiler_params=pltpu.CompilerParams(vmem_limit_bytes=32 * 1024 * 1024),
        cost_estimate=pl.CostEstimate(
            flops=2 * rows * right.size, bytes_accessed=2 * right.size, transcendentals=0
        ),
    )(mine.reshape(1), left, right, *bases, *after)


def local(query, key, value, grad_out, out_weight, plan, segments):
    rank_count = lax.axis_size("dp")
    my_rank = lax.axis_index("dp")
    my_lane = lax.axis_index("tensor")
    row_count = query.shape[0]
    block_count = row_count // ROWBLK
    local_heads = query.shape[1] // HD
    group = HEADS // KV
    bits = [1 << at for at in range(rank_count.bit_length() - 1)]
    kv_head = my_lane * local_heads // group
    own_key = lax.dynamic_slice_in_dim(key, kv_head * HD, HD, 1)
    own_value = lax.dynamic_slice_in_dim(value, kv_head * HD, HD, 1)

    own_places = positions_of(segments).reshape(1, block_count, ROWBLK)
    pair_places = jnp.concatenate([own_places, swap(own_places, 1)], axis=0)
    places_all = jnp.concatenate(
        [pair_places] + [swap(pair_places, step) for step in range(2, rank_count, 2)], axis=0
    ).reshape(-1, ROWBLK)
    values = spread(own_value)
    up = jnp.dot(grad_out, out_weight, preferred_element_type=jnp.float32).astype(jnp.bfloat16)

    mine = my_rank * block_count + jnp.arange(block_count, dtype=jnp.int32)
    hit = plan[None, :] == mine[:, None]
    dest = jnp.sum(
        jnp.where(hit, jnp.arange(plan.shape[0], dtype=jnp.int32)[None, :], 0), axis=1
    )
    run = dest // RUN_BLOCKS
    slot = dest % RUN_BLOCKS
    places = jnp.take(places_all, (run ^ my_rank) * RUN_BLOCKS + slot, axis=0)
    need = slot - (slot * ROWBLK - places[:, 0]) // ROWBLK + 1
    cosine, sine = rope_tables(places.reshape(row_count), HD)
    key_f = own_key.astype(jnp.float32)
    rot_key = (key_f * cosine + swap_halves(key_f) * sine).astype(jnp.bfloat16)
    keys = spread(rot_key)

    distance = (plan // block_count) ^ my_rank
    within = plan % block_count
    half_place = (distance & 1) * (rank_count // 2) + distance // 2
    tables = (
        half_place * block_count + within,
        distance * block_count + within,
        run,
        slot,
        need,
    )
    grad_query, attn_t, gkey_keep, gkey_send, gvalue_keep, gvalue_send = attend(
        tables, query, up, cosine, sine, places, keys, values
    )
    value_keep, value_sends = chip_sum(gvalue_keep, gvalue_send)
    value_received = exchange(value_sends)
    key_keep, key_sends = chip_sum(gkey_keep, gkey_send)
    key_received = exchange(key_sends)

    width = attn_t.shape[0]
    odd = my_rank & 1
    halves = attn_t.reshape(2, width // 2, row_count)
    pair_rows = grad_out.shape[1] // (rank_count // 2)

    def half_of(which):
        return lax.dynamic_index_in_dim(halves, which, 0, keepdims=False)

    first = swap(product(my_rank // 2, half_of(1 - odd), grad_out, None, key_sends), 1)
    value_partial = final_sum(value_keep, value_received, (), ())
    value_all, value_pieces = lane_gather(value_partial, my_lane)
    kept, *sends = product(my_rank // 2, half_of(odd), grad_out, first, [value_partial])
    key_partial = final_sum(key_keep, key_received, (cosine, sine), [sends[0], value_pieces[0]])
    key_all, key_pieces = lane_gather(key_partial, my_lane)
    total = kept
    for item in exchange(sends):
        total = total + item.astype(jnp.float32)
    low, high = total[:, : pair_rows // 2], total[:, pair_rows // 2 :]
    is_odd = odd > 0
    other = swap(jnp.where(is_odd, low, high).astype(jnp.bfloat16), 1).astype(jnp.float32)
    mine_half = jnp.where(is_odd, high, low)
    weight_grad = jnp.concatenate(
        [jnp.where(is_odd, other, mine_half), jnp.where(is_odd, mine_half, other)], axis=0
    ).T
    lanes_per_key = group // local_heads

    def combine(gathered):
        if lanes_per_key == 1:
            return gathered
        merged = (
            gathered.astype(jnp.float32).reshape(row_count, KV, lanes_per_key, HD).sum(axis=2)
        )
        return merged.astype(jnp.bfloat16).reshape(row_count, KV * HD)

    return (grad_query, combine(key_all), combine(value_all), weight_grad * (1.0 / rank_count))


def solution(mesh):
    in_specs = (
        P("dp", "tensor"),
        P("dp", None),
        P("dp", None),
        P("dp", None),
        P(None, "tensor"),
        P(),
        P("dp"),
    )
    out_specs = (P("dp", "tensor"), P("dp", None), P("dp", None), P("dp", "tensor"))
    return jax.shard_map(local, mesh=mesh, in_specs=in_specs, out_specs=out_specs, check_vma=False)
```

```python
from functools import partial
import math

import jax
import jax.numpy as jnp
from jax import lax
from jax.experimental import pallas as pl
from jax.experimental.pallas import tpu as pltpu
from jax.sharding import PartitionSpec as P

KV = 4
HD = 128
HEADS = 16
ROWBLK = 128
RUN_BLOCKS = 8
VMEM_BYTES = 58 * 1024 * 1024
NO_COST = pl.CostEstimate(flops=0, bytes_accessed=0, transcendentals=0)


rope_base = 1000000.0
yarn_factor = 4.0
yarn_context = 32768.0
beta_fast = 32.0
beta_slow = 1.0
masked_score = -1e30


def yarn_frequencies(head_size):
    half_size = head_size // 2

    def correction(rotations):
        return (
            head_size
            * math.log(yarn_context / (rotations * 2.0 * math.pi))
            / (2.0 * math.log(rope_base))
        )

    lower_bound = max(math.floor(correction(beta_fast)), 0)
    upper_bound = min(math.ceil(correction(beta_slow)), head_size - 1)
    ramp_span = max(upper_bound - lower_bound, 0.001)
    row_index = jnp.arange(half_size).astype(jnp.float32)
    extrap_freq = rope_base ** (-2.0 * row_index / head_size)
    interp_freq = extrap_freq / yarn_factor
    ramp_weight = jnp.clip((row_index - lower_bound) / ramp_span, 0.0, 1.0)
    return interp_freq * ramp_weight + extrap_freq * (1.0 - ramp_weight)


def positions_of(segments):
    row_count = segments.shape[-1]
    row_index = jnp.arange(row_count, dtype=jnp.int32)
    is_start = jnp.concatenate(
        [
            jnp.ones(segments.shape[:-1] + (1,), dtype=jnp.bool_),
            segments[..., 1:] != segments[..., :-1],
        ],
        axis=-1,
    )
    seg_start = lax.cummax(jnp.where(is_start, row_index, 0), axis=segments.ndim - 1)
    return row_index - seg_start


def rope_tables(places, head_size):
    angles = places.astype(jnp.float32)[:, None] * yarn_frequencies(head_size)[None, :]
    factor = 0.1 * math.log(yarn_factor) + 1.0
    cosine = jnp.cos(angles) * factor
    sine = jnp.sin(angles) * factor
    return (
        jnp.concatenate([cosine, cosine], axis=1),
        jnp.concatenate([-sine, sine], axis=1),
    )


def swap_halves(values):
    half = values.shape[-1] // 2
    return jnp.concatenate([values[..., half:], values[..., :half]], axis=-1)


NT = (((1,), (1,)), ((), ()))
TN = (((0,), (0,)), ((), ()))


def attend_kernel(
    heads,
    ranks,
    target_ref,
    source_ref,
    run_ref,
    slot_ref,
    need_ref,
    odd_ref,
    query_ref,
    up_ref,
    cos_ref,
    sin_ref,
    place_ref,
    *refs,
):
    key_parts, refs = refs[:ranks], refs[ranks:]
    value_parts, refs = refs[:ranks], refs[ranks:]
    gquery_ref, out_ref, gkey_keep, gkey_send, gvalue_keep, gvalue_send = refs[:6]
    key_ref, value_ref, gkey_ref, gvalue_ref, key_win, value_win, sems = refs[6:]
    rows_each = query_ref.shape[0]
    scale = 1.0 / math.sqrt(HD)
    to_exp2 = scale * math.log2(math.e)
    wide = min(2, heads)
    cols = wide * ROWBLK

    loads = []
    for item, (parts, whole) in enumerate(((key_parts, key_ref), (value_parts, value_ref))):
        for rank in range(ranks):
            copy = pltpu.make_async_copy(
                parts[rank], whole.at[pl.ds(rank * rows_each, rows_each)], sems.at[item, rank]
            )
            copy.start()
            loads.append(copy)
    gkey_ref[...] = jnp.zeros_like(gkey_ref)
    gvalue_ref[...] = jnp.zeros_like(gvalue_ref)
    for copy in loads:
        copy.wait()

    def window(count, block):
        slot = slot_ref[block]
        run = run_ref[block]
        first = jnp.maximum(slot + 1 - count, 0)
        rows = count * ROWBLK
        for step in range(count):
            source = source_ref[run * RUN_BLOCKS + first + step]
            start = pl.multiple_of(source * ROWBLK, ROWBLK)
            key_win[pl.ds(step * ROWBLK, ROWBLK), :] = key_ref[pl.ds(start, ROWBLK), :]
            value_win[pl.ds(step * ROWBLK, ROWBLK), :] = value_ref[pl.ds(start, ROWBLK), :]
        base = pl.multiple_of(block * ROWBLK, ROWBLK)
        cosine = cos_ref[pl.ds(base, ROWBLK), :]
        sine = sin_ref[pl.ds(base, ROWBLK), :]
        place = place_ref[pl.ds(block, 1), :]
        lane = lax.broadcasted_iota(jnp.int32, (1, ROWBLK), 1)
        last = (slot - first) * ROWBLK + lane
        last_all = jnp.concatenate([last] * wide, axis=1)
        start_all = jnp.concatenate([last - place] * wide, axis=1)
        key_index = lax.broadcasted_iota(jnp.int32, (rows, cols), 0)
        allowed = (key_index >= start_all) & (key_index <= last_all)
        keys = key_win[pl.ds(0, rows), :]
        values = value_win[pl.ds(0, rows), :]
        gkey = jnp.zeros((rows, HD), jnp.float32)
        gvalue = jnp.zeros((rows, HD), jnp.float32)
        for group in range(heads // wide):
            queries = []
            ups = []
            for item in range(wide):
                at = (group * wide + item) * HD
                raw = query_ref[pl.ds(base, ROWBLK), pl.ds(at, HD)].astype(jnp.float32)
                turned = raw * cosine + pltpu.roll(raw, HD // 2, 1) * sine
                queries.append(turned.astype(jnp.bfloat16))
                ups.append(up_ref[pl.ds(base, ROWBLK), pl.ds(at, HD)])
            query = jnp.concatenate(queries, axis=0)
            up = jnp.concatenate(ups, axis=0)
            up_t = jnp.concatenate([u.astype(jnp.float32).T for u in ups], axis=1)
            score = lax.dot_general(keys, query, NT, preferred_element_type=jnp.float32)
            score = jnp.where(allowed, score, masked_score)
            peak = jnp.max(score, axis=0, keepdims=True)
            raised = jnp.exp2((score - peak) * to_exp2)
            total = jnp.sum(raised, axis=0, keepdims=True)
            prob = raised * (1.0 / total)
            prob_b = prob.astype(jnp.bfloat16)
            out_t = lax.dot_general(values, prob_b, TN, preferred_element_type=jnp.float32)
            out_b = out_t.astype(jnp.bfloat16)
            delta = jnp.sum(up_t * out_b.astype(jnp.float32), axis=0, keepdims=True)
            gprob = lax.dot_general(values, up, NT, preferred_element_type=jnp.float32)
            gscore = (prob * (gprob - delta)).astype(jnp.bfloat16)
            gquery_t = lax.dot_general(keys, gscore, TN, preferred_element_type=jnp.float32)
            gkey = gkey + jnp.dot(gscore, query, preferred_element_type=jnp.float32)
            gvalue = gvalue + jnp.dot(prob_b, up, preferred_element_type=jnp.float32)
            for item in range(wide):
                at = (group * wide + item) * HD
                part = slice(item * ROWBLK, (item + 1) * ROWBLK)
                head = group * wide + item
                half, row = head * 2 // heads, head % (heads // 2) * HD
                out_ref[half ^ odd_ref[0], pl.ds(row, HD), pl.ds(base, ROWBLK)] = out_b[:, part]
                grad = gquery_t[:, part].T * scale
                back = grad * cosine - pltpu.roll(grad, HD // 2, 1) * sine
                gquery_ref[pl.ds(base, ROWBLK), pl.ds(at, HD)] = back.astype(jnp.bfloat16)
        gkey = (gkey * scale).astype(jnp.bfloat16)
        gvalue = gvalue.astype(jnp.bfloat16)
        for step in range(count):
            block_id = run * RUN_BLOCKS + first + step
            part = slice(step * ROWBLK, (step + 1) * ROWBLK)
            start = pl.multiple_of(target_ref[block_id] * ROWBLK, ROWBLK)
            gkey_ref[pl.ds(start, ROWBLK), :] = gkey[part]
            gvalue_ref[pl.ds(start, ROWBLK), :] = gvalue[part]

    def body(block, carry):
        need = need_ref[block]
        floor = 0
        for size in (1, 2, 3, 4, 6, 8):
            pl.when((need > floor) & (need <= size))(partial(window, size, block))
            floor = size
        return carry

    lax.fori_loop(0, rows_each // ROWBLK, body, 0)
    half = ranks * rows_each // 2
    stores = []
    for item, (whole, keep, send) in enumerate(
        ((gkey_ref, gkey_keep, gkey_send), (gvalue_ref, gvalue_keep, gvalue_send))
    ):
        for place, target in enumerate((keep, send)):
            copy = pltpu.make_async_copy(
                whole.at[pl.ds(place * half, half)], target, sems.at[item, place]
            )
            copy.start()
            stores.append(copy)
    for copy in stores:
        copy.wait()


def attend(tables, query, up, cosine, sine, places, keys, values):
    rows, width = query.shape
    heads = width // HD
    ranks = len(keys)
    every = rows * ranks
    smem = pl.BlockSpec(memory_space=pltpu.SMEM)
    vmem = pl.BlockSpec(memory_space=pltpu.VMEM)
    hbm = pl.BlockSpec(memory_space=pl.ANY)
    half = jax.ShapeDtypeStruct((every // 2, HD), jnp.bfloat16)
    return pl.pallas_call(
        partial(attend_kernel, heads, ranks),
        out_shape=(
            jax.ShapeDtypeStruct((rows, width), jnp.bfloat16),
            jax.ShapeDtypeStruct((2, width // 2, rows), jnp.bfloat16),
            half,
            half,
            half,
            half,
        ),
        in_specs=[smem] * 6 + [vmem] * 5 + [hbm] * (2 * ranks),
        out_specs=(vmem, vmem, hbm, hbm, hbm, hbm),
        scratch_shapes=[pltpu.VMEM((every, HD), jnp.bfloat16)] * 4
        + [pltpu.VMEM((RUN_BLOCKS * ROWBLK, HD), jnp.bfloat16)] * 2
        + [pltpu.SemaphoreType.DMA((2, ranks))],
        compiler_params=pltpu.CompilerParams(vmem_limit_bytes=VMEM_BYTES),
        cost_estimate=NO_COST,
    )(*tables, query, up, cosine, sine, places, *keys, *values)


def assemble_kernel(count, column_ref, active_ref, *refs):
    out_ref, sems = refs[count:]

    def copy_of(index):
        column = pl.multiple_of(column_ref[index] * HD, HD)
        return pltpu.make_async_copy(
            refs[index], out_ref.at[:, pl.ds(column, HD)], sems.at[index]
        )

    for index in range(count):
        pl.when(active_ref[index] > 0)(lambda index=index: copy_of(index).start())
    for index in range(count):
        pl.when(active_ref[index] > 0)(lambda index=index: copy_of(index).wait())


def assemble(columns, active, pieces, lanes):
    rows = pieces[0].shape[0]
    smem = pl.BlockSpec(memory_space=pltpu.SMEM)
    vmem = pl.BlockSpec(memory_space=pltpu.VMEM)
    return pl.pallas_call(
        partial(assemble_kernel, len(pieces)),
        out_shape=jax.ShapeDtypeStruct((rows, lanes * HD), pieces[0].dtype),
        in_specs=[smem, smem] + [vmem] * len(pieces),
        out_specs=pl.BlockSpec(memory_space=pl.ANY),
        scratch_shapes=[pltpu.SemaphoreType.DMA((len(pieces),))],
        compiler_params=pltpu.CompilerParams(vmem_limit_bytes=VMEM_BYTES),
        cost_estimate=NO_COST,
    )(columns, active, *pieces)


def lane_gather(array, my_lane):
    lanes = lax.axis_size("tensor")

    def send(item, pairs):
        return lax.ppermute(item, "tensor", pairs)

    if lanes == 4:
        second = send(array, [(0, 2), (2, 0), (1, 3), (3, 1)])
        first = send(array, [(0, 1), (1, 0), (2, 3), (3, 2)])
        inner = send(array, [(1, 2), (2, 1)])
        outer = send(second, [(1, 0), (2, 3)])
        middle = (my_lane == 1) | (my_lane == 2)
        pieces = [array, first, second, inner, outer]
        columns = my_lane ^ jnp.array([0, 1, 2, 3, 3], jnp.int32)
        always = jnp.array([True, True, True, False, False])
        at_inner = jnp.array([False, False, False, True, False])
        active = always | (at_inner & middle) | (~always & ~at_inner & ~middle)
    else:
        pieces = [array]
        for unused in range(lanes - 1):
            pieces.append(send(pieces[-1], [(lane, (lane + 1) % lanes) for lane in range(lanes)]))
        columns = (my_lane - jnp.arange(lanes, dtype=jnp.int32)) % lanes
        active = jnp.ones((lanes,), jnp.bool_)
    return assemble(columns, active.astype(jnp.int32), pieces, lanes), pieces[1:]


def swap(array, bit):
    ranks = lax.axis_size("dp")
    return lax.ppermute(array, "dp", [(rank, rank ^ bit) for rank in range(ranks)])


def spread(array):
    found = [array, swap(array, 1)]
    others = [swap(array, step) for step in range(2, lax.axis_size("dp"), 2)]
    for other in others:
        found += [other, swap(other, 1)]
    return found


def added(left, right):
    return left.astype(jnp.float32) + right.astype(jnp.float32)


def chip_sum(keep, send):
    received = swap(send, 1)
    count = lax.axis_size("dp") // 2
    rows = keep.shape[0] // count
    total = [
        added(keep[at * rows : (at + 1) * rows], received[at * rows : (at + 1) * rows])
        for at in range(count)
    ]
    return total[0], [item.astype(keep.dtype) for item in total[1:]]


def exchange(sends):
    return [swap(item, 2 * at + 2) for at, item in enumerate(sends)]


def final_kernel(count, rotary, *refs):
    total = refs[0][...].astype(jnp.float32)
    for ref in refs[1 : 1 + count]:
        total = total + ref[...].astype(jnp.float32)
    if rotary:
        total = total * refs[1 + count][...] - pltpu.roll(total, HD // 2, 1) * refs[2 + count][...]
    out_ref = refs[-1]
    out_ref[...] = total.astype(out_ref.dtype)


def final_sum(keep, received, tables, after, kind=jnp.bfloat16):
    vmem = pl.BlockSpec(memory_space=pltpu.VMEM)
    hbm = pl.BlockSpec(memory_space=pl.ANY)
    parts = [keep, *received, *tables]
    return pl.pallas_call(
        partial(final_kernel, len(received), len(tables) > 0),
        out_shape=jax.ShapeDtypeStruct(keep.shape, kind),
        in_specs=[vmem] * len(parts) + [hbm] * len(after),
        out_specs=vmem,
        compiler_params=pltpu.CompilerParams(vmem_limit_bytes=VMEM_BYTES),
        cost_estimate=NO_COST,
    )(*parts, *after)


def up_kernel(rows_ref, weight_ref, *refs):
    total = jnp.dot(rows_ref[...], weight_ref[...], preferred_element_type=jnp.float32)
    refs[-1][...] = total.astype(refs[-1].dtype)


def up_product(rows, weight, after):
    height, depth = rows.shape
    steps = 4
    return pl.pallas_call(
        up_kernel,
        grid=(steps,),
        out_shape=jax.ShapeDtypeStruct((height, weight.shape[1]), jnp.bfloat16),
        in_specs=[
            pl.BlockSpec((height // steps, depth), lambda step: (step, 0)),
            pl.BlockSpec(weight.shape, lambda step: (0, 0)),
        ]
        + [pl.BlockSpec(memory_space=pl.ANY)] * len(after),
        out_specs=pl.BlockSpec((height // steps, weight.shape[1]), lambda step: (step, 0)),
        compiler_params=pltpu.CompilerParams(vmem_limit_bytes=VMEM_BYTES),
        cost_estimate=NO_COST,
    )(rows, weight, *after)


def product_kernel(my_ref, left_ref, right_ref, thru_ref, out_ref, unused):
    total = jnp.dot(left_ref[0], right_ref[...], preferred_element_type=jnp.float32)
    out_ref[0] = total.astype(out_ref.dtype)


def product_sum_kernel(count, my_ref, left_ref, right_ref, base_ref, *refs):
    total = jnp.dot(left_ref[0], right_ref[...], preferred_element_type=jnp.float32)
    total = total + base_ref[0].astype(jnp.float32)
    for at, out_ref in enumerate(refs[-count:]):

        @pl.when(pl.program_id(0) == at)
        def store():
            out_ref[...] = total.astype(out_ref.dtype)


def product_specs(left, which, right):
    count = lax.axis_size("dp") // 2
    rows, cols = left.shape[1], right.shape[1] // count
    stacked = pl.BlockSpec((1, rows, cols), lambda step, my_ref: (step, 0, 0))
    ins = [
        pl.BlockSpec((1,) + left.shape[1:], lambda step, my_ref: (which, 0, 0)),
        pl.BlockSpec((right.shape[0], cols), lambda step, my_ref: (0, step ^ my_ref[0])),
    ]
    return count, rows, cols, stacked, ins


def plain_pieces(mine, left, right):
    count = lax.axis_size("dp") // 2
    total = jnp.dot(left, right, preferred_element_type=jnp.float32)
    pieces = jnp.moveaxis(total.reshape(left.shape[0], count, -1), 1, 0)
    return jnp.take(pieces, jnp.arange(count, dtype=jnp.int32) ^ mine, axis=0)


def product(mine, left, right, thru):
    count, rows, cols, stacked, ins = product_specs(left, 1, right)
    if cols % 128:
        return plain_pieces(mine, left[1], right).astype(jnp.bfloat16), thru
    hbm = pl.BlockSpec(memory_space=pl.ANY)
    return pl.pallas_call(
        product_kernel,
        grid_spec=pltpu.PrefetchScalarGridSpec(
            num_scalar_prefetch=1, grid=(count,), in_specs=ins + [hbm], out_specs=[stacked, hbm]
        ),
        out_shape=[
            jax.ShapeDtypeStruct((count, rows, cols), jnp.bfloat16),
            jax.ShapeDtypeStruct(thru.shape, thru.dtype),
        ],
        input_output_aliases={3: 1},
        compiler_params=pltpu.CompilerParams(vmem_limit_bytes=VMEM_BYTES),
        cost_estimate=NO_COST,
    )(mine.reshape(1), left, right, thru)


def product_sum(mine, left, right, base, after):
    count, rows, cols, stacked, ins = product_specs(left, 0, right)
    if cols % 128:
        pieces = plain_pieces(mine, left[0], right) + base.astype(jnp.float32)
        return [pieces[0]] + [pieces[at].astype(jnp.bfloat16) for at in range(1, count)]
    return pl.pallas_call(
        partial(product_sum_kernel, count),
        grid_spec=pltpu.PrefetchScalarGridSpec(
            num_scalar_prefetch=1,
            grid=(count,),
            in_specs=ins + [stacked] + [pl.BlockSpec(memory_space=pl.ANY)] * len(after),
            out_specs=[pl.BlockSpec((rows, cols), lambda step, my_ref: (0, 0))] * count,
        ),
        out_shape=[
            jax.ShapeDtypeStruct((rows, cols), jnp.bfloat16 if at else jnp.float32)
            for at in range(count)
        ],
        compiler_params=pltpu.CompilerParams(vmem_limit_bytes=VMEM_BYTES),
        cost_estimate=NO_COST,
    )(mine.reshape(1), left, right, base, *after)


def local(query, key, value, grad_out, out_weight, plan, segments):
    rank_count = lax.axis_size("dp")
    my_rank = lax.axis_index("dp")
    my_lane = lax.axis_index("tensor")
    row_count = query.shape[0]
    block_count = row_count // ROWBLK
    local_heads = query.shape[1] // HD
    group = HEADS // KV
    bits = [1 << at for at in range(rank_count.bit_length() - 1)]
    kv_head = my_lane * local_heads // group
    own_key = lax.dynamic_slice_in_dim(key, kv_head * HD, HD, 1)
    own_value = lax.dynamic_slice_in_dim(value, kv_head * HD, HD, 1)

    own_places = positions_of(segments).reshape(1, block_count, ROWBLK)
    places_all = lax.all_to_all(
        jnp.broadcast_to(own_places, (rank_count, block_count, ROWBLK)),
        "dp",
        split_axis=0,
        concat_axis=0,
        tiled=True,
    ).reshape(-1, ROWBLK)
    values = spread(own_value)

    mine = my_rank * block_count + jnp.arange(block_count, dtype=jnp.int32)
    hit = plan[None, :] == mine[:, None]
    dest = jnp.sum(
        jnp.where(hit, jnp.arange(plan.shape[0], dtype=jnp.int32)[None, :], 0), axis=1
    )
    run = dest // RUN_BLOCKS
    slot = dest % RUN_BLOCKS
    places = jnp.take(places_all, dest, axis=0)
    need = slot - (slot * ROWBLK - places[:, 0]) // ROWBLK + 1
    cosine, sine = rope_tables(places.reshape(row_count), HD)
    key_f = own_key.astype(jnp.float32)
    rot_key = (key_f * cosine + swap_halves(key_f) * sine).astype(jnp.bfloat16)
    keys = spread(rot_key)
    up = up_product(grad_out, out_weight, [rot_key])

    distance = (plan // block_count) ^ my_rank
    within = plan % block_count
    half_place = (distance & 1) * (rank_count // 2) + distance // 2
    tables = (
        half_place * block_count + within,
        distance * block_count + within,
        run,
        slot,
        need,
        (my_rank & 1).reshape(1),
    )
    grad_query, attn_t, gkey_keep, gkey_send, gvalue_keep, gvalue_send = attend(
        tables, query, up, cosine, sine, places, keys, values
    )
    mine_pair = my_rank // 2
    value_keep, value_sends = chip_sum(gvalue_keep, gvalue_send)
    value_received = exchange(value_sends)
    first, gkey_keep = product(mine_pair, attn_t, grad_out, gkey_keep)
    first = swap(first, 1)
    key_keep, key_sends = chip_sum(gkey_keep, gkey_send)
    key_received = exchange(key_sends)
    value_partial = final_sum(value_keep, value_received, (), key_sends)
    value_all, value_pieces = lane_gather(value_partial, my_lane)
    kept, *sends = product_sum(mine_pair, attn_t, grad_out, first, [value_partial])
    received = exchange(sends)
    key_partial = final_sum(
        key_keep, key_received, (cosine, sine), [sends[0], value_pieces[0], value_pieces[2]]
    )
    key_all, key_pieces = lane_gather(key_partial, my_lane)
    total = final_sum(kept, received, (), key_pieces[:3] + value_pieces[3:], jnp.float32)
    odd = my_rank & 1
    pair_rows = grad_out.shape[1] // (rank_count // 2)
    low, high = total[:, : pair_rows // 2], total[:, pair_rows // 2 :]
    is_odd = odd > 0
    other = swap(jnp.where(is_odd, low, high).astype(jnp.bfloat16), 1).astype(jnp.float32)
    mine_half = jnp.where(is_odd, high, low)
    weight_grad = jnp.concatenate(
        [jnp.where(is_odd, other, mine_half), jnp.where(is_odd, mine_half, other)], axis=0
    ).T
    lanes_per_key = group // local_heads

    def combine(gathered):
        if lanes_per_key == 1:
            return gathered
        merged = (
            gathered.astype(jnp.float32).reshape(row_count, KV, lanes_per_key, HD).sum(axis=2)
        )
        return merged.astype(jnp.bfloat16).reshape(row_count, KV * HD)

    return (grad_query, combine(key_all), combine(value_all), weight_grad * (1.0 / rank_count))


def solution(mesh):
    in_specs = (
        P("dp", "tensor"),
        P("dp", None),
        P("dp", None),
        P("dp", None),
        P(None, "tensor"),
        P(),
        P("dp"),
    )
    out_specs = (P("dp", "tensor"), P("dp", None), P("dp", None), P("dp", "tensor"))
    return jax.shard_map(local, mesh=mesh, in_specs=in_specs, out_specs=out_specs, check_vma=False)
```

```python
from functools import partial
import math

import jax
import jax.numpy as jnp
from jax import lax
from jax.experimental import pallas as pl
from jax.experimental.pallas import tpu as pltpu
from jax.sharding import PartitionSpec as P

KV = 4
HD = 128
HEADS = 16
ROWBLK = 128
RUN_BLOCKS = 8
VMEM_BYTES = 58 * 1024 * 1024
NO_COST = pl.CostEstimate(flops=0, bytes_accessed=0, transcendentals=0)


rope_base = 1000000.0
yarn_factor = 4.0
yarn_context = 32768.0
beta_fast = 32.0
beta_slow = 1.0
masked_score = -1e30


def yarn_frequencies(head_size):
    half_size = head_size // 2

    def correction(rotations):
        return (
            head_size
            * math.log(yarn_context / (rotations * 2.0 * math.pi))
            / (2.0 * math.log(rope_base))
        )

    lower_bound = max(math.floor(correction(beta_fast)), 0)
    upper_bound = min(math.ceil(correction(beta_slow)), head_size - 1)
    ramp_span = max(upper_bound - lower_bound, 0.001)
    row_index = jnp.arange(half_size).astype(jnp.float32)
    extrap_freq = rope_base ** (-2.0 * row_index / head_size)
    interp_freq = extrap_freq / yarn_factor
    ramp_weight = jnp.clip((row_index - lower_bound) / ramp_span, 0.0, 1.0)
    return interp_freq * ramp_weight + extrap_freq * (1.0 - ramp_weight)


def positions_of(segments):
    row_count = segments.shape[-1]
    row_index = jnp.arange(row_count, dtype=jnp.int32)
    is_start = jnp.concatenate(
        [
            jnp.ones(segments.shape[:-1] + (1,), dtype=jnp.bool_),
            segments[..., 1:] != segments[..., :-1],
        ],
        axis=-1,
    )
    seg_start = lax.cummax(jnp.where(is_start, row_index, 0), axis=segments.ndim - 1)
    return row_index - seg_start


def rope_tables(places, head_size):
    angles = places.astype(jnp.float32)[:, None] * yarn_frequencies(head_size)[None, :]
    factor = 0.1 * math.log(yarn_factor) + 1.0
    cosine = jnp.cos(angles) * factor
    sine = jnp.sin(angles) * factor
    return (
        jnp.concatenate([cosine, cosine], axis=1),
        jnp.concatenate([-sine, sine], axis=1),
    )


def swap_halves(values):
    half = values.shape[-1] // 2
    return jnp.concatenate([values[..., half:], values[..., :half]], axis=-1)


NT = (((1,), (1,)), ((), ()))
TN = (((0,), (0,)), ((), ()))


def attend_kernel(
    heads,
    ranks,
    target_ref,
    source_ref,
    run_ref,
    slot_ref,
    need_ref,
    odd_ref,
    query_ref,
    up_ref,
    cos_ref,
    sin_ref,
    place_ref,
    *refs,
):
    key_parts, refs = refs[:ranks], refs[ranks:]
    value_parts, refs = refs[:ranks], refs[ranks:]
    gquery_ref, out_ref, gkey_keep, gkey_send, gvalue_keep, gvalue_send = refs[:6]
    key_ref, value_ref, gkey_ref, gvalue_ref, key_win, value_win, sems = refs[6:]
    rows_each = query_ref.shape[0]
    scale = 1.0 / math.sqrt(HD)
    to_exp2 = scale * math.log2(math.e)
    wide = min(2, heads)
    cols = wide * ROWBLK

    loads = []
    for item, (parts, whole) in enumerate(((key_parts, key_ref), (value_parts, value_ref))):
        for rank in range(ranks):
            copy = pltpu.make_async_copy(
                parts[rank], whole.at[pl.ds(rank * rows_each, rows_each)], sems.at[item, rank]
            )
            copy.start()
            loads.append(copy)
    gkey_ref[...] = jnp.zeros_like(gkey_ref)
    gvalue_ref[...] = jnp.zeros_like(gvalue_ref)
    for copy in loads:
        copy.wait()

    def window(count, block):
        slot = slot_ref[block]
        run = run_ref[block]
        first = jnp.maximum(slot + 1 - count, 0)
        rows = count * ROWBLK
        for step in range(count):
            source = source_ref[run * RUN_BLOCKS + first + step]
            start = pl.multiple_of(source * ROWBLK, ROWBLK)
            key_win[pl.ds(step * ROWBLK, ROWBLK), :] = key_ref[pl.ds(start, ROWBLK), :]
            value_win[pl.ds(step * ROWBLK, ROWBLK), :] = value_ref[pl.ds(start, ROWBLK), :]
        base = pl.multiple_of(block * ROWBLK, ROWBLK)
        cosine = cos_ref[pl.ds(base, ROWBLK), :]
        sine = sin_ref[pl.ds(base, ROWBLK), :]
        place = place_ref[pl.ds(block, 1), :]
        lane = lax.broadcasted_iota(jnp.int32, (1, ROWBLK), 1)
        last = (slot - first) * ROWBLK + lane
        last_all = jnp.concatenate([last] * wide, axis=1)
        start_all = jnp.concatenate([last - place] * wide, axis=1)
        key_index = lax.broadcasted_iota(jnp.int32, (rows, cols), 0)
        allowed = (key_index >= start_all) & (key_index <= last_all)
        keys = key_win[pl.ds(0, rows), :]
        values = value_win[pl.ds(0, rows), :]
        gkey = jnp.zeros((rows, HD), jnp.float32)
        gvalue = jnp.zeros((rows, HD), jnp.float32)
        for group in range(heads // wide):
            queries = []
            ups = []
            for item in range(wide):
                at = (group * wide + item) * HD
                raw = query_ref[pl.ds(base, ROWBLK), pl.ds(at, HD)].astype(jnp.float32)
                turned = raw * cosine + pltpu.roll(raw, HD // 2, 1) * sine
                queries.append(turned.astype(jnp.bfloat16))
                ups.append(up_ref[pl.ds(base, ROWBLK), pl.ds(at, HD)])
            query = jnp.concatenate(queries, axis=0)
            up = jnp.concatenate(ups, axis=0)
            up_t = jnp.concatenate([u.astype(jnp.float32).T for u in ups], axis=1)
            score = lax.dot_general(keys, query, NT, preferred_element_type=jnp.float32)
            score = jnp.where(allowed, score, masked_score)
            peak = jnp.max(score, axis=0, keepdims=True)
            raised = jnp.exp2((score - peak) * to_exp2)
            total = jnp.sum(raised, axis=0, keepdims=True)
            prob = raised * (1.0 / total)
            prob_b = prob.astype(jnp.bfloat16)
            out_t = lax.dot_general(values, prob_b, TN, preferred_element_type=jnp.float32)
            out_b = out_t.astype(jnp.bfloat16)
            delta = jnp.sum(up_t * out_b.astype(jnp.float32), axis=0, keepdims=True)
            gprob = lax.dot_general(values, up, NT, preferred_element_type=jnp.float32)
            gscore = (prob * (gprob - delta)).astype(jnp.bfloat16)
            gquery_t = lax.dot_general(keys, gscore, TN, preferred_element_type=jnp.float32)
            gkey = gkey + jnp.dot(gscore, query, preferred_element_type=jnp.float32)
            gvalue = gvalue + jnp.dot(prob_b, up, preferred_element_type=jnp.float32)
            for item in range(wide):
                at = (group * wide + item) * HD
                part = slice(item * ROWBLK, (item + 1) * ROWBLK)
                head = group * wide + item
                half, row = head * 2 // heads, head % (heads // 2) * HD
                out_ref[half ^ odd_ref[0], pl.ds(row, HD), pl.ds(base, ROWBLK)] = out_b[:, part]
                grad = gquery_t[:, part].T * scale
                back = grad * cosine - pltpu.roll(grad, HD // 2, 1) * sine
                gquery_ref[pl.ds(base, ROWBLK), pl.ds(at, HD)] = back.astype(jnp.bfloat16)
        gkey = (gkey * scale).astype(jnp.bfloat16)
        gvalue = gvalue.astype(jnp.bfloat16)
        for step in range(count):
            block_id = run * RUN_BLOCKS + first + step
            part = slice(step * ROWBLK, (step + 1) * ROWBLK)
            start = pl.multiple_of(target_ref[block_id] * ROWBLK, ROWBLK)
            gkey_ref[pl.ds(start, ROWBLK), :] = gkey[part]
            gvalue_ref[pl.ds(start, ROWBLK), :] = gvalue[part]

    def body(block, carry):
        need = need_ref[block]
        floor = 0
        for size in (1, 2, 3, 4, 6, 8):
            pl.when((need > floor) & (need <= size))(partial(window, size, block))
            floor = size
        return carry

    lax.fori_loop(0, rows_each // ROWBLK, body, 0)
    half = ranks * rows_each // 2
    stores = []
    for item, (whole, keep, send) in enumerate(
        ((gkey_ref, gkey_keep, gkey_send), (gvalue_ref, gvalue_keep, gvalue_send))
    ):
        for place, target in enumerate((keep, send)):
            copy = pltpu.make_async_copy(
                whole.at[pl.ds(place * half, half)], target, sems.at[item, place]
            )
            copy.start()
            stores.append(copy)
    for copy in stores:
        copy.wait()


def attend(tables, query, up, cosine, sine, places, keys, values):
    rows, width = query.shape
    heads = width // HD
    ranks = len(keys)
    every = rows * ranks
    smem = pl.BlockSpec(memory_space=pltpu.SMEM)
    vmem = pl.BlockSpec(memory_space=pltpu.VMEM)
    hbm = pl.BlockSpec(memory_space=pl.ANY)
    half = jax.ShapeDtypeStruct((every // 2, HD), jnp.bfloat16)
    return pl.pallas_call(
        partial(attend_kernel, heads, ranks),
        out_shape=(
            jax.ShapeDtypeStruct((rows, width), jnp.bfloat16),
            jax.ShapeDtypeStruct((2, width // 2, rows), jnp.bfloat16),
            half,
            half,
            half,
            half,
        ),
        in_specs=[smem] * 6 + [vmem] * 5 + [hbm] * (2 * ranks),
        out_specs=(vmem, vmem, hbm, hbm, hbm, hbm),
        scratch_shapes=[pltpu.VMEM((every, HD), jnp.bfloat16)] * 4
        + [pltpu.VMEM((RUN_BLOCKS * ROWBLK, HD), jnp.bfloat16)] * 2
        + [pltpu.SemaphoreType.DMA((2, ranks))],
        compiler_params=pltpu.CompilerParams(vmem_limit_bytes=VMEM_BYTES),
        cost_estimate=NO_COST,
    )(*tables, query, up, cosine, sine, places, *keys, *values)


def assemble_kernel(count, column_ref, active_ref, *refs):
    out_ref, sems = refs[count:]

    def copy_of(index):
        column = pl.multiple_of(column_ref[index] * HD, HD)
        return pltpu.make_async_copy(
            refs[index], out_ref.at[:, pl.ds(column, HD)], sems.at[index]
        )

    for index in range(count):
        pl.when(active_ref[index] > 0)(lambda index=index: copy_of(index).start())
    for index in range(count):
        pl.when(active_ref[index] > 0)(lambda index=index: copy_of(index).wait())


def assemble(columns, active, pieces, lanes):
    rows = pieces[0].shape[0]
    smem = pl.BlockSpec(memory_space=pltpu.SMEM)
    vmem = pl.BlockSpec(memory_space=pltpu.VMEM)
    return pl.pallas_call(
        partial(assemble_kernel, len(pieces)),
        out_shape=jax.ShapeDtypeStruct((rows, lanes * HD), pieces[0].dtype),
        in_specs=[smem, smem] + [vmem] * len(pieces),
        out_specs=pl.BlockSpec(memory_space=pl.ANY),
        scratch_shapes=[pltpu.SemaphoreType.DMA((len(pieces),))],
        compiler_params=pltpu.CompilerParams(vmem_limit_bytes=VMEM_BYTES),
        cost_estimate=NO_COST,
    )(columns, active, *pieces)


def lane_gather(array, my_lane):
    lanes = lax.axis_size("tensor")

    def send(item, pairs):
        return lax.ppermute(item, "tensor", pairs)

    if lanes == 4:
        second = send(array, [(0, 2), (2, 0), (1, 3), (3, 1)])
        first = send(array, [(0, 1), (1, 0), (2, 3), (3, 2)])
        inner = send(array, [(1, 2), (2, 1)])
        outer = send(second, [(1, 0), (2, 3)])
        middle = (my_lane == 1) | (my_lane == 2)
        pieces = [array, first, second, inner, outer]
        columns = my_lane ^ jnp.array([0, 1, 2, 3, 3], jnp.int32)
        always = jnp.array([True, True, True, False, False])
        at_inner = jnp.array([False, False, False, True, False])
        active = always | (at_inner & middle) | (~always & ~at_inner & ~middle)
    else:
        pieces = [array]
        for unused in range(lanes - 1):
            pieces.append(send(pieces[-1], [(lane, (lane + 1) % lanes) for lane in range(lanes)]))
        columns = (my_lane - jnp.arange(lanes, dtype=jnp.int32)) % lanes
        active = jnp.ones((lanes,), jnp.bool_)
    return assemble(columns, active.astype(jnp.int32), pieces, lanes), pieces[1:]


def swap(array, bit):
    ranks = lax.axis_size("dp")
    return lax.ppermute(array, "dp", [(rank, rank ^ bit) for rank in range(ranks)])


def spread(array):
    found = [array, swap(array, 1)]
    others = [swap(array, step) for step in range(2, lax.axis_size("dp"), 2)]
    for other in others:
        found += [other, swap(other, 1)]
    return found


def added(left, right):
    return left.astype(jnp.float32) + right.astype(jnp.float32)


def halved(keep, received, last):
    half = keep.shape[0] // 2
    send = added(keep[half:], received[half:]).astype(jnp.bfloat16)
    kept = added(keep[:half], received[:half])
    return (kept if last else kept.astype(jnp.bfloat16)), send


def sum_stages(keeps, receives, bits, between=None):
    orders = (bits[1:], bits[:0:-1])
    for stage in range(len(bits) - 1):
        last = stage == len(bits) - 2
        pairs = [halved(keep, received, last) for keep, received in zip(keeps, receives)]
        keeps = [pair[0] for pair in pairs]
        receives = [swap(pair[1], orders[part][stage]) for part, pair in enumerate(pairs)]
        if stage == 0 and between is not None:
            keeps[0] = between(keeps[0], pairs[0][1])
    return keeps, receives


def final_kernel(rotary, *refs):
    out_ref = refs[-1]
    half = refs[0].shape[0]
    for part in range(2):
        rows = pl.ds(part * half, half)
        total = refs[part][...].astype(jnp.float32) + refs[2 + part][...].astype(jnp.float32)
        if rotary:
            total = total * refs[4][rows, :] - pltpu.roll(total, HD // 2, 1) * refs[5][rows, :]
        out_ref[rows, :] = total.astype(out_ref.dtype)


def final_sum(keeps, received, tables, after, kind=jnp.bfloat16):
    vmem = pl.BlockSpec(memory_space=pltpu.VMEM)
    hbm = pl.BlockSpec(memory_space=pl.ANY)
    parts = [*keeps, *received, *tables]
    rows, cols = keeps[0].shape
    return pl.pallas_call(
        partial(final_kernel, len(tables) > 0),
        out_shape=jax.ShapeDtypeStruct((2 * rows, cols), kind),
        in_specs=[vmem] * len(parts) + [hbm] * len(after),
        out_specs=vmem,
        compiler_params=pltpu.CompilerParams(vmem_limit_bytes=VMEM_BYTES),
        cost_estimate=NO_COST,
    )(*parts, *after)


def up_kernel(rows_ref, weight_ref, *refs):
    out_ref, total_ref = refs[-2:]
    part = jnp.dot(rows_ref[...], weight_ref[...], preferred_element_type=jnp.float32)
    step = pl.program_id(0)

    @pl.when(step == 0)
    def first():
        total_ref[...] = part

    @pl.when(step > 0)
    def later():
        total_ref[...] += part

    @pl.when(step == pl.num_programs(0) - 1)
    def last():
        out_ref[...] = total_ref[...].astype(out_ref.dtype)


def up_product(rows, weight, after):
    height, depth = rows.shape
    width = weight.shape[1]
    piece = 512
    return pl.pallas_call(
        up_kernel,
        grid=(depth // piece,),
        out_shape=jax.ShapeDtypeStruct((height, width), jnp.bfloat16),
        in_specs=[
            pl.BlockSpec((height, piece), lambda step: (0, step)),
            pl.BlockSpec((piece, width), lambda step: (step, 0)),
        ]
        + [pl.BlockSpec(memory_space=pl.ANY)] * len(after),
        out_specs=pl.BlockSpec((height, width), lambda step: (0, 0)),
        scratch_shapes=[pltpu.VMEM((height, width), jnp.float32)],
        compiler_params=pltpu.CompilerParams(vmem_limit_bytes=VMEM_BYTES),
        cost_estimate=pl.CostEstimate(
            flops=2 * height * weight.size, bytes_accessed=2 * rows.size, transcendentals=0
        ),
    )(rows, weight, *after)


def take_heads_kernel(at_ref, key_ref, value_ref, after_ref, own_key_ref, own_value_ref):
    own_key_ref[...] = key_ref[...]
    own_value_ref[...] = value_ref[...]


def take_heads(key, value, kv_head, after):
    rows = key.shape[0]
    steps = 2
    picked = pl.BlockSpec((rows // steps, HD), lambda step, at_ref: (step, at_ref[0]))
    own = pl.BlockSpec((rows // steps, HD), lambda step, at_ref: (step, 0))
    shape = jax.ShapeDtypeStruct((rows, HD), key.dtype)
    return pl.pallas_call(
        take_heads_kernel,
        grid_spec=pltpu.PrefetchScalarGridSpec(
            num_scalar_prefetch=1,
            grid=(steps,),
            in_specs=[picked, picked, pl.BlockSpec(memory_space=pl.ANY)],
            out_specs=[own, own],
        ),
        out_shape=[shape, shape],
        cost_estimate=NO_COST,
    )(kv_head.reshape(1), key, value, after)


def place_of(distance, bits):
    place = distance * 0
    for bit in bits:
        place = place * 2 + (distance & bit) // bit
    return place


def product_kernel(orders, my_ref, left_ref, right_ref, *refs):
    outs = refs[-6:-2]
    width = left_ref.shape[0] * left_ref.shape[1]
    left = left_ref[...].reshape(width, left_ref.shape[2])
    total = jnp.dot(left, right_ref[...], preferred_element_type=jnp.float32)
    for at, out_ref in enumerate(outs):
        out_ref[0] = total[at * width // 4 : (at + 1) * width // 4].astype(out_ref.dtype)


def product(mine, left, right, thru, after, bits):
    count = lax.axis_size("dp") // 2
    width, depth = left.shape[0] * left.shape[1], left.shape[2]
    rows, cols = width // 4, right.shape[1] // count
    orders = ([bit // 2 for bit in bits[1:]], [bit // 2 for bit in bits[:0:-1]])
    if cols % 128:
        total = jnp.dot(left.reshape(width, depth), right, preferred_element_type=jnp.float32)
        pieces = jnp.moveaxis(total.astype(jnp.bfloat16).reshape(width, count, cols), 1, 0)
        stacks = []
        for at in range(4):
            order = sorted(range(count), key=lambda step: place_of(step, orders[at % 2]))
            picked = jnp.take(pieces, jnp.array(order, jnp.int32) ^ mine, axis=0)
            stacks.append(picked[:, at * rows : (at + 1) * rows])
        return stacks, thru
    hbm = pl.BlockSpec(memory_space=pl.ANY)
    outs = [
        pl.BlockSpec(
            (1, rows, cols), lambda step, my_ref, at=at: (place_of(step, orders[at % 2]), 0, 0)
        )
        for at in range(4)
    ]
    inputs = [mine.reshape(1), left, right, *after, *thru]
    results = pl.pallas_call(
        partial(product_kernel, orders),
        grid_spec=pltpu.PrefetchScalarGridSpec(
            num_scalar_prefetch=1,
            grid=(count,),
            in_specs=[
                pl.BlockSpec(left.shape, lambda step, my_ref: (0, 0, 0)),
                pl.BlockSpec((depth, cols), lambda step, my_ref: (0, step ^ my_ref[0])),
            ]
            + [hbm] * (len(after) + 2),
            out_specs=outs + [hbm] * 2,
        ),
        out_shape=[jax.ShapeDtypeStruct((count, rows, cols), jnp.bfloat16)] * 4
        + [jax.ShapeDtypeStruct(item.shape, item.dtype) for item in thru],
        input_output_aliases={len(inputs) - 2: 4, len(inputs) - 1: 5},
        compiler_params=pltpu.CompilerParams(vmem_limit_bytes=VMEM_BYTES),
        cost_estimate=pl.CostEstimate(
            flops=2 * width * right.size, bytes_accessed=2 * right.size, transcendentals=0
        ),
    )(*inputs)
    return results[:4], results[4:]


def local(query, key, value, grad_out, out_weight, plan, segments):
    rank_count = lax.axis_size("dp")
    my_rank = lax.axis_index("dp")
    my_lane = lax.axis_index("tensor")
    row_count = query.shape[0]
    block_count = row_count // ROWBLK
    local_heads = query.shape[1] // HD
    group = HEADS // KV
    bits = [1 << at for at in range(rank_count.bit_length() - 1)]
    kv_head = my_lane * local_heads // group
    own_places = positions_of(segments).reshape(1, block_count, ROWBLK)
    places_all = lax.all_to_all(
        jnp.broadcast_to(own_places, (rank_count, block_count, ROWBLK)),
        "dp",
        split_axis=0,
        concat_axis=0,
        tiled=True,
    ).reshape(-1, ROWBLK)
    own_key, own_value = take_heads(key, value, kv_head, places_all)
    values = spread(own_value)

    mine = my_rank * block_count + jnp.arange(block_count, dtype=jnp.int32)
    hit = plan[None, :] == mine[:, None]
    dest = jnp.sum(
        jnp.where(hit, jnp.arange(plan.shape[0], dtype=jnp.int32)[None, :], 0), axis=1
    )
    run = dest // RUN_BLOCKS
    slot = dest % RUN_BLOCKS
    places = jnp.take(places_all, dest, axis=0)
    need = slot - (slot * ROWBLK - places[:, 0]) // ROWBLK + 1
    cosine, sine = rope_tables(places.reshape(row_count), HD)
    key_f = own_key.astype(jnp.float32)
    rot_key = (key_f * cosine + swap_halves(key_f) * sine).astype(jnp.bfloat16)
    keys = spread(rot_key)
    up = up_product(grad_out, out_weight, [rot_key])

    distance = (plan // block_count) ^ my_rank
    within = plan % block_count
    part_blocks = block_count // 2
    stage_place = jnp.where(
        within < part_blocks, place_of(distance, bits[1:]), place_of(distance, bits[:0:-1])
    )
    quarter = (distance & 1) * 2 + within // part_blocks
    target = (quarter * (rank_count // 2) + stage_place) * part_blocks + within % part_blocks
    tables = (
        target,
        distance * block_count + within,
        run,
        slot,
        need,
        (my_rank & 1).reshape(1),
    )
    grad_query, attn_t, gkey_keep, gkey_send, gvalue_keep, gvalue_send = attend(
        tables, query, up, cosine, sine, places, keys, values
    )
    def parts_of(array):
        return [array[: array.shape[0] // 2], array[array.shape[0] // 2 :]]

    held = {}

    def weight_product(keep, send):
        stacks, (held["send"], keep) = product(
            my_rank // 2, attn_t, grad_out, (gkey_send, keep), [send], bits
        )
        held["stacks"] = stacks
        return keep

    value_keeps, value_received = sum_stages(
        parts_of(gvalue_keep), parts_of(swap(gvalue_send, 1)), bits, weight_product
    )
    stacks = held["stacks"]
    weight_received = [swap(item, 1) for item in stacks[2:]]
    value_partial = final_sum(value_keeps, value_received, (), ())
    value_all, value_pieces = lane_gather(value_partial, my_lane)

    key_keeps, key_received = sum_stages(
        parts_of(gkey_keep), parts_of(swap(held["send"], 1)), bits
    )
    key_partial = final_sum(key_keeps, key_received, (cosine, sine), value_pieces[:1])
    key_all, key_pieces = lane_gather(key_partial, my_lane)

    weight_keeps, weight_received = sum_stages(stacks[:2], weight_received, bits)
    total = final_sum(
        [item[0] for item in weight_keeps],
        [item[0] for item in weight_received],
        (),
        [*key_pieces[:3], value_all],
        jnp.float32,
    )
    odd = my_rank & 1
    pair_rows = grad_out.shape[1] // (rank_count // 2)
    low, high = total[:, : pair_rows // 2], total[:, pair_rows // 2 :]
    is_odd = odd > 0
    other = swap(jnp.where(is_odd, low, high).astype(jnp.bfloat16), 1).astype(jnp.float32)
    mine_half = jnp.where(is_odd, high, low)
    weight_grad = jnp.concatenate(
        [jnp.where(is_odd, other, mine_half), jnp.where(is_odd, mine_half, other)], axis=0
    ).T
    lanes_per_key = group // local_heads

    def combine(gathered):
        if lanes_per_key == 1:
            return gathered
        merged = (
            gathered.astype(jnp.float32).reshape(row_count, KV, lanes_per_key, HD).sum(axis=2)
        )
        return merged.astype(jnp.bfloat16).reshape(row_count, KV * HD)

    return (grad_query, combine(key_all), combine(value_all), weight_grad * (1.0 / rank_count))


def solution(mesh):
    in_specs = (
        P("dp", "tensor"),
        P("dp", None),
        P("dp", None),
        P("dp", None),
        P(None, "tensor"),
        P(),
        P("dp"),
    )
    out_specs = (P("dp", "tensor"), P("dp", None), P("dp", None), P("dp", "tensor"))
    return jax.shard_map(local, mesh=mesh, in_specs=in_specs, out_specs=out_specs, check_vma=False)
```

```python
from functools import partial
import math

import jax
import jax.numpy as jnp
from jax import lax
from jax.experimental import pallas as pl
from jax.experimental.pallas import tpu as pltpu
from jax.sharding import PartitionSpec as P

KV = 4
HD = 128
HEADS = 16
ROWBLK = 128
RUN_BLOCKS = 8
VMEM_BYTES = 58 * 1024 * 1024
NO_COST = pl.CostEstimate(flops=0, bytes_accessed=0, transcendentals=0)


rope_base = 1000000.0
yarn_factor = 4.0
yarn_context = 32768.0
beta_fast = 32.0
beta_slow = 1.0
masked_score = -1e30


def yarn_frequencies(head_size):
    half_size = head_size // 2

    def correction(rotations):
        return (
            head_size
            * math.log(yarn_context / (rotations * 2.0 * math.pi))
            / (2.0 * math.log(rope_base))
        )

    lower_bound = max(math.floor(correction(beta_fast)), 0)
    upper_bound = min(math.ceil(correction(beta_slow)), head_size - 1)
    ramp_span = max(upper_bound - lower_bound, 0.001)
    row_index = jnp.arange(half_size).astype(jnp.float32)
    extrap_freq = rope_base ** (-2.0 * row_index / head_size)
    interp_freq = extrap_freq / yarn_factor
    ramp_weight = jnp.clip((row_index - lower_bound) / ramp_span, 0.0, 1.0)
    return interp_freq * ramp_weight + extrap_freq * (1.0 - ramp_weight)


def positions_of(segments):
    row_count = segments.shape[-1]
    row_index = jnp.arange(row_count, dtype=jnp.int32)
    is_start = jnp.concatenate(
        [
            jnp.ones(segments.shape[:-1] + (1,), dtype=jnp.bool_),
            segments[..., 1:] != segments[..., :-1],
        ],
        axis=-1,
    )
    seg_start = lax.cummax(jnp.where(is_start, row_index, 0), axis=segments.ndim - 1)
    return row_index - seg_start


def rope_tables(places, head_size):
    angles = places.astype(jnp.float32)[:, None] * yarn_frequencies(head_size)[None, :]
    factor = 0.1 * math.log(yarn_factor) + 1.0
    cosine = jnp.cos(angles) * factor
    sine = jnp.sin(angles) * factor
    return (
        jnp.concatenate([cosine, cosine], axis=1),
        jnp.concatenate([-sine, sine], axis=1),
    )


def swap_halves(values):
    half = values.shape[-1] // 2
    return jnp.concatenate([values[..., half:], values[..., :half]], axis=-1)


NT = (((1,), (1,)), ((), ()))
TN = (((0,), (0,)), ((), ()))


def attend_kernel(
    heads,
    ranks,
    target_ref,
    source_ref,
    run_ref,
    slot_ref,
    need_ref,
    odd_ref,
    query_ref,
    up_ref,
    cos_ref,
    sin_ref,
    place_ref,
    *refs,
):
    key_parts, refs = refs[:ranks], refs[ranks:]
    value_parts, refs = refs[:ranks], refs[ranks:]
    gquery_ref, out_ref, gkey_keep, gkey_send, gvalue_keep, gvalue_send = refs[:6]
    key_ref, value_ref, gkey_ref, gvalue_ref, key_win, value_win, sems = refs[6:]
    rows_each = query_ref.shape[0]
    scale = 1.0 / math.sqrt(HD)
    to_exp2 = scale * math.log2(math.e)
    wide = min(2, heads)
    cols = wide * ROWBLK

    loads = []
    for item, (parts, whole) in enumerate(((key_parts, key_ref), (value_parts, value_ref))):
        for rank in range(ranks):
            copy = pltpu.make_async_copy(
                parts[rank], whole.at[pl.ds(rank * rows_each, rows_each)], sems.at[item, rank]
            )
            copy.start()
            loads.append(copy)
    gkey_ref[...] = jnp.zeros_like(gkey_ref)
    gvalue_ref[...] = jnp.zeros_like(gvalue_ref)
    for copy in loads:
        copy.wait()

    def window(count, block):
        slot = slot_ref[block]
        run = run_ref[block]
        first = jnp.maximum(slot + 1 - count, 0)
        rows = count * ROWBLK
        for step in range(count):
            source = source_ref[run * RUN_BLOCKS + first + step]
            start = pl.multiple_of(source * ROWBLK, ROWBLK)
            key_win[pl.ds(step * ROWBLK, ROWBLK), :] = key_ref[pl.ds(start, ROWBLK), :]
            value_win[pl.ds(step * ROWBLK, ROWBLK), :] = value_ref[pl.ds(start, ROWBLK), :]
        base = pl.multiple_of(block * ROWBLK, ROWBLK)
        cosine = cos_ref[pl.ds(base, ROWBLK), :]
        sine = sin_ref[pl.ds(base, ROWBLK), :]
        place = place_ref[pl.ds(block, 1), :]
        lane = lax.broadcasted_iota(jnp.int32, (1, ROWBLK), 1)
        last = (slot - first) * ROWBLK + lane
        last_all = jnp.concatenate([last] * wide, axis=1)
        start_all = jnp.concatenate([last - place] * wide, axis=1)
        key_index = lax.broadcasted_iota(jnp.int32, (rows, cols), 0)
        allowed = (key_index >= start_all) & (key_index <= last_all)
        keys = key_win[pl.ds(0, rows), :]
        values = value_win[pl.ds(0, rows), :]
        gkey = jnp.zeros((rows, HD), jnp.float32)
        gvalue = jnp.zeros((rows, HD), jnp.float32)
        for group in range(heads // wide):
            queries = []
            ups = []
            for item in range(wide):
                at = (group * wide + item) * HD
                raw = query_ref[pl.ds(base, ROWBLK), pl.ds(at, HD)].astype(jnp.float32)
                turned = raw * cosine + pltpu.roll(raw, HD // 2, 1) * sine
                queries.append(turned.astype(jnp.bfloat16))
                ups.append(up_ref[pl.ds(base, ROWBLK), pl.ds(at, HD)])
            query = jnp.concatenate(queries, axis=0)
            up = jnp.concatenate(ups, axis=0)
            up_t = jnp.concatenate([u.astype(jnp.float32).T for u in ups], axis=1)
            score = lax.dot_general(keys, query, NT, preferred_element_type=jnp.float32)
            score = jnp.where(allowed, score, masked_score)
            peak = jnp.max(score, axis=0, keepdims=True)
            raised = jnp.exp2((score - peak) * to_exp2)
            total = jnp.sum(raised, axis=0, keepdims=True)
            prob = raised * (1.0 / total)
            prob_b = prob.astype(jnp.bfloat16)
            out_t = lax.dot_general(values, prob_b, TN, preferred_element_type=jnp.float32)
            out_b = out_t.astype(jnp.bfloat16)
            delta = jnp.sum(up_t * out_b.astype(jnp.float32), axis=0, keepdims=True)
            gprob = lax.dot_general(values, up, NT, preferred_element_type=jnp.float32)
            gscore = (prob * (gprob - delta)).astype(jnp.bfloat16)
            gquery_t = lax.dot_general(keys, gscore, TN, preferred_element_type=jnp.float32)
            gkey = gkey + jnp.dot(gscore, query, preferred_element_type=jnp.float32)
            gvalue = gvalue + jnp.dot(prob_b, up, preferred_element_type=jnp.float32)
            for item in range(wide):
                at = (group * wide + item) * HD
                part = slice(item * ROWBLK, (item + 1) * ROWBLK)
                head = group * wide + item
                half, row = head * 2 // heads, head % (heads // 2) * HD
                out_ref[half ^ odd_ref[0], pl.ds(row, HD), pl.ds(base, ROWBLK)] = out_b[:, part]
                grad = gquery_t[:, part].T * scale
                back = grad * cosine - pltpu.roll(grad, HD // 2, 1) * sine
                gquery_ref[pl.ds(base, ROWBLK), pl.ds(at, HD)] = back.astype(jnp.bfloat16)
        gkey = (gkey * scale).astype(jnp.bfloat16)
        gvalue = gvalue.astype(jnp.bfloat16)
        for step in range(count):
            block_id = run * RUN_BLOCKS + first + step
            part = slice(step * ROWBLK, (step + 1) * ROWBLK)
            start = pl.multiple_of(target_ref[block_id] * ROWBLK, ROWBLK)
            gkey_ref[pl.ds(start, ROWBLK), :] = gkey[part]
            gvalue_ref[pl.ds(start, ROWBLK), :] = gvalue[part]

    def body(block, carry):
        need = need_ref[block]
        floor = 0
        for size in (1, 2, 3, 4, 6, 8):
            pl.when((need > floor) & (need <= size))(partial(window, size, block))
            floor = size
        return carry

    lax.fori_loop(0, rows_each // ROWBLK, body, 0)
    half = ranks * rows_each // 2
    stores = []
    for item, (whole, keep, send) in enumerate(
        ((gkey_ref, gkey_keep, gkey_send), (gvalue_ref, gvalue_keep, gvalue_send))
    ):
        for place, target in enumerate((keep, send)):
            copy = pltpu.make_async_copy(
                whole.at[pl.ds(place * half, half)], target, sems.at[item, place]
            )
            copy.start()
            stores.append(copy)
    for copy in stores:
        copy.wait()


def attend(tables, query, up, cosine, sine, places, keys, values):
    rows, width = query.shape
    heads = width // HD
    ranks = len(keys)
    every = rows * ranks
    smem = pl.BlockSpec(memory_space=pltpu.SMEM)
    vmem = pl.BlockSpec(memory_space=pltpu.VMEM)
    hbm = pl.BlockSpec(memory_space=pl.ANY)
    half = jax.ShapeDtypeStruct((every // 2, HD), jnp.bfloat16)
    return pl.pallas_call(
        partial(attend_kernel, heads, ranks),
        out_shape=(
            jax.ShapeDtypeStruct((rows, width), jnp.bfloat16),
            jax.ShapeDtypeStruct((2, width // 2, rows), jnp.bfloat16),
            half,
            half,
            half,
            half,
        ),
        in_specs=[smem] * 6 + [vmem] * 5 + [hbm] * (2 * ranks),
        out_specs=(vmem, vmem, hbm, hbm, hbm, hbm),
        scratch_shapes=[pltpu.VMEM((every, HD), jnp.bfloat16)] * 4
        + [pltpu.VMEM((RUN_BLOCKS * ROWBLK, HD), jnp.bfloat16)] * 2
        + [pltpu.SemaphoreType.DMA((2, ranks))],
        compiler_params=pltpu.CompilerParams(vmem_limit_bytes=VMEM_BYTES),
        cost_estimate=NO_COST,
    )(*tables, query, up, cosine, sine, places, *keys, *values)


def assemble_kernel(count, column_ref, active_ref, *refs):
    out_ref, sems = refs[count:]

    def copy_of(index):
        column = pl.multiple_of(column_ref[index] * HD, HD)
        return pltpu.make_async_copy(
            refs[index], out_ref.at[:, pl.ds(column, HD)], sems.at[index]
        )

    for index in range(count):
        pl.when(active_ref[index] > 0)(lambda index=index: copy_of(index).start())
    for index in range(count):
        pl.when(active_ref[index] > 0)(lambda index=index: copy_of(index).wait())


def assemble(columns, active, pieces, lanes):
    rows = pieces[0].shape[0]
    smem = pl.BlockSpec(memory_space=pltpu.SMEM)
    vmem = pl.BlockSpec(memory_space=pltpu.VMEM)
    return pl.pallas_call(
        partial(assemble_kernel, len(pieces)),
        out_shape=jax.ShapeDtypeStruct((rows, lanes * HD), pieces[0].dtype),
        in_specs=[smem, smem] + [vmem] * len(pieces),
        out_specs=pl.BlockSpec(memory_space=pl.ANY),
        scratch_shapes=[pltpu.SemaphoreType.DMA((len(pieces),))],
        compiler_params=pltpu.CompilerParams(vmem_limit_bytes=VMEM_BYTES),
        cost_estimate=NO_COST,
    )(columns, active, *pieces)


def lane_gather(array, my_lane):
    lanes = lax.axis_size("tensor")

    def send(item, pairs):
        return lax.ppermute(item, "tensor", pairs)

    if lanes == 4:
        second = send(array, [(0, 2), (2, 0), (1, 3), (3, 1)])
        first = send(array, [(0, 1), (1, 0), (2, 3), (3, 2)])
        inner = send(array, [(1, 2), (2, 1)])
        outer = send(second, [(1, 0), (2, 3)])
        middle = (my_lane == 1) | (my_lane == 2)
        pieces = [array, first, second, inner, outer]
        columns = my_lane ^ jnp.array([0, 1, 2, 3, 3], jnp.int32)
        always = jnp.array([True, True, True, False, False])
        at_inner = jnp.array([False, False, False, True, False])
        active = always | (at_inner & middle) | (~always & ~at_inner & ~middle)
    else:
        pieces = [array]
        for unused in range(lanes - 1):
            pieces.append(send(pieces[-1], [(lane, (lane + 1) % lanes) for lane in range(lanes)]))
        columns = (my_lane - jnp.arange(lanes, dtype=jnp.int32)) % lanes
        active = jnp.ones((lanes,), jnp.bool_)
    return assemble(columns, active.astype(jnp.int32), pieces, lanes), pieces[1:]


def swap(array, bit):
    ranks = lax.axis_size("dp")
    return lax.ppermute(array, "dp", [(rank, rank ^ bit) for rank in range(ranks)])


def spread(array):
    found = [array, swap(array, 1)]
    others = [swap(array, step) for step in range(2, lax.axis_size("dp"), 2)]
    for other in others:
        found += [other, swap(other, 1)]
    return found


def added(left, right):
    return left.astype(jnp.float32) + right.astype(jnp.float32)


def chip_sum(keep, received):
    count = lax.axis_size("dp") // 2
    rows = keep.shape[0] // count
    total = [
        added(keep[at * rows : (at + 1) * rows], received[at * rows : (at + 1) * rows])
        for at in range(count)
    ]
    return total[0], [item.astype(keep.dtype) for item in total[1:]]


def exchange(sends):
    return [swap(item, 2 * at + 2) for at, item in enumerate(sends)]


def final_kernel(count, rotary, out_at, *refs):
    total = refs[0][...].astype(jnp.float32)
    for ref in refs[1 : 1 + count]:
        total = total + ref[...].astype(jnp.float32)
    if rotary:
        total = total * refs[1 + count][...] - pltpu.roll(total, HD // 2, 1) * refs[2 + count][...]
    refs[out_at][...] = total.astype(refs[out_at].dtype)


def final_sum(keep, received, tables, after, kind=jnp.bfloat16, thru=()):
    vmem = pl.BlockSpec(memory_space=pltpu.VMEM)
    hbm = pl.BlockSpec(memory_space=pl.ANY)
    parts = [keep, *received, *tables]
    inputs = len(parts) + len(after) + len(thru)
    results = pl.pallas_call(
        partial(final_kernel, len(received), len(tables) > 0, inputs),
        out_shape=[jax.ShapeDtypeStruct(keep.shape, kind)]
        + [jax.ShapeDtypeStruct(item.shape, item.dtype) for item in thru],
        in_specs=[vmem] * len(parts) + [hbm] * (len(after) + len(thru)),
        out_specs=[vmem] + [hbm] * len(thru),
        input_output_aliases={inputs - len(thru) + at: 1 + at for at in range(len(thru))},
        compiler_params=pltpu.CompilerParams(vmem_limit_bytes=VMEM_BYTES),
        cost_estimate=NO_COST,
    )(*parts, *after, *thru)
    return results if thru else results[0]


def up_kernel(rows_ref, weight_ref, *refs):
    total = jnp.dot(rows_ref[...], weight_ref[...], preferred_element_type=jnp.float32)
    refs[-1][...] = total.astype(refs[-1].dtype)


def up_product(rows, weight, after):
    height, depth = rows.shape
    steps = 4
    return pl.pallas_call(
        up_kernel,
        grid=(steps,),
        out_shape=jax.ShapeDtypeStruct((height, weight.shape[1]), jnp.bfloat16),
        in_specs=[
            pl.BlockSpec((height // steps, depth), lambda step: (step, 0)),
            pl.BlockSpec(weight.shape, lambda step: (0, 0)),
        ]
        + [pl.BlockSpec(memory_space=pl.ANY)] * len(after),
        out_specs=pl.BlockSpec((height // steps, weight.shape[1]), lambda step: (step, 0)),
        compiler_params=pltpu.CompilerParams(vmem_limit_bytes=VMEM_BYTES),
        cost_estimate=pl.CostEstimate(
            flops=2 * height * weight.size, bytes_accessed=2 * rows.size, transcendentals=0
        ),
    )(rows, weight, *after)


def product_kernel(my_ref, left_ref, right_ref, *refs):
    keep_ref, send_ref = refs[-3:-1]
    half = left_ref.shape[1]
    left = left_ref[...].reshape(2 * half, left_ref.shape[2])
    total = jnp.dot(left, right_ref[...], preferred_element_type=jnp.float32)
    keep_ref[0] = total[:half].astype(keep_ref.dtype)
    send_ref[0] = total[half:].astype(send_ref.dtype)


def product(mine, left, right, thru, after):
    count = lax.axis_size("dp") // 2
    half, depth = left.shape[1:]
    cols = right.shape[1] // count
    if cols % 128:
        total = jnp.dot(left.reshape(2 * half, depth), right, preferred_element_type=jnp.float32)
        pieces = jnp.moveaxis(total.astype(jnp.bfloat16).reshape(2 * half, count, cols), 1, 0)
        pieces = jnp.take(pieces, jnp.arange(count, dtype=jnp.int32) ^ mine, axis=0)
        return pieces[:, :half], pieces[:, half:], thru
    hbm = pl.BlockSpec(memory_space=pl.ANY)
    stacked = pl.BlockSpec((1, half, cols), lambda step, my_ref: (step, 0, 0))
    stack = jax.ShapeDtypeStruct((count, half, cols), jnp.bfloat16)
    inputs = [mine.reshape(1), left, right, *after, thru]
    return pl.pallas_call(
        product_kernel,
        grid_spec=pltpu.PrefetchScalarGridSpec(
            num_scalar_prefetch=1,
            grid=(count,),
            in_specs=[
                pl.BlockSpec(left.shape, lambda step, my_ref: (0, 0, 0)),
                pl.BlockSpec((depth, cols), lambda step, my_ref: (0, step ^ my_ref[0])),
            ]
            + [hbm] * (len(after) + 1),
            out_specs=[stacked, stacked, hbm],
        ),
        out_shape=[stack, stack, jax.ShapeDtypeStruct(thru.shape, thru.dtype)],
        input_output_aliases={len(inputs) - 1: 2},
        compiler_params=pltpu.CompilerParams(vmem_limit_bytes=VMEM_BYTES),
        cost_estimate=NO_COST,
    )(*inputs)


def local(query, key, value, grad_out, out_weight, plan, segments):
    rank_count = lax.axis_size("dp")
    my_rank = lax.axis_index("dp")
    my_lane = lax.axis_index("tensor")
    row_count = query.shape[0]
    block_count = row_count // ROWBLK
    local_heads = query.shape[1] // HD
    group = HEADS // KV
    bits = [1 << at for at in range(rank_count.bit_length() - 1)]
    kv_head = my_lane * local_heads // group
    own_key = lax.dynamic_slice_in_dim(key, kv_head * HD, HD, 1)
    own_value = lax.dynamic_slice_in_dim(value, kv_head * HD, HD, 1)

    own_places = positions_of(segments).reshape(1, block_count, ROWBLK)
    places_all = lax.all_to_all(
        jnp.broadcast_to(own_places, (rank_count, block_count, ROWBLK)),
        "dp",
        split_axis=0,
        concat_axis=0,
        tiled=True,
    ).reshape(-1, ROWBLK)
    values = spread(own_value)

    mine = my_rank * block_count + jnp.arange(block_count, dtype=jnp.int32)
    hit = plan[None, :] == mine[:, None]
    dest = jnp.sum(
        jnp.where(hit, jnp.arange(plan.shape[0], dtype=jnp.int32)[None, :], 0), axis=1
    )
    run = dest // RUN_BLOCKS
    slot = dest % RUN_BLOCKS
    places = jnp.take(places_all, dest, axis=0)
    need = slot - (slot * ROWBLK - places[:, 0]) // ROWBLK + 1
    cosine, sine = rope_tables(places.reshape(row_count), HD)
    key_f = own_key.astype(jnp.float32)
    rot_key = (key_f * cosine + swap_halves(key_f) * sine).astype(jnp.bfloat16)
    keys = spread(rot_key)
    up = up_product(grad_out, out_weight, [rot_key])

    distance = (plan // block_count) ^ my_rank
    within = plan % block_count
    half_place = (distance & 1) * (rank_count // 2) + distance // 2
    tables = (
        half_place * block_count + within,
        distance * block_count + within,
        run,
        slot,
        need,
        (my_rank & 1).reshape(1),
    )
    grad_query, attn_t, gkey_keep, gkey_send, gvalue_keep, gvalue_send = attend(
        tables, query, up, cosine, sine, places, keys, values
    )
    value_keep, value_sends = chip_sum(gvalue_keep, swap(gvalue_send, 1))
    value_received = exchange(value_sends)
    key_keep, key_sends = chip_sum(gkey_keep, swap(gkey_send, 1))
    key_received = exchange(key_sends)
    weight_keep, weight_send, value_keep = product(
        my_rank // 2, attn_t, grad_out, value_keep, [value_sends[0], key_sends[0]]
    )
    value_partial, weight_send = final_sum(
        value_keep, value_received, (), (), thru=[weight_send]
    )
    value_all, value_pieces = lane_gather(value_partial, my_lane)
    weight_other = swap(weight_send, 1)
    key_partial, weight_keep = final_sum(
        key_keep, key_received, (cosine, sine), value_pieces[:1], thru=[weight_keep]
    )
    key_all, key_pieces = lane_gather(key_partial, my_lane)
    weight_keep, weight_sends = chip_sum(weight_keep, weight_other)
    weight_received = exchange(weight_sends)
    total = final_sum(
        weight_keep, weight_received, (), [*key_pieces[:3], value_all], jnp.float32
    )[0]
    odd = my_rank & 1
    pair_rows = grad_out.shape[1] // (rank_count // 2)
    low, high = total[:, : pair_rows // 2], total[:, pair_rows // 2 :]
    is_odd = odd > 0
    other = swap(jnp.where(is_odd, low, high).astype(jnp.bfloat16), 1).astype(jnp.float32)
    mine_half = jnp.where(is_odd, high, low)
    weight_grad = jnp.concatenate(
        [jnp.where(is_odd, other, mine_half), jnp.where(is_odd, mine_half, other)], axis=0
    ).T
    lanes_per_key = group // local_heads

    def combine(gathered):
        if lanes_per_key == 1:
            return gathered
        merged = (
            gathered.astype(jnp.float32).reshape(row_count, KV, lanes_per_key, HD).sum(axis=2)
        )
        return merged.astype(jnp.bfloat16).reshape(row_count, KV * HD)

    return (grad_query, combine(key_all), combine(value_all), weight_grad * (1.0 / rank_count))


def solution(mesh):
    in_specs = (
        P("dp", "tensor"),
        P("dp", None),
        P("dp", None),
        P("dp", None),
        P(None, "tensor"),
        P(),
        P("dp"),
    )
    out_specs = (P("dp", "tensor"), P("dp", None), P("dp", None), P("dp", "tensor"))
    return jax.shard_map(local, mesh=mesh, in_specs=in_specs, out_specs=out_specs, check_vma=False)
```

```python
from functools import partial
import math

import jax
import jax.numpy as jnp
from jax import lax
from jax.experimental import pallas as pl
from jax.experimental.pallas import tpu as pltpu
from jax.sharding import PartitionSpec as P

KV = 4
HD = 128
HEADS = 16
ROWBLK = 128
RUN_BLOCKS = 8
VMEM_BYTES = 58 * 1024 * 1024
NO_COST = pl.CostEstimate(flops=0, bytes_accessed=0, transcendentals=0)


rope_base = 1000000.0
yarn_factor = 4.0
yarn_context = 32768.0
beta_fast = 32.0
beta_slow = 1.0
masked_score = -1e30


def yarn_frequencies(head_size):
    half_size = head_size // 2

    def correction(rotations):
        return (
            head_size
            * math.log(yarn_context / (rotations * 2.0 * math.pi))
            / (2.0 * math.log(rope_base))
        )

    lower_bound = max(math.floor(correction(beta_fast)), 0)
    upper_bound = min(math.ceil(correction(beta_slow)), head_size - 1)
    ramp_span = max(upper_bound - lower_bound, 0.001)
    row_index = jnp.arange(half_size).astype(jnp.float32)
    extrap_freq = rope_base ** (-2.0 * row_index / head_size)
    interp_freq = extrap_freq / yarn_factor
    ramp_weight = jnp.clip((row_index - lower_bound) / ramp_span, 0.0, 1.0)
    return interp_freq * ramp_weight + extrap_freq * (1.0 - ramp_weight)


def positions_of(segments):
    row_count = segments.shape[-1]
    row_index = jnp.arange(row_count, dtype=jnp.int32)
    is_start = jnp.concatenate(
        [
            jnp.ones(segments.shape[:-1] + (1,), dtype=jnp.bool_),
            segments[..., 1:] != segments[..., :-1],
        ],
        axis=-1,
    )
    seg_start = lax.cummax(jnp.where(is_start, row_index, 0), axis=segments.ndim - 1)
    return row_index - seg_start


def rope_tables(places, head_size):
    angles = places.astype(jnp.float32)[:, None] * yarn_frequencies(head_size)[None, :]
    factor = 0.1 * math.log(yarn_factor) + 1.0
    cosine = jnp.cos(angles) * factor
    sine = jnp.sin(angles) * factor
    return (
        jnp.concatenate([cosine, cosine], axis=1),
        jnp.concatenate([-sine, sine], axis=1),
    )


def swap_halves(values):
    half = values.shape[-1] // 2
    return jnp.concatenate([values[..., half:], values[..., :half]], axis=-1)


NT = (((1,), (1,)), ((), ()))
TN = (((0,), (0,)), ((), ()))


def attend_kernel(
    heads,
    ranks,
    target_ref,
    source_ref,
    run_ref,
    slot_ref,
    need_ref,
    odd_ref,
    query_ref,
    up_ref,
    cos_ref,
    sin_ref,
    place_ref,
    *refs,
):
    key_parts, refs = refs[:ranks], refs[ranks:]
    value_parts, refs = refs[:ranks], refs[ranks:]
    gquery_ref, out_ref, *halves = refs[:6]
    key_ref, value_ref, gkey_ref, gvalue_ref, key_win, value_win, load_sems, sems = refs[6:]
    rows_each = query_ref.shape[0]
    half_blocks = ranks * RUN_BLOCKS // 2
    scale = 1.0 / math.sqrt(HD)
    to_exp2 = scale * math.log2(math.e)

    loads = []
    for item, (parts, whole) in enumerate(((key_parts, key_ref), (value_parts, value_ref))):
        for rank in range(ranks):
            copy = pltpu.make_async_copy(
                parts[rank], whole.at[pl.ds(rank * rows_each, rows_each)], load_sems.at[item, rank]
            )
            copy.start()
            loads.append(copy)
    for copy in loads:
        copy.wait()

    def stores(block, act):
        side = block % 2
        for step in range(RUN_BLOCKS):
            target = target_ref[run_ref[block] * RUN_BLOCKS + step]
            for place in range(2):

                @pl.when(target // half_blocks == place)
                def one_half():
                    start = pl.multiple_of(target % half_blocks * ROWBLK, ROWBLK)
                    for item, source in enumerate((gkey_ref, gvalue_ref)):
                        act(
                            pltpu.make_async_copy(
                                source.at[side, pl.ds(step * ROWBLK, ROWBLK)],
                                halves[2 * item + place].at[pl.ds(start, ROWBLK)],
                                sems.at[side, item, step],
                            )
                        )

    def window(count, block):
        slot = slot_ref[block]
        run = run_ref[block]
        first = jnp.maximum(slot + 1 - count, 0)
        rows = count * ROWBLK
        for step in range(count):
            source = source_ref[run * RUN_BLOCKS + first + step]
            start = pl.multiple_of(source * ROWBLK, ROWBLK)
            key_win[pl.ds(step * ROWBLK, ROWBLK), :] = key_ref[pl.ds(start, ROWBLK), :]
            value_win[pl.ds(step * ROWBLK, ROWBLK), :] = value_ref[pl.ds(start, ROWBLK), :]
        wide = heads if count <= 4 else min(2, heads)
        cols = wide * ROWBLK
        base = pl.multiple_of(block * ROWBLK, ROWBLK)
        cosine = cos_ref[pl.ds(base, ROWBLK), :]
        sine = sin_ref[pl.ds(base, ROWBLK), :]
        place = place_ref[pl.ds(block, 1), :]
        lane = lax.broadcasted_iota(jnp.int32, (1, ROWBLK), 1)
        last = (slot - first) * ROWBLK + lane
        last_all = jnp.concatenate([last] * wide, axis=1)
        start_all = jnp.concatenate([last - place] * wide, axis=1)
        key_index = lax.broadcasted_iota(jnp.int32, (rows, cols), 0)
        allowed = (key_index >= start_all) & (key_index <= last_all)
        keys = key_win[pl.ds(0, rows), :]
        values = value_win[pl.ds(0, rows), :]
        gkey = jnp.zeros((rows, HD), jnp.float32)
        gvalue = jnp.zeros((rows, HD), jnp.float32)
        for group in range(heads // wide):
            queries = []
            ups = []
            for item in range(wide):
                at = (group * wide + item) * HD
                raw = query_ref[pl.ds(base, ROWBLK), pl.ds(at, HD)].astype(jnp.float32)
                turned = raw * cosine + pltpu.roll(raw, HD // 2, 1) * sine
                queries.append(turned.astype(jnp.bfloat16))
                ups.append(up_ref[pl.ds(base, ROWBLK), pl.ds(at, HD)])
            query = jnp.concatenate(queries, axis=0)
            up = jnp.concatenate(ups, axis=0)
            up_t = jnp.concatenate([u.astype(jnp.float32).T for u in ups], axis=1)
            score = lax.dot_general(keys, query, NT, preferred_element_type=jnp.float32)
            score = jnp.where(allowed, score, masked_score)
            peak = jnp.max(score, axis=0, keepdims=True)
            raised = jnp.exp2((score - peak) * to_exp2)
            total = jnp.sum(raised, axis=0, keepdims=True)
            prob = raised * (1.0 / total)
            prob_b = prob.astype(jnp.bfloat16)
            out_t = lax.dot_general(values, prob_b, TN, preferred_element_type=jnp.float32)
            out_b = out_t.astype(jnp.bfloat16)
            delta = jnp.sum(up_t * out_b.astype(jnp.float32), axis=0, keepdims=True)
            gprob = lax.dot_general(values, up, NT, preferred_element_type=jnp.float32)
            gscore = (prob * (gprob - delta)).astype(jnp.bfloat16)
            gquery_t = lax.dot_general(keys, gscore, TN, preferred_element_type=jnp.float32)
            gkey = gkey + jnp.dot(gscore, query, preferred_element_type=jnp.float32)
            gvalue = gvalue + jnp.dot(prob_b, up, preferred_element_type=jnp.float32)
            for item in range(wide):
                at = (group * wide + item) * HD
                part = slice(item * ROWBLK, (item + 1) * ROWBLK)
                head = group * wide + item
                half, row = head * 2 // heads, head % (heads // 2) * HD
                out_ref[half ^ odd_ref[0], pl.ds(row, HD), pl.ds(base, ROWBLK)] = out_b[:, part]
                grad = gquery_t[:, part].T * scale
                back = grad * cosine - pltpu.roll(grad, HD // 2, 1) * sine
                gquery_ref[pl.ds(base, ROWBLK), pl.ds(at, HD)] = back.astype(jnp.bfloat16)
        gkey = (gkey * scale).astype(jnp.bfloat16)
        gvalue = gvalue.astype(jnp.bfloat16)
        place_at = pl.ds(pl.multiple_of(first * ROWBLK, ROWBLK), rows)
        gkey_ref[block % 2, place_at, :] = gkey
        gvalue_ref[block % 2, place_at, :] = gvalue

    def body(block, carry):
        pl.when(block >= 2)(lambda: stores(block - 2, lambda copy: copy.wait()))
        blank = jnp.zeros(gkey_ref.shape[1:], jnp.bfloat16)
        gkey_ref[block % 2] = blank
        gvalue_ref[block % 2] = blank
        need = need_ref[block]
        floor = 0
        for size in (1, 2, 3, 4, 6, 8):
            pl.when((need > floor) & (need <= size))(partial(window, size, block))
            floor = size
        stores(block, lambda copy: copy.start())
        return carry

    blocks = rows_each // ROWBLK
    lax.fori_loop(0, blocks, body, 0)
    for block in range(max(blocks - 2, 0), blocks):
        stores(block, lambda copy: copy.wait())


def attend(tables, query, up, cosine, sine, places, keys, values):
    rows, width = query.shape
    heads = width // HD
    ranks = len(keys)
    every = rows * ranks
    smem = pl.BlockSpec(memory_space=pltpu.SMEM)
    vmem = pl.BlockSpec(memory_space=pltpu.VMEM)
    hbm = pl.BlockSpec(memory_space=pl.ANY)
    half = jax.ShapeDtypeStruct((every // 2, HD), jnp.bfloat16)
    return pl.pallas_call(
        partial(attend_kernel, heads, ranks),
        out_shape=(
            jax.ShapeDtypeStruct((rows, width), jnp.bfloat16),
            jax.ShapeDtypeStruct((2, width // 2, rows), jnp.bfloat16),
            half,
            half,
            half,
            half,
        ),
        in_specs=[smem] * 6 + [vmem] * 5 + [hbm] * (2 * ranks),
        out_specs=(vmem, vmem, hbm, hbm, hbm, hbm),
        scratch_shapes=[pltpu.VMEM((every, HD), jnp.bfloat16)] * 2
        + [pltpu.VMEM((2, RUN_BLOCKS * ROWBLK, HD), jnp.bfloat16)] * 2
        + [pltpu.VMEM((RUN_BLOCKS * ROWBLK, HD), jnp.bfloat16)] * 2
        + [pltpu.SemaphoreType.DMA((2, ranks)), pltpu.SemaphoreType.DMA((2, 2, RUN_BLOCKS))],
        compiler_params=pltpu.CompilerParams(vmem_limit_bytes=VMEM_BYTES),
        cost_estimate=NO_COST,
    )(*tables, query, up, cosine, sine, places, *keys, *values)


def assemble_kernel(lanes, my_ref, *refs):
    out_ref, sems = refs[lanes:]
    copies = []
    for index in range(lanes):
        column = pl.multiple_of((my_ref[0] ^ index) * HD, HD)
        copy = pltpu.make_async_copy(
            refs[index], out_ref.at[:, pl.ds(column, HD)], sems.at[index]
        )
        copy.start()
        copies.append(copy)
    for copy in copies:
        copy.wait()


def assemble(my_lane, pieces):
    rows = pieces[0].shape[0]
    lanes = len(pieces)
    vmem = pl.BlockSpec(memory_space=pltpu.VMEM)
    return pl.pallas_call(
        partial(assemble_kernel, lanes),
        out_shape=jax.ShapeDtypeStruct((rows, lanes * HD), pieces[0].dtype),
        in_specs=[pl.BlockSpec(memory_space=pltpu.SMEM)] + [vmem] * lanes,
        out_specs=pl.BlockSpec(memory_space=pl.ANY),
        scratch_shapes=[pltpu.SemaphoreType.DMA((lanes,))],
        compiler_params=pltpu.CompilerParams(vmem_limit_bytes=VMEM_BYTES),
        cost_estimate=NO_COST,
    )(my_lane.reshape(1), *pieces)


def lane_gather(array, my_lane):
    lanes = lax.axis_size("tensor")
    pieces = {0: array}
    bit = lanes // 2
    while bit:
        pairs = [(lane, lane ^ bit) for lane in range(lanes)]
        pieces.update(
            {at | bit: lax.ppermute(item, "tensor", pairs) for at, item in list(pieces.items())}
        )
        bit //= 2
    pieces = [pieces[at] for at in range(lanes)]
    return assemble(my_lane, pieces), pieces[1:]


def swap(array, bit):
    ranks = lax.axis_size("dp")
    return lax.ppermute(array, "dp", [(rank, rank ^ bit) for rank in range(ranks)])


def spread(array):
    found = [array, swap(array, 1)]
    others = [swap(array, step) for step in range(2, lax.axis_size("dp"), 2)]
    for other in others:
        found += [other, swap(other, 1)]
    return found


def added(left, right):
    return left.astype(jnp.float32) + right.astype(jnp.float32)


def chip_sum(keep, received):
    count = lax.axis_size("dp") // 2
    rows = keep.shape[0] // count
    total = [
        added(keep[at * rows : (at + 1) * rows], received[at * rows : (at + 1) * rows])
        for at in range(count)
    ]
    return total[0], [item.astype(keep.dtype) for item in total[1:]]


def exchange(sends):
    return [swap(item, 2 * at + 2) for at, item in enumerate(sends)]


def final_kernel(count, rotary, out_at, *refs):
    total = refs[0][...].astype(jnp.float32)
    for ref in refs[1 : 1 + count]:
        total = total + ref[...].astype(jnp.float32)
    if rotary:
        total = total * refs[1 + count][...] - pltpu.roll(total, HD // 2, 1) * refs[2 + count][...]
    refs[out_at][...] = total.astype(refs[out_at].dtype)


def final_sum(keep, received, tables, after, kind=jnp.bfloat16, thru=()):
    vmem = pl.BlockSpec(memory_space=pltpu.VMEM)
    hbm = pl.BlockSpec(memory_space=pl.ANY)
    parts = [keep, *received, *tables]
    inputs = len(parts) + len(after) + len(thru)
    results = pl.pallas_call(
        partial(final_kernel, len(received), len(tables) > 0, inputs),
        out_shape=[jax.ShapeDtypeStruct(keep.shape, kind)]
        + [jax.ShapeDtypeStruct(item.shape, item.dtype) for item in thru],
        in_specs=[vmem] * len(parts) + [hbm] * (len(after) + len(thru)),
        out_specs=[vmem] + [hbm] * len(thru),
        input_output_aliases={inputs - len(thru) + at: 1 + at for at in range(len(thru))},
        compiler_params=pltpu.CompilerParams(vmem_limit_bytes=VMEM_BYTES),
        cost_estimate=NO_COST,
    )(*parts, *after, *thru)
    return results if thru else results[0]


def up_kernel(rows_ref, weight_ref, *refs):
    total = jnp.dot(rows_ref[...], weight_ref[...], preferred_element_type=jnp.float32)
    refs[-1][...] = total.astype(refs[-1].dtype)


def up_product(rows, weight, after):
    height, depth = rows.shape
    steps = 4
    return pl.pallas_call(
        up_kernel,
        grid=(steps,),
        out_shape=jax.ShapeDtypeStruct((height, weight.shape[1]), jnp.bfloat16),
        in_specs=[
            pl.BlockSpec((height // steps, depth), lambda step: (step, 0)),
            pl.BlockSpec(weight.shape, lambda step: (0, 0)),
        ]
        + [pl.BlockSpec(memory_space=pl.ANY)] * len(after),
        out_specs=pl.BlockSpec((height // steps, weight.shape[1]), lambda step: (step, 0)),
        compiler_params=pltpu.CompilerParams(vmem_limit_bytes=VMEM_BYTES),
        cost_estimate=pl.CostEstimate(
            flops=2 * height * weight.size, bytes_accessed=2 * rows.size, transcendentals=0
        ),
    )(rows, weight, *after)


def product_kernel(my_ref, left_ref, right_ref, *refs):
    keep_ref, send_ref = refs[-3:-1]
    half = left_ref.shape[1]
    left = left_ref[...].reshape(2 * half, left_ref.shape[2])
    total = jnp.dot(left, right_ref[...], preferred_element_type=jnp.float32)
    keep_ref[0] = total[:half].astype(keep_ref.dtype)
    send_ref[0] = total[half:].astype(send_ref.dtype)


def product(mine, left, right, thru, after):
    count = lax.axis_size("dp") // 2
    half, depth = left.shape[1:]
    cols = right.shape[1] // count
    if cols % 128:
        total = jnp.dot(left.reshape(2 * half, depth), right, preferred_element_type=jnp.float32)
        pieces = jnp.moveaxis(total.astype(jnp.bfloat16).reshape(2 * half, count, cols), 1, 0)
        pieces = jnp.take(pieces, jnp.arange(count, dtype=jnp.int32) ^ mine, axis=0)
        return pieces[:, :half], pieces[:, half:], thru
    hbm = pl.BlockSpec(memory_space=pl.ANY)
    stacked = pl.BlockSpec((1, half, cols), lambda step, my_ref: (step, 0, 0))
    stack = jax.ShapeDtypeStruct((count, half, cols), jnp.bfloat16)
    inputs = [mine.reshape(1), left, right, *after, thru]
    return pl.pallas_call(
        product_kernel,
        grid_spec=pltpu.PrefetchScalarGridSpec(
            num_scalar_prefetch=1,
            grid=(count,),
            in_specs=[
                pl.BlockSpec(left.shape, lambda step, my_ref: (0, 0, 0)),
                pl.BlockSpec((depth, cols), lambda step, my_ref: (0, step ^ my_ref[0])),
            ]
            + [hbm] * (len(after) + 1),
            out_specs=[stacked, stacked, hbm],
        ),
        out_shape=[stack, stack, jax.ShapeDtypeStruct(thru.shape, thru.dtype)],
        input_output_aliases={len(inputs) - 1: 2},
        compiler_params=pltpu.CompilerParams(vmem_limit_bytes=VMEM_BYTES),
        cost_estimate=NO_COST,
    )(*inputs)


def local(query, key, value, grad_out, out_weight, plan, segments):
    rank_count = lax.axis_size("dp")
    my_rank = lax.axis_index("dp")
    my_lane = lax.axis_index("tensor")
    row_count = query.shape[0]
    block_count = row_count // ROWBLK
    local_heads = query.shape[1] // HD
    group = HEADS // KV
    bits = [1 << at for at in range(rank_count.bit_length() - 1)]
    kv_head = my_lane * local_heads // group
    own_key = lax.dynamic_slice_in_dim(key, kv_head * HD, HD, 1)
    own_value = lax.dynamic_slice_in_dim(value, kv_head * HD, HD, 1)

    own_places = positions_of(segments).reshape(1, block_count, ROWBLK)
    places_all = lax.all_to_all(
        jnp.broadcast_to(own_places, (rank_count, block_count, ROWBLK)),
        "dp",
        split_axis=0,
        concat_axis=0,
        tiled=True,
    ).reshape(-1, ROWBLK)
    values = spread(own_value)

    mine = my_rank * block_count + jnp.arange(block_count, dtype=jnp.int32)
    hit = plan[None, :] == mine[:, None]
    dest = jnp.sum(
        jnp.where(hit, jnp.arange(plan.shape[0], dtype=jnp.int32)[None, :], 0), axis=1
    )
    run = dest // RUN_BLOCKS
    slot = dest % RUN_BLOCKS
    places = jnp.take(places_all, dest, axis=0)
    need = slot - (slot * ROWBLK - places[:, 0]) // ROWBLK + 1
    cosine, sine = rope_tables(places.reshape(row_count), HD)
    key_f = own_key.astype(jnp.float32)
    rot_key = (key_f * cosine + swap_halves(key_f) * sine).astype(jnp.bfloat16)
    keys = spread(rot_key)
    up = up_product(grad_out, out_weight, [rot_key])

    distance = (plan // block_count) ^ my_rank
    within = plan % block_count
    half_place = (distance & 1) * (rank_count // 2) + distance // 2
    tables = (
        half_place * block_count + within,
        distance * block_count + within,
        run,
        slot,
        need,
        (my_rank & 1).reshape(1),
    )
    grad_query, attn_t, gkey_keep, gkey_send, gvalue_keep, gvalue_send = attend(
        tables, query, up, cosine, sine, places, keys, values
    )
    value_keep, value_sends = chip_sum(gvalue_keep, swap(gvalue_send, 1))
    value_received = exchange(value_sends)
    key_keep, key_sends = chip_sum(gkey_keep, swap(gkey_send, 1))
    key_received = exchange(key_sends)
    weight_keep, weight_send, value_keep = product(
        my_rank // 2, attn_t, grad_out, value_keep, [value_sends[0], key_sends[0]]
    )
    value_partial, weight_send = final_sum(
        value_keep, value_received, (), (), thru=[weight_send]
    )
    value_all, value_pieces = lane_gather(value_partial, my_lane)
    weight_other = swap(weight_send, 1)
    key_partial, weight_keep = final_sum(
        key_keep, key_received, (cosine, sine), value_pieces[:1], thru=[weight_keep]
    )
    key_all, key_pieces = lane_gather(key_partial, my_lane)
    weight_keep, weight_sends = chip_sum(weight_keep, weight_other)
    weight_received = exchange(weight_sends)
    total = final_sum(
        weight_keep, weight_received, (), [*key_pieces[:2], value_all], jnp.float32
    )[0]
    odd = my_rank & 1
    pair_rows = grad_out.shape[1] // (rank_count // 2)
    low, high = total[:, : pair_rows // 2], total[:, pair_rows // 2 :]
    is_odd = odd > 0
    other = swap(jnp.where(is_odd, low, high).astype(jnp.bfloat16), 1).astype(jnp.float32)
    mine_half = jnp.where(is_odd, high, low)
    weight_grad = jnp.concatenate(
        [jnp.where(is_odd, other, mine_half), jnp.where(is_odd, mine_half, other)], axis=0
    ).T
    lanes_per_key = group // local_heads

    def combine(gathered):
        if lanes_per_key == 1:
            return gathered
        merged = (
            gathered.astype(jnp.float32).reshape(row_count, KV, lanes_per_key, HD).sum(axis=2)
        )
        return merged.astype(jnp.bfloat16).reshape(row_count, KV * HD)

    return (grad_query, combine(key_all), combine(value_all), weight_grad * (1.0 / rank_count))


def solution(mesh):
    in_specs = (
        P("dp", "tensor"),
        P("dp", None),
        P("dp", None),
        P("dp", None),
        P(None, "tensor"),
        P(),
        P("dp"),
    )
    out_specs = (P("dp", "tensor"), P("dp", None), P("dp", None), P("dp", "tensor"))
    return jax.shard_map(local, mesh=mesh, in_specs=in_specs, out_specs=out_specs, check_vma=False)
```

```python
from functools import partial
import math

import jax
import jax.numpy as jnp
from jax import lax
from jax.experimental import pallas as pl
from jax.experimental.pallas import tpu as pltpu
from jax.sharding import PartitionSpec as P

KV = 4
HD = 128
HEADS = 16
ROWBLK = 128
RUN_BLOCKS = 8
VMEM_BYTES = 58 * 1024 * 1024
NO_COST = pl.CostEstimate(flops=0, bytes_accessed=0, transcendentals=0)


rope_base = 1000000.0
yarn_factor = 4.0
yarn_context = 32768.0
beta_fast = 32.0
beta_slow = 1.0
masked_score = -1e30


def yarn_frequencies(head_size):
    half_size = head_size // 2

    def correction(rotations):
        return (
            head_size
            * math.log(yarn_context / (rotations * 2.0 * math.pi))
            / (2.0 * math.log(rope_base))
        )

    lower_bound = max(math.floor(correction(beta_fast)), 0)
    upper_bound = min(math.ceil(correction(beta_slow)), head_size - 1)
    ramp_span = max(upper_bound - lower_bound, 0.001)
    row_index = jnp.arange(half_size).astype(jnp.float32)
    extrap_freq = rope_base ** (-2.0 * row_index / head_size)
    interp_freq = extrap_freq / yarn_factor
    ramp_weight = jnp.clip((row_index - lower_bound) / ramp_span, 0.0, 1.0)
    return interp_freq * ramp_weight + extrap_freq * (1.0 - ramp_weight)


def positions_of(segments):
    row_count = segments.shape[-1]
    row_index = jnp.arange(row_count, dtype=jnp.int32)
    is_start = jnp.concatenate(
        [
            jnp.ones(segments.shape[:-1] + (1,), dtype=jnp.bool_),
            segments[..., 1:] != segments[..., :-1],
        ],
        axis=-1,
    )
    seg_start = lax.cummax(jnp.where(is_start, row_index, 0), axis=segments.ndim - 1)
    return row_index - seg_start


def rope_tables(places, head_size):
    angles = places.astype(jnp.float32)[:, None] * yarn_frequencies(head_size)[None, :]
    factor = 0.1 * math.log(yarn_factor) + 1.0
    cosine = jnp.cos(angles) * factor
    sine = jnp.sin(angles) * factor
    return (
        jnp.concatenate([cosine, cosine], axis=1),
        jnp.concatenate([-sine, sine], axis=1),
    )


def swap_halves(values):
    half = values.shape[-1] // 2
    return jnp.concatenate([values[..., half:], values[..., :half]], axis=-1)


NT = (((1,), (1,)), ((), ()))
TN = (((0,), (0,)), ((), ()))


def attend_kernel(
    heads,
    ranks,
    target_ref,
    source_ref,
    run_ref,
    slot_ref,
    need_ref,
    odd_ref,
    query_ref,
    up_ref,
    up_t_ref,
    place_ref,
    *refs,
):
    key_parts, refs = refs[:ranks], refs[ranks:]
    value_parts, refs = refs[:ranks], refs[ranks:]
    gquery_ref, out_ref, *halves = refs[:6]
    key_ref, value_ref, gkey_ref, gvalue_ref, key_win, value_win, load_sems, sems = refs[6:]
    rows_each = query_ref.shape[0]
    half_blocks = ranks * RUN_BLOCKS // 2
    scale = 1.0 / math.sqrt(HD)
    to_exp2 = scale * math.log2(math.e)

    loads = []
    for item, (parts, whole) in enumerate(((key_parts, key_ref), (value_parts, value_ref))):
        for rank in range(ranks):
            copy = pltpu.make_async_copy(
                parts[rank], whole.at[pl.ds(rank * rows_each, rows_each)], load_sems.at[item, rank]
            )
            copy.start()
            loads.append(copy)
    for copy in loads:
        copy.wait()

    def stores(block, act):
        side = block % 2
        for step in range(RUN_BLOCKS):
            target = target_ref[run_ref[block] * RUN_BLOCKS + step]
            for place in range(2):

                @pl.when(target // half_blocks == place)
                def one_half():
                    start = pl.multiple_of(target % half_blocks * ROWBLK, ROWBLK)
                    for item, source in enumerate((gkey_ref, gvalue_ref)):
                        act(
                            pltpu.make_async_copy(
                                source.at[side, pl.ds(step * ROWBLK, ROWBLK)],
                                halves[2 * item + place].at[pl.ds(start, ROWBLK)],
                                sems.at[side, item, step],
                            )
                        )

    def window(count, block):
        slot = slot_ref[block]
        run = run_ref[block]
        first = jnp.maximum(slot + 1 - count, 0)
        rows = count * ROWBLK
        for step in range(count):
            source = source_ref[run * RUN_BLOCKS + first + step]
            start = pl.multiple_of(source * ROWBLK, ROWBLK)
            key_win[pl.ds(step * ROWBLK, ROWBLK), :] = key_ref[pl.ds(start, ROWBLK), :]
            value_win[pl.ds(step * ROWBLK, ROWBLK), :] = value_ref[pl.ds(start, ROWBLK), :]
        wide = heads if count <= 4 else min(2, heads)
        cols = wide * ROWBLK
        base = pl.multiple_of(block * ROWBLK, ROWBLK)
        place = place_ref[pl.ds(block, 1), :]
        lane = lax.broadcasted_iota(jnp.int32, (1, ROWBLK), 1)
        last = (slot - first) * ROWBLK + lane
        last_all = jnp.concatenate([last] * wide, axis=1)
        start_all = jnp.concatenate([last - place] * wide, axis=1)
        key_index = lax.broadcasted_iota(jnp.int32, (rows, cols), 0)
        allowed = (key_index >= start_all) & (key_index <= last_all)
        keys = key_win[pl.ds(0, rows), :]
        values = value_win[pl.ds(0, rows), :]
        gkey = jnp.zeros((rows, HD), jnp.float32)
        gvalue = jnp.zeros((rows, HD), jnp.float32)
        for group in range(heads // wide):
            columns = [pl.ds((group * wide + item) * HD, HD) for item in range(wide)]
            at_rows = pl.ds(base, ROWBLK)
            query = jnp.concatenate([query_ref[at_rows, at] for at in columns], axis=0)
            up = jnp.concatenate([up_ref[at_rows, at] for at in columns], axis=0)
            up_t = jnp.concatenate([up_t_ref[at, at_rows] for at in columns], axis=1)
            score = lax.dot_general(keys, query, NT, preferred_element_type=jnp.float32)
            score = jnp.where(allowed, score, masked_score)
            peak = jnp.max(score, axis=0, keepdims=True)
            raised = jnp.exp2((score - peak) * to_exp2)
            total = jnp.sum(raised, axis=0, keepdims=True)
            prob = raised * (1.0 / total)
            prob_b = prob.astype(jnp.bfloat16)
            out_t = lax.dot_general(values, prob_b, TN, preferred_element_type=jnp.float32)
            out_b = out_t.astype(jnp.bfloat16)
            delta = jnp.sum(
                up_t.astype(jnp.float32) * out_b.astype(jnp.float32), axis=0, keepdims=True
            )
            gprob = lax.dot_general(values, up, NT, preferred_element_type=jnp.float32)
            gscore = (prob * (gprob - delta)).astype(jnp.bfloat16)
            gquery_t = lax.dot_general(keys, gscore, TN, preferred_element_type=jnp.float32)
            gkey = gkey + jnp.dot(gscore, query, preferred_element_type=jnp.float32)
            gvalue = gvalue + jnp.dot(prob_b, up, preferred_element_type=jnp.float32)
            for item in range(wide):
                part = slice(item * ROWBLK, (item + 1) * ROWBLK)
                head = group * wide + item
                half, row = head * 2 // heads, head % (heads // 2) * HD
                out_ref[half ^ odd_ref[0], pl.ds(row, HD), at_rows] = out_b[:, part]
                gquery_ref[columns[item], at_rows] = gquery_t[:, part]
        gkey = (gkey * scale).astype(jnp.bfloat16)
        gvalue = gvalue.astype(jnp.bfloat16)
        place_at = pl.ds(pl.multiple_of(first * ROWBLK, ROWBLK), rows)
        gkey_ref[block % 2, place_at, :] = gkey
        gvalue_ref[block % 2, place_at, :] = gvalue

    def body(block, carry):
        pl.when(block >= 2)(lambda: stores(block - 2, lambda copy: copy.wait()))
        blank = jnp.zeros(gkey_ref.shape[1:], jnp.bfloat16)
        gkey_ref[block % 2] = blank
        gvalue_ref[block % 2] = blank
        need = need_ref[block]
        floor = 0
        for size in (1, 2, 3, 4, 6, 8):
            pl.when((need > floor) & (need <= size))(partial(window, size, block))
            floor = size
        stores(block, lambda copy: copy.start())
        return carry

    blocks = rows_each // ROWBLK
    lax.fori_loop(0, blocks, body, 0)
    for block in range(max(blocks - 2, 0), blocks):
        stores(block, lambda copy: copy.wait())


def attend(tables, query, up, up_t, places, keys, values):
    rows, width = query.shape
    heads = width // HD
    ranks = len(keys)
    every = rows * ranks
    smem = pl.BlockSpec(memory_space=pltpu.SMEM)
    vmem = pl.BlockSpec(memory_space=pltpu.VMEM)
    hbm = pl.BlockSpec(memory_space=pl.ANY)
    half = jax.ShapeDtypeStruct((every // 2, HD), jnp.bfloat16)
    return pl.pallas_call(
        partial(attend_kernel, heads, ranks),
        out_shape=(
            jax.ShapeDtypeStruct((width, rows), jnp.float32),
            jax.ShapeDtypeStruct((2, width // 2, rows), jnp.bfloat16),
            half,
            half,
            half,
            half,
        ),
        in_specs=[smem] * 6 + [vmem] * 4 + [hbm] * (2 * ranks),
        out_specs=(vmem, vmem, hbm, hbm, hbm, hbm),
        scratch_shapes=[pltpu.VMEM((every, HD), jnp.bfloat16)] * 2
        + [pltpu.VMEM((2, RUN_BLOCKS * ROWBLK, HD), jnp.bfloat16)] * 2
        + [pltpu.VMEM((RUN_BLOCKS * ROWBLK, HD), jnp.bfloat16)] * 2
        + [pltpu.SemaphoreType.DMA((2, ranks)), pltpu.SemaphoreType.DMA((2, 2, RUN_BLOCKS))],
        compiler_params=pltpu.CompilerParams(vmem_limit_bytes=VMEM_BYTES),
        cost_estimate=NO_COST,
    )(*tables, query, up, up_t, places, *keys, *values)


def assemble_kernel(lanes, my_ref, *refs):
    out_ref, sems = refs[lanes:]
    copies = []
    for index in range(lanes):
        column = pl.multiple_of((my_ref[0] ^ index) * HD, HD)
        copy = pltpu.make_async_copy(
            refs[index], out_ref.at[:, pl.ds(column, HD)], sems.at[index]
        )
        copy.start()
        copies.append(copy)
    for copy in copies:
        copy.wait()


def assemble(my_lane, pieces):
    rows = pieces[0].shape[0]
    lanes = len(pieces)
    vmem = pl.BlockSpec(memory_space=pltpu.VMEM)
    return pl.pallas_call(
        partial(assemble_kernel, lanes),
        out_shape=jax.ShapeDtypeStruct((rows, lanes * HD), pieces[0].dtype),
        in_specs=[pl.BlockSpec(memory_space=pltpu.SMEM)] + [vmem] * lanes,
        out_specs=pl.BlockSpec(memory_space=pl.ANY),
        scratch_shapes=[pltpu.SemaphoreType.DMA((lanes,))],
        compiler_params=pltpu.CompilerParams(vmem_limit_bytes=VMEM_BYTES),
        cost_estimate=NO_COST,
    )(my_lane.reshape(1), *pieces)


def lane_gather(array, my_lane):
    lanes = lax.axis_size("tensor")
    pieces = {0: array}
    bit = lanes // 2
    while bit:
        pairs = [(lane, lane ^ bit) for lane in range(lanes)]
        pieces.update(
            {at | bit: lax.ppermute(item, "tensor", pairs) for at, item in list(pieces.items())}
        )
        bit //= 2
    pieces = [pieces[at] for at in range(lanes)]
    return assemble(my_lane, pieces), pieces[1:]


def swap(array, bit):
    ranks = lax.axis_size("dp")
    return lax.ppermute(array, "dp", [(rank, rank ^ bit) for rank in range(ranks)])


def spread(array):
    found = [array, swap(array, 1)]
    others = [swap(array, step) for step in range(2, lax.axis_size("dp"), 2)]
    for other in others:
        found += [other, swap(other, 1)]
    return found


def added(left, right):
    return left.astype(jnp.float32) + right.astype(jnp.float32)


def chip_sum(keep, received):
    count = lax.axis_size("dp") // 2
    rows = keep.shape[0] // count
    total = [
        added(keep[at * rows : (at + 1) * rows], received[at * rows : (at + 1) * rows])
        for at in range(count)
    ]
    return total[0], [item.astype(keep.dtype) for item in total[1:]]


def exchange(sends):
    return [swap(item, 2 * at + 2) for at, item in enumerate(sends)]


def final_kernel(count, rotary, out_at, *refs):
    total = refs[0][...].astype(jnp.float32)
    for ref in refs[1 : 1 + count]:
        total = total + ref[...].astype(jnp.float32)
    if rotary:
        total = total * refs[1 + count][...] - pltpu.roll(total, HD // 2, 1) * refs[2 + count][...]
    refs[out_at][...] = total.astype(refs[out_at].dtype)


def final_sum(keep, received, tables, after, kind=jnp.bfloat16, thru=()):
    vmem = pl.BlockSpec(memory_space=pltpu.VMEM)
    hbm = pl.BlockSpec(memory_space=pl.ANY)
    parts = [keep, *received, *tables]
    inputs = len(parts) + len(after) + len(thru)
    results = pl.pallas_call(
        partial(final_kernel, len(received), len(tables) > 0, inputs),
        out_shape=[jax.ShapeDtypeStruct(keep.shape, kind)]
        + [jax.ShapeDtypeStruct(item.shape, item.dtype) for item in thru],
        in_specs=[vmem] * len(parts) + [hbm] * (len(after) + len(thru)),
        out_specs=[vmem] + [hbm] * len(thru),
        input_output_aliases={inputs - len(thru) + at: 1 + at for at in range(len(thru))},
        compiler_params=pltpu.CompilerParams(vmem_limit_bytes=VMEM_BYTES),
        cost_estimate=NO_COST,
    )(*parts, *after, *thru)
    return results if thru else results[0]


def prepare_kernel(
    rows_ref, weight_ref, query_ref, cos_ref, sin_ref, *refs
):
    up_ref, up_t_ref, turned_ref = refs[-3:]
    total = jnp.dot(rows_ref[...], weight_ref[...], preferred_element_type=jnp.float32)
    up_ref[...] = total.astype(up_ref.dtype)
    up_t_ref[...] = total.T.astype(up_t_ref.dtype)
    for at in range(0, query_ref.shape[1], HD):
        raw = query_ref[:, at : at + HD].astype(jnp.float32)
        turned = raw * cos_ref[...] + pltpu.roll(raw, HD // 2, 1) * sin_ref[...]
        turned_ref[:, at : at + HD] = turned.astype(turned_ref.dtype)


def prepare(rows, weight, query, cosine, sine, after):
    height, depth = rows.shape
    width = weight.shape[1]
    steps = 4
    tall = height // steps
    across = lambda columns: pl.BlockSpec((tall, columns), lambda step: (step, 0))
    return pl.pallas_call(
        prepare_kernel,
        grid=(steps,),
        out_shape=[
            jax.ShapeDtypeStruct((height, width), jnp.bfloat16),
            jax.ShapeDtypeStruct((width, height), jnp.bfloat16),
            jax.ShapeDtypeStruct(query.shape, jnp.bfloat16),
        ],
        in_specs=[
            across(depth),
            pl.BlockSpec(weight.shape, lambda step: (0, 0)),
            across(width),
            across(HD),
            across(HD),
        ]
        + [pl.BlockSpec(memory_space=pl.ANY)] * len(after),
        out_specs=[
            across(width),
            pl.BlockSpec((width, tall), lambda step: (0, step)),
            across(width),
        ],
        compiler_params=pltpu.CompilerParams(vmem_limit_bytes=VMEM_BYTES),
        cost_estimate=pl.CostEstimate(
            flops=2 * height * weight.size, bytes_accessed=2 * rows.size, transcendentals=0
        ),
    )(rows, weight, query, cosine, sine, *after)


def turn_back_kernel(grad_ref, cos_ref, sin_ref, *refs):
    out_ref = refs[-1]
    scale = 1.0 / math.sqrt(HD)
    for at in range(0, grad_ref.shape[0], HD):
        grad = grad_ref[at : at + HD, :].T * scale
        back = grad * cos_ref[...] - pltpu.roll(grad, HD // 2, 1) * sin_ref[...]
        out_ref[:, at : at + HD] = back.astype(out_ref.dtype)


def turn_back(grad_t, cosine, sine, after):
    width, height = grad_t.shape
    steps = 4
    tall = height // steps
    return pl.pallas_call(
        turn_back_kernel,
        grid=(steps,),
        out_shape=jax.ShapeDtypeStruct((height, width), jnp.bfloat16),
        in_specs=[
            pl.BlockSpec((width, tall), lambda step: (0, step)),
            pl.BlockSpec((tall, HD), lambda step: (step, 0)),
            pl.BlockSpec((tall, HD), lambda step: (step, 0)),
        ]
        + [pl.BlockSpec(memory_space=pl.ANY)] * len(after),
        out_specs=pl.BlockSpec((tall, width), lambda step: (step, 0)),
        compiler_params=pltpu.CompilerParams(vmem_limit_bytes=VMEM_BYTES),
        cost_estimate=NO_COST,
    )(grad_t, cosine, sine, *after)


def take_heads_kernel(at_ref, key_ref, value_ref, after_ref, own_key_ref, own_value_ref):
    own_key_ref[...] = key_ref[...]
    own_value_ref[...] = value_ref[...]


def take_heads(key, value, kv_head, after):
    rows = key.shape[0]
    picked = pl.BlockSpec((rows, HD), lambda step, at_ref: (0, at_ref[0]))
    own = pl.BlockSpec((rows, HD), lambda step, at_ref: (0, 0))
    shape = jax.ShapeDtypeStruct((rows, HD), key.dtype)
    return pl.pallas_call(
        take_heads_kernel,
        grid_spec=pltpu.PrefetchScalarGridSpec(
            num_scalar_prefetch=1,
            grid=(1,),
            in_specs=[picked, picked, pl.BlockSpec(memory_space=pl.ANY)],
            out_specs=[own, own],
        ),
        out_shape=[shape, shape],
        cost_estimate=NO_COST,
    )(kv_head.reshape(1), key, value, after)


def product_kernel(my_ref, left_ref, right_ref, *refs):
    keep_ref, send_ref = refs[-3:-1]
    half = left_ref.shape[1]
    left = left_ref[...].reshape(2 * half, left_ref.shape[2])
    total = jnp.dot(left, right_ref[...], preferred_element_type=jnp.float32)
    keep_ref[0] = total[:half].astype(keep_ref.dtype)
    send_ref[0] = total[half:].astype(send_ref.dtype)


def product(mine, left, right, thru, after):
    count = lax.axis_size("dp") // 2
    half, depth = left.shape[1:]
    cols = right.shape[1] // count
    if cols % 128:
        total = jnp.dot(left.reshape(2 * half, depth), right, preferred_element_type=jnp.float32)
        pieces = jnp.moveaxis(total.astype(jnp.bfloat16).reshape(2 * half, count, cols), 1, 0)
        pieces = jnp.take(pieces, jnp.arange(count, dtype=jnp.int32) ^ mine, axis=0)
        return pieces[:, :half], pieces[:, half:], thru
    hbm = pl.BlockSpec(memory_space=pl.ANY)
    stacked = pl.BlockSpec((1, half, cols), lambda step, my_ref: (step, 0, 0))
    stack = jax.ShapeDtypeStruct((count, half, cols), jnp.bfloat16)
    inputs = [mine.reshape(1), left, right, *after, thru]
    return pl.pallas_call(
        product_kernel,
        grid_spec=pltpu.PrefetchScalarGridSpec(
            num_scalar_prefetch=1,
            grid=(count,),
            in_specs=[
                pl.BlockSpec(left.shape, lambda step, my_ref: (0, 0, 0)),
                pl.BlockSpec((depth, cols), lambda step, my_ref: (0, step ^ my_ref[0])),
            ]
            + [hbm] * (len(after) + 1),
            out_specs=[stacked, stacked, hbm],
        ),
        out_shape=[stack, stack, jax.ShapeDtypeStruct(thru.shape, thru.dtype)],
        input_output_aliases={len(inputs) - 1: 2},
        compiler_params=pltpu.CompilerParams(vmem_limit_bytes=VMEM_BYTES),
        cost_estimate=NO_COST,
    )(*inputs)


def local(query, key, value, grad_out, out_weight, plan, segments):
    rank_count = lax.axis_size("dp")
    my_rank = lax.axis_index("dp")
    my_lane = lax.axis_index("tensor")
    row_count = query.shape[0]
    block_count = row_count // ROWBLK
    local_heads = query.shape[1] // HD
    group = HEADS // KV
    bits = [1 << at for at in range(rank_count.bit_length() - 1)]
    kv_head = my_lane * local_heads // group
    own_places = positions_of(segments).reshape(1, block_count, ROWBLK)
    pair_places = jnp.concatenate([own_places, swap(own_places, 1)], axis=0)
    places_all = jnp.concatenate(
        [pair_places] + [swap(pair_places, step) for step in range(2, rank_count, 2)], axis=0
    ).reshape(-1, ROWBLK)
    own_key, own_value = take_heads(key, value, kv_head, pair_places)
    values = spread(own_value)

    mine = my_rank * block_count + jnp.arange(block_count, dtype=jnp.int32)
    hit = plan[None, :] == mine[:, None]
    dest = jnp.sum(
        jnp.where(hit, jnp.arange(plan.shape[0], dtype=jnp.int32)[None, :], 0), axis=1
    )
    run = dest // RUN_BLOCKS
    slot = dest % RUN_BLOCKS
    places = jnp.take(places_all, (run ^ my_rank) * RUN_BLOCKS + slot, axis=0)
    need = slot - (slot * ROWBLK - places[:, 0]) // ROWBLK + 1
    cosine, sine = rope_tables(places.reshape(row_count), HD)
    key_f = own_key.astype(jnp.float32)
    rot_key = (key_f * cosine + swap_halves(key_f) * sine).astype(jnp.bfloat16)
    keys = spread(rot_key)
    up, up_t, turned = prepare(grad_out, out_weight, query, cosine, sine, [rot_key])

    distance = (plan // block_count) ^ my_rank
    within = plan % block_count
    half_place = (distance & 1) * (rank_count // 2) + distance // 2
    tables = (
        half_place * block_count + within,
        distance * block_count + within,
        run,
        slot,
        need,
        (my_rank & 1).reshape(1),
    )
    grad_query_t, attn_t, gkey_keep, gkey_send, gvalue_keep, gvalue_send = attend(
        tables, turned, up, up_t, places, keys, values
    )
    value_keep, value_sends = chip_sum(gvalue_keep, swap(gvalue_send, 1))
    value_received = exchange(value_sends)
    key_keep, key_sends = chip_sum(gkey_keep, swap(gkey_send, 1))
    key_received = exchange(key_sends)
    weight_keep, weight_send, value_keep = product(
        my_rank // 2, attn_t, grad_out, value_keep, [value_sends[0], key_sends[0]]
    )
    value_partial, weight_send = final_sum(
        value_keep, value_received, (), (), thru=[weight_send]
    )
    value_all, value_pieces = lane_gather(value_partial, my_lane)
    weight_other = swap(weight_send, 1)
    grad_query = turn_back(grad_query_t, cosine, sine, [weight_send])
    weight_keep, weight_sends = chip_sum(weight_keep, weight_other)
    weight_received = exchange(weight_sends)
    key_partial = final_sum(
        key_keep, key_received, (cosine, sine), [weight_sends[0], grad_query]
    )
    key_all, key_pieces = lane_gather(key_partial, my_lane)
    total = final_sum(
        weight_keep, weight_received, (), [*key_pieces[:2], value_all], jnp.float32
    )[0]
    odd = my_rank & 1
    pair_rows = grad_out.shape[1] // (rank_count // 2)
    low, high = total[:, : pair_rows // 2], total[:, pair_rows // 2 :]
    is_odd = odd > 0
    other = swap(jnp.where(is_odd, low, high).astype(jnp.bfloat16), 1).astype(jnp.float32)
    mine_half = jnp.where(is_odd, high, low)
    weight_grad = jnp.concatenate(
        [jnp.where(is_odd, other, mine_half), jnp.where(is_odd, mine_half, other)], axis=0
    ).T
    lanes_per_key = group // local_heads

    def combine(gathered):
        if lanes_per_key == 1:
            return gathered
        merged = (
            gathered.astype(jnp.float32).reshape(row_count, KV, lanes_per_key, HD).sum(axis=2)
        )
        return merged.astype(jnp.bfloat16).reshape(row_count, KV * HD)

    return (grad_query, combine(key_all), combine(value_all), weight_grad * (1.0 / rank_count))


def solution(mesh):
    in_specs = (
        P("dp", "tensor"),
        P("dp", None),
        P("dp", None),
        P("dp", None),
        P(None, "tensor"),
        P(),
        P("dp"),
    )
    out_specs = (P("dp", "tensor"), P("dp", None), P("dp", None), P("dp", "tensor"))
    return jax.shard_map(local, mesh=mesh, in_specs=in_specs, out_specs=out_specs, check_vma=False)
```

```python
from functools import partial
import math

import jax
import jax.numpy as jnp
from jax import lax
from jax.experimental import pallas as pl
from jax.experimental.pallas import tpu as pltpu
from jax.sharding import PartitionSpec as P

KV = 4
HD = 128
HEADS = 16
ROWBLK = 128
RUN_BLOCKS = 8
VMEM_BYTES = 58 * 1024 * 1024
NO_COST = pl.CostEstimate(flops=0, bytes_accessed=0, transcendentals=0)


rope_base = 1000000.0
yarn_factor = 4.0
yarn_context = 32768.0
beta_fast = 32.0
beta_slow = 1.0
masked_score = -1e30


def yarn_frequencies(head_size):
    half_size = head_size // 2

    def correction(rotations):
        return (
            head_size
            * math.log(yarn_context / (rotations * 2.0 * math.pi))
            / (2.0 * math.log(rope_base))
        )

    lower_bound = max(math.floor(correction(beta_fast)), 0)
    upper_bound = min(math.ceil(correction(beta_slow)), head_size - 1)
    ramp_span = max(upper_bound - lower_bound, 0.001)
    row_index = jnp.arange(half_size).astype(jnp.float32)
    extrap_freq = rope_base ** (-2.0 * row_index / head_size)
    interp_freq = extrap_freq / yarn_factor
    ramp_weight = jnp.clip((row_index - lower_bound) / ramp_span, 0.0, 1.0)
    return interp_freq * ramp_weight + extrap_freq * (1.0 - ramp_weight)


def positions_of(segments):
    row_count = segments.shape[-1]
    row_index = jnp.arange(row_count, dtype=jnp.int32)
    is_start = jnp.concatenate(
        [
            jnp.ones(segments.shape[:-1] + (1,), dtype=jnp.bool_),
            segments[..., 1:] != segments[..., :-1],
        ],
        axis=-1,
    )
    seg_start = lax.cummax(jnp.where(is_start, row_index, 0), axis=segments.ndim - 1)
    return row_index - seg_start


def rope_tables(places, head_size):
    angles = places.astype(jnp.float32)[:, None] * yarn_frequencies(head_size)[None, :]
    factor = 0.1 * math.log(yarn_factor) + 1.0
    cosine = jnp.cos(angles) * factor
    sine = jnp.sin(angles) * factor
    return (
        jnp.concatenate([cosine, cosine], axis=1),
        jnp.concatenate([-sine, sine], axis=1),
    )


def swap_halves(values):
    half = values.shape[-1] // 2
    return jnp.concatenate([values[..., half:], values[..., :half]], axis=-1)


NT = (((1,), (1,)), ((), ()))
TN = (((0,), (0,)), ((), ()))


def attend_kernel(
    heads,
    ranks,
    target_ref,
    source_ref,
    run_ref,
    slot_ref,
    need_ref,
    query_ref,
    up_ref,
    up_t_ref,
    place_ref,
    *refs,
):
    key_parts, refs = refs[:ranks], refs[ranks:]
    value_parts, refs = refs[:ranks], refs[ranks:]
    gquery_ref, out_ref, *halves = refs[:6]
    key_ref, value_ref, gkey_ref, gvalue_ref, key_win, value_win = refs[6:12]
    score_ref, prob_ref, gscore_ref, load_sems, sems = refs[12:]
    rows_each = query_ref.shape[0]
    half_blocks = ranks * RUN_BLOCKS // 2
    scale = 1.0 / math.sqrt(HD)
    to_exp2 = scale * math.log2(math.e)

    loads = []
    for item, (parts, whole) in enumerate(((key_parts, key_ref), (value_parts, value_ref))):
        for rank in range(ranks):
            copy = pltpu.make_async_copy(
                parts[rank], whole.at[pl.ds(rank * rows_each, rows_each)], load_sems.at[item, rank]
            )
            copy.start()
            loads.append(copy)
    for copy in loads:
        copy.wait()

    def stores(block, act):
        side = block % 2
        for step in range(RUN_BLOCKS):
            target = target_ref[run_ref[block] * RUN_BLOCKS + step]
            for place in range(2):

                @pl.when(target // half_blocks == place)
                def one_half():
                    start = pl.multiple_of(target % half_blocks * ROWBLK, ROWBLK)
                    for item, source in enumerate((gkey_ref, gvalue_ref)):
                        act(
                            pltpu.make_async_copy(
                                source.at[side, pl.ds(step * ROWBLK, ROWBLK)],
                                halves[2 * item + place].at[pl.ds(start, ROWBLK)],
                                sems.at[side, item, step],
                            )
                        )

    def window(count, block):
        slot = slot_ref[block]
        run = run_ref[block]
        first = jnp.maximum(slot + 1 - count, 0)
        rows = count * ROWBLK
        for step in range(count):
            source = source_ref[run * RUN_BLOCKS + first + step]
            start = pl.multiple_of(source * ROWBLK, ROWBLK)
            key_win[pl.ds(step * ROWBLK, ROWBLK), :] = key_ref[pl.ds(start, ROWBLK), :]
            value_win[pl.ds(step * ROWBLK, ROWBLK), :] = value_ref[pl.ds(start, ROWBLK), :]
        wide = min(2, heads)
        base = pl.multiple_of(block * ROWBLK, ROWBLK)
        at_rows = pl.ds(base, ROWBLK)
        place = place_ref[pl.ds(block, 1), :]
        lane = lax.broadcasted_iota(jnp.int32, (1, ROWBLK), 1)
        last = (slot - first) * ROWBLK + lane
        last_all = jnp.concatenate([last] * wide, axis=1)
        start_all = jnp.concatenate([last - place] * wide, axis=1)
        key_index = lax.broadcasted_iota(jnp.int32, (ROWBLK, wide * ROWBLK), 0)
        keys = key_win[pl.ds(0, rows), :]
        values = value_win[pl.ds(0, rows), :]
        columns = [pl.ds(head * HD, HD) for head in range(heads)]
        query = jnp.concatenate([query_ref[at_rows, at] for at in columns], axis=0)
        up = jnp.concatenate([up_ref[at_rows, at] for at in columns], axis=0)
        folded = lambda tile: tile.reshape(ROWBLK // 8, 8, tile.shape[1])
        tiles = [pl.ds(step * ROWBLK, ROWBLK) for step in range(count)]
        groups = heads // wide
        spans = [slice(at * wide * ROWBLK, (at + 1) * wide * ROWBLK) for at in range(groups)]

        score = lax.dot_general(keys, query, NT, preferred_element_type=jnp.float32)
        gprob = lax.dot_general(values, up, NT, preferred_element_type=jnp.float32)
        peaks = [None] * groups
        for step, tile in enumerate(tiles):
            seen = key_index >= start_all - step * ROWBLK
            if step == count - 1:
                seen = seen & (key_index <= last_all - step * ROWBLK)
            for at, span in enumerate(spans):
                part = jnp.where(
                    seen, score[step * ROWBLK : (step + 1) * ROWBLK, span], masked_score
                )
                score_ref[tile, span] = part
                most = jnp.max(folded(part), axis=0)
                peaks[at] = most if peaks[at] is None else jnp.maximum(peaks[at], most)
        peaks = [jnp.max(item, axis=0, keepdims=True) for item in peaks]
        totals = [None] * groups
        for tile in tiles:
            for at, span in enumerate(spans):
                part = jnp.exp2((score_ref[tile, span] - peaks[at]) * to_exp2)
                score_ref[tile, span] = part
                some = jnp.sum(folded(part), axis=0)
                totals[at] = some if totals[at] is None else totals[at] + some
        shares = [1.0 / jnp.sum(item, axis=0, keepdims=True) for item in totals]
        for tile in tiles:
            for at, span in enumerate(spans):
                prob_ref[tile, span] = (score_ref[tile, span] * shares[at]).astype(jnp.bfloat16)
        prob_b = prob_ref[pl.ds(0, rows), :]
        out_t = lax.dot_general(values, prob_b, TN, preferred_element_type=jnp.float32)
        out_b = out_t.astype(jnp.bfloat16)
        deltas = []
        for at in range(groups):
            up_t = jnp.concatenate(
                [up_t_ref[item, at_rows] for item in columns[at * wide : (at + 1) * wide]], axis=1
            ).astype(jnp.float32)
            deltas.append(
                jnp.sum(up_t * out_b[:, spans[at]].astype(jnp.float32), axis=0, keepdims=True)
            )
        for step, tile in enumerate(tiles):
            for at, span in enumerate(spans):
                prob = score_ref[tile, span] * shares[at]
                part = gprob[step * ROWBLK : (step + 1) * ROWBLK, span] - deltas[at]
                gscore_ref[tile, span] = (prob * part).astype(jnp.bfloat16)
        gscore = gscore_ref[pl.ds(0, rows), :]
        gquery_t = lax.dot_general(keys, gscore, TN, preferred_element_type=jnp.float32)
        gkey = jnp.dot(gscore, query, preferred_element_type=jnp.float32)
        gvalue = jnp.dot(prob_b, up, preferred_element_type=jnp.float32)
        for head in range(heads):
            part = slice(head * ROWBLK, (head + 1) * ROWBLK)
            out_ref[columns[head], at_rows] = out_b[:, part]
            gquery_ref[columns[head], at_rows] = gquery_t[:, part]
        gkey = (gkey * scale).astype(jnp.bfloat16)
        gvalue = gvalue.astype(jnp.bfloat16)
        place_at = pl.ds(pl.multiple_of(first * ROWBLK, ROWBLK), rows)
        gkey_ref[block % 2, place_at, :] = gkey
        gvalue_ref[block % 2, place_at, :] = gvalue

    def body(block, carry):
        pl.when(block >= 2)(lambda: stores(block - 2, lambda copy: copy.wait()))
        blank = jnp.zeros(gkey_ref.shape[1:], jnp.bfloat16)
        gkey_ref[block % 2] = blank
        gvalue_ref[block % 2] = blank
        need = need_ref[block]
        floor = 0
        for size in range(1, RUN_BLOCKS + 1):
            pl.when((need > floor) & (need <= size))(partial(window, size, block))
            floor = size
        stores(block, lambda copy: copy.start())
        return carry

    blocks = rows_each // ROWBLK
    lax.fori_loop(0, blocks, body, 0)
    for block in range(max(blocks - 2, 0), blocks):
        stores(block, lambda copy: copy.wait())


def attend(tables, query, up, up_t, places, keys, values):
    rows, width = query.shape
    heads = width // HD
    ranks = len(keys)
    every = rows * ranks
    smem = pl.BlockSpec(memory_space=pltpu.SMEM)
    vmem = pl.BlockSpec(memory_space=pltpu.VMEM)
    hbm = pl.BlockSpec(memory_space=pl.ANY)
    half = jax.ShapeDtypeStruct((every // 2, HD), jnp.bfloat16)
    return pl.pallas_call(
        partial(attend_kernel, heads, ranks),
        out_shape=(
            jax.ShapeDtypeStruct((width, rows), jnp.float32),
            jax.ShapeDtypeStruct((width, rows), jnp.bfloat16),
            half,
            half,
            half,
            half,
        ),
        in_specs=[smem] * 5 + [vmem] * 4 + [hbm] * (2 * ranks),
        out_specs=(vmem, vmem, hbm, hbm, hbm, hbm),
        scratch_shapes=[pltpu.VMEM((every, HD), jnp.bfloat16)] * 2
        + [pltpu.VMEM((2, RUN_BLOCKS * ROWBLK, HD), jnp.bfloat16)] * 2
        + [pltpu.VMEM((RUN_BLOCKS * ROWBLK, HD), jnp.bfloat16)] * 2
        + [pltpu.VMEM((RUN_BLOCKS * ROWBLK, heads * ROWBLK), jnp.float32)]
        + [pltpu.VMEM((RUN_BLOCKS * ROWBLK, heads * ROWBLK), jnp.bfloat16)] * 2
        + [pltpu.SemaphoreType.DMA((2, ranks)), pltpu.SemaphoreType.DMA((2, 2, RUN_BLOCKS))],
        compiler_params=pltpu.CompilerParams(vmem_limit_bytes=VMEM_BYTES),
        cost_estimate=NO_COST,
    )(*tables, query, up, up_t, places, *keys, *values)


def assemble_kernel(lanes, my_ref, *refs):
    out_ref, sems = refs[lanes:]
    copies = []
    for index in range(lanes):
        column = pl.multiple_of((my_ref[0] ^ index) * HD, HD)
        copy = pltpu.make_async_copy(
            refs[index], out_ref.at[:, pl.ds(column, HD)], sems.at[index]
        )
        copy.start()
        copies.append(copy)
    for copy in copies:
        copy.wait()


def assemble(my_lane, pieces):
    rows = pieces[0].shape[0]
    lanes = len(pieces)
    vmem = pl.BlockSpec(memory_space=pltpu.VMEM)
    return pl.pallas_call(
        partial(assemble_kernel, lanes),
        out_shape=jax.ShapeDtypeStruct((rows, lanes * HD), pieces[0].dtype),
        in_specs=[pl.BlockSpec(memory_space=pltpu.SMEM)] + [vmem] * lanes,
        out_specs=pl.BlockSpec(memory_space=pl.ANY),
        scratch_shapes=[pltpu.SemaphoreType.DMA((lanes,))],
        compiler_params=pltpu.CompilerParams(vmem_limit_bytes=VMEM_BYTES),
        cost_estimate=NO_COST,
    )(my_lane.reshape(1), *pieces)


def lane_swap(array, bit):
    lanes = lax.axis_size("tensor")
    return lax.ppermute(array, "tensor", [(lane, lane ^ bit) for lane in range(lanes)])


def lane_pieces(pieces, bit):
    lanes = lax.axis_size("tensor")
    while bit:
        pieces = {**pieces, **{at | bit: lane_swap(item, bit) for at, item in pieces.items()}}
        bit //= 2
    return [pieces[at] for at in range(lanes)]


def swap(array, bit):
    ranks = lax.axis_size("dp")
    return lax.ppermute(array, "dp", [(rank, rank ^ bit) for rank in range(ranks)])


def spread(array):
    found = [array, swap(array, 1)]
    others = [swap(array, step) for step in range(2, lax.axis_size("dp"), 2)]
    for other in others:
        found += [other, swap(other, 1)]
    return found


def added(left, right):
    return left.astype(jnp.float32) + right.astype(jnp.float32)


def chip_sum(keep, received):
    count = lax.axis_size("dp") // 2
    rows = keep.shape[0] // count
    total = [
        added(keep[at * rows : (at + 1) * rows], received[at * rows : (at + 1) * rows])
        for at in range(count)
    ]
    return total[0], [item.astype(keep.dtype) for item in total[1:]]


def exchange(sends):
    return [swap(item, 2 * at + 2) for at, item in enumerate(sends)]


def final_kernel(count, rotary, outs, *refs):
    total = refs[0][...].astype(jnp.float32)
    for ref in refs[1 : 1 + count]:
        total = total + ref[...].astype(jnp.float32)
    if rotary:
        total = total * refs[1 + count][...] - pltpu.roll(total, HD // 2, 1) * refs[2 + count][...]
    for at in outs:
        refs[at][...] = total.astype(refs[at].dtype)


def final_sum(keep, received, tables, after, thru=(), copies=1):
    vmem = pl.BlockSpec(memory_space=pltpu.VMEM)
    hbm = pl.BlockSpec(memory_space=pl.ANY)
    parts = [keep, *received, *tables]
    inputs = len(parts) + len(after) + len(thru)
    results = pl.pallas_call(
        partial(
            final_kernel, len(received), len(tables) > 0, range(inputs, inputs + copies)
        ),
        out_shape=[jax.ShapeDtypeStruct(keep.shape, jnp.bfloat16)] * copies
        + [jax.ShapeDtypeStruct(item.shape, item.dtype) for item in thru],
        in_specs=[vmem] * len(parts) + [hbm] * (len(after) + len(thru)),
        out_specs=[vmem] * copies + [hbm] * len(thru),
        input_output_aliases={inputs - len(thru) + at: copies + at for at in range(len(thru))},
        compiler_params=pltpu.CompilerParams(vmem_limit_bytes=VMEM_BYTES),
        cost_estimate=NO_COST,
    )(*parts, *after, *thru)
    return results


def prepare_kernel(
    rows_ref, weight_ref, query_ref, cos_ref, sin_ref, *refs
):
    up_ref, up_t_ref, turned_ref = refs[-3:]
    total = jnp.dot(rows_ref[...], weight_ref[...], preferred_element_type=jnp.float32)
    up_ref[...] = total.astype(up_ref.dtype)
    up_t_ref[...] = total.T.astype(up_t_ref.dtype)
    for at in range(0, query_ref.shape[1], HD):
        raw = query_ref[:, at : at + HD].astype(jnp.float32)
        turned = raw * cos_ref[...] + pltpu.roll(raw, HD // 2, 1) * sin_ref[...]
        turned_ref[:, at : at + HD] = turned.astype(turned_ref.dtype)


def prepare(rows, weight, query, cosine, sine, after):
    height, depth = rows.shape
    width = weight.shape[1]
    steps = 4
    tall = height // steps
    across = lambda columns: pl.BlockSpec((tall, columns), lambda step: (step, 0))
    return pl.pallas_call(
        prepare_kernel,
        grid=(steps,),
        out_shape=[
            jax.ShapeDtypeStruct((height, width), jnp.bfloat16),
            jax.ShapeDtypeStruct((width, height), jnp.bfloat16),
            jax.ShapeDtypeStruct(query.shape, jnp.bfloat16),
        ],
        in_specs=[
            across(depth),
            pl.BlockSpec(weight.shape, lambda step: (0, 0)),
            across(width),
            across(HD),
            across(HD),
        ]
        + [pl.BlockSpec(memory_space=pl.ANY)] * len(after),
        out_specs=[
            across(width),
            pl.BlockSpec((width, tall), lambda step: (0, step)),
            across(width),
        ],
        compiler_params=pltpu.CompilerParams(vmem_limit_bytes=VMEM_BYTES),
        cost_estimate=pl.CostEstimate(
            flops=2 * height * weight.size, bytes_accessed=2 * rows.size, transcendentals=0
        ),
    )(rows, weight, query, cosine, sine, *after)


def turn_back_kernel(grad_ref, cos_ref, sin_ref, *refs):
    out_ref = refs[-1]
    scale = 1.0 / math.sqrt(HD)
    for at in range(0, grad_ref.shape[0], HD):
        grad = grad_ref[at : at + HD, :].T * scale
        back = grad * cos_ref[...] - pltpu.roll(grad, HD // 2, 1) * sin_ref[...]
        out_ref[:, at : at + HD] = back.astype(out_ref.dtype)


def turn_back(grad_t, cosine, sine, after):
    width, height = grad_t.shape
    steps = 4
    tall = height // steps
    return pl.pallas_call(
        turn_back_kernel,
        grid=(steps,),
        out_shape=jax.ShapeDtypeStruct((height, width), jnp.bfloat16),
        in_specs=[
            pl.BlockSpec((width, tall), lambda step: (0, step)),
            pl.BlockSpec((tall, HD), lambda step: (step, 0)),
            pl.BlockSpec((tall, HD), lambda step: (step, 0)),
        ]
        + [pl.BlockSpec(memory_space=pl.ANY)] * len(after),
        out_specs=pl.BlockSpec((tall, width), lambda step: (step, 0)),
        compiler_params=pltpu.CompilerParams(vmem_limit_bytes=VMEM_BYTES),
        cost_estimate=NO_COST,
    )(grad_t, cosine, sine, *after)


def hold_kernel(*refs):
    pass


def hold(array, after):
    hbm = pl.BlockSpec(memory_space=pl.ANY)
    return pl.pallas_call(
        hold_kernel,
        out_shape=jax.ShapeDtypeStruct(array.shape, array.dtype),
        in_specs=[hbm] * (1 + len(after)),
        out_specs=hbm,
        input_output_aliases={0: 0},
        cost_estimate=NO_COST,
    )(array, *after)


def product_kernel(my_ref, left_ref, right_ref, *refs):
    keep_ref, send_ref = refs[-3:-1]
    half = keep_ref.shape[1]
    total = jnp.dot(left_ref[...], right_ref[...], preferred_element_type=jnp.float32)
    total = total.astype(keep_ref.dtype).T
    odd = my_ref[1]

    @pl.when(odd == 0)
    def even_core():
        keep_ref[0] = total[:half]
        send_ref[0] = total[half:]

    @pl.when(odd == 1)
    def odd_core():
        keep_ref[0] = total[half:]
        send_ref[0] = total[:half]


def product(my_rank, left, right, thru, after):
    count = lax.axis_size("dp") // 2
    width, depth = left.shape
    cols = right.shape[1] // count
    mine, odd = my_rank // 2, my_rank & 1
    if cols % 128:
        total = jnp.dot(left, right, preferred_element_type=jnp.float32).astype(jnp.bfloat16)
        pieces = total.T.reshape(count, 2, cols // 2, width)
        pieces = jnp.take(pieces, jnp.arange(count, dtype=jnp.int32) ^ mine, axis=0)
        low, high = pieces[:, 0], pieces[:, 1]
        return jnp.where(odd > 0, high, low), jnp.where(odd > 0, low, high), thru
    hbm = pl.BlockSpec(memory_space=pl.ANY)
    stacked = pl.BlockSpec((1, cols // 2, width), lambda step, my_ref: (step, 0, 0))
    stack = jax.ShapeDtypeStruct((count, cols // 2, width), jnp.bfloat16)
    inputs = [jnp.stack([mine, odd]), left, right, *after, thru]
    return pl.pallas_call(
        product_kernel,
        grid_spec=pltpu.PrefetchScalarGridSpec(
            num_scalar_prefetch=1,
            grid=(count,),
            in_specs=[
                pl.BlockSpec(left.shape, lambda step, my_ref: (0, 0)),
                pl.BlockSpec((depth, cols), lambda step, my_ref: (0, step ^ my_ref[0])),
            ]
            + [hbm] * (len(after) + 1),
            out_specs=[stacked, stacked, hbm],
        ),
        out_shape=[stack, stack, jax.ShapeDtypeStruct(thru.shape, thru.dtype)],
        input_output_aliases={len(inputs) - 1: 2},
        compiler_params=pltpu.CompilerParams(vmem_limit_bytes=VMEM_BYTES),
        cost_estimate=NO_COST,
    )(*inputs)


def weight_final_kernel(count, factor, *refs):
    total = refs[0][0].astype(jnp.float32)
    for ref in refs[1 : 1 + count]:
        total = total + ref[0].astype(jnp.float32)
    refs[-1][...] = total * factor


def weight_final(keep, received, factor, after):
    vmem = pl.BlockSpec(memory_space=pltpu.VMEM)
    hbm = pl.BlockSpec(memory_space=pl.ANY)
    return pl.pallas_call(
        partial(weight_final_kernel, len(received), factor),
        out_shape=jax.ShapeDtypeStruct(keep.shape[1:], jnp.float32),
        in_specs=[vmem] * (1 + len(received)) + [hbm] * len(after),
        out_specs=vmem,
        compiler_params=pltpu.CompilerParams(vmem_limit_bytes=VMEM_BYTES),
        cost_estimate=NO_COST,
    )(keep, *received, *after)


def local(query, key, value, grad_out, out_weight, plan, segments):
    rank_count = lax.axis_size("dp")
    my_rank = lax.axis_index("dp")
    my_lane = lax.axis_index("tensor")
    row_count = query.shape[0]
    block_count = row_count // ROWBLK
    local_heads = query.shape[1] // HD
    group = HEADS // KV
    bits = [1 << at for at in range(rank_count.bit_length() - 1)]
    kv_head = my_lane * local_heads // group
    own_key = lax.dynamic_slice_in_dim(key, kv_head * HD, HD, 1)
    own_value = lax.dynamic_slice_in_dim(value, kv_head * HD, HD, 1)
    own_places = positions_of(segments).reshape(1, block_count, ROWBLK)
    places_all = lax.all_to_all(
        jnp.broadcast_to(own_places, (rank_count, block_count, ROWBLK)),
        "dp",
        split_axis=0,
        concat_axis=0,
        tiled=True,
    ).reshape(-1, ROWBLK)
    values = spread(own_value)

    mine = my_rank * block_count + jnp.arange(block_count, dtype=jnp.int32)
    hit = plan[None, :] == mine[:, None]
    dest = jnp.sum(
        jnp.where(hit, jnp.arange(plan.shape[0], dtype=jnp.int32)[None, :], 0), axis=1
    )
    run = dest // RUN_BLOCKS
    slot = dest % RUN_BLOCKS
    places = jnp.take(places_all, dest, axis=0)
    need = slot - (slot * ROWBLK - places[:, 0]) // ROWBLK + 1
    cosine, sine = rope_tables(places.reshape(row_count), HD)
    key_f = own_key.astype(jnp.float32)
    rot_key = (key_f * cosine + swap_halves(key_f) * sine).astype(jnp.bfloat16)
    keys = spread(rot_key)
    up, up_t, turned = prepare(grad_out, out_weight, query, cosine, sine, [rot_key])

    distance = (plan // block_count) ^ my_rank
    within = plan % block_count
    half_place = (distance & 1) * (rank_count // 2) + distance // 2
    tables = (
        half_place * block_count + within,
        distance * block_count + within,
        run,
        slot,
        need,
    )
    grad_query_t, attn_t, gkey_keep, gkey_send, gvalue_keep, gvalue_send = attend(
        tables, turned, up, up_t, places, keys, values
    )
    value_keep, value_sends = chip_sum(gvalue_keep, swap(gvalue_send, 1))
    value_received = exchange(value_sends)
    key_keep, key_sends = chip_sum(gkey_keep, swap(gkey_send, 1))
    key_received = exchange(key_sends)
    weight_keep, weight_send, value_keep = product(
        my_rank, attn_t, grad_out, value_keep, [value_sends[0], key_sends[0]]
    )
    far = lax.axis_size("tensor") // 2
    value_partial, value_near, weight_send = final_sum(
        value_keep, value_received, (), (), thru=[weight_send], copies=2
    )
    value_far = lane_swap(value_partial, far)
    weight_keep, weight_sends = chip_sum(weight_keep, swap(weight_send, 1))
    weight_received = exchange(weight_sends)
    value_near = hold(value_near, weight_sends[:1])
    grad_query = turn_back(grad_query_t, cosine, sine, weight_sends[:1])
    key_partial, value_far = final_sum(
        key_keep, key_received, (cosine, sine), [grad_query], thru=[value_far]
    )
    value_all = assemble(my_lane, lane_pieces({0: value_near, far: value_far}, far // 2))
    key_pieces = lane_pieces({0: key_partial}, far)
    key_all = assemble(my_lane, key_pieces)
    weight_grad = weight_final(
        weight_keep, weight_received, 1.0 / rank_count, [*key_pieces[1:3], value_all]
    )
    lanes_per_key = group // local_heads

    def combine(gathered):
        if lanes_per_key == 1:
            return gathered
        merged = (
            gathered.astype(jnp.float32).reshape(row_count, KV, lanes_per_key, HD).sum(axis=2)
        )
        return merged.astype(jnp.bfloat16).reshape(row_count, KV * HD)

    return (grad_query, combine(key_all), combine(value_all), weight_grad)


def solution(mesh):
    in_specs = (
        P("dp", "tensor"),
        P("dp", None),
        P("dp", None),
        P("dp", None),
        P(None, "tensor"),
        P(),
        P("dp"),
    )
    out_specs = (P("dp", "tensor"), P("dp", None), P("dp", None), P("dp", "tensor"))
    return jax.shard_map(local, mesh=mesh, in_specs=in_specs, out_specs=out_specs, check_vma=False)
```

```python
from functools import partial
import math

import jax
import jax.numpy as jnp
from jax import lax
from jax.experimental import pallas as pl
from jax.experimental.pallas import tpu as pltpu
from jax.sharding import PartitionSpec as P

KV = 4
HD = 128
HEADS = 16
ROWBLK = 128
RUN_BLOCKS = 8
VMEM_BYTES = 58 * 1024 * 1024
NO_COST = pl.CostEstimate(flops=0, bytes_accessed=0, transcendentals=0)


rope_base = 1000000.0
yarn_factor = 4.0
yarn_context = 32768.0
beta_fast = 32.0
beta_slow = 1.0
masked_score = -1e30


def yarn_frequencies(head_size):
    half_size = head_size // 2

    def correction(rotations):
        return (
            head_size
            * math.log(yarn_context / (rotations * 2.0 * math.pi))
            / (2.0 * math.log(rope_base))
        )

    lower_bound = max(math.floor(correction(beta_fast)), 0)
    upper_bound = min(math.ceil(correction(beta_slow)), head_size - 1)
    ramp_span = max(upper_bound - lower_bound, 0.001)
    row_index = jnp.arange(half_size).astype(jnp.float32)
    extrap_freq = rope_base ** (-2.0 * row_index / head_size)
    interp_freq = extrap_freq / yarn_factor
    ramp_weight = jnp.clip((row_index - lower_bound) / ramp_span, 0.0, 1.0)
    return interp_freq * ramp_weight + extrap_freq * (1.0 - ramp_weight)


def positions_of(segments):
    row_count = segments.shape[-1]
    row_index = jnp.arange(row_count, dtype=jnp.int32)
    is_start = jnp.concatenate(
        [
            jnp.ones(segments.shape[:-1] + (1,), dtype=jnp.bool_),
            segments[..., 1:] != segments[..., :-1],
        ],
        axis=-1,
    )
    seg_start = lax.cummax(jnp.where(is_start, row_index, 0), axis=segments.ndim - 1)
    return row_index - seg_start


def rope_tables(places, head_size):
    angles = places.astype(jnp.float32)[:, None] * yarn_frequencies(head_size)[None, :]
    factor = 0.1 * math.log(yarn_factor) + 1.0
    cosine = jnp.cos(angles) * factor
    sine = jnp.sin(angles) * factor
    return (
        jnp.concatenate([cosine, cosine], axis=1),
        jnp.concatenate([-sine, sine], axis=1),
    )


def swap_halves(values):
    half = values.shape[-1] // 2
    return jnp.concatenate([values[..., half:], values[..., :half]], axis=-1)


NT = (((1,), (1,)), ((), ()))
TN = (((0,), (0,)), ((), ()))


def attend_kernel(
    heads,
    ranks,
    key_target_ref,
    value_target_ref,
    source_ref,
    run_ref,
    slot_ref,
    need_ref,
    place_ref,
    query_in,
    up_in,
    up_t_in,
    *refs,
):
    key_parts, refs = refs[:ranks], refs[ranks:]
    value_parts, refs = refs[:ranks], refs[ranks:]
    gquery_out, out_out, *halves = refs[:6]
    key_ref, value_ref, gkey_ref, gvalue_ref, key_win, value_win = refs[6:12]
    score_ref, prob_ref, gscore_ref, query_ref, up_ref, up_t_ref = refs[12:18]
    gquery_ref, out_ref, load_sems, sems = refs[18:]
    rows_each = query_ref.shape[0]
    half_blocks = ranks * RUN_BLOCKS // 2
    scale = 1.0 / math.sqrt(HD)
    to_exp2 = scale * math.log2(math.e)

    loads = []
    for item, (parts, whole) in enumerate(((key_parts, key_ref), (value_parts, value_ref))):
        for rank in range(ranks):
            copy = pltpu.make_async_copy(
                parts[rank], whole.at[pl.ds(rank * rows_each, rows_each)], load_sems.at[item, rank]
            )
            copy.start()
            loads.append(copy)
    for item, (source, whole) in enumerate(
        ((query_in, query_ref), (up_in, up_ref), (up_t_in, up_t_ref))
    ):
        copy = pltpu.make_async_copy(source, whole, load_sems.at[2, item])
        copy.start()
        loads.append(copy)
    for copy in loads:
        copy.wait()

    def stores(block, act):
        side = block % 2
        columns = pl.ds(pl.multiple_of(block * ROWBLK, ROWBLK), ROWBLK)
        for item, (source, whole) in enumerate(((gquery_ref, gquery_out), (out_ref, out_out))):
            act(
                pltpu.make_async_copy(
                    source.at[side], whole.at[:, columns], sems.at[side, 2, item]
                )
            )
        for item, (source, target_ref) in enumerate(
            ((gkey_ref, key_target_ref), (gvalue_ref, value_target_ref))
        ):
            for step in range(RUN_BLOCKS):
                target = target_ref[run_ref[block] * RUN_BLOCKS + step]
                start = pl.multiple_of(target % half_blocks * ROWBLK, ROWBLK)
                for place in range(2):

                    @pl.when(target // half_blocks == place)
                    def one_half():
                        act(
                            pltpu.make_async_copy(
                                source.at[side, pl.ds(step * ROWBLK, ROWBLK)],
                                halves[2 * item + place].at[pl.ds(start, ROWBLK)],
                                sems.at[side, item, step],
                            )
                        )

    def window(count, block):
        slot = slot_ref[block]
        run = run_ref[block]
        first = jnp.maximum(slot + 1 - count, 0)
        rows = count * ROWBLK
        for step in range(count):
            source = source_ref[run * RUN_BLOCKS + first + step]
            start = pl.multiple_of(source * ROWBLK, ROWBLK)
            key_win[pl.ds(step * ROWBLK, ROWBLK), :] = key_ref[pl.ds(start, ROWBLK), :]
            value_win[pl.ds(step * ROWBLK, ROWBLK), :] = value_ref[pl.ds(start, ROWBLK), :]
        wide = min(2, heads)
        base = pl.multiple_of(block * ROWBLK, ROWBLK)
        at_rows = pl.ds(base, ROWBLK)
        place = place_ref[pl.ds(block, 1), :]
        lane = lax.broadcasted_iota(jnp.int32, (1, ROWBLK), 1)
        last = (slot - first) * ROWBLK + lane
        last_all = jnp.concatenate([last] * wide, axis=1)
        start_all = jnp.concatenate([last - place] * wide, axis=1)
        key_index = lax.broadcasted_iota(jnp.int32, (ROWBLK, wide * ROWBLK), 0)
        keys = key_win[pl.ds(0, rows), :]
        values = value_win[pl.ds(0, rows), :]
        columns = [pl.ds(head * HD, HD) for head in range(heads)]
        query = jnp.concatenate([query_ref[at_rows, at] for at in columns], axis=0)
        up = jnp.concatenate([up_ref[at_rows, at] for at in columns], axis=0)
        folded = lambda tile: tile.reshape(ROWBLK // 8, 8, tile.shape[1])
        tiles = [pl.ds(step * ROWBLK, ROWBLK) for step in range(count)]
        groups = heads // wide
        spans = [slice(at * wide * ROWBLK, (at + 1) * wide * ROWBLK) for at in range(groups)]

        score = lax.dot_general(keys, query, NT, preferred_element_type=jnp.float32)
        gprob = lax.dot_general(values, up, NT, preferred_element_type=jnp.float32)
        peaks = [None] * groups
        for step, tile in enumerate(tiles):
            seen = key_index >= start_all - step * ROWBLK
            if step == count - 1:
                seen = seen & (key_index <= last_all - step * ROWBLK)
            for at, span in enumerate(spans):
                part = jnp.where(
                    seen, score[step * ROWBLK : (step + 1) * ROWBLK, span], masked_score
                )
                score_ref[tile, span] = part
                most = jnp.max(folded(part), axis=0)
                peaks[at] = most if peaks[at] is None else jnp.maximum(peaks[at], most)
        peaks = [jnp.max(item, axis=0, keepdims=True) for item in peaks]
        totals = [None] * groups
        for tile in tiles:
            for at, span in enumerate(spans):
                part = jnp.exp2((score_ref[tile, span] - peaks[at]) * to_exp2)
                score_ref[tile, span] = part
                some = jnp.sum(folded(part), axis=0)
                totals[at] = some if totals[at] is None else totals[at] + some
        shares = [1.0 / jnp.sum(item, axis=0, keepdims=True) for item in totals]
        for tile in tiles:
            for at, span in enumerate(spans):
                prob_ref[tile, span] = (score_ref[tile, span] * shares[at]).astype(jnp.bfloat16)
        prob_b = prob_ref[pl.ds(0, rows), :]
        out_t = lax.dot_general(values, prob_b, TN, preferred_element_type=jnp.float32)
        out_b = out_t.astype(jnp.bfloat16)
        deltas = []
        for at in range(groups):
            up_t = jnp.concatenate(
                [up_t_ref[item, at_rows] for item in columns[at * wide : (at + 1) * wide]], axis=1
            ).astype(jnp.float32)
            deltas.append(
                jnp.sum(up_t * out_b[:, spans[at]].astype(jnp.float32), axis=0, keepdims=True)
            )
        for step, tile in enumerate(tiles):
            for at, span in enumerate(spans):
                prob = score_ref[tile, span] * shares[at]
                part = gprob[step * ROWBLK : (step + 1) * ROWBLK, span] - deltas[at]
                gscore_ref[tile, span] = (prob * part).astype(jnp.bfloat16)
        gscore = gscore_ref[pl.ds(0, rows), :]
        gquery_t = lax.dot_general(keys, gscore, TN, preferred_element_type=jnp.float32)
        gkey = jnp.dot(gscore, query, preferred_element_type=jnp.float32)
        gvalue = jnp.dot(prob_b, up, preferred_element_type=jnp.float32)
        for head in range(heads):
            part = slice(head * ROWBLK, (head + 1) * ROWBLK)
            out_ref[block % 2, columns[head], :] = out_b[:, part]
            gquery_ref[block % 2, columns[head], :] = gquery_t[:, part]
        gkey = (gkey * scale).astype(jnp.bfloat16)
        gvalue = gvalue.astype(jnp.bfloat16)
        place_at = pl.ds(pl.multiple_of(first * ROWBLK, ROWBLK), rows)
        gkey_ref[block % 2, place_at, :] = gkey
        gvalue_ref[block % 2, place_at, :] = gvalue

    def body(block, carry):
        pl.when(block >= 2)(lambda: stores(block - 2, lambda copy: copy.wait()))
        blank = jnp.zeros(gkey_ref.shape[1:], jnp.bfloat16)
        gkey_ref[block % 2] = blank
        gvalue_ref[block % 2] = blank
        need = need_ref[block]
        floor = 0
        for size in range(1, RUN_BLOCKS + 1):
            pl.when((need > floor) & (need <= size))(partial(window, size, block))
            floor = size
        stores(block, lambda copy: copy.start())
        return carry

    blocks = rows_each // ROWBLK
    lax.fori_loop(0, blocks, body, 0)
    for block in range(max(blocks - 2, 0), blocks):
        stores(block, lambda copy: copy.wait())


def attend(tables, places, query, up, up_t, keys, values):
    rows, width = query.shape
    heads = width // HD
    ranks = len(keys)
    every = rows * ranks
    smem = pl.BlockSpec(memory_space=pltpu.SMEM)
    vmem = pl.BlockSpec(memory_space=pltpu.VMEM)
    hbm = pl.BlockSpec(memory_space=pl.ANY)
    half = jax.ShapeDtypeStruct((every // 2, HD), jnp.bfloat16)
    return pl.pallas_call(
        partial(attend_kernel, heads, ranks),
        out_shape=(
            jax.ShapeDtypeStruct((width, rows), jnp.float32),
            jax.ShapeDtypeStruct((width, rows), jnp.bfloat16),
            half,
            half,
            half,
            half,
        ),
        in_specs=[smem] * 6 + [vmem] + [hbm] * (3 + 2 * ranks),
        out_specs=[hbm] * 6,
        scratch_shapes=[pltpu.VMEM((every, HD), jnp.bfloat16)] * 2
        + [pltpu.VMEM((2, RUN_BLOCKS * ROWBLK, HD), jnp.bfloat16)] * 2
        + [pltpu.VMEM((RUN_BLOCKS * ROWBLK, HD), jnp.bfloat16)] * 2
        + [pltpu.VMEM((RUN_BLOCKS * ROWBLK, heads * ROWBLK), jnp.float32)]
        + [pltpu.VMEM((RUN_BLOCKS * ROWBLK, heads * ROWBLK), jnp.bfloat16)] * 2
        + [pltpu.VMEM((rows, width), jnp.bfloat16)] * 2
        + [pltpu.VMEM((width, rows), jnp.bfloat16)]
        + [pltpu.VMEM((2, width, ROWBLK), jnp.float32)]
        + [pltpu.VMEM((2, width, ROWBLK), jnp.bfloat16)]
        + [pltpu.SemaphoreType.DMA((3, ranks)), pltpu.SemaphoreType.DMA((2, 3, RUN_BLOCKS))],
        compiler_params=pltpu.CompilerParams(vmem_limit_bytes=VMEM_BYTES),
        cost_estimate=NO_COST,
    )(*tables, places, query, up, up_t, *keys, *values)


def assemble_kernel(lanes, my_ref, *refs):
    out_ref, sems = refs[lanes:]
    copies = []
    for index in range(lanes):
        column = pl.multiple_of((my_ref[0] ^ index) * HD, HD)
        copy = pltpu.make_async_copy(
            refs[index], out_ref.at[:, pl.ds(column, HD)], sems.at[index]
        )
        copy.start()
        copies.append(copy)
    for copy in copies:
        copy.wait()


def assemble(my_lane, pieces):
    rows = pieces[0].shape[0]
    lanes = len(pieces)
    vmem = pl.BlockSpec(memory_space=pltpu.VMEM)
    return pl.pallas_call(
        partial(assemble_kernel, lanes),
        out_shape=jax.ShapeDtypeStruct((rows, lanes * HD), pieces[0].dtype),
        in_specs=[pl.BlockSpec(memory_space=pltpu.SMEM)] + [vmem] * lanes,
        out_specs=pl.BlockSpec(memory_space=pl.ANY),
        scratch_shapes=[pltpu.SemaphoreType.DMA((lanes,))],
        compiler_params=pltpu.CompilerParams(vmem_limit_bytes=VMEM_BYTES),
        cost_estimate=NO_COST,
    )(my_lane.reshape(1), *pieces)


def lane_swap(array, bit):
    lanes = lax.axis_size("tensor")
    return lax.ppermute(array, "tensor", [(lane, lane ^ bit) for lane in range(lanes)])


def lane_pieces(pieces, bit):
    lanes = lax.axis_size("tensor")
    while bit:
        pieces = {**pieces, **{at | bit: lane_swap(item, bit) for at, item in pieces.items()}}
        bit //= 2
    return [pieces[at] for at in range(lanes)]


def swap(array, bit):
    ranks = lax.axis_size("dp")
    return lax.ppermute(array, "dp", [(rank, rank ^ bit) for rank in range(ranks)])


def spread(array):
    found = [array, swap(array, 1)]
    others = [swap(array, step) for step in range(2, lax.axis_size("dp"), 2)]
    for other in others:
        found += [other, swap(other, 1)]
    return found


def added(left, right):
    return left.astype(jnp.float32) + right.astype(jnp.float32)


def chip_sum(keep, received):
    count = lax.axis_size("dp") // 2
    rows = keep.shape[0] // count
    total = [
        added(keep[at * rows : (at + 1) * rows], received[at * rows : (at + 1) * rows])
        for at in range(count)
    ]
    return total[0], [item.astype(keep.dtype) for item in total[1:]]


def exchange(sends):
    return [swap(item, 2 * at + 2) for at, item in enumerate(sends)]


def place_of(distance, bits):
    place = distance * 0
    for bit in bits:
        place = place * 2 + (distance & bit) // bit
    return place


def halved(keep, received):
    half = keep.shape[0] // 2
    send = added(keep[half:], received[half:]).astype(jnp.bfloat16)
    return added(keep[:half], received[:half]), send


def parts_of(array):
    return [array[: array.shape[0] // 2], array[array.shape[0] // 2 :]]


def final_kernel(counts, rotary, outs, *refs):
    at = 0
    rows = 0
    tables = refs[sum(counts) : sum(counts) + 2]
    for count in counts:
        span = pl.ds(rows, refs[at].shape[0])
        rows += refs[at].shape[0]
        total = refs[at][...].astype(jnp.float32)
        for ref in refs[at + 1 : at + count]:
            total = total + ref[...].astype(jnp.float32)
        at += count
        if rotary:
            total = total * tables[0][span, :] - pltpu.roll(total, HD // 2, 1) * tables[1][span, :]
        for out in outs:
            refs[out][span, :] = total.astype(refs[out].dtype)


def final_sum(parts, tables, after, thru=(), copies=1):
    vmem = pl.BlockSpec(memory_space=pltpu.VMEM)
    hbm = pl.BlockSpec(memory_space=pl.ANY)
    loaded = [item for part in parts for item in part] + [*tables]
    rows = sum(part[0].shape[0] for part in parts)
    inputs = len(loaded) + len(after) + len(thru)
    return pl.pallas_call(
        partial(
            final_kernel,
            [len(part) for part in parts],
            len(tables) > 0,
            range(inputs, inputs + copies),
        ),
        out_shape=[jax.ShapeDtypeStruct((rows, HD), jnp.bfloat16)] * copies
        + [jax.ShapeDtypeStruct(item.shape, item.dtype) for item in thru],
        in_specs=[vmem] * len(loaded) + [hbm] * (len(after) + len(thru)),
        out_specs=[vmem] * copies + [hbm] * len(thru),
        input_output_aliases={inputs - len(thru) + at: copies + at for at in range(len(thru))},
        compiler_params=pltpu.CompilerParams(vmem_limit_bytes=VMEM_BYTES),
        cost_estimate=NO_COST,
    )(*loaded, *after, *thru)


def prepare_kernel(
    rows_ref, weight_ref, query_ref, cos_ref, sin_ref, *refs
):
    up_ref, up_t_ref, turned_ref = refs[-3:]
    total = jnp.dot(rows_ref[...], weight_ref[...], preferred_element_type=jnp.float32)
    up_ref[...] = total.astype(up_ref.dtype)
    up_t_ref[...] = total.T.astype(up_t_ref.dtype)
    for at in range(0, query_ref.shape[1], HD):
        raw = query_ref[:, at : at + HD].astype(jnp.float32)
        turned = raw * cos_ref[...] + pltpu.roll(raw, HD // 2, 1) * sin_ref[...]
        turned_ref[:, at : at + HD] = turned.astype(turned_ref.dtype)


def prepare(rows, weight, query, cosine, sine, after):
    height, depth = rows.shape
    width = weight.shape[1]
    steps = 4
    tall = height // steps
    across = lambda columns: pl.BlockSpec((tall, columns), lambda step: (step, 0))
    return pl.pallas_call(
        prepare_kernel,
        grid=(steps,),
        out_shape=[
            jax.ShapeDtypeStruct((height, width), jnp.bfloat16),
            jax.ShapeDtypeStruct((width, height), jnp.bfloat16),
            jax.ShapeDtypeStruct(query.shape, jnp.bfloat16),
        ],
        in_specs=[
            across(depth),
            pl.BlockSpec(weight.shape, lambda step: (0, 0)),
            across(width),
            across(HD),
            across(HD),
        ]
        + [pl.BlockSpec(memory_space=pl.ANY)] * len(after),
        out_specs=[
            across(width),
            pl.BlockSpec((width, tall), lambda step: (0, step)),
            across(width),
        ],
        compiler_params=pltpu.CompilerParams(vmem_limit_bytes=VMEM_BYTES),
        cost_estimate=pl.CostEstimate(
            flops=2 * height * weight.size, bytes_accessed=2 * rows.size, transcendentals=0
        ),
    )(rows, weight, query, cosine, sine, *after)


def turn_back_kernel(grad_ref, cos_ref, sin_ref, *refs):
    out_ref = refs[-1]
    scale = 1.0 / math.sqrt(HD)
    for at in range(0, grad_ref.shape[0], HD):
        grad = grad_ref[at : at + HD, :].T * scale
        back = grad * cos_ref[...] - pltpu.roll(grad, HD // 2, 1) * sin_ref[...]
        out_ref[:, at : at + HD] = back.astype(out_ref.dtype)


def turn_back(grad_t, cosine, sine, after):
    width, height = grad_t.shape
    steps = 4
    tall = height // steps
    return pl.pallas_call(
        turn_back_kernel,
        grid=(steps,),
        out_shape=jax.ShapeDtypeStruct((height, width), jnp.bfloat16),
        in_specs=[
            pl.BlockSpec((width, tall), lambda step: (0, step)),
            pl.BlockSpec((tall, HD), lambda step: (step, 0)),
            pl.BlockSpec((tall, HD), lambda step: (step, 0)),
        ]
        + [pl.BlockSpec(memory_space=pl.ANY)] * len(after),
        out_specs=pl.BlockSpec((tall, width), lambda step: (step, 0)),
        compiler_params=pltpu.CompilerParams(vmem_limit_bytes=VMEM_BYTES),
        cost_estimate=NO_COST,
    )(grad_t, cosine, sine, *after)


def hold_kernel(*refs):
    pass


def hold(array, after):
    hbm = pl.BlockSpec(memory_space=pl.ANY)
    return pl.pallas_call(
        hold_kernel,
        out_shape=jax.ShapeDtypeStruct(array.shape, array.dtype),
        in_specs=[hbm] * (1 + len(after)),
        out_specs=hbm,
        input_output_aliases={0: 0},
        cost_estimate=NO_COST,
    )(array, *after)


def product_kernel(my_ref, left_ref, right_ref, *refs):
    keep_ref, send_ref = refs[-3:-1]
    half = keep_ref.shape[1]
    total = jnp.dot(left_ref[...], right_ref[...], preferred_element_type=jnp.float32)
    total = total.astype(keep_ref.dtype).T
    odd = my_ref[1]

    @pl.when(odd == 0)
    def even_core():
        keep_ref[0] = total[:half]
        send_ref[0] = total[half:]

    @pl.when(odd == 1)
    def odd_core():
        keep_ref[0] = total[half:]
        send_ref[0] = total[:half]


def product(my_rank, left, right, thru, after):
    count = lax.axis_size("dp") // 2
    width, depth = left.shape
    cols = right.shape[1] // count
    mine, odd = my_rank // 2, my_rank & 1
    if cols % 128:
        total = jnp.dot(left, right, preferred_element_type=jnp.float32).astype(jnp.bfloat16)
        pieces = total.T.reshape(count, 2, cols // 2, width)
        pieces = jnp.take(pieces, jnp.arange(count, dtype=jnp.int32) ^ mine, axis=0)
        low, high = pieces[:, 0], pieces[:, 1]
        return jnp.where(odd > 0, high, low), jnp.where(odd > 0, low, high), thru
    hbm = pl.BlockSpec(memory_space=pl.ANY)
    stacked = pl.BlockSpec((1, cols // 2, width), lambda step, my_ref: (step, 0, 0))
    stack = jax.ShapeDtypeStruct((count, cols // 2, width), jnp.bfloat16)
    inputs = [jnp.stack([mine, odd]), left, right, *after, thru]
    return pl.pallas_call(
        product_kernel,
        grid_spec=pltpu.PrefetchScalarGridSpec(
            num_scalar_prefetch=1,
            grid=(count,),
            in_specs=[
                pl.BlockSpec(left.shape, lambda step, my_ref: (0, 0)),
                pl.BlockSpec((depth, cols), lambda step, my_ref: (0, step ^ my_ref[0])),
            ]
            + [hbm] * (len(after) + 1),
            out_specs=[stacked, stacked, hbm],
        ),
        out_shape=[stack, stack, jax.ShapeDtypeStruct(thru.shape, thru.dtype)],
        input_output_aliases={len(inputs) - 1: 2},
        compiler_params=pltpu.CompilerParams(vmem_limit_bytes=VMEM_BYTES),
        cost_estimate=NO_COST,
    )(*inputs)


def weight_final_kernel(count, factor, *refs):
    total = refs[0][0].astype(jnp.float32)
    for ref in refs[1 : 1 + count]:
        total = total + ref[0].astype(jnp.float32)
    refs[-1][...] = total * factor


def weight_final(keep, received, factor, after):
    vmem = pl.BlockSpec(memory_space=pltpu.VMEM)
    hbm = pl.BlockSpec(memory_space=pl.ANY)
    return pl.pallas_call(
        partial(weight_final_kernel, len(received), factor),
        out_shape=jax.ShapeDtypeStruct(keep.shape[1:], jnp.float32),
        in_specs=[vmem] * (1 + len(received)) + [hbm] * len(after),
        out_specs=vmem,
        compiler_params=pltpu.CompilerParams(vmem_limit_bytes=VMEM_BYTES),
        cost_estimate=NO_COST,
    )(keep, *received, *after)


def local(query, key, value, grad_out, out_weight, plan, segments):
    rank_count = lax.axis_size("dp")
    my_rank = lax.axis_index("dp")
    my_lane = lax.axis_index("tensor")
    row_count = query.shape[0]
    block_count = row_count // ROWBLK
    local_heads = query.shape[1] // HD
    group = HEADS // KV
    bits = [1 << at for at in range(rank_count.bit_length() - 1)]
    kv_head = my_lane * local_heads // group
    own_key = lax.dynamic_slice_in_dim(key, kv_head * HD, HD, 1)
    own_value = lax.dynamic_slice_in_dim(value, kv_head * HD, HD, 1)
    own_places = positions_of(segments).reshape(1, block_count, ROWBLK)
    places_all = lax.all_to_all(
        jnp.broadcast_to(own_places, (rank_count, block_count, ROWBLK)),
        "dp",
        split_axis=0,
        concat_axis=0,
        tiled=True,
    ).reshape(-1, ROWBLK)
    values = spread(own_value)

    mine = my_rank * block_count + jnp.arange(block_count, dtype=jnp.int32)
    hit = plan[None, :] == mine[:, None]
    dest = jnp.sum(
        jnp.where(hit, jnp.arange(plan.shape[0], dtype=jnp.int32)[None, :], 0), axis=1
    )
    run = dest // RUN_BLOCKS
    slot = dest % RUN_BLOCKS
    places = jnp.take(places_all, dest, axis=0)
    need = slot - (slot * ROWBLK - places[:, 0]) // ROWBLK + 1
    cosine, sine = rope_tables(places.reshape(row_count), HD)
    key_f = own_key.astype(jnp.float32)
    rot_key = (key_f * cosine + swap_halves(key_f) * sine).astype(jnp.bfloat16)
    keys = spread(rot_key)
    up, up_t, turned = prepare(grad_out, out_weight, query, cosine, sine, [rot_key])

    distance = (plan // block_count) ^ my_rank
    within = plan % block_count
    half_place = (distance & 1) * (rank_count // 2) + distance // 2
    part_blocks = block_count // 2
    stage_place = jnp.where(
        within < part_blocks, place_of(distance, bits[1:]), place_of(distance, bits[:0:-1])
    )
    quarter = (distance & 1) * 2 + within // part_blocks
    key_target = (quarter * (rank_count // 2) + stage_place) * part_blocks + within % part_blocks
    tables = (
        key_target,
        half_place * block_count + within,
        distance * block_count + within,
        run,
        slot,
        need,
    )
    grad_query_t, attn_t, gkey_keep, gkey_send, gvalue_keep, gvalue_send = attend(
        tables, places, turned, up, up_t, keys, values
    )
    value_keep, value_sends = chip_sum(gvalue_keep, swap(gvalue_send, 1))
    value_received = exchange(value_sends)
    key_received = parts_of(swap(gkey_send, 1))
    key_keeps = parts_of(gkey_keep)
    for stage in range(len(bits) - 1):
        key_sums = [halved(keep, item) for keep, item in zip(key_keeps, key_received)]
        key_keeps = [item[0] for item in key_sums]
        key_sends = [item[1] for item in key_sums]
        steps = (bits[1 + stage], bits[len(bits) - 1 - stage])
        key_received = [swap(item, step) for item, step in zip(key_sends, steps)]
        if stage == 0:
            first_received = key_received
            weight_keep, weight_send, value_keep = product(
                my_rank, attn_t, grad_out, value_keep, [*value_sends, *key_sends]
            )
    far = lax.axis_size("tensor") // 2
    value_partial, value_near, weight_send = final_sum(
        [[value_keep, *value_received]], (), first_received, thru=[weight_send], copies=2
    )
    value_far = lane_swap(value_partial, far)
    weight_keep, weight_sends = chip_sum(weight_keep, swap(weight_send, 1))
    weight_received = exchange(weight_sends)
    value_near = hold(value_near, weight_sends[:1])
    key_partial, value_far = final_sum(
        [list(part) for part in zip(key_keeps, key_received)], (cosine, sine), weight_sends[:1],
        thru=[value_far],
    )
    value_all = assemble(my_lane, lane_pieces({0: value_near, far: value_far}, far // 2))
    key_pieces = lane_pieces({0: key_partial}, far)
    key_all = assemble(my_lane, key_pieces)
    grad_query = turn_back(grad_query_t, cosine, sine, [key_partial])
    weight_grad = weight_final(
        weight_keep,
        weight_received,
        1.0 / rank_count,
        [*key_pieces[1:3], value_all, grad_query],
    )
    lanes_per_key = group // local_heads

    def combine(gathered):
        if lanes_per_key == 1:
            return gathered
        merged = (
            gathered.astype(jnp.float32).reshape(row_count, KV, lanes_per_key, HD).sum(axis=2)
        )
        return merged.astype(jnp.bfloat16).reshape(row_count, KV * HD)

    return (grad_query, combine(key_all), combine(value_all), weight_grad)


def solution(mesh):
    in_specs = (
        P("dp", "tensor"),
        P("dp", None),
        P("dp", None),
        P("dp", None),
        P(None, "tensor"),
        P(),
        P("dp"),
    )
    out_specs = (P("dp", "tensor"), P("dp", None), P("dp", None), P("dp", "tensor"))
    return jax.shard_map(local, mesh=mesh, in_specs=in_specs, out_specs=out_specs, check_vma=False)
```

```python
from functools import partial
import math

import jax
import jax.numpy as jnp
from jax import lax
from jax.experimental import pallas as pl
from jax.experimental.pallas import tpu as pltpu
from jax.sharding import PartitionSpec as P

KV = 4
HD = 128
HEADS = 16
ROWBLK = 128
RUN_BLOCKS = 8
VMEM_BYTES = 58 * 1024 * 1024
NO_COST = pl.CostEstimate(flops=0, bytes_accessed=0, transcendentals=0)


rope_base = 1000000.0
yarn_factor = 4.0
yarn_context = 32768.0
beta_fast = 32.0
beta_slow = 1.0
masked_score = -1e30


def yarn_frequencies(head_size):
    half_size = head_size // 2

    def correction(rotations):
        return (
            head_size
            * math.log(yarn_context / (rotations * 2.0 * math.pi))
            / (2.0 * math.log(rope_base))
        )

    lower_bound = max(math.floor(correction(beta_fast)), 0)
    upper_bound = min(math.ceil(correction(beta_slow)), head_size - 1)
    ramp_span = max(upper_bound - lower_bound, 0.001)
    row_index = jnp.arange(half_size).astype(jnp.float32)
    extrap_freq = rope_base ** (-2.0 * row_index / head_size)
    interp_freq = extrap_freq / yarn_factor
    ramp_weight = jnp.clip((row_index - lower_bound) / ramp_span, 0.0, 1.0)
    return interp_freq * ramp_weight + extrap_freq * (1.0 - ramp_weight)


def positions_of(segments):
    row_count = segments.shape[-1]
    row_index = jnp.arange(row_count, dtype=jnp.int32)
    is_start = jnp.concatenate(
        [
            jnp.ones(segments.shape[:-1] + (1,), dtype=jnp.bool_),
            segments[..., 1:] != segments[..., :-1],
        ],
        axis=-1,
    )
    seg_start = lax.cummax(jnp.where(is_start, row_index, 0), axis=segments.ndim - 1)
    return row_index - seg_start


def rope_kernel(at_ref, dest_ref, places_ref, freq_ref, key_ref, *refs):
    cos_ref, sin_ref, turned_ref, own_ref = refs
    factor = 0.1 * math.log(yarn_factor) + 1.0
    half = lax.broadcasted_iota(jnp.int32, (ROWBLK, HD), 1) < HD // 2
    for block in range(own_ref.shape[0]):
        rows = pl.ds(block * ROWBLK, ROWBLK)
        place = places_ref[pl.ds(dest_ref[block], 1), :]
        own_ref[pl.ds(block, 1), :] = place
        spread_out = jnp.broadcast_to(place.astype(jnp.float32), (ROWBLK, HD)).T
        angles = spread_out * freq_ref[...]
        cosine = jnp.cos(angles) * factor
        sine = jnp.sin(angles) * factor
        sine = jnp.where(half, -sine, sine)
        cos_ref[rows, :] = cosine
        sin_ref[rows, :] = sine
        raw = key_ref[rows, :].astype(jnp.float32)
        turned = raw * cosine + pltpu.roll(raw, HD // 2, 1) * sine
        turned_ref[rows, :] = turned.astype(turned_ref.dtype)


def rope(kv_head, dest, places_all, key):
    rows = key.shape[0]
    blocks = rows // ROWBLK
    freq = yarn_frequencies(HD)
    freq = jnp.concatenate([freq, freq]).reshape(1, HD)
    whole = lambda shape: pl.BlockSpec(shape, lambda step, *refs: (0,) * len(shape))
    table = jax.ShapeDtypeStruct((rows, HD), jnp.float32)
    return pl.pallas_call(
        rope_kernel,
        grid_spec=pltpu.PrefetchScalarGridSpec(
            num_scalar_prefetch=2,
            grid=(1,),
            in_specs=[
                whole(places_all.shape),
                whole((1, HD)),
                pl.BlockSpec((rows, HD), lambda step, at_ref, dest_ref: (0, at_ref[0])),
            ],
            out_specs=[whole((rows, HD))] * 3 + [whole((blocks, ROWBLK))],
        ),
        out_shape=[
            table,
            table,
            jax.ShapeDtypeStruct((rows, HD), key.dtype),
            jax.ShapeDtypeStruct((blocks, ROWBLK), jnp.int32),
        ],
        cost_estimate=NO_COST,
    )(kv_head.reshape(1), dest, places_all, freq, key)


NT = (((1,), (1,)), ((), ()))
TN = (((0,), (0,)), ((), ()))


def attend_kernel(
    heads,
    ranks,
    target_ref,
    source_ref,
    run_ref,
    slot_ref,
    need_ref,
    query_ref,
    up_ref,
    up_t_ref,
    place_ref,
    *refs,
):
    key_parts, refs = refs[:ranks], refs[ranks:]
    value_parts, refs = refs[:ranks], refs[ranks:]
    gquery_ref, out_ref, *halves = refs[:6]
    key_ref, value_ref, gkey_ref, gvalue_ref, key_win, value_win = refs[6:12]
    score_ref, prob_ref, gscore_ref, load_sems, sems = refs[12:]
    rows_each = query_ref.shape[0]
    half_blocks = ranks * RUN_BLOCKS // 2
    scale = 1.0 / math.sqrt(HD)
    to_exp2 = scale * math.log2(math.e)

    loads = []
    for item, (parts, whole) in enumerate(((key_parts, key_ref), (value_parts, value_ref))):
        for rank in range(ranks):
            copy = pltpu.make_async_copy(
                parts[rank], whole.at[pl.ds(rank * rows_each, rows_each)], load_sems.at[item, rank]
            )
            copy.start()
            loads.append(copy)
    for copy in loads:
        copy.wait()

    def stores(block, act):
        side = block % 2
        for step in range(RUN_BLOCKS):
            target = target_ref[run_ref[block] * RUN_BLOCKS + step]
            for place in range(2):

                @pl.when(target // half_blocks == place)
                def one_half():
                    start = pl.multiple_of(target % half_blocks * ROWBLK, ROWBLK)
                    for item, source in enumerate((gkey_ref, gvalue_ref)):
                        act(
                            pltpu.make_async_copy(
                                source.at[side, pl.ds(step * ROWBLK, ROWBLK)],
                                halves[2 * item + place].at[pl.ds(start, ROWBLK)],
                                sems.at[side, item, step],
                            )
                        )

    def window(count, block):
        slot = slot_ref[block]
        run = run_ref[block]
        first = jnp.maximum(slot + 1 - count, 0)
        rows = count * ROWBLK
        for step in range(count):
            source = source_ref[run * RUN_BLOCKS + first + step]
            start = pl.multiple_of(source * ROWBLK, ROWBLK)
            key_win[pl.ds(step * ROWBLK, ROWBLK), :] = key_ref[pl.ds(start, ROWBLK), :]
            value_win[pl.ds(step * ROWBLK, ROWBLK), :] = value_ref[pl.ds(start, ROWBLK), :]
        wide = min(2, heads)
        base = pl.multiple_of(block * ROWBLK, ROWBLK)
        at_rows = pl.ds(base, ROWBLK)
        place = place_ref[pl.ds(block, 1), :]
        lane = lax.broadcasted_iota(jnp.int32, (1, ROWBLK), 1)
        last = (slot - first) * ROWBLK + lane
        last_all = jnp.concatenate([last] * wide, axis=1)
        start_all = jnp.concatenate([last - place] * wide, axis=1)
        key_index = lax.broadcasted_iota(jnp.int32, (ROWBLK, wide * ROWBLK), 0)
        keys = key_win[pl.ds(0, rows), :]
        values = value_win[pl.ds(0, rows), :]
        columns = [pl.ds(head * HD, HD) for head in range(heads)]
        query = jnp.concatenate([query_ref[at_rows, at] for at in columns], axis=0)
        up = jnp.concatenate([up_ref[at_rows, at] for at in columns], axis=0)
        folded = lambda tile: tile.reshape(ROWBLK // 8, 8, tile.shape[1])
        tiles = [pl.ds(step * ROWBLK, ROWBLK) for step in range(count)]
        groups = heads // wide
        spans = [slice(at * wide * ROWBLK, (at + 1) * wide * ROWBLK) for at in range(groups)]

        score = lax.dot_general(keys, query, NT, preferred_element_type=jnp.float32)
        gprob = lax.dot_general(values, up, NT, preferred_element_type=jnp.float32)
        peaks = [None] * groups
        for step, tile in enumerate(tiles):
            seen = key_index >= start_all - step * ROWBLK
            if step == count - 1:
                seen = seen & (key_index <= last_all - step * ROWBLK)
            for at, span in enumerate(spans):
                part = jnp.where(
                    seen, score[step * ROWBLK : (step + 1) * ROWBLK, span], masked_score
                )
                score_ref[tile, span] = part
                most = jnp.max(folded(part), axis=0)
                peaks[at] = most if peaks[at] is None else jnp.maximum(peaks[at], most)
        peaks = [jnp.max(item, axis=0, keepdims=True) for item in peaks]
        totals = [None] * groups
        for tile in tiles:
            for at, span in enumerate(spans):
                part = jnp.exp2((score_ref[tile, span] - peaks[at]) * to_exp2)
                score_ref[tile, span] = part
                some = jnp.sum(folded(part), axis=0)
                totals[at] = some if totals[at] is None else totals[at] + some
        shares = [1.0 / jnp.sum(item, axis=0, keepdims=True) for item in totals]
        for tile in tiles:
            for at, span in enumerate(spans):
                prob_ref[tile, span] = (score_ref[tile, span] * shares[at]).astype(jnp.bfloat16)
        prob_b = prob_ref[pl.ds(0, rows), :]
        out_t = lax.dot_general(values, prob_b, TN, preferred_element_type=jnp.float32)
        out_b = out_t.astype(jnp.bfloat16)
        deltas = []
        for at in range(groups):
            up_t = jnp.concatenate(
                [up_t_ref[item, at_rows] for item in columns[at * wide : (at + 1) * wide]], axis=1
            ).astype(jnp.float32)
            deltas.append(
                jnp.sum(up_t * out_b[:, spans[at]].astype(jnp.float32), axis=0, keepdims=True)
            )
        for step, tile in enumerate(tiles):
            for at, span in enumerate(spans):
                prob = score_ref[tile, span] * shares[at]
                part = gprob[step * ROWBLK : (step + 1) * ROWBLK, span] - deltas[at]
                gscore_ref[tile, span] = (prob * part).astype(jnp.bfloat16)
        gscore = gscore_ref[pl.ds(0, rows), :]
        gquery_t = lax.dot_general(keys, gscore, TN, preferred_element_type=jnp.float32)
        gkey = jnp.dot(gscore, query, preferred_element_type=jnp.float32)
        gvalue = jnp.dot(prob_b, up, preferred_element_type=jnp.float32)
        for head in range(heads):
            part = slice(head * ROWBLK, (head + 1) * ROWBLK)
            out_ref[columns[head], at_rows] = out_b[:, part]
            gquery_ref[columns[head], at_rows] = gquery_t[:, part]
        gkey = (gkey * scale).astype(jnp.bfloat16)
        gvalue = gvalue.astype(jnp.bfloat16)
        place_at = pl.ds(pl.multiple_of(first * ROWBLK, ROWBLK), rows)
        gkey_ref[block % 2, place_at, :] = gkey
        gvalue_ref[block % 2, place_at, :] = gvalue

    def body(block, carry):
        pl.when(block >= 2)(lambda: stores(block - 2, lambda copy: copy.wait()))
        blank = jnp.zeros(gkey_ref.shape[1:], jnp.bfloat16)
        gkey_ref[block % 2] = blank
        gvalue_ref[block % 2] = blank
        need = need_ref[block]
        floor = 0
        for size in range(1, RUN_BLOCKS + 1):
            pl.when((need > floor) & (need <= size))(partial(window, size, block))
            floor = size
        stores(block, lambda copy: copy.start())
        return carry

    blocks = rows_each // ROWBLK
    lax.fori_loop(0, blocks, body, 0)
    for block in range(max(blocks - 2, 0), blocks):
        stores(block, lambda copy: copy.wait())


def attend(tables, query, up, up_t, places, keys, values):
    rows, width = query.shape
    heads = width // HD
    ranks = len(keys)
    every = rows * ranks
    smem = pl.BlockSpec(memory_space=pltpu.SMEM)
    vmem = pl.BlockSpec(memory_space=pltpu.VMEM)
    hbm = pl.BlockSpec(memory_space=pl.ANY)
    half = jax.ShapeDtypeStruct((every // 2, HD), jnp.bfloat16)
    return pl.pallas_call(
        partial(attend_kernel, heads, ranks),
        out_shape=(
            jax.ShapeDtypeStruct((width, rows), jnp.float32),
            jax.ShapeDtypeStruct((width, rows), jnp.bfloat16),
            half,
            half,
            half,
            half,
        ),
        in_specs=[smem] * 5 + [vmem] * 4 + [hbm] * (2 * ranks),
        out_specs=(vmem, vmem, hbm, hbm, hbm, hbm),
        scratch_shapes=[pltpu.VMEM((every, HD), jnp.bfloat16)] * 2
        + [pltpu.VMEM((2, RUN_BLOCKS * ROWBLK, HD), jnp.bfloat16)] * 2
        + [pltpu.VMEM((RUN_BLOCKS * ROWBLK, HD), jnp.bfloat16)] * 2
        + [pltpu.VMEM((RUN_BLOCKS * ROWBLK, heads * ROWBLK), jnp.float32)]
        + [pltpu.VMEM((RUN_BLOCKS * ROWBLK, heads * ROWBLK), jnp.bfloat16)] * 2
        + [pltpu.SemaphoreType.DMA((2, ranks)), pltpu.SemaphoreType.DMA((2, 2, RUN_BLOCKS))],
        compiler_params=pltpu.CompilerParams(vmem_limit_bytes=VMEM_BYTES),
        cost_estimate=NO_COST,
    )(*tables, query, up, up_t, places, *keys, *values)


def assemble_kernel(lanes, my_ref, *refs):
    out_ref, sems = refs[lanes:]
    copies = []
    for index in range(lanes):
        column = pl.multiple_of((my_ref[0] ^ index) * HD, HD)
        copy = pltpu.make_async_copy(
            refs[index], out_ref.at[:, pl.ds(column, HD)], sems.at[index]
        )
        copy.start()
        copies.append(copy)
    for copy in copies:
        copy.wait()


def assemble(my_lane, pieces):
    rows = pieces[0].shape[0]
    lanes = len(pieces)
    vmem = pl.BlockSpec(memory_space=pltpu.VMEM)
    return pl.pallas_call(
        partial(assemble_kernel, lanes),
        out_shape=jax.ShapeDtypeStruct((rows, lanes * HD), pieces[0].dtype),
        in_specs=[pl.BlockSpec(memory_space=pltpu.SMEM)] + [vmem] * lanes,
        out_specs=pl.BlockSpec(memory_space=pl.ANY),
        scratch_shapes=[pltpu.SemaphoreType.DMA((lanes,))],
        compiler_params=pltpu.CompilerParams(vmem_limit_bytes=VMEM_BYTES),
        cost_estimate=NO_COST,
    )(my_lane.reshape(1), *pieces)


def lane_swap(array, bit):
    lanes = lax.axis_size("tensor")
    return lax.ppermute(array, "tensor", [(lane, lane ^ bit) for lane in range(lanes)])


def lane_pieces(pieces, bit):
    lanes = lax.axis_size("tensor")
    while bit:
        pieces = {**pieces, **{at | bit: lane_swap(item, bit) for at, item in pieces.items()}}
        bit //= 2
    return [pieces[at] for at in range(lanes)]


def swap(array, bit):
    ranks = lax.axis_size("dp")
    return lax.ppermute(array, "dp", [(rank, rank ^ bit) for rank in range(ranks)])


def spread(array):
    found = [array, swap(array, 1)]
    others = [swap(array, step) for step in range(2, lax.axis_size("dp"), 2)]
    for other in others:
        found += [other, swap(other, 1)]
    return found


def added(left, right):
    return left.astype(jnp.float32) + right.astype(jnp.float32)


def chip_sum(keep, received):
    count = lax.axis_size("dp") // 2
    rows = keep.shape[0] // count
    total = [
        added(keep[at * rows : (at + 1) * rows], received[at * rows : (at + 1) * rows])
        for at in range(count)
    ]
    return total[0], [item.astype(keep.dtype) for item in total[1:]]


def exchange(sends):
    return [swap(item, 2 * at + 2) for at, item in enumerate(sends)]


def final_kernel(count, rotary, outs, *refs):
    total = refs[0][...].astype(jnp.float32)
    for ref in refs[1 : 1 + count]:
        total = total + ref[...].astype(jnp.float32)
    if rotary:
        total = total * refs[1 + count][...] - pltpu.roll(total, HD // 2, 1) * refs[2 + count][...]
    for at in outs:
        refs[at][...] = total.astype(refs[at].dtype)


def final_sum(keep, received, tables, after, thru=(), copies=1):
    vmem = pl.BlockSpec(memory_space=pltpu.VMEM)
    hbm = pl.BlockSpec(memory_space=pl.ANY)
    parts = [keep, *received, *tables]
    inputs = len(parts) + len(after) + len(thru)
    results = pl.pallas_call(
        partial(
            final_kernel, len(received), len(tables) > 0, range(inputs, inputs + copies)
        ),
        out_shape=[jax.ShapeDtypeStruct(keep.shape, jnp.bfloat16)] * copies
        + [jax.ShapeDtypeStruct(item.shape, item.dtype) for item in thru],
        in_specs=[vmem] * len(parts) + [hbm] * (len(after) + len(thru)),
        out_specs=[vmem] * copies + [hbm] * len(thru),
        input_output_aliases={inputs - len(thru) + at: copies + at for at in range(len(thru))},
        compiler_params=pltpu.CompilerParams(vmem_limit_bytes=VMEM_BYTES),
        cost_estimate=NO_COST,
    )(*parts, *after, *thru)
    return results


def prepare_kernel(
    rows_ref, weight_ref, query_ref, cos_ref, sin_ref, *refs
):
    up_ref, up_t_ref, turned_ref = refs[-3:]
    total = jnp.dot(rows_ref[...], weight_ref[...], preferred_element_type=jnp.float32)
    up_ref[...] = total.astype(up_ref.dtype)
    up_t_ref[...] = total.T.astype(up_t_ref.dtype)
    for at in range(0, query_ref.shape[1], HD):
        raw = query_ref[:, at : at + HD].astype(jnp.float32)
        turned = raw * cos_ref[...] + pltpu.roll(raw, HD // 2, 1) * sin_ref[...]
        turned_ref[:, at : at + HD] = turned.astype(turned_ref.dtype)


def prepare(rows, weight, query, cosine, sine, after):
    height, depth = rows.shape
    width = weight.shape[1]
    steps = 4
    tall = height // steps
    across = lambda columns: pl.BlockSpec((tall, columns), lambda step: (step, 0))
    return pl.pallas_call(
        prepare_kernel,
        grid=(steps,),
        out_shape=[
            jax.ShapeDtypeStruct((height, width), jnp.bfloat16),
            jax.ShapeDtypeStruct((width, height), jnp.bfloat16),
            jax.ShapeDtypeStruct(query.shape, jnp.bfloat16),
        ],
        in_specs=[
            across(depth),
            pl.BlockSpec(weight.shape, lambda step: (0, 0)),
            across(width),
            across(HD),
            across(HD),
        ]
        + [pl.BlockSpec(memory_space=pl.ANY)] * len(after),
        out_specs=[
            across(width),
            pl.BlockSpec((width, tall), lambda step: (0, step)),
            across(width),
        ],
        compiler_params=pltpu.CompilerParams(vmem_limit_bytes=VMEM_BYTES),
        cost_estimate=pl.CostEstimate(
            flops=2 * height * weight.size, bytes_accessed=2 * rows.size, transcendentals=0
        ),
    )(rows, weight, query, cosine, sine, *after)


def turn_back_kernel(grad_ref, cos_ref, sin_ref, *refs):
    out_ref = refs[-1]
    scale = 1.0 / math.sqrt(HD)
    for at in range(0, grad_ref.shape[0], HD):
        grad = grad_ref[at : at + HD, :].T * scale
        back = grad * cos_ref[...] - pltpu.roll(grad, HD // 2, 1) * sin_ref[...]
        out_ref[:, at : at + HD] = back.astype(out_ref.dtype)


def turn_back(grad_t, cosine, sine, after):
    width, height = grad_t.shape
    steps = 4
    tall = height // steps
    return pl.pallas_call(
        turn_back_kernel,
        grid=(steps,),
        out_shape=jax.ShapeDtypeStruct((height, width), jnp.bfloat16),
        in_specs=[
            pl.BlockSpec((width, tall), lambda step: (0, step)),
            pl.BlockSpec((tall, HD), lambda step: (step, 0)),
            pl.BlockSpec((tall, HD), lambda step: (step, 0)),
        ]
        + [pl.BlockSpec(memory_space=pl.ANY)] * len(after),
        out_specs=pl.BlockSpec((tall, width), lambda step: (step, 0)),
        compiler_params=pltpu.CompilerParams(vmem_limit_bytes=VMEM_BYTES),
        cost_estimate=NO_COST,
    )(grad_t, cosine, sine, *after)


def hold_kernel(*refs):
    pass


def hold(array, after):
    hbm = pl.BlockSpec(memory_space=pl.ANY)
    return pl.pallas_call(
        hold_kernel,
        out_shape=jax.ShapeDtypeStruct(array.shape, array.dtype),
        in_specs=[hbm] * (1 + len(after)),
        out_specs=hbm,
        input_output_aliases={0: 0},
        cost_estimate=NO_COST,
    )(array, *after)


def product_kernel(my_ref, left_ref, right_ref, *refs):
    keep_ref, send_ref = refs[-3:-1]
    half = keep_ref.shape[1]
    total = jnp.dot(left_ref[...], right_ref[...], preferred_element_type=jnp.float32)
    total = total.astype(keep_ref.dtype).T
    odd = my_ref[1]

    @pl.when(odd == 0)
    def even_core():
        keep_ref[0] = total[:half]
        send_ref[0] = total[half:]

    @pl.when(odd == 1)
    def odd_core():
        keep_ref[0] = total[half:]
        send_ref[0] = total[:half]


def product(my_rank, left, right, thru, after):
    count = lax.axis_size("dp") // 2
    width, depth = left.shape
    cols = right.shape[1] // count
    mine, odd = my_rank // 2, my_rank & 1
    if cols % 128:
        total = jnp.dot(left, right, preferred_element_type=jnp.float32).astype(jnp.bfloat16)
        pieces = total.T.reshape(count, 2, cols // 2, width)
        pieces = jnp.take(pieces, jnp.arange(count, dtype=jnp.int32) ^ mine, axis=0)
        low, high = pieces[:, 0], pieces[:, 1]
        return jnp.where(odd > 0, high, low), jnp.where(odd > 0, low, high), thru
    hbm = pl.BlockSpec(memory_space=pl.ANY)
    stacked = pl.BlockSpec((1, cols // 2, width), lambda step, my_ref: (step, 0, 0))
    stack = jax.ShapeDtypeStruct((count, cols // 2, width), jnp.bfloat16)
    inputs = [jnp.stack([mine, odd]), left, right, *after, thru]
    return pl.pallas_call(
        product_kernel,
        grid_spec=pltpu.PrefetchScalarGridSpec(
            num_scalar_prefetch=1,
            grid=(count,),
            in_specs=[
                pl.BlockSpec(left.shape, lambda step, my_ref: (0, 0)),
                pl.BlockSpec((depth, cols), lambda step, my_ref: (0, step ^ my_ref[0])),
            ]
            + [hbm] * (len(after) + 1),
            out_specs=[stacked, stacked, hbm],
        ),
        out_shape=[stack, stack, jax.ShapeDtypeStruct(thru.shape, thru.dtype)],
        input_output_aliases={len(inputs) - 1: 2},
        compiler_params=pltpu.CompilerParams(vmem_limit_bytes=VMEM_BYTES),
        cost_estimate=NO_COST,
    )(*inputs)


def weight_final_kernel(count, factor, *refs):
    total = refs[0][0].astype(jnp.float32)
    for ref in refs[1 : 1 + count]:
        total = total + ref[0].astype(jnp.float32)
    refs[-1][...] = total * factor


def weight_final(keep, received, factor, after):
    vmem = pl.BlockSpec(memory_space=pltpu.VMEM)
    hbm = pl.BlockSpec(memory_space=pl.ANY)
    return pl.pallas_call(
        partial(weight_final_kernel, len(received), factor),
        out_shape=jax.ShapeDtypeStruct(keep.shape[1:], jnp.float32),
        in_specs=[vmem] * (1 + len(received)) + [hbm] * len(after),
        out_specs=vmem,
        compiler_params=pltpu.CompilerParams(vmem_limit_bytes=VMEM_BYTES),
        cost_estimate=NO_COST,
    )(keep, *received, *after)


def local(query, key, value, grad_out, out_weight, plan, segments):
    rank_count = lax.axis_size("dp")
    my_rank = lax.axis_index("dp")
    my_lane = lax.axis_index("tensor")
    row_count = query.shape[0]
    block_count = row_count // ROWBLK
    local_heads = query.shape[1] // HD
    group = HEADS // KV
    bits = [1 << at for at in range(rank_count.bit_length() - 1)]
    kv_head = my_lane * local_heads // group
    own_value = lax.dynamic_slice_in_dim(value, kv_head * HD, HD, 1)
    own_places = positions_of(segments).reshape(1, block_count, ROWBLK)
    places_all = lax.all_to_all(
        jnp.broadcast_to(own_places, (rank_count, block_count, ROWBLK)),
        "dp",
        split_axis=0,
        concat_axis=0,
        tiled=True,
    ).reshape(-1, ROWBLK)
    values = spread(own_value)

    mine = my_rank * block_count + jnp.arange(block_count, dtype=jnp.int32)
    hit = plan[None, :] == mine[:, None]
    dest = jnp.sum(
        jnp.where(hit, jnp.arange(plan.shape[0], dtype=jnp.int32)[None, :], 0), axis=1
    )
    run = dest // RUN_BLOCKS
    slot = dest % RUN_BLOCKS
    cosine, sine, rot_key, places = rope(kv_head, dest, places_all, key)
    need = slot - (slot * ROWBLK - places[:, 0]) // ROWBLK + 1
    keys = spread(rot_key)
    up, up_t, turned = prepare(grad_out, out_weight, query, cosine, sine, [rot_key])

    distance = (plan // block_count) ^ my_rank
    within = plan % block_count
    half_place = (distance & 1) * (rank_count // 2) + distance // 2
    tables = (
        half_place * block_count + within,
        distance * block_count + within,
        run,
        slot,
        need,
    )
    grad_query_t, attn_t, gkey_keep, gkey_send, gvalue_keep, gvalue_send = attend(
        tables, turned, up, up_t, places, keys, values
    )
    value_keep, value_sends = chip_sum(gvalue_keep, swap(gvalue_send, 1))
    value_received = exchange(value_sends)
    key_keep, key_sends = chip_sum(gkey_keep, swap(gkey_send, 1))
    key_received = exchange(key_sends)
    weight_keep, weight_send, value_keep = product(
        my_rank, attn_t, grad_out, value_keep, [value_sends[0], key_sends[0]]
    )
    far = lax.axis_size("tensor") // 2
    value_partial, value_near, weight_send = final_sum(
        value_keep, value_received, (), (), thru=[weight_send], copies=2
    )
    value_far = lane_swap(value_partial, far)
    weight_keep, weight_sends = chip_sum(weight_keep, swap(weight_send, 1))
    weight_received = exchange(weight_sends)
    value_near = hold(value_near, weight_sends[:1])
    grad_query = turn_back(grad_query_t, cosine, sine, weight_sends[:1])
    value_far = hold(value_far, [grad_query])
    value_pieces = lane_pieces({0: value_near, far: value_far}, far // 2)
    value_all = assemble(my_lane, value_pieces)
    (key_partial,) = final_sum(
        key_keep, key_received, (cosine, sine), [grad_query, value_pieces[1]]
    )
    key_pieces = lane_pieces({0: key_partial}, far)
    key_all = assemble(my_lane, key_pieces)
    weight_grad = weight_final(
        weight_keep, weight_received, 1.0 / rank_count, [*key_pieces[1:3], value_all]
    )
    lanes_per_key = group // local_heads

    def combine(gathered):
        if lanes_per_key == 1:
            return gathered
        merged = (
            gathered.astype(jnp.float32).reshape(row_count, KV, lanes_per_key, HD).sum(axis=2)
        )
        return merged.astype(jnp.bfloat16).reshape(row_count, KV * HD)

    return (grad_query, combine(key_all), combine(value_all), weight_grad)


def solution(mesh):
    in_specs = (
        P("dp", "tensor"),
        P("dp", None),
        P("dp", None),
        P("dp", None),
        P(None, "tensor"),
        P(),
        P("dp"),
    )
    out_specs = (P("dp", "tensor"), P("dp", None), P("dp", None), P("dp", "tensor"))
    return jax.shard_map(local, mesh=mesh, in_specs=in_specs, out_specs=out_specs, check_vma=False)
```

```python
from functools import partial
import math

import jax
import jax.numpy as jnp
from jax import lax
from jax.experimental import pallas as pl
from jax.experimental.pallas import tpu as pltpu
from jax.sharding import PartitionSpec as P

KV = 4
HD = 128
HEADS = 16
ROWBLK = 128
RUN_BLOCKS = 8
VMEM_BYTES = 58 * 1024 * 1024
NO_COST = pl.CostEstimate(flops=0, bytes_accessed=0, transcendentals=0)


rope_base = 1000000.0
yarn_factor = 4.0
yarn_context = 32768.0
beta_fast = 32.0
beta_slow = 1.0
masked_score = -1e30


def yarn_frequencies(head_size):
    half_size = head_size // 2

    def correction(rotations):
        return (
            head_size
            * math.log(yarn_context / (rotations * 2.0 * math.pi))
            / (2.0 * math.log(rope_base))
        )

    lower_bound = max(math.floor(correction(beta_fast)), 0)
    upper_bound = min(math.ceil(correction(beta_slow)), head_size - 1)
    ramp_span = max(upper_bound - lower_bound, 0.001)
    row_index = jnp.arange(half_size).astype(jnp.float32)
    extrap_freq = rope_base ** (-2.0 * row_index / head_size)
    interp_freq = extrap_freq / yarn_factor
    ramp_weight = jnp.clip((row_index - lower_bound) / ramp_span, 0.0, 1.0)
    return interp_freq * ramp_weight + extrap_freq * (1.0 - ramp_weight)


def positions_of(segments):
    row_count = segments.shape[-1]
    row_index = jnp.arange(row_count, dtype=jnp.int32)
    is_start = jnp.concatenate(
        [
            jnp.ones(segments.shape[:-1] + (1,), dtype=jnp.bool_),
            segments[..., 1:] != segments[..., :-1],
        ],
        axis=-1,
    )
    seg_start = lax.cummax(jnp.where(is_start, row_index, 0), axis=segments.ndim - 1)
    return row_index - seg_start


def rope_kernel(at_ref, dest_ref, places_ref, freq_ref, key_ref, *refs):
    cos_ref, sin_ref, turned_ref, own_ref = refs
    factor = 0.1 * math.log(yarn_factor) + 1.0
    half = lax.broadcasted_iota(jnp.int32, (ROWBLK, HD), 1) < HD // 2
    for block in range(own_ref.shape[0]):
        rows = pl.ds(block * ROWBLK, ROWBLK)
        place = places_ref[pl.ds(dest_ref[block], 1), :]
        own_ref[pl.ds(block, 1), :] = place
        spread_out = jnp.broadcast_to(place.astype(jnp.float32), (ROWBLK, HD)).T
        angles = spread_out * freq_ref[...]
        cosine = jnp.cos(angles) * factor
        sine = jnp.sin(angles) * factor
        sine = jnp.where(half, -sine, sine)
        cos_ref[rows, :] = cosine
        sin_ref[rows, :] = sine
        raw = key_ref[rows, :].astype(jnp.float32)
        turned = raw * cosine + pltpu.roll(raw, HD // 2, 1) * sine
        turned_ref[rows, :] = turned.astype(turned_ref.dtype)


def rope(kv_head, dest, places_all, key):
    rows = key.shape[0]
    blocks = rows // ROWBLK
    freq = yarn_frequencies(HD)
    freq = jnp.concatenate([freq, freq]).reshape(1, HD)
    whole = lambda shape: pl.BlockSpec(shape, lambda step, *refs: (0,) * len(shape))
    table = jax.ShapeDtypeStruct((rows, HD), jnp.float32)
    return pl.pallas_call(
        rope_kernel,
        grid_spec=pltpu.PrefetchScalarGridSpec(
            num_scalar_prefetch=2,
            grid=(1,),
            in_specs=[
                whole(places_all.shape),
                whole((1, HD)),
                pl.BlockSpec((rows, HD), lambda step, at_ref, dest_ref: (0, at_ref[0])),
            ],
            out_specs=[whole((rows, HD))] * 3 + [whole((blocks, ROWBLK))],
        ),
        out_shape=[
            table,
            table,
            jax.ShapeDtypeStruct((rows, HD), key.dtype),
            jax.ShapeDtypeStruct((blocks, ROWBLK), jnp.int32),
        ],
        cost_estimate=NO_COST,
    )(kv_head.reshape(1), dest, places_all, freq, key)


NT = (((1,), (1,)), ((), ()))
TN = (((0,), (0,)), ((), ()))


def attend_kernel(
    heads,
    ranks,
    target_ref,
    source_ref,
    run_ref,
    slot_ref,
    need_ref,
    query_ref,
    up_ref,
    up_t_ref,
    place_ref,
    *refs,
):
    key_parts, refs = refs[:ranks], refs[ranks:]
    value_parts, refs = refs[:ranks], refs[ranks:]
    gquery_ref, out_ref, *halves = refs[:6]
    key_ref, value_ref, gkey_ref, gvalue_ref, key_win, value_win = refs[6:12]
    score_ref, prob_ref, gscore_ref, load_sems, sems = refs[12:]
    rows_each = query_ref.shape[0]
    half_blocks = ranks * RUN_BLOCKS // 2
    scale = 1.0 / math.sqrt(HD)
    to_exp2 = scale * math.log2(math.e)

    loads = []
    for item, (parts, whole) in enumerate(((key_parts, key_ref), (value_parts, value_ref))):
        for rank in range(ranks):
            copy = pltpu.make_async_copy(
                parts[rank], whole.at[pl.ds(rank * rows_each, rows_each)], load_sems.at[item, rank]
            )
            copy.start()
            loads.append(copy)
    for copy in loads:
        copy.wait()

    def stores(block, act):
        side = block % 2
        for step in range(RUN_BLOCKS):
            target = target_ref[run_ref[block] * RUN_BLOCKS + step]
            for place in range(2):

                @pl.when(target // half_blocks == place)
                def one_half():
                    start = pl.multiple_of(target % half_blocks * ROWBLK, ROWBLK)
                    for item, source in enumerate((gkey_ref, gvalue_ref)):
                        act(
                            pltpu.make_async_copy(
                                source.at[side, pl.ds(step * ROWBLK, ROWBLK)],
                                halves[2 * item + place].at[pl.ds(start, ROWBLK)],
                                sems.at[side, item, step],
                            )
                        )

    def window(count, block):
        slot = slot_ref[block]
        run = run_ref[block]
        first = jnp.maximum(slot + 1 - count, 0)
        rows = count * ROWBLK
        for step in range(count):
            source = source_ref[run * RUN_BLOCKS + first + step]
            start = pl.multiple_of(source * ROWBLK, ROWBLK)
            key_win[pl.ds(step * ROWBLK, ROWBLK), :] = key_ref[pl.ds(start, ROWBLK), :]
            value_win[pl.ds(step * ROWBLK, ROWBLK), :] = value_ref[pl.ds(start, ROWBLK), :]
        wide = min(2, heads)
        base = pl.multiple_of(block * ROWBLK, ROWBLK)
        at_rows = pl.ds(base, ROWBLK)
        place = place_ref[pl.ds(block, 1), :]
        lane = lax.broadcasted_iota(jnp.int32, (1, ROWBLK), 1)
        last = (slot - first) * ROWBLK + lane
        last_all = jnp.concatenate([last] * wide, axis=1)
        start_all = jnp.concatenate([last - place] * wide, axis=1)
        key_index = lax.broadcasted_iota(jnp.int32, (ROWBLK, wide * ROWBLK), 0)
        keys = key_win[pl.ds(0, rows), :]
        values = value_win[pl.ds(0, rows), :]
        columns = [pl.ds(head * HD, HD) for head in range(heads)]
        query = jnp.concatenate([query_ref[at_rows, at] for at in columns], axis=0)
        up = jnp.concatenate([up_ref[at_rows, at] for at in columns], axis=0)
        folded = lambda tile: tile.reshape(ROWBLK // 8, 8, tile.shape[1])
        tiles = [pl.ds(step * ROWBLK, ROWBLK) for step in range(count)]
        groups = heads // wide
        spans = [slice(at * wide * ROWBLK, (at + 1) * wide * ROWBLK) for at in range(groups)]

        score = lax.dot_general(keys, query, NT, preferred_element_type=jnp.float32)
        gprob = lax.dot_general(values, up, NT, preferred_element_type=jnp.float32)
        peaks = [None] * groups
        for step, tile in enumerate(tiles):
            seen = key_index >= start_all - step * ROWBLK
            if step == count - 1:
                seen = seen & (key_index <= last_all - step * ROWBLK)
            for at, span in enumerate(spans):
                part = jnp.where(
                    seen, score[step * ROWBLK : (step + 1) * ROWBLK, span], masked_score
                )
                score_ref[tile, span] = part
                most = jnp.max(folded(part), axis=0)
                peaks[at] = most if peaks[at] is None else jnp.maximum(peaks[at], most)
        peaks = [jnp.max(item, axis=0, keepdims=True) for item in peaks]
        totals = [None] * groups
        for tile in tiles:
            for at, span in enumerate(spans):
                part = jnp.exp2((score_ref[tile, span] - peaks[at]) * to_exp2)
                score_ref[tile, span] = part
                some = jnp.sum(folded(part), axis=0)
                totals[at] = some if totals[at] is None else totals[at] + some
        shares = [1.0 / jnp.sum(item, axis=0, keepdims=True) for item in totals]
        for tile in tiles:
            for at, span in enumerate(spans):
                prob_ref[tile, span] = (score_ref[tile, span] * shares[at]).astype(jnp.bfloat16)
        prob_b = prob_ref[pl.ds(0, rows), :]
        out_t = lax.dot_general(values, prob_b, TN, preferred_element_type=jnp.float32)
        out_b = out_t.astype(jnp.bfloat16)
        deltas = []
        for at in range(groups):
            up_t = jnp.concatenate(
                [up_t_ref[item, at_rows] for item in columns[at * wide : (at + 1) * wide]], axis=1
            ).astype(jnp.float32)
            deltas.append(
                jnp.sum(up_t * out_b[:, spans[at]].astype(jnp.float32), axis=0, keepdims=True)
            )
        for step, tile in enumerate(tiles):
            for at, span in enumerate(spans):
                prob = score_ref[tile, span] * shares[at]
                part = gprob[step * ROWBLK : (step + 1) * ROWBLK, span] - deltas[at]
                gscore_ref[tile, span] = (prob * part).astype(jnp.bfloat16)
        gscore = gscore_ref[pl.ds(0, rows), :]
        gquery_t = lax.dot_general(keys, gscore, TN, preferred_element_type=jnp.float32)
        gkey = jnp.dot(gscore, query, preferred_element_type=jnp.float32)
        gvalue = jnp.dot(prob_b, up, preferred_element_type=jnp.float32)
        for head in range(heads):
            part = slice(head * ROWBLK, (head + 1) * ROWBLK)
            out_ref[columns[head], at_rows] = out_b[:, part]
            gquery_ref[columns[head], at_rows] = gquery_t[:, part]
        gkey = (gkey * scale).astype(jnp.bfloat16)
        gvalue = gvalue.astype(jnp.bfloat16)
        place_at = pl.ds(pl.multiple_of(first * ROWBLK, ROWBLK), rows)
        gkey_ref[block % 2, place_at, :] = gkey
        gvalue_ref[block % 2, place_at, :] = gvalue

    def body(block, carry):
        pl.when(block >= 2)(lambda: stores(block - 2, lambda copy: copy.wait()))
        blank = jnp.zeros(gkey_ref.shape[1:], jnp.bfloat16)
        gkey_ref[block % 2] = blank
        gvalue_ref[block % 2] = blank
        need = need_ref[block]
        floor = 0
        for size in range(1, RUN_BLOCKS + 1):
            pl.when((need > floor) & (need <= size))(partial(window, size, block))
            floor = size
        stores(block, lambda copy: copy.start())
        return carry

    blocks = rows_each // ROWBLK
    lax.fori_loop(0, blocks, body, 0)
    for block in range(max(blocks - 2, 0), blocks):
        stores(block, lambda copy: copy.wait())


def attend(tables, query, up, up_t, places, keys, values):
    rows, width = query.shape
    heads = width // HD
    ranks = len(keys)
    every = rows * ranks
    smem = pl.BlockSpec(memory_space=pltpu.SMEM)
    vmem = pl.BlockSpec(memory_space=pltpu.VMEM)
    hbm = pl.BlockSpec(memory_space=pl.ANY)
    half = jax.ShapeDtypeStruct((every // 2, HD), jnp.bfloat16)
    return pl.pallas_call(
        partial(attend_kernel, heads, ranks),
        out_shape=(
            jax.ShapeDtypeStruct((width, rows), jnp.float32),
            jax.ShapeDtypeStruct((width, rows), jnp.bfloat16),
            half,
            half,
            half,
            half,
        ),
        in_specs=[smem] * 5 + [vmem] * 4 + [hbm] * (2 * ranks),
        out_specs=(vmem, vmem, hbm, hbm, hbm, hbm),
        scratch_shapes=[pltpu.VMEM((every, HD), jnp.bfloat16)] * 2
        + [pltpu.VMEM((2, RUN_BLOCKS * ROWBLK, HD), jnp.bfloat16)] * 2
        + [pltpu.VMEM((RUN_BLOCKS * ROWBLK, HD), jnp.bfloat16)] * 2
        + [pltpu.VMEM((RUN_BLOCKS * ROWBLK, heads * ROWBLK), jnp.float32)]
        + [pltpu.VMEM((RUN_BLOCKS * ROWBLK, heads * ROWBLK), jnp.bfloat16)] * 2
        + [pltpu.SemaphoreType.DMA((2, ranks)), pltpu.SemaphoreType.DMA((2, 2, RUN_BLOCKS))],
        compiler_params=pltpu.CompilerParams(vmem_limit_bytes=VMEM_BYTES),
        cost_estimate=NO_COST,
    )(*tables, query, up, up_t, places, *keys, *values)


def assemble_kernel(lanes, my_ref, *refs):
    out_ref, sems = refs[lanes:]
    copies = []
    for index in range(lanes):
        column = pl.multiple_of((my_ref[0] ^ index) * HD, HD)
        copy = pltpu.make_async_copy(
            refs[index], out_ref.at[:, pl.ds(column, HD)], sems.at[index]
        )
        copy.start()
        copies.append(copy)
    for copy in copies:
        copy.wait()


def assemble(my_lane, pieces):
    rows = pieces[0].shape[0]
    lanes = len(pieces)
    vmem = pl.BlockSpec(memory_space=pltpu.VMEM)
    return pl.pallas_call(
        partial(assemble_kernel, lanes),
        out_shape=jax.ShapeDtypeStruct((rows, lanes * HD), pieces[0].dtype),
        in_specs=[pl.BlockSpec(memory_space=pltpu.SMEM)] + [vmem] * lanes,
        out_specs=pl.BlockSpec(memory_space=pl.ANY),
        scratch_shapes=[pltpu.SemaphoreType.DMA((lanes,))],
        compiler_params=pltpu.CompilerParams(vmem_limit_bytes=VMEM_BYTES),
        cost_estimate=NO_COST,
    )(my_lane.reshape(1), *pieces)


def lane_swap(array, bit):
    lanes = lax.axis_size("tensor")
    return lax.ppermute(array, "tensor", [(lane, lane ^ bit) for lane in range(lanes)])


def lane_pieces(pieces, bit):
    lanes = lax.axis_size("tensor")
    while bit:
        pieces = {**pieces, **{at | bit: lane_swap(item, bit) for at, item in pieces.items()}}
        bit //= 2
    return [pieces[at] for at in range(lanes)]


def swap(array, bit):
    ranks = lax.axis_size("dp")
    return lax.ppermute(array, "dp", [(rank, rank ^ bit) for rank in range(ranks)])


def spread(array):
    found = [array, swap(array, 1)]
    others = [swap(array, step) for step in range(2, lax.axis_size("dp"), 2)]
    for other in others:
        found += [other, swap(other, 1)]
    return found


def added(left, right):
    return left.astype(jnp.float32) + right.astype(jnp.float32)


def chip_sum(keep, received):
    count = lax.axis_size("dp") // 2
    rows = keep.shape[0] // count
    total = [
        added(keep[at * rows : (at + 1) * rows], received[at * rows : (at + 1) * rows])
        for at in range(count)
    ]
    return total[0], [item.astype(keep.dtype) for item in total[1:]]


def exchange(sends):
    return [swap(item, 2 * at + 2) for at, item in enumerate(sends)]


def final_kernel(count, rotary, outs, *refs):
    total = refs[0][...].astype(jnp.float32)
    for ref in refs[1 : 1 + count]:
        total = total + ref[...].astype(jnp.float32)
    if rotary:
        total = total * refs[1 + count][...] - pltpu.roll(total, HD // 2, 1) * refs[2 + count][...]
    for at in outs:
        refs[at][...] = total.astype(refs[at].dtype)


def final_sum(keep, received, tables, after, thru=(), copies=1):
    vmem = pl.BlockSpec(memory_space=pltpu.VMEM)
    hbm = pl.BlockSpec(memory_space=pl.ANY)
    parts = [keep, *received, *tables]
    inputs = len(parts) + len(after) + len(thru)
    results = pl.pallas_call(
        partial(
            final_kernel, len(received), len(tables) > 0, range(inputs, inputs + copies)
        ),
        out_shape=[jax.ShapeDtypeStruct(keep.shape, jnp.bfloat16)] * copies
        + [jax.ShapeDtypeStruct(item.shape, item.dtype) for item in thru],
        in_specs=[vmem] * len(parts) + [hbm] * (len(after) + len(thru)),
        out_specs=[vmem] * copies + [hbm] * len(thru),
        input_output_aliases={inputs - len(thru) + at: copies + at for at in range(len(thru))},
        compiler_params=pltpu.CompilerParams(vmem_limit_bytes=VMEM_BYTES),
        cost_estimate=NO_COST,
    )(*parts, *after, *thru)
    return results


def prepare_kernel(
    rows_ref, weight_ref, query_ref, cos_ref, sin_ref, *refs
):
    up_ref, up_t_ref, turned_ref = refs[-3:]
    total = jnp.dot(rows_ref[...], weight_ref[...], preferred_element_type=jnp.float32)
    up_ref[...] = total.astype(up_ref.dtype)
    up_t_ref[...] = total.T.astype(up_t_ref.dtype)
    for at in range(0, query_ref.shape[1], HD):
        raw = query_ref[:, at : at + HD].astype(jnp.float32)
        turned = raw * cos_ref[...] + pltpu.roll(raw, HD // 2, 1) * sin_ref[...]
        turned_ref[:, at : at + HD] = turned.astype(turned_ref.dtype)


def prepare(rows, weight, query, cosine, sine, after):
    height, depth = rows.shape
    width = weight.shape[1]
    steps = 4
    tall = height // steps
    across = lambda columns: pl.BlockSpec((tall, columns), lambda step: (step, 0))
    return pl.pallas_call(
        prepare_kernel,
        grid=(steps,),
        out_shape=[
            jax.ShapeDtypeStruct((height, width), jnp.bfloat16),
            jax.ShapeDtypeStruct((width, height), jnp.bfloat16),
            jax.ShapeDtypeStruct(query.shape, jnp.bfloat16),
        ],
        in_specs=[
            across(depth),
            pl.BlockSpec(weight.shape, lambda step: (0, 0)),
            across(width),
            across(HD),
            across(HD),
        ]
        + [pl.BlockSpec(memory_space=pl.ANY)] * len(after),
        out_specs=[
            across(width),
            pl.BlockSpec((width, tall), lambda step: (0, step)),
            across(width),
        ],
        compiler_params=pltpu.CompilerParams(vmem_limit_bytes=VMEM_BYTES),
        cost_estimate=pl.CostEstimate(
            flops=2 * height * weight.size, bytes_accessed=2 * rows.size, transcendentals=0
        ),
    )(rows, weight, query, cosine, sine, *after)


def turn_back_kernel(grad_ref, cos_ref, sin_ref, *refs):
    out_ref = refs[-1]
    scale = 1.0 / math.sqrt(HD)
    for at in range(0, grad_ref.shape[0], HD):
        grad = grad_ref[at : at + HD, :].T * scale
        back = grad * cos_ref[...] - pltpu.roll(grad, HD // 2, 1) * sin_ref[...]
        out_ref[:, at : at + HD] = back.astype(out_ref.dtype)


def turn_back(grad_t, cosine, sine, after):
    width, height = grad_t.shape
    steps = 4
    tall = height // steps
    return pl.pallas_call(
        turn_back_kernel,
        grid=(steps,),
        out_shape=jax.ShapeDtypeStruct((height, width), jnp.bfloat16),
        in_specs=[
            pl.BlockSpec((width, tall), lambda step: (0, step)),
            pl.BlockSpec((tall, HD), lambda step: (step, 0)),
            pl.BlockSpec((tall, HD), lambda step: (step, 0)),
        ]
        + [pl.BlockSpec(memory_space=pl.ANY)] * len(after),
        out_specs=pl.BlockSpec((tall, width), lambda step: (step, 0)),
        compiler_params=pltpu.CompilerParams(vmem_limit_bytes=VMEM_BYTES),
        cost_estimate=NO_COST,
    )(grad_t, cosine, sine, *after)


def hold_kernel(*refs):
    pass


def hold(array, after):
    hbm = pl.BlockSpec(memory_space=pl.ANY)
    return pl.pallas_call(
        hold_kernel,
        out_shape=jax.ShapeDtypeStruct(array.shape, array.dtype),
        in_specs=[hbm] * (1 + len(after)),
        out_specs=hbm,
        input_output_aliases={0: 0},
        cost_estimate=NO_COST,
    )(array, *after)


def product_kernel(my_ref, left_ref, right_ref, *refs):
    keep_ref, send_ref = refs[-3:-1]
    half = keep_ref.shape[1]
    total = jnp.dot(left_ref[...], right_ref[...], preferred_element_type=jnp.float32)
    total = total.astype(keep_ref.dtype).T
    odd = my_ref[1]

    @pl.when(odd == 0)
    def even_core():
        keep_ref[0] = total[:half]
        send_ref[0] = total[half:]

    @pl.when(odd == 1)
    def odd_core():
        keep_ref[0] = total[half:]
        send_ref[0] = total[:half]


def product(my_rank, left, right, thru, after):
    count = lax.axis_size("dp") // 2
    width, depth = left.shape
    cols = right.shape[1] // count
    mine, odd = my_rank // 2, my_rank & 1
    if cols % 128:
        total = jnp.dot(left, right, preferred_element_type=jnp.float32).astype(jnp.bfloat16)
        pieces = total.T.reshape(count, 2, cols // 2, width)
        pieces = jnp.take(pieces, jnp.arange(count, dtype=jnp.int32) ^ mine, axis=0)
        low, high = pieces[:, 0], pieces[:, 1]
        return jnp.where(odd > 0, high, low), jnp.where(odd > 0, low, high), thru
    hbm = pl.BlockSpec(memory_space=pl.ANY)
    stacked = pl.BlockSpec((1, cols // 2, width), lambda step, my_ref: (step, 0, 0))
    stack = jax.ShapeDtypeStruct((count, cols // 2, width), jnp.bfloat16)
    inputs = [jnp.stack([mine, odd]), left, right, *after, thru]
    return pl.pallas_call(
        product_kernel,
        grid_spec=pltpu.PrefetchScalarGridSpec(
            num_scalar_prefetch=1,
            grid=(count,),
            in_specs=[
                pl.BlockSpec(left.shape, lambda step, my_ref: (0, 0)),
                pl.BlockSpec((depth, cols), lambda step, my_ref: (0, step ^ my_ref[0])),
            ]
            + [hbm] * (len(after) + 1),
            out_specs=[stacked, stacked, hbm],
        ),
        out_shape=[stack, stack, jax.ShapeDtypeStruct(thru.shape, thru.dtype)],
        input_output_aliases={len(inputs) - 1: 2},
        compiler_params=pltpu.CompilerParams(vmem_limit_bytes=VMEM_BYTES),
        cost_estimate=NO_COST,
    )(*inputs)


def weight_final_kernel(count, factor, *refs):
    total = refs[0][0].astype(jnp.float32)
    for ref in refs[1 : 1 + count]:
        total = total + ref[0].astype(jnp.float32)
    refs[-1][...] = total * factor


def weight_final(keep, received, factor, after):
    vmem = pl.BlockSpec(memory_space=pltpu.VMEM)
    hbm = pl.BlockSpec(memory_space=pl.ANY)
    return pl.pallas_call(
        partial(weight_final_kernel, len(received), factor),
        out_shape=jax.ShapeDtypeStruct(keep.shape[1:], jnp.float32),
        in_specs=[vmem] * (1 + len(received)) + [hbm] * len(after),
        out_specs=vmem,
        compiler_params=pltpu.CompilerParams(vmem_limit_bytes=VMEM_BYTES),
        cost_estimate=NO_COST,
    )(keep, *received, *after)


def local(query, key, value, grad_out, out_weight, plan, segments):
    rank_count = lax.axis_size("dp")
    my_rank = lax.axis_index("dp")
    my_lane = lax.axis_index("tensor")
    row_count = query.shape[0]
    block_count = row_count // ROWBLK
    local_heads = query.shape[1] // HD
    group = HEADS // KV
    bits = [1 << at for at in range(rank_count.bit_length() - 1)]
    kv_head = my_lane * local_heads // group
    own_value = lax.dynamic_slice_in_dim(value, kv_head * HD, HD, 1)
    own_places = positions_of(segments).reshape(1, block_count, ROWBLK)
    places_all = lax.all_to_all(
        jnp.broadcast_to(own_places, (rank_count, block_count, ROWBLK)),
        "dp",
        split_axis=0,
        concat_axis=0,
        tiled=True,
    ).reshape(-1, ROWBLK)
    values = spread(own_value)

    mine = my_rank * block_count + jnp.arange(block_count, dtype=jnp.int32)
    hit = plan[None, :] == mine[:, None]
    dest = jnp.sum(
        jnp.where(hit, jnp.arange(plan.shape[0], dtype=jnp.int32)[None, :], 0), axis=1
    )
    run = dest // RUN_BLOCKS
    slot = dest % RUN_BLOCKS
    cosine, sine, rot_key, places = rope(kv_head, dest, places_all, key)
    need = slot - (slot * ROWBLK - places[:, 0]) // ROWBLK + 1
    keys = spread(rot_key)
    up, up_t, turned = prepare(grad_out, out_weight, query, cosine, sine, [rot_key])

    distance = (plan // block_count) ^ my_rank
    within = plan % block_count
    half_place = (distance & 1) * (rank_count // 2) + distance // 2
    tables = (
        half_place * block_count + within,
        distance * block_count + within,
        run,
        slot,
        need,
    )
    grad_query_t, attn_t, gkey_keep, gkey_send, gvalue_keep, gvalue_send = attend(
        tables, turned, up, up_t, places, keys, values
    )
    value_keep, value_sends = chip_sum(gvalue_keep, swap(gvalue_send, 1))
    value_received = exchange(value_sends)
    key_keep, key_sends = chip_sum(gkey_keep, swap(gkey_send, 1))
    key_received = exchange(key_sends)
    weight_keep, weight_send, value_keep = product(
        my_rank, attn_t, grad_out, value_keep, [value_sends[0], key_sends[0]]
    )
    far = lax.axis_size("tensor") // 2
    value_partial, value_near, weight_send = final_sum(
        value_keep, value_received, (), (), thru=[weight_send], copies=2
    )
    value_far = lane_swap(value_partial, far)
    weight_keep, weight_sends = chip_sum(weight_keep, swap(weight_send, 1))
    weight_received = exchange(weight_sends)
    value_near = hold(value_near, weight_sends[:1])
    grad_query = turn_back(grad_query_t, cosine, sine, weight_sends[:1])
    value_far = hold(value_far, [grad_query])
    value_pieces = lane_pieces({0: value_near, far: value_far}, far // 2)
    value_all = assemble(my_lane, value_pieces)
    (key_partial,) = final_sum(
        key_keep, key_received, (cosine, sine), [grad_query, value_far, value_pieces[1]]
    )
    key_far = hold(lane_swap(key_partial, far), weight_received)
    key_all = assemble(my_lane, lane_pieces({0: key_partial, far: key_far}, far // 2))
    weight_grad = weight_final(
        weight_keep, weight_received, 1.0 / rank_count, [key_far, value_all]
    )
    lanes_per_key = group // local_heads

    def combine(gathered):
        if lanes_per_key == 1:
            return gathered
        merged = (
            gathered.astype(jnp.float32).reshape(row_count, KV, lanes_per_key, HD).sum(axis=2)
        )
        return merged.astype(jnp.bfloat16).reshape(row_count, KV * HD)

    return (grad_query, combine(key_all), combine(value_all), weight_grad)


def solution(mesh):
    in_specs = (
        P("dp", "tensor"),
        P("dp", None),
        P("dp", None),
        P("dp", None),
        P(None, "tensor"),
        P(),
        P("dp"),
    )
    out_specs = (P("dp", "tensor"), P("dp", None), P("dp", None), P("dp", "tensor"))
    return jax.shard_map(local, mesh=mesh, in_specs=in_specs, out_specs=out_specs, check_vma=False)
```

```python
from functools import partial
import math

import jax
import jax.numpy as jnp
from jax import lax
from jax.experimental import pallas as pl
from jax.experimental.pallas import tpu as pltpu
from jax.sharding import PartitionSpec as P

KV = 4
HD = 128
HEADS = 16
ROWBLK = 128
RUN_BLOCKS = 8
VMEM_BYTES = 58 * 1024 * 1024
NO_COST = pl.CostEstimate(flops=0, bytes_accessed=0, transcendentals=0)


rope_base = 1000000.0
yarn_factor = 4.0
yarn_context = 32768.0
beta_fast = 32.0
beta_slow = 1.0
masked_score = -1e30


def yarn_frequencies(head_size):
    half_size = head_size // 2

    def correction(rotations):
        return (
            head_size
            * math.log(yarn_context / (rotations * 2.0 * math.pi))
            / (2.0 * math.log(rope_base))
        )

    lower_bound = max(math.floor(correction(beta_fast)), 0)
    upper_bound = min(math.ceil(correction(beta_slow)), head_size - 1)
    ramp_span = max(upper_bound - lower_bound, 0.001)
    row_index = jnp.arange(half_size).astype(jnp.float32)
    extrap_freq = rope_base ** (-2.0 * row_index / head_size)
    interp_freq = extrap_freq / yarn_factor
    ramp_weight = jnp.clip((row_index - lower_bound) / ramp_span, 0.0, 1.0)
    return interp_freq * ramp_weight + extrap_freq * (1.0 - ramp_weight)


def positions_of(segments):
    row_count = segments.shape[-1]
    row_index = jnp.arange(row_count, dtype=jnp.int32)
    is_start = jnp.concatenate(
        [
            jnp.ones(segments.shape[:-1] + (1,), dtype=jnp.bool_),
            segments[..., 1:] != segments[..., :-1],
        ],
        axis=-1,
    )
    seg_start = lax.cummax(jnp.where(is_start, row_index, 0), axis=segments.ndim - 1)
    return row_index - seg_start


def rope_kernel(at_ref, dest_ref, places_ref, freq_ref, key_ref, *refs):
    cos_ref, sin_ref, turned_ref, own_ref = refs
    factor = 0.1 * math.log(yarn_factor) + 1.0
    half = lax.broadcasted_iota(jnp.int32, (ROWBLK, HD), 1) < HD // 2
    each = key_ref.shape[0] // ROWBLK
    for item in range(each):
        block = pl.program_id(0) * each + item
        rows = pl.ds(item * ROWBLK, ROWBLK)
        place = places_ref[pl.ds(dest_ref[block], 1), :]
        own_ref[pl.ds(block, 1), :] = place
        spread_out = jnp.broadcast_to(place.astype(jnp.float32), (ROWBLK, HD)).T
        angles = spread_out * freq_ref[...]
        cosine = jnp.cos(angles) * factor
        sine = jnp.sin(angles) * factor
        sine = jnp.where(half, -sine, sine)
        cos_ref[rows, :] = cosine
        sin_ref[rows, :] = sine
        raw = key_ref[rows, :].astype(jnp.float32)
        turned = raw * cosine + pltpu.roll(raw, HD // 2, 1) * sine
        turned_ref[rows, :] = turned.astype(turned_ref.dtype)


def rope(kv_head, dest, places_all, key):
    rows = key.shape[0]
    blocks = rows // ROWBLK
    steps = 4
    freq = yarn_frequencies(HD)
    freq = jnp.concatenate([freq, freq]).reshape(1, HD)
    whole = lambda shape: pl.BlockSpec(shape, lambda step, *refs: (0,) * len(shape))
    table = jax.ShapeDtypeStruct((rows, HD), jnp.float32)
    return pl.pallas_call(
        rope_kernel,
        grid_spec=pltpu.PrefetchScalarGridSpec(
            num_scalar_prefetch=2,
            grid=(steps,),
            in_specs=[
                whole(places_all.shape),
                whole((1, HD)),
                pl.BlockSpec((rows // steps, HD), lambda step, at_ref, dest_ref: (step, at_ref[0])),
            ],
            out_specs=[pl.BlockSpec((rows // steps, HD), lambda step, *refs: (step, 0))] * 3
            + [whole((blocks, ROWBLK))],
        ),
        out_shape=[
            table,
            table,
            jax.ShapeDtypeStruct((rows, HD), key.dtype),
            jax.ShapeDtypeStruct((blocks, ROWBLK), jnp.int32),
        ],
        cost_estimate=NO_COST,
    )(kv_head.reshape(1), dest, places_all, freq, key)


NT = (((1,), (1,)), ((), ()))
TN = (((0,), (0,)), ((), ()))


def attend_kernel(
    heads,
    ranks,
    table_ref,
    query_ref,
    up_ref,
    up_t_ref,
    place_ref,
    *refs,
):
    key_parts, refs = refs[:ranks], refs[ranks:]
    value_parts, refs = refs[:ranks], refs[ranks:]
    gquery_ref, out_ref, *halves = refs[:6]
    key_ref, value_ref, gkey_ref, gvalue_ref, key_win, value_win = refs[6:12]
    score_ref, prob_ref, gscore_ref, load_sems, sems = refs[12:]
    rows_each = query_ref.shape[0]
    total_blocks = ranks * RUN_BLOCKS
    target_ref = table_ref.at[pl.ds(0, total_blocks)]
    source_ref = table_ref.at[pl.ds(total_blocks, total_blocks)]
    run_ref, slot_ref, need_ref = (
        table_ref.at[pl.ds(2 * total_blocks + at * RUN_BLOCKS, RUN_BLOCKS)] for at in range(3)
    )
    half_blocks = ranks * RUN_BLOCKS // 2
    scale = 1.0 / math.sqrt(HD)
    to_exp2 = scale * math.log2(math.e)

    loads = []
    for item, (parts, whole) in enumerate(((key_parts, key_ref), (value_parts, value_ref))):
        for rank in range(ranks):
            copy = pltpu.make_async_copy(
                parts[rank], whole.at[pl.ds(rank * rows_each, rows_each)], load_sems.at[item, rank]
            )
            copy.start()
            loads.append(copy)
    for copy in loads:
        copy.wait()

    def stores(block, act):
        side = block % 2
        for step in range(RUN_BLOCKS):
            target = target_ref[run_ref[block] * RUN_BLOCKS + step]
            for place in range(2):

                @pl.when(target // half_blocks == place)
                def one_half():
                    start = pl.multiple_of(target % half_blocks * ROWBLK, ROWBLK)
                    for item, source in enumerate((gkey_ref, gvalue_ref)):
                        act(
                            pltpu.make_async_copy(
                                source.at[side, pl.ds(step * ROWBLK, ROWBLK)],
                                halves[2 * item + place].at[pl.ds(start, ROWBLK)],
                                sems.at[side, item, step],
                            )
                        )

    def window(count, block):
        slot = slot_ref[block]
        run = run_ref[block]
        first = jnp.maximum(slot + 1 - count, 0)
        rows = count * ROWBLK
        for step in range(count):
            source = source_ref[run * RUN_BLOCKS + first + step]
            start = pl.multiple_of(source * ROWBLK, ROWBLK)
            key_win[pl.ds(step * ROWBLK, ROWBLK), :] = key_ref[pl.ds(start, ROWBLK), :]
            value_win[pl.ds(step * ROWBLK, ROWBLK), :] = value_ref[pl.ds(start, ROWBLK), :]
        wide = min(2, heads)
        base = pl.multiple_of(block * ROWBLK, ROWBLK)
        at_rows = pl.ds(base, ROWBLK)
        place = place_ref[pl.ds(block, 1), :]
        lane = lax.broadcasted_iota(jnp.int32, (1, ROWBLK), 1)
        last = (slot - first) * ROWBLK + lane
        last_all = jnp.concatenate([last] * wide, axis=1)
        start_all = jnp.concatenate([last - place] * wide, axis=1)
        key_index = lax.broadcasted_iota(jnp.int32, (ROWBLK, wide * ROWBLK), 0)
        keys = key_win[pl.ds(0, rows), :]
        values = value_win[pl.ds(0, rows), :]
        columns = [pl.ds(head * HD, HD) for head in range(heads)]
        query = jnp.concatenate([query_ref[at_rows, at] for at in columns], axis=0)
        up = jnp.concatenate([up_ref[at_rows, at] for at in columns], axis=0)
        folded = lambda tile: tile.reshape(ROWBLK // 8, 8, tile.shape[1])
        tiles = [pl.ds(step * ROWBLK, ROWBLK) for step in range(count)]
        groups = heads // wide
        spans = [slice(at * wide * ROWBLK, (at + 1) * wide * ROWBLK) for at in range(groups)]

        score = lax.dot_general(keys, query, NT, preferred_element_type=jnp.float32)
        gprob = lax.dot_general(values, up, NT, preferred_element_type=jnp.float32)
        peaks = [None] * groups
        for step, tile in enumerate(tiles):
            seen = key_index >= start_all - step * ROWBLK
            if step == count - 1:
                seen = seen & (key_index <= last_all - step * ROWBLK)
            for at, span in enumerate(spans):
                part = jnp.where(
                    seen, score[step * ROWBLK : (step + 1) * ROWBLK, span], masked_score
                )
                score_ref[tile, span] = part
                most = jnp.max(folded(part), axis=0)
                peaks[at] = most if peaks[at] is None else jnp.maximum(peaks[at], most)
        peaks = [jnp.max(item, axis=0, keepdims=True) for item in peaks]
        totals = [None] * groups
        for tile in tiles:
            for at, span in enumerate(spans):
                part = jnp.exp2((score_ref[tile, span] - peaks[at]) * to_exp2)
                score_ref[tile, span] = part
                some = jnp.sum(folded(part), axis=0)
                totals[at] = some if totals[at] is None else totals[at] + some
        shares = [1.0 / jnp.sum(item, axis=0, keepdims=True) for item in totals]
        for tile in tiles:
            for at, span in enumerate(spans):
                prob_ref[tile, span] = (score_ref[tile, span] * shares[at]).astype(jnp.bfloat16)
        prob_b = prob_ref[pl.ds(0, rows), :]
        out_t = lax.dot_general(values, prob_b, TN, preferred_element_type=jnp.float32)
        out_b = out_t.astype(jnp.bfloat16)
        deltas = []
        for at in range(groups):
            up_t = jnp.concatenate(
                [up_t_ref[item, at_rows] for item in columns[at * wide : (at + 1) * wide]], axis=1
            ).astype(jnp.float32)
            deltas.append(
                jnp.sum(up_t * out_b[:, spans[at]].astype(jnp.float32), axis=0, keepdims=True)
            )
        for step, tile in enumerate(tiles):
            for at, span in enumerate(spans):
                prob = score_ref[tile, span] * shares[at]
                part = gprob[step * ROWBLK : (step + 1) * ROWBLK, span] - deltas[at]
                gscore_ref[tile, span] = (prob * part).astype(jnp.bfloat16)
        gscore = gscore_ref[pl.ds(0, rows), :]
        gquery_t = lax.dot_general(keys, gscore, TN, preferred_element_type=jnp.float32)
        gkey = jnp.dot(gscore, query, preferred_element_type=jnp.float32)
        gvalue = jnp.dot(prob_b, up, preferred_element_type=jnp.float32)
        for head in range(heads):
            part = slice(head * ROWBLK, (head + 1) * ROWBLK)
            out_ref[columns[head], at_rows] = out_b[:, part]
            gquery_ref[columns[head], at_rows] = gquery_t[:, part]
        gkey = (gkey * scale).astype(jnp.bfloat16)
        gvalue = gvalue.astype(jnp.bfloat16)
        place_at = pl.ds(pl.multiple_of(first * ROWBLK, ROWBLK), rows)
        gkey_ref[block % 2, place_at, :] = gkey
        gvalue_ref[block % 2, place_at, :] = gvalue

    def body(block, carry):
        pl.when(block >= 2)(lambda: stores(block - 2, lambda copy: copy.wait()))
        blank = jnp.zeros(gkey_ref.shape[1:], jnp.bfloat16)
        gkey_ref[block % 2] = blank
        gvalue_ref[block % 2] = blank
        need = need_ref[block]
        floor = 0
        for size in range(1, RUN_BLOCKS + 1):
            pl.when((need > floor) & (need <= size))(partial(window, size, block))
            floor = size
        stores(block, lambda copy: copy.start())
        return carry

    blocks = rows_each // ROWBLK
    lax.fori_loop(0, blocks, body, 0)
    for block in range(max(blocks - 2, 0), blocks):
        stores(block, lambda copy: copy.wait())


def attend(tables, query, up, up_t, places, keys, values):
    rows, width = query.shape
    heads = width // HD
    ranks = len(keys)
    every = rows * ranks
    smem = pl.BlockSpec(memory_space=pltpu.SMEM)
    vmem = pl.BlockSpec(memory_space=pltpu.VMEM)
    hbm = pl.BlockSpec(memory_space=pl.ANY)
    half = jax.ShapeDtypeStruct((every // 2, HD), jnp.bfloat16)
    return pl.pallas_call(
        partial(attend_kernel, heads, ranks),
        out_shape=(
            jax.ShapeDtypeStruct((width, rows), jnp.float32),
            jax.ShapeDtypeStruct((width, rows), jnp.bfloat16),
            half,
            half,
            half,
            half,
        ),
        in_specs=[smem] + [vmem] * 4 + [hbm] * (2 * ranks),
        out_specs=(vmem, vmem, hbm, hbm, hbm, hbm),
        scratch_shapes=[pltpu.VMEM((every, HD), jnp.bfloat16)] * 2
        + [pltpu.VMEM((2, RUN_BLOCKS * ROWBLK, HD), jnp.bfloat16)] * 2
        + [pltpu.VMEM((RUN_BLOCKS * ROWBLK, HD), jnp.bfloat16)] * 2
        + [pltpu.VMEM((RUN_BLOCKS * ROWBLK, heads * ROWBLK), jnp.float32)]
        + [pltpu.VMEM((RUN_BLOCKS * ROWBLK, heads * ROWBLK), jnp.bfloat16)] * 2
        + [pltpu.SemaphoreType.DMA((2, ranks)), pltpu.SemaphoreType.DMA((2, 2, RUN_BLOCKS))],
        compiler_params=pltpu.CompilerParams(vmem_limit_bytes=VMEM_BYTES),
        cost_estimate=NO_COST,
    )(jnp.concatenate(tables), query, up, up_t, places, *keys, *values)


def assemble_kernel(lanes, my_ref, *refs):
    out_ref, sems = refs[lanes:]
    copies = []
    for index in range(lanes):
        column = pl.multiple_of((my_ref[0] ^ index) * HD, HD)
        copy = pltpu.make_async_copy(
            refs[index], out_ref.at[:, pl.ds(column, HD)], sems.at[index]
        )
        copy.start()
        copies.append(copy)
    for copy in copies:
        copy.wait()


def assemble(my_lane, pieces):
    rows = pieces[0].shape[0]
    lanes = len(pieces)
    vmem = pl.BlockSpec(memory_space=pltpu.VMEM)
    return pl.pallas_call(
        partial(assemble_kernel, lanes),
        out_shape=jax.ShapeDtypeStruct((rows, lanes * HD), pieces[0].dtype),
        in_specs=[pl.BlockSpec(memory_space=pltpu.SMEM)] + [vmem] * lanes,
        out_specs=pl.BlockSpec(memory_space=pl.ANY),
        scratch_shapes=[pltpu.SemaphoreType.DMA((lanes,))],
        compiler_params=pltpu.CompilerParams(vmem_limit_bytes=VMEM_BYTES),
        cost_estimate=NO_COST,
    )(my_lane.reshape(1), *pieces)


def lane_swap(array, bit):
    lanes = lax.axis_size("tensor")
    return lax.ppermute(array, "tensor", [(lane, lane ^ bit) for lane in range(lanes)])


def lane_pieces(pieces, bit):
    lanes = lax.axis_size("tensor")
    while bit:
        pieces = {**pieces, **{at | bit: lane_swap(item, bit) for at, item in pieces.items()}}
        bit //= 2
    return [pieces[at] for at in range(lanes)]


def swap(array, bit):
    ranks = lax.axis_size("dp")
    return lax.ppermute(array, "dp", [(rank, rank ^ bit) for rank in range(ranks)])


def spread(array):
    found = [array, swap(array, 1)]
    others = [swap(array, step) for step in range(2, lax.axis_size("dp"), 2)]
    for other in others:
        found += [other, swap(other, 1)]
    return found


def added(left, right):
    return left.astype(jnp.float32) + right.astype(jnp.float32)


def chip_sum(keep, received):
    count = lax.axis_size("dp") // 2
    rows = keep.shape[0] // count
    total = [
        added(keep[at * rows : (at + 1) * rows], received[at * rows : (at + 1) * rows])
        for at in range(count)
    ]
    return total[0], [item.astype(keep.dtype) for item in total[1:]]


def exchange(sends):
    return [swap(item, 2 * at + 2) for at, item in enumerate(sends)]


def final_kernel(count, rotary, outs, *refs):
    total = refs[0][...].astype(jnp.float32)
    for ref in refs[1 : 1 + count]:
        total = total + ref[...].astype(jnp.float32)
    if rotary:
        total = total * refs[1 + count][...] - pltpu.roll(total, HD // 2, 1) * refs[2 + count][...]
    for at in outs:
        refs[at][...] = total.astype(refs[at].dtype)


def final_sum(keep, received, tables, after, thru=(), copies=1):
    vmem = pl.BlockSpec(memory_space=pltpu.VMEM)
    hbm = pl.BlockSpec(memory_space=pl.ANY)
    parts = [keep, *received, *tables]
    inputs = len(parts) + len(after) + len(thru)
    results = pl.pallas_call(
        partial(
            final_kernel, len(received), len(tables) > 0, range(inputs, inputs + copies)
        ),
        out_shape=[jax.ShapeDtypeStruct(keep.shape, jnp.bfloat16)] * copies
        + [jax.ShapeDtypeStruct(item.shape, item.dtype) for item in thru],
        in_specs=[vmem] * len(parts) + [hbm] * (len(after) + len(thru)),
        out_specs=[vmem] * copies + [hbm] * len(thru),
        input_output_aliases={inputs - len(thru) + at: copies + at for at in range(len(thru))},
        compiler_params=pltpu.CompilerParams(vmem_limit_bytes=VMEM_BYTES),
        cost_estimate=NO_COST,
    )(*parts, *after, *thru)
    return results


def prepare_kernel(
    rows_ref, weight_ref, query_ref, cos_ref, sin_ref, *refs
):
    up_ref, up_t_ref, turned_ref = refs[-3:]
    total = jnp.dot(rows_ref[...], weight_ref[...], preferred_element_type=jnp.float32)
    up_ref[...] = total.astype(up_ref.dtype)
    up_t_ref[...] = total.T.astype(up_t_ref.dtype)
    for at in range(0, query_ref.shape[1], HD):
        raw = query_ref[:, at : at + HD].astype(jnp.float32)
        turned = raw * cos_ref[...] + pltpu.roll(raw, HD // 2, 1) * sin_ref[...]
        turned_ref[:, at : at + HD] = turned.astype(turned_ref.dtype)


def prepare(rows, weight, query, cosine, sine, after):
    height, depth = rows.shape
    width = weight.shape[1]
    steps = 4
    tall = height // steps
    across = lambda columns: pl.BlockSpec((tall, columns), lambda step: (step, 0))
    return pl.pallas_call(
        prepare_kernel,
        grid=(steps,),
        out_shape=[
            jax.ShapeDtypeStruct((height, width), jnp.bfloat16),
            jax.ShapeDtypeStruct((width, height), jnp.bfloat16),
            jax.ShapeDtypeStruct(query.shape, jnp.bfloat16),
        ],
        in_specs=[
            across(depth),
            pl.BlockSpec(weight.shape, lambda step: (0, 0)),
            across(width),
            across(HD),
            across(HD),
        ]
        + [pl.BlockSpec(memory_space=pl.ANY)] * len(after),
        out_specs=[
            across(width),
            pl.BlockSpec((width, tall), lambda step: (0, step)),
            across(width),
        ],
        compiler_params=pltpu.CompilerParams(vmem_limit_bytes=VMEM_BYTES),
        cost_estimate=pl.CostEstimate(
            flops=2 * height * weight.size, bytes_accessed=2 * rows.size, transcendentals=0
        ),
    )(rows, weight, query, cosine, sine, *after)


def turn_back_kernel(grad_ref, cos_ref, sin_ref, *refs):
    out_ref = refs[-1]
    scale = 1.0 / math.sqrt(HD)
    for at in range(0, grad_ref.shape[0], HD):
        grad = grad_ref[at : at + HD, :].T * scale
        back = grad * cos_ref[...] - pltpu.roll(grad, HD // 2, 1) * sin_ref[...]
        out_ref[:, at : at + HD] = back.astype(out_ref.dtype)


def turn_back(grad_t, cosine, sine, after):
    width, height = grad_t.shape
    steps = 4
    tall = height // steps
    return pl.pallas_call(
        turn_back_kernel,
        grid=(steps,),
        out_shape=jax.ShapeDtypeStruct((height, width), jnp.bfloat16),
        in_specs=[
            pl.BlockSpec((width, tall), lambda step: (0, step)),
            pl.BlockSpec((tall, HD), lambda step: (step, 0)),
            pl.BlockSpec((tall, HD), lambda step: (step, 0)),
        ]
        + [pl.BlockSpec(memory_space=pl.ANY)] * len(after),
        out_specs=pl.BlockSpec((tall, width), lambda step: (step, 0)),
        compiler_params=pltpu.CompilerParams(vmem_limit_bytes=VMEM_BYTES),
        cost_estimate=NO_COST,
    )(grad_t, cosine, sine, *after)


def hold_kernel(*refs):
    pass


def hold(array, after):
    hbm = pl.BlockSpec(memory_space=pl.ANY)
    return pl.pallas_call(
        hold_kernel,
        out_shape=jax.ShapeDtypeStruct(array.shape, array.dtype),
        in_specs=[hbm] * (1 + len(after)),
        out_specs=hbm,
        input_output_aliases={0: 0},
        cost_estimate=NO_COST,
    )(array, *after)


def product_kernel(my_ref, left_ref, right_ref, *refs):
    keep_ref, send_ref = refs[-3:-1]
    half = keep_ref.shape[1]
    total = jnp.dot(left_ref[...], right_ref[...], preferred_element_type=jnp.float32)
    total = total.astype(keep_ref.dtype).T
    odd = my_ref[1]

    @pl.when(odd == 0)
    def even_core():
        keep_ref[0] = total[:half]
        send_ref[0] = total[half:]

    @pl.when(odd == 1)
    def odd_core():
        keep_ref[0] = total[half:]
        send_ref[0] = total[:half]


def product(my_rank, left, right, thru, after):
    count = lax.axis_size("dp") // 2
    width, depth = left.shape
    cols = right.shape[1] // count
    mine, odd = my_rank // 2, my_rank & 1
    if cols % 128:
        total = jnp.dot(left, right, preferred_element_type=jnp.float32).astype(jnp.bfloat16)
        pieces = total.T.reshape(count, 2, cols // 2, width)
        pieces = jnp.take(pieces, jnp.arange(count, dtype=jnp.int32) ^ mine, axis=0)
        low, high = pieces[:, 0], pieces[:, 1]
        return jnp.where(odd > 0, high, low), jnp.where(odd > 0, low, high), thru
    hbm = pl.BlockSpec(memory_space=pl.ANY)
    stacked = pl.BlockSpec((1, cols // 2, width), lambda step, my_ref: (step, 0, 0))
    stack = jax.ShapeDtypeStruct((count, cols // 2, width), jnp.bfloat16)
    inputs = [jnp.stack([mine, odd]), left, right, *after, thru]
    return pl.pallas_call(
        product_kernel,
        grid_spec=pltpu.PrefetchScalarGridSpec(
            num_scalar_prefetch=1,
            grid=(count,),
            in_specs=[
                pl.BlockSpec(left.shape, lambda step, my_ref: (0, 0)),
                pl.BlockSpec((depth, cols), lambda step, my_ref: (0, step ^ my_ref[0])),
            ]
            + [hbm] * (len(after) + 1),
            out_specs=[stacked, stacked, hbm],
        ),
        out_shape=[stack, stack, jax.ShapeDtypeStruct(thru.shape, thru.dtype)],
        input_output_aliases={len(inputs) - 1: 2},
        compiler_params=pltpu.CompilerParams(vmem_limit_bytes=VMEM_BYTES),
        cost_estimate=NO_COST,
    )(*inputs)


def weight_final_kernel(count, factor, *refs):
    total = refs[0][0].astype(jnp.float32)
    for ref in refs[1 : 1 + count]:
        total = total + ref[0].astype(jnp.float32)
    refs[-1][...] = total * factor


def weight_final(keep, received, factor, after):
    vmem = pl.BlockSpec(memory_space=pltpu.VMEM)
    hbm = pl.BlockSpec(memory_space=pl.ANY)
    return pl.pallas_call(
        partial(weight_final_kernel, len(received), factor),
        out_shape=jax.ShapeDtypeStruct(keep.shape[1:], jnp.float32),
        in_specs=[vmem] * (1 + len(received)) + [hbm] * len(after),
        out_specs=vmem,
        compiler_params=pltpu.CompilerParams(vmem_limit_bytes=VMEM_BYTES),
        cost_estimate=NO_COST,
    )(keep, *received, *after)


def local(query, key, value, grad_out, out_weight, plan, segments):
    rank_count = lax.axis_size("dp")
    my_rank = lax.axis_index("dp")
    my_lane = lax.axis_index("tensor")
    row_count = query.shape[0]
    block_count = row_count // ROWBLK
    local_heads = query.shape[1] // HD
    group = HEADS // KV
    bits = [1 << at for at in range(rank_count.bit_length() - 1)]
    kv_head = my_lane * local_heads // group
    own_value = lax.dynamic_slice_in_dim(value, kv_head * HD, HD, 1)
    own_places = positions_of(segments).reshape(1, block_count, ROWBLK)
    places_all = lax.all_to_all(
        jnp.broadcast_to(own_places, (rank_count, block_count, ROWBLK)),
        "dp",
        split_axis=0,
        concat_axis=0,
        tiled=True,
    ).reshape(-1, ROWBLK)
    values = spread(own_value)

    mine = my_rank * block_count + jnp.arange(block_count, dtype=jnp.int32)
    hit = plan[None, :] == mine[:, None]
    dest = jnp.sum(
        jnp.where(hit, jnp.arange(plan.shape[0], dtype=jnp.int32)[None, :], 0), axis=1
    )
    run = dest // RUN_BLOCKS
    slot = dest % RUN_BLOCKS
    cosine, sine, rot_key, places = rope(kv_head, dest, places_all, key)
    need = slot - (slot * ROWBLK - places[:, 0]) // ROWBLK + 1
    keys = spread(rot_key)
    up, up_t, turned = prepare(grad_out, out_weight, query, cosine, sine, [rot_key])

    distance = (plan // block_count) ^ my_rank
    within = plan % block_count
    half_place = (distance & 1) * (rank_count // 2) + distance // 2
    tables = (
        half_place * block_count + within,
        distance * block_count + within,
        run,
        slot,
        need,
    )
    grad_query_t, attn_t, gkey_keep, gkey_send, gvalue_keep, gvalue_send = attend(
        tables, turned, up, up_t, places, keys, values
    )
    value_keep, value_sends = chip_sum(gvalue_keep, swap(gvalue_send, 1))
    value_received = exchange(value_sends)
    key_keep, key_sends = chip_sum(gkey_keep, swap(gkey_send, 1))
    key_received = exchange(key_sends)
    weight_keep, weight_send, value_keep = product(
        my_rank, attn_t, grad_out, value_keep, [value_sends[0], key_sends[0]]
    )
    far = lax.axis_size("tensor") // 2
    value_partial, value_near, weight_send = final_sum(
        value_keep, value_received, (), (), thru=[weight_send], copies=2
    )
    value_far = lane_swap(value_partial, far)
    weight_keep, weight_sends = chip_sum(weight_keep, swap(weight_send, 1))
    weight_received = exchange(weight_sends)
    value_near = hold(value_near, weight_sends[:1])
    value_far = hold(value_far, weight_sends[:1])
    value_pieces = lane_pieces({0: value_near, far: value_far}, far // 2)
    value_all = assemble(my_lane, value_pieces)
    (key_partial,) = final_sum(
        key_keep, key_received, (cosine, sine), [value_far, value_pieces[1]]
    )
    grad_query = turn_back(grad_query_t, cosine, sine, [key_partial])
    key_far = hold(lane_swap(key_partial, far), [*weight_received, grad_query])
    key_all = assemble(my_lane, lane_pieces({0: key_partial, far: key_far}, far // 2))
    weight_grad = weight_final(
        weight_keep, weight_received, 1.0 / rank_count, [key_far, value_all]
    )
    lanes_per_key = group // local_heads

    def combine(gathered):
        if lanes_per_key == 1:
            return gathered
        merged = (
            gathered.astype(jnp.float32).reshape(row_count, KV, lanes_per_key, HD).sum(axis=2)
        )
        return merged.astype(jnp.bfloat16).reshape(row_count, KV * HD)

    return (grad_query, combine(key_all), combine(value_all), weight_grad)


def solution(mesh):
    in_specs = (
        P("dp", "tensor"),
        P("dp", None),
        P("dp", None),
        P("dp", None),
        P(None, "tensor"),
        P(),
        P("dp"),
    )
    out_specs = (P("dp", "tensor"), P("dp", None), P("dp", None), P("dp", "tensor"))
    return jax.shard_map(local, mesh=mesh, in_specs=in_specs, out_specs=out_specs, check_vma=False)
```

```python
from functools import partial
import math

import jax
import jax.numpy as jnp
from jax import lax
from jax.experimental import pallas as pl
from jax.experimental.pallas import tpu as pltpu
from jax.sharding import PartitionSpec as P

KV = 4
HD = 128
HEADS = 16
ROWBLK = 128
RUN_BLOCKS = 8
VMEM_BYTES = 58 * 1024 * 1024
NO_COST = pl.CostEstimate(flops=0, bytes_accessed=0, transcendentals=0)


rope_base = 1000000.0
yarn_factor = 4.0
yarn_context = 32768.0
beta_fast = 32.0
beta_slow = 1.0
masked_score = -1e30


def yarn_frequencies(head_size):
    half_size = head_size // 2

    def correction(rotations):
        return (
            head_size
            * math.log(yarn_context / (rotations * 2.0 * math.pi))
            / (2.0 * math.log(rope_base))
        )

    lower_bound = max(math.floor(correction(beta_fast)), 0)
    upper_bound = min(math.ceil(correction(beta_slow)), head_size - 1)
    ramp_span = max(upper_bound - lower_bound, 0.001)
    row_index = jnp.arange(half_size).astype(jnp.float32)
    extrap_freq = rope_base ** (-2.0 * row_index / head_size)
    interp_freq = extrap_freq / yarn_factor
    ramp_weight = jnp.clip((row_index - lower_bound) / ramp_span, 0.0, 1.0)
    return interp_freq * ramp_weight + extrap_freq * (1.0 - ramp_weight)


def positions_of(segments):
    row_count = segments.shape[-1]
    row_index = jnp.arange(row_count, dtype=jnp.int32)
    is_start = jnp.concatenate(
        [
            jnp.ones(segments.shape[:-1] + (1,), dtype=jnp.bool_),
            segments[..., 1:] != segments[..., :-1],
        ],
        axis=-1,
    )
    seg_start = lax.cummax(jnp.where(is_start, row_index, 0), axis=segments.ndim - 1)
    return row_index - seg_start


def rope_kernel(at_ref, dest_ref, places_ref, freq_ref, key_ref, *refs):
    cos_ref, sin_ref, turned_ref, own_ref = refs
    factor = 0.1 * math.log(yarn_factor) + 1.0
    half = lax.broadcasted_iota(jnp.int32, (ROWBLK, HD), 1) < HD // 2
    for block in range(own_ref.shape[0]):
        rows = pl.ds(block * ROWBLK, ROWBLK)
        place = places_ref[pl.ds(dest_ref[block], 1), :]
        own_ref[pl.ds(block, 1), :] = place
        spread_out = jnp.broadcast_to(place.astype(jnp.float32), (ROWBLK, HD)).T
        angles = spread_out * freq_ref[...]
        cosine = jnp.cos(angles) * factor
        sine = jnp.sin(angles) * factor
        sine = jnp.where(half, -sine, sine)
        cos_ref[rows, :] = cosine
        sin_ref[rows, :] = sine
        raw = key_ref[rows, :].astype(jnp.float32)
        turned = raw * cosine + pltpu.roll(raw, HD // 2, 1) * sine
        turned_ref[rows, :] = turned.astype(turned_ref.dtype)


def rope(kv_head, dest, places_all, key):
    rows = key.shape[0]
    blocks = rows // ROWBLK
    freq = yarn_frequencies(HD)
    freq = jnp.concatenate([freq, freq]).reshape(1, HD)
    whole = lambda shape: pl.BlockSpec(shape, lambda step, *refs: (0,) * len(shape))
    table = jax.ShapeDtypeStruct((rows, HD), jnp.float32)
    return pl.pallas_call(
        rope_kernel,
        grid_spec=pltpu.PrefetchScalarGridSpec(
            num_scalar_prefetch=2,
            grid=(1,),
            in_specs=[
                whole(places_all.shape),
                whole((1, HD)),
                pl.BlockSpec((rows, HD), lambda step, at_ref, dest_ref: (0, at_ref[0])),
            ],
            out_specs=[whole((rows, HD))] * 3 + [whole((blocks, ROWBLK))],
        ),
        out_shape=[
            table,
            table,
            jax.ShapeDtypeStruct((rows, HD), key.dtype),
            jax.ShapeDtypeStruct((blocks, ROWBLK), jnp.int32),
        ],
        cost_estimate=NO_COST,
    )(kv_head.reshape(1), dest, places_all, freq, key)


NT = (((1,), (1,)), ((), ()))
TN = (((0,), (0,)), ((), ()))


def attend_kernel(
    heads,
    ranks,
    target_ref,
    source_ref,
    run_ref,
    slot_ref,
    need_ref,
    query_ref,
    up_ref,
    up_t_ref,
    place_ref,
    *refs,
):
    key_parts, refs = refs[:ranks], refs[ranks:]
    value_parts, refs = refs[:ranks], refs[ranks:]
    gquery_ref, out_ref, *halves = refs[:6]
    key_ref, value_ref, gkey_ref, gvalue_ref, key_win, value_win = refs[6:12]
    score_ref, prob_ref, gscore_ref, load_sems, sems = refs[12:]
    rows_each = query_ref.shape[0]
    half_blocks = ranks * RUN_BLOCKS // 2
    scale = 1.0 / math.sqrt(HD)
    to_exp2 = scale * math.log2(math.e)

    loads = []
    for item, (parts, whole) in enumerate(((key_parts, key_ref), (value_parts, value_ref))):
        for rank in range(ranks):
            copy = pltpu.make_async_copy(
                parts[rank], whole.at[pl.ds(rank * rows_each, rows_each)], load_sems.at[item, rank]
            )
            copy.start()
            loads.append(copy)
    for copy in loads:
        copy.wait()

    def stores(block, act):
        side = block % 2
        for step in range(RUN_BLOCKS):
            target = target_ref[run_ref[block] * RUN_BLOCKS + step]
            for place in range(2):

                @pl.when(target // half_blocks == place)
                def one_half():
                    start = pl.multiple_of(target % half_blocks * ROWBLK, ROWBLK)
                    for item, source in enumerate((gkey_ref, gvalue_ref)):
                        act(
                            pltpu.make_async_copy(
                                source.at[side, pl.ds(step * ROWBLK, ROWBLK)],
                                halves[2 * item + place].at[pl.ds(start, ROWBLK)],
                                sems.at[side, item, step],
                            )
                        )

    def window(count, block):
        slot = slot_ref[block]
        run = run_ref[block]
        first = jnp.maximum(slot + 1 - count, 0)
        rows = count * ROWBLK
        for step in range(count):
            source = source_ref[run * RUN_BLOCKS + first + step]
            start = pl.multiple_of(source * ROWBLK, ROWBLK)
            key_win[pl.ds(step * ROWBLK, ROWBLK), :] = key_ref[pl.ds(start, ROWBLK), :]
            value_win[pl.ds(step * ROWBLK, ROWBLK), :] = value_ref[pl.ds(start, ROWBLK), :]
        wide = min(2, heads)
        base = pl.multiple_of(block * ROWBLK, ROWBLK)
        at_rows = pl.ds(base, ROWBLK)
        place = place_ref[pl.ds(block, 1), :]
        lane = lax.broadcasted_iota(jnp.int32, (1, ROWBLK), 1)
        last = (slot - first) * ROWBLK + lane
        last_all = jnp.concatenate([last] * wide, axis=1)
        start_all = jnp.concatenate([last - place] * wide, axis=1)
        key_index = lax.broadcasted_iota(jnp.int32, (ROWBLK, wide * ROWBLK), 0)
        keys = key_win[pl.ds(0, rows), :]
        values = value_win[pl.ds(0, rows), :]
        columns = [pl.ds(head * HD, HD) for head in range(heads)]
        query = jnp.concatenate([query_ref[at_rows, at] for at in columns], axis=0)
        up = jnp.concatenate([up_ref[at_rows, at] for at in columns], axis=0)
        folded = lambda tile: tile.reshape(ROWBLK // 8, 8, tile.shape[1])
        tiles = [pl.ds(step * ROWBLK, ROWBLK) for step in range(count)]
        groups = heads // wide
        spans = [slice(at * wide * ROWBLK, (at + 1) * wide * ROWBLK) for at in range(groups)]

        score = lax.dot_general(keys, query, NT, preferred_element_type=jnp.float32)
        gprob = lax.dot_general(values, up, NT, preferred_element_type=jnp.float32)
        peaks = [None] * groups
        for step, tile in enumerate(tiles):
            seen = key_index >= start_all - step * ROWBLK
            if step == count - 1:
                seen = seen & (key_index <= last_all - step * ROWBLK)
            for at, span in enumerate(spans):
                part = jnp.where(
                    seen, score[step * ROWBLK : (step + 1) * ROWBLK, span], masked_score
                )
                score_ref[tile, span] = part
                most = jnp.max(folded(part), axis=0)
                peaks[at] = most if peaks[at] is None else jnp.maximum(peaks[at], most)
        peaks = [jnp.max(item, axis=0, keepdims=True) for item in peaks]
        totals = [None] * groups
        for tile in tiles:
            for at, span in enumerate(spans):
                part = jnp.exp2((score_ref[tile, span] - peaks[at]) * to_exp2)
                score_ref[tile, span] = part
                some = jnp.sum(folded(part), axis=0)
                totals[at] = some if totals[at] is None else totals[at] + some
        shares = [1.0 / jnp.sum(item, axis=0, keepdims=True) for item in totals]
        for tile in tiles:
            for at, span in enumerate(spans):
                prob_ref[tile, span] = (score_ref[tile, span] * shares[at]).astype(jnp.bfloat16)
        prob_b = prob_ref[pl.ds(0, rows), :]
        out_t = lax.dot_general(values, prob_b, TN, preferred_element_type=jnp.float32)
        out_b = out_t.astype(jnp.bfloat16)
        deltas = []
        for at in range(groups):
            up_t = jnp.concatenate(
                [up_t_ref[item, at_rows] for item in columns[at * wide : (at + 1) * wide]], axis=1
            ).astype(jnp.float32)
            deltas.append(
                jnp.sum(up_t * out_b[:, spans[at]].astype(jnp.float32), axis=0, keepdims=True)
            )
        for step, tile in enumerate(tiles):
            for at, span in enumerate(spans):
                prob = score_ref[tile, span] * shares[at]
                part = gprob[step * ROWBLK : (step + 1) * ROWBLK, span] - deltas[at]
                gscore_ref[tile, span] = (prob * part).astype(jnp.bfloat16)
        gscore = gscore_ref[pl.ds(0, rows), :]
        gquery_t = lax.dot_general(keys, gscore, TN, preferred_element_type=jnp.float32)
        gkey = jnp.dot(gscore, query, preferred_element_type=jnp.float32)
        gvalue = jnp.dot(prob_b, up, preferred_element_type=jnp.float32)
        for head in range(heads):
            part = slice(head * ROWBLK, (head + 1) * ROWBLK)
            out_ref[columns[head], at_rows] = out_b[:, part]
            gquery_ref[columns[head], at_rows] = gquery_t[:, part]
        gkey = (gkey * scale).astype(jnp.bfloat16)
        gvalue = gvalue.astype(jnp.bfloat16)
        place_at = pl.ds(pl.multiple_of(first * ROWBLK, ROWBLK), rows)
        gkey_ref[block % 2, place_at, :] = gkey
        gvalue_ref[block % 2, place_at, :] = gvalue

    def body(block, carry):
        pl.when(block >= 2)(lambda: stores(block - 2, lambda copy: copy.wait()))
        blank = jnp.zeros(gkey_ref.shape[1:], jnp.bfloat16)
        gkey_ref[block % 2] = blank
        gvalue_ref[block % 2] = blank
        need = need_ref[block]
        floor = 0
        for size in range(1, RUN_BLOCKS + 1):
            pl.when((need > floor) & (need <= size))(partial(window, size, block))
            floor = size
        stores(block, lambda copy: copy.start())
        return carry

    blocks = rows_each // ROWBLK
    lax.fori_loop(0, blocks, body, 0)
    for block in range(max(blocks - 2, 0), blocks):
        stores(block, lambda copy: copy.wait())


def attend(tables, query, up, up_t, places, keys, values):
    rows, width = query.shape
    heads = width // HD
    ranks = len(keys)
    every = rows * ranks
    smem = pl.BlockSpec(memory_space=pltpu.SMEM)
    vmem = pl.BlockSpec(memory_space=pltpu.VMEM)
    hbm = pl.BlockSpec(memory_space=pl.ANY)
    half = jax.ShapeDtypeStruct((every // 2, HD), jnp.bfloat16)
    return pl.pallas_call(
        partial(attend_kernel, heads, ranks),
        out_shape=(
            jax.ShapeDtypeStruct((width, rows), jnp.float32),
            jax.ShapeDtypeStruct((width, rows), jnp.bfloat16),
            half,
            half,
            half,
            half,
        ),
        in_specs=[smem] * 5 + [vmem] * 4 + [hbm] * (2 * ranks),
        out_specs=(vmem, vmem, hbm, hbm, hbm, hbm),
        scratch_shapes=[pltpu.VMEM((every, HD), jnp.bfloat16)] * 2
        + [pltpu.VMEM((2, RUN_BLOCKS * ROWBLK, HD), jnp.bfloat16)] * 2
        + [pltpu.VMEM((RUN_BLOCKS * ROWBLK, HD), jnp.bfloat16)] * 2
        + [pltpu.VMEM((RUN_BLOCKS * ROWBLK, heads * ROWBLK), jnp.float32)]
        + [pltpu.VMEM((RUN_BLOCKS * ROWBLK, heads * ROWBLK), jnp.bfloat16)] * 2
        + [pltpu.SemaphoreType.DMA((2, ranks)), pltpu.SemaphoreType.DMA((2, 2, RUN_BLOCKS))],
        compiler_params=pltpu.CompilerParams(vmem_limit_bytes=VMEM_BYTES),
        cost_estimate=NO_COST,
    )(*tables, query, up, up_t, places, *keys, *values)


def assemble_kernel(lanes, my_ref, *refs):
    out_ref, sems = refs[lanes:]
    copies = []
    for index in range(lanes):
        column = pl.multiple_of((my_ref[0] ^ index) * HD, HD)
        copy = pltpu.make_async_copy(
            refs[index], out_ref.at[:, pl.ds(column, HD)], sems.at[index]
        )
        copy.start()
        copies.append(copy)
    for copy in copies:
        copy.wait()


def assemble(my_lane, pieces):
    rows = pieces[0].shape[0]
    lanes = len(pieces)
    vmem = pl.BlockSpec(memory_space=pltpu.VMEM)
    return pl.pallas_call(
        partial(assemble_kernel, lanes),
        out_shape=jax.ShapeDtypeStruct((rows, lanes * HD), pieces[0].dtype),
        in_specs=[pl.BlockSpec(memory_space=pltpu.SMEM)] + [vmem] * lanes,
        out_specs=pl.BlockSpec(memory_space=pl.ANY),
        scratch_shapes=[pltpu.SemaphoreType.DMA((lanes,))],
        compiler_params=pltpu.CompilerParams(vmem_limit_bytes=VMEM_BYTES),
        cost_estimate=NO_COST,
    )(my_lane.reshape(1), *pieces)


def lane_swap(array, bit):
    lanes = lax.axis_size("tensor")
    return lax.ppermute(array, "tensor", [(lane, lane ^ bit) for lane in range(lanes)])


def lane_pieces(pieces, bit):
    lanes = lax.axis_size("tensor")
    while bit:
        pieces = {**pieces, **{at | bit: lane_swap(item, bit) for at, item in pieces.items()}}
        bit //= 2
    return [pieces[at] for at in range(lanes)]


def swap(array, bit):
    ranks = lax.axis_size("dp")
    return lax.ppermute(array, "dp", [(rank, rank ^ bit) for rank in range(ranks)])


def spread(array):
    found = [array, swap(array, 1)]
    others = [swap(array, step) for step in range(2, lax.axis_size("dp"), 2)]
    for other in others:
        found += [other, swap(other, 1)]
    return found


def added(left, right):
    return left.astype(jnp.float32) + right.astype(jnp.float32)


def chip_sum(keep, received):
    count = lax.axis_size("dp") // 2
    rows = keep.shape[0] // count
    total = [
        added(keep[at * rows : (at + 1) * rows], received[at * rows : (at + 1) * rows])
        for at in range(count)
    ]
    return total[0], [item.astype(keep.dtype) for item in total[1:]]


def exchange(sends):
    return [swap(item, 2 * at + 2) for at, item in enumerate(sends)]


def final_kernel(count, rotary, outs, *refs):
    total = refs[0][...].astype(jnp.float32)
    for ref in refs[1 : 1 + count]:
        total = total + ref[...].astype(jnp.float32)
    if rotary:
        total = total * refs[1 + count][...] - pltpu.roll(total, HD // 2, 1) * refs[2 + count][...]
    for at in outs:
        refs[at][...] = total.astype(refs[at].dtype)


def final_sum(keep, received, tables, after, thru=(), copies=1):
    vmem = pl.BlockSpec(memory_space=pltpu.VMEM)
    hbm = pl.BlockSpec(memory_space=pl.ANY)
    parts = [keep, *received, *tables]
    inputs = len(parts) + len(after) + len(thru)
    results = pl.pallas_call(
        partial(
            final_kernel, len(received), len(tables) > 0, range(inputs, inputs + copies)
        ),
        out_shape=[jax.ShapeDtypeStruct(keep.shape, jnp.bfloat16)] * copies
        + [jax.ShapeDtypeStruct(item.shape, item.dtype) for item in thru],
        in_specs=[vmem] * len(parts) + [hbm] * (len(after) + len(thru)),
        out_specs=[vmem] * copies + [hbm] * len(thru),
        input_output_aliases={inputs - len(thru) + at: copies + at for at in range(len(thru))},
        compiler_params=pltpu.CompilerParams(vmem_limit_bytes=VMEM_BYTES),
        cost_estimate=NO_COST,
    )(*parts, *after, *thru)
    return results


def prepare_kernel(
    rows_ref, weight_ref, query_ref, cos_ref, sin_ref, *refs
):
    up_ref, up_t_ref, turned_ref = refs[-3:]
    total = jnp.dot(rows_ref[...], weight_ref[...], preferred_element_type=jnp.float32)
    up_ref[...] = total.astype(up_ref.dtype)
    up_t_ref[...] = total.T.astype(up_t_ref.dtype)
    for at in range(0, query_ref.shape[1], HD):
        raw = query_ref[:, at : at + HD].astype(jnp.float32)
        turned = raw * cos_ref[...] + pltpu.roll(raw, HD // 2, 1) * sin_ref[...]
        turned_ref[:, at : at + HD] = turned.astype(turned_ref.dtype)


def prepare(rows, weight, query, cosine, sine, after):
    height, depth = rows.shape
    width = weight.shape[1]
    steps = 4
    tall = height // steps
    across = lambda columns: pl.BlockSpec((tall, columns), lambda step: (step, 0))
    return pl.pallas_call(
        prepare_kernel,
        grid=(steps,),
        out_shape=[
            jax.ShapeDtypeStruct((height, width), jnp.bfloat16),
            jax.ShapeDtypeStruct((width, height), jnp.bfloat16),
            jax.ShapeDtypeStruct(query.shape, jnp.bfloat16),
        ],
        in_specs=[
            across(depth),
            pl.BlockSpec(weight.shape, lambda step: (0, 0)),
            across(width),
            across(HD),
            across(HD),
        ]
        + [pl.BlockSpec(memory_space=pl.ANY)] * len(after),
        out_specs=[
            across(width),
            pl.BlockSpec((width, tall), lambda step: (0, step)),
            across(width),
        ],
        compiler_params=pltpu.CompilerParams(vmem_limit_bytes=VMEM_BYTES),
        cost_estimate=pl.CostEstimate(
            flops=2 * height * weight.size, bytes_accessed=2 * rows.size, transcendentals=0
        ),
    )(rows, weight, query, cosine, sine, *after)


def turn_back_kernel(grad_ref, cos_ref, sin_ref, *refs):
    out_ref = refs[-1]
    scale = 1.0 / math.sqrt(HD)
    for at in range(0, grad_ref.shape[0], HD):
        grad = grad_ref[at : at + HD, :].T * scale
        back = grad * cos_ref[...] - pltpu.roll(grad, HD // 2, 1) * sin_ref[...]
        out_ref[:, at : at + HD] = back.astype(out_ref.dtype)


def turn_back(grad_t, cosine, sine, after):
    width, height = grad_t.shape
    steps = 4
    tall = height // steps
    return pl.pallas_call(
        turn_back_kernel,
        grid=(steps,),
        out_shape=jax.ShapeDtypeStruct((height, width), jnp.bfloat16),
        in_specs=[
            pl.BlockSpec((width, tall), lambda step: (0, step)),
            pl.BlockSpec((tall, HD), lambda step: (step, 0)),
            pl.BlockSpec((tall, HD), lambda step: (step, 0)),
        ]
        + [pl.BlockSpec(memory_space=pl.ANY)] * len(after),
        out_specs=pl.BlockSpec((tall, width), lambda step: (step, 0)),
        compiler_params=pltpu.CompilerParams(vmem_limit_bytes=VMEM_BYTES),
        cost_estimate=NO_COST,
    )(grad_t, cosine, sine, *after)


def hold_kernel(*refs):
    pass


def hold(array, after):
    hbm = pl.BlockSpec(memory_space=pl.ANY)
    return pl.pallas_call(
        hold_kernel,
        out_shape=jax.ShapeDtypeStruct(array.shape, array.dtype),
        in_specs=[hbm] * (1 + len(after)),
        out_specs=hbm,
        input_output_aliases={0: 0},
        cost_estimate=NO_COST,
    )(array, *after)


def product_kernel(my_ref, left_ref, right_ref, *refs):
    keep_ref, send_ref = refs[-3:-1]
    half = keep_ref.shape[1]
    total = jnp.dot(left_ref[...], right_ref[...], preferred_element_type=jnp.float32)
    total = total.astype(keep_ref.dtype).T
    odd = my_ref[1]

    @pl.when(odd == 0)
    def even_core():
        keep_ref[0] = total[:half]
        send_ref[0] = total[half:]

    @pl.when(odd == 1)
    def odd_core():
        keep_ref[0] = total[half:]
        send_ref[0] = total[:half]


def product(my_rank, left, right, thru, after):
    count = lax.axis_size("dp") // 2
    width, depth = left.shape
    cols = right.shape[1] // count
    mine, odd = my_rank // 2, my_rank & 1
    if cols % 128:
        total = jnp.dot(left, right, preferred_element_type=jnp.float32).astype(jnp.bfloat16)
        pieces = total.T.reshape(count, 2, cols // 2, width)
        pieces = jnp.take(pieces, jnp.arange(count, dtype=jnp.int32) ^ mine, axis=0)
        low, high = pieces[:, 0], pieces[:, 1]
        return jnp.where(odd > 0, high, low), jnp.where(odd > 0, low, high), thru
    hbm = pl.BlockSpec(memory_space=pl.ANY)
    stacked = pl.BlockSpec((1, cols // 2, width), lambda step, my_ref: (step, 0, 0))
    stack = jax.ShapeDtypeStruct((count, cols // 2, width), jnp.bfloat16)
    inputs = [jnp.stack([mine, odd]), left, right, *after, thru]
    return pl.pallas_call(
        product_kernel,
        grid_spec=pltpu.PrefetchScalarGridSpec(
            num_scalar_prefetch=1,
            grid=(count,),
            in_specs=[
                pl.BlockSpec(left.shape, lambda step, my_ref: (0, 0)),
                pl.BlockSpec((depth, cols), lambda step, my_ref: (0, step ^ my_ref[0])),
            ]
            + [hbm] * (len(after) + 1),
            out_specs=[stacked, stacked, hbm],
        ),
        out_shape=[stack, stack, jax.ShapeDtypeStruct(thru.shape, thru.dtype)],
        input_output_aliases={len(inputs) - 1: 2},
        compiler_params=pltpu.CompilerParams(vmem_limit_bytes=VMEM_BYTES),
        cost_estimate=NO_COST,
    )(*inputs)


def weight_final_kernel(count, factor, *refs):
    total = refs[0][0].astype(jnp.float32)
    for ref in refs[1 : 1 + count]:
        total = total + ref[0].astype(jnp.float32)
    refs[-1][...] = total * factor


def weight_final(keep, received, factor, after):
    vmem = pl.BlockSpec(memory_space=pltpu.VMEM)
    hbm = pl.BlockSpec(memory_space=pl.ANY)
    return pl.pallas_call(
        partial(weight_final_kernel, len(received), factor),
        out_shape=jax.ShapeDtypeStruct(keep.shape[1:], jnp.float32),
        in_specs=[vmem] * (1 + len(received)) + [hbm] * len(after),
        out_specs=vmem,
        compiler_params=pltpu.CompilerParams(vmem_limit_bytes=VMEM_BYTES),
        cost_estimate=NO_COST,
    )(keep, *received, *after)


def local(query, key, value, grad_out, out_weight, plan, segments):
    rank_count = lax.axis_size("dp")
    my_rank = lax.axis_index("dp")
    my_lane = lax.axis_index("tensor")
    row_count = query.shape[0]
    block_count = row_count // ROWBLK
    local_heads = query.shape[1] // HD
    group = HEADS // KV
    bits = [1 << at for at in range(rank_count.bit_length() - 1)]
    kv_head = my_lane * local_heads // group
    own_value = lax.dynamic_slice_in_dim(value, kv_head * HD, HD, 1)
    own_places = positions_of(segments).reshape(1, block_count, ROWBLK)
    places_all = lax.all_to_all(
        jnp.broadcast_to(own_places, (rank_count, block_count, ROWBLK)),
        "dp",
        split_axis=0,
        concat_axis=0,
        tiled=True,
    ).reshape(-1, ROWBLK)
    values = spread(own_value)

    mine = my_rank * block_count + jnp.arange(block_count, dtype=jnp.int32)
    hit = plan[None, :] == mine[:, None]
    dest = jnp.sum(
        jnp.where(hit, jnp.arange(plan.shape[0], dtype=jnp.int32)[None, :], 0), axis=1
    )
    run = dest // RUN_BLOCKS
    slot = dest % RUN_BLOCKS
    cosine, sine, rot_key, places = rope(kv_head, dest, places_all, key)
    need = slot - (slot * ROWBLK - places[:, 0]) // ROWBLK + 1
    keys = spread(rot_key)
    up, up_t, turned = prepare(grad_out, out_weight, query, cosine, sine, [rot_key])

    distance = (plan // block_count) ^ my_rank
    within = plan % block_count
    half_place = (distance & 1) * (rank_count // 2) + distance // 2
    tables = (
        half_place * block_count + within,
        distance * block_count + within,
        run,
        slot,
        need,
    )
    grad_query_t, attn_t, gkey_keep, gkey_send, gvalue_keep, gvalue_send = attend(
        tables, turned, up, up_t, places, keys, values
    )
    value_keep, value_sends = chip_sum(gvalue_keep, swap(gvalue_send, 1))
    value_received = exchange(value_sends)
    key_keep, key_sends = chip_sum(gkey_keep, swap(gkey_send, 1))
    key_received = exchange(key_sends)
    weight_keep, weight_send, value_keep = product(
        my_rank, attn_t, grad_out, value_keep, [value_sends[0], key_sends[0]]
    )
    far = lax.axis_size("tensor") // 2
    value_partial, value_near, weight_send = final_sum(
        value_keep, value_received, (), (), thru=[weight_send], copies=2
    )
    value_far = lane_swap(value_partial, far)
    weight_keep, weight_sends = chip_sum(weight_keep, swap(weight_send, 1))
    weight_received = exchange(weight_sends)
    value_near = hold(value_near, weight_sends[:1])
    value_far = hold(value_far, weight_sends[:1])
    value_pieces = lane_pieces({0: value_near, far: value_far}, far // 2)
    value_all = assemble(my_lane, value_pieces)
    (key_partial,) = final_sum(
        key_keep, key_received, (cosine, sine), [value_far, value_pieces[1]]
    )
    grad_query = turn_back(grad_query_t, cosine, sine, [key_partial])
    key_far = hold(lane_swap(key_partial, far), [*weight_received, grad_query])
    key_all = assemble(my_lane, lane_pieces({0: key_partial, far: key_far}, far // 2))
    weight_grad = weight_final(
        weight_keep, weight_received, 1.0 / rank_count, [key_far, value_all]
    )
    lanes_per_key = group // local_heads

    def combine(gathered):
        if lanes_per_key == 1:
            return gathered
        merged = (
            gathered.astype(jnp.float32).reshape(row_count, KV, lanes_per_key, HD).sum(axis=2)
        )
        return merged.astype(jnp.bfloat16).reshape(row_count, KV * HD)

    return (grad_query, combine(key_all), combine(value_all), weight_grad)


def solution(mesh):
    in_specs = (
        P("dp", "tensor"),
        P("dp", None),
        P("dp", None),
        P("dp", None),
        P(None, "tensor"),
        P(),
        P("dp"),
    )
    out_specs = (P("dp", "tensor"), P("dp", None), P("dp", None), P("dp", "tensor"))
    return jax.shard_map(local, mesh=mesh, in_specs=in_specs, out_specs=out_specs, check_vma=False)
```

```python
from functools import partial
import math

import jax
import jax.numpy as jnp
from jax import lax
from jax.experimental import pallas as pl
from jax.experimental.pallas import tpu as pltpu
from jax.sharding import PartitionSpec as P

KV = 4
HD = 128
HEADS = 16
ROWBLK = 128
RUN_BLOCKS = 8
VMEM_BYTES = 58 * 1024 * 1024
NO_COST = pl.CostEstimate(flops=0, bytes_accessed=0, transcendentals=0)


rope_base = 1000000.0
yarn_factor = 4.0
yarn_context = 32768.0
beta_fast = 32.0
beta_slow = 1.0
masked_score = -1e30


def yarn_frequencies(head_size):
    half_size = head_size // 2

    def correction(rotations):
        return (
            head_size
            * math.log(yarn_context / (rotations * 2.0 * math.pi))
            / (2.0 * math.log(rope_base))
        )

    lower_bound = max(math.floor(correction(beta_fast)), 0)
    upper_bound = min(math.ceil(correction(beta_slow)), head_size - 1)
    ramp_span = max(upper_bound - lower_bound, 0.001)
    row_index = jnp.arange(half_size).astype(jnp.float32)
    extrap_freq = rope_base ** (-2.0 * row_index / head_size)
    interp_freq = extrap_freq / yarn_factor
    ramp_weight = jnp.clip((row_index - lower_bound) / ramp_span, 0.0, 1.0)
    return interp_freq * ramp_weight + extrap_freq * (1.0 - ramp_weight)


def positions_of(segments):
    row_count = segments.shape[-1]
    row_index = jnp.arange(row_count, dtype=jnp.int32)
    is_start = jnp.concatenate(
        [
            jnp.ones(segments.shape[:-1] + (1,), dtype=jnp.bool_),
            segments[..., 1:] != segments[..., :-1],
        ],
        axis=-1,
    )
    seg_start = lax.cummax(jnp.where(is_start, row_index, 0), axis=segments.ndim - 1)
    return row_index - seg_start


def rope_kernel(at_ref, dest_ref, places_ref, freq_ref, key_ref, *refs):
    cos_ref, sin_ref, turned_ref, own_ref = refs
    factor = 0.1 * math.log(yarn_factor) + 1.0
    half = lax.broadcasted_iota(jnp.int32, (ROWBLK, HD), 1) < HD // 2
    for block in range(own_ref.shape[0]):
        rows = pl.ds(block * ROWBLK, ROWBLK)
        place = places_ref[pl.ds(dest_ref[block], 1), :]
        own_ref[pl.ds(block, 1), :] = place
        spread_out = jnp.broadcast_to(place.astype(jnp.float32), (ROWBLK, HD)).T
        angles = spread_out * freq_ref[...]
        cosine = jnp.cos(angles) * factor
        sine = jnp.sin(angles) * factor
        sine = jnp.where(half, -sine, sine)
        cos_ref[rows, :] = cosine
        sin_ref[rows, :] = sine
        raw = key_ref[rows, :].astype(jnp.float32)
        turned = raw * cosine + pltpu.roll(raw, HD // 2, 1) * sine
        turned_ref[rows, :] = turned.astype(turned_ref.dtype)


def rope(kv_head, dest, places_all, key):
    rows = key.shape[0]
    blocks = rows // ROWBLK
    freq = yarn_frequencies(HD)
    freq = jnp.concatenate([freq, freq]).reshape(1, HD)
    whole = lambda shape: pl.BlockSpec(shape, lambda step, *refs: (0,) * len(shape))
    table = jax.ShapeDtypeStruct((rows, HD), jnp.float32)
    return pl.pallas_call(
        rope_kernel,
        grid_spec=pltpu.PrefetchScalarGridSpec(
            num_scalar_prefetch=2,
            grid=(1,),
            in_specs=[
                whole(places_all.shape),
                whole((1, HD)),
                pl.BlockSpec((rows, HD), lambda step, at_ref, dest_ref: (0, at_ref[0])),
            ],
            out_specs=[whole((rows, HD))] * 3 + [whole((blocks, ROWBLK))],
        ),
        out_shape=[
            table,
            table,
            jax.ShapeDtypeStruct((rows, HD), key.dtype),
            jax.ShapeDtypeStruct((blocks, ROWBLK), jnp.int32),
        ],
        cost_estimate=NO_COST,
    )(kv_head.reshape(1), dest, places_all, freq, key)


NT = (((1,), (1,)), ((), ()))
TN = (((0,), (0,)), ((), ()))


def attend_kernel(
    heads,
    ranks,
    target_ref,
    source_ref,
    run_ref,
    slot_ref,
    need_ref,
    query_ref,
    up_ref,
    up_t_ref,
    place_ref,
    *refs,
):
    key_parts, refs = refs[:ranks], refs[ranks:]
    value_parts, refs = refs[:ranks], refs[ranks:]
    gquery_ref, out_ref, *halves = refs[:6]
    key_ref, value_ref, gkey_ref, gvalue_ref, key_win, value_win = refs[6:12]
    score_ref, prob_ref, gscore_ref, load_sems, sems = refs[12:]
    rows_each = query_ref.shape[0]
    half_blocks = ranks * RUN_BLOCKS // 2
    scale = 1.0 / math.sqrt(HD)
    to_exp2 = scale * math.log2(math.e)

    loads = []
    for item, (parts, whole) in enumerate(((key_parts, key_ref), (value_parts, value_ref))):
        for rank in range(ranks):
            copy = pltpu.make_async_copy(
                parts[rank], whole.at[pl.ds(rank * rows_each, rows_each)], load_sems.at[item, rank]
            )
            copy.start()
            loads.append(copy)
    for copy in loads:
        copy.wait()

    if ranks > rows_each // ROWBLK:
        gkey_ref[0] = jnp.zeros(gkey_ref.shape[1:], jnp.bfloat16)
        fills = []
        for item, whole in enumerate(halves):
            for part in range(ranks // 2):
                copy = pltpu.make_async_copy(
                    gkey_ref.at[0],
                    whole.at[pl.ds(part * rows_each, rows_each)],
                    load_sems.at[item // 2, item % 2 * (ranks // 2) + part],
                )
                copy.start()
                fills.append(copy)
        for copy in fills:
            copy.wait()

    def stores(block, act):
        side = block % 2
        for step in range(RUN_BLOCKS):
            target = target_ref[run_ref[block] * RUN_BLOCKS + step]
            for place in range(2):

                @pl.when(target // half_blocks == place)
                def one_half():
                    start = pl.multiple_of(target % half_blocks * ROWBLK, ROWBLK)
                    for item, source in enumerate((gkey_ref, gvalue_ref)):
                        act(
                            pltpu.make_async_copy(
                                source.at[side, pl.ds(step * ROWBLK, ROWBLK)],
                                halves[2 * item + place].at[pl.ds(start, ROWBLK)],
                                sems.at[side, item, step],
                            )
                        )

    def window(count, block):
        slot = slot_ref[block]
        run = run_ref[block]
        first = jnp.maximum(slot + 1 - count, 0)
        rows = count * ROWBLK
        for step in range(count):
            source = source_ref[run * RUN_BLOCKS + first + step]
            start = pl.multiple_of(source * ROWBLK, ROWBLK)
            key_win[pl.ds(step * ROWBLK, ROWBLK), :] = key_ref[pl.ds(start, ROWBLK), :]
            value_win[pl.ds(step * ROWBLK, ROWBLK), :] = value_ref[pl.ds(start, ROWBLK), :]
        wide = min(2, heads)
        base = pl.multiple_of(block * ROWBLK, ROWBLK)
        at_rows = pl.ds(base, ROWBLK)
        place = place_ref[pl.ds(block, 1), :]
        lane = lax.broadcasted_iota(jnp.int32, (1, ROWBLK), 1)
        last = (slot - first) * ROWBLK + lane
        last_all = jnp.concatenate([last] * wide, axis=1)
        start_all = jnp.concatenate([last - place] * wide, axis=1)
        key_index = lax.broadcasted_iota(jnp.int32, (ROWBLK, wide * ROWBLK), 0)
        keys = key_win[pl.ds(0, rows), :]
        values = value_win[pl.ds(0, rows), :]
        columns = [pl.ds(head * HD, HD) for head in range(heads)]
        query = jnp.concatenate([query_ref[at_rows, at] for at in columns], axis=0)
        up = jnp.concatenate([up_ref[at_rows, at] for at in columns], axis=0)
        folded = lambda tile: tile.reshape(ROWBLK // 8, 8, tile.shape[1])
        tiles = [pl.ds(step * ROWBLK, ROWBLK) for step in range(count)]
        groups = heads // wide
        spans = [slice(at * wide * ROWBLK, (at + 1) * wide * ROWBLK) for at in range(groups)]

        score = lax.dot_general(keys, query, NT, preferred_element_type=jnp.float32)
        gprob = lax.dot_general(values, up, NT, preferred_element_type=jnp.float32)
        peaks = [None] * groups
        for step, tile in enumerate(tiles):
            seen = key_index >= start_all - step * ROWBLK
            if step == count - 1:
                seen = seen & (key_index <= last_all - step * ROWBLK)
            for at, span in enumerate(spans):
                part = jnp.where(
                    seen, score[step * ROWBLK : (step + 1) * ROWBLK, span], masked_score
                )
                score_ref[tile, span] = part
                most = jnp.max(folded(part), axis=0)
                peaks[at] = most if peaks[at] is None else jnp.maximum(peaks[at], most)
        peaks = [jnp.max(item, axis=0, keepdims=True) for item in peaks]
        totals = [None] * groups
        for tile in tiles:
            for at, span in enumerate(spans):
                part = jnp.exp2((score_ref[tile, span] - peaks[at]) * to_exp2)
                score_ref[tile, span] = part
                some = jnp.sum(folded(part), axis=0)
                totals[at] = some if totals[at] is None else totals[at] + some
        shares = [1.0 / jnp.sum(item, axis=0, keepdims=True) for item in totals]
        for tile in tiles:
            for at, span in enumerate(spans):
                prob_ref[tile, span] = (score_ref[tile, span] * shares[at]).astype(jnp.bfloat16)
        prob_b = prob_ref[pl.ds(0, rows), :]
        out_t = lax.dot_general(values, prob_b, TN, preferred_element_type=jnp.float32)
        out_b = out_t.astype(jnp.bfloat16)
        deltas = []
        for at in range(groups):
            up_t = jnp.concatenate(
                [up_t_ref[item, at_rows] for item in columns[at * wide : (at + 1) * wide]], axis=1
            ).astype(jnp.float32)
            deltas.append(
                jnp.sum(up_t * out_b[:, spans[at]].astype(jnp.float32), axis=0, keepdims=True)
            )
        for step, tile in enumerate(tiles):
            for at, span in enumerate(spans):
                prob = score_ref[tile, span] * shares[at]
                part = gprob[step * ROWBLK : (step + 1) * ROWBLK, span] - deltas[at]
                gscore_ref[tile, span] = (prob * part).astype(jnp.bfloat16)
        gscore = gscore_ref[pl.ds(0, rows), :]
        gquery_t = lax.dot_general(keys, gscore, TN, preferred_element_type=jnp.float32)
        gkey = jnp.dot(gscore, query, preferred_element_type=jnp.float32)
        gvalue = jnp.dot(prob_b, up, preferred_element_type=jnp.float32)
        for head in range(heads):
            part = slice(head * ROWBLK, (head + 1) * ROWBLK)
            out_ref[columns[head], at_rows] = out_b[:, part]
            gquery_ref[columns[head], at_rows] = gquery_t[:, part]
        gkey = (gkey * scale).astype(jnp.bfloat16)
        gvalue = gvalue.astype(jnp.bfloat16)
        place_at = pl.ds(pl.multiple_of(first * ROWBLK, ROWBLK), rows)
        gkey_ref[block % 2, place_at, :] = gkey
        gvalue_ref[block % 2, place_at, :] = gvalue

    def body(block, carry):
        pl.when(block >= 2)(lambda: stores(block - 2, lambda copy: copy.wait()))
        blank = jnp.zeros(gkey_ref.shape[1:], jnp.bfloat16)
        gkey_ref[block % 2] = blank
        gvalue_ref[block % 2] = blank
        need = need_ref[block]
        floor = 0
        for size in range(1, RUN_BLOCKS + 1):
            pl.when((need > floor) & (need <= size))(partial(window, size, block))
            floor = size
        stores(block, lambda copy: copy.start())
        return carry

    blocks = rows_each // ROWBLK
    lax.fori_loop(0, blocks, body, 0)
    for block in range(max(blocks - 2, 0), blocks):
        stores(block, lambda copy: copy.wait())


def attend(tables, query, up, up_t, places, keys, values):
    rows, width = query.shape
    heads = width // HD
    ranks = len(keys)
    every = rows * ranks
    smem = pl.BlockSpec(memory_space=pltpu.SMEM)
    vmem = pl.BlockSpec(memory_space=pltpu.VMEM)
    hbm = pl.BlockSpec(memory_space=pl.ANY)
    half = jax.ShapeDtypeStruct((every // 2, HD), jnp.bfloat16)
    return pl.pallas_call(
        partial(attend_kernel, heads, ranks),
        out_shape=(
            jax.ShapeDtypeStruct((width, rows), jnp.float32),
            jax.ShapeDtypeStruct((width, rows), jnp.bfloat16),
            half,
            half,
            half,
            half,
        ),
        in_specs=[smem] * 5 + [vmem] * 4 + [hbm] * (2 * ranks),
        out_specs=(vmem, vmem, hbm, hbm, hbm, hbm),
        scratch_shapes=[pltpu.VMEM((every, HD), jnp.bfloat16)] * 2
        + [pltpu.VMEM((2, RUN_BLOCKS * ROWBLK, HD), jnp.bfloat16)] * 2
        + [pltpu.VMEM((RUN_BLOCKS * ROWBLK, HD), jnp.bfloat16)] * 2
        + [pltpu.VMEM((RUN_BLOCKS * ROWBLK, heads * ROWBLK), jnp.float32)]
        + [pltpu.VMEM((RUN_BLOCKS * ROWBLK, heads * ROWBLK), jnp.bfloat16)] * 2
        + [pltpu.SemaphoreType.DMA((2, ranks)), pltpu.SemaphoreType.DMA((2, 2, RUN_BLOCKS))],
        compiler_params=pltpu.CompilerParams(vmem_limit_bytes=VMEM_BYTES),
        cost_estimate=NO_COST,
    )(*tables, query, up, up_t, places, *keys, *values)


def assemble_kernel(lanes, my_ref, *refs):
    out_ref, sems = refs[lanes:]
    copies = []
    for index in range(lanes):
        column = pl.multiple_of((my_ref[0] ^ index) * HD, HD)
        copy = pltpu.make_async_copy(
            refs[index], out_ref.at[:, pl.ds(column, HD)], sems.at[index]
        )
        copy.start()
        copies.append(copy)
    for copy in copies:
        copy.wait()


def assemble(my_lane, pieces):
    rows = pieces[0].shape[0]
    lanes = len(pieces)
    vmem = pl.BlockSpec(memory_space=pltpu.VMEM)
    return pl.pallas_call(
        partial(assemble_kernel, lanes),
        out_shape=jax.ShapeDtypeStruct((rows, lanes * HD), pieces[0].dtype),
        in_specs=[pl.BlockSpec(memory_space=pltpu.SMEM)] + [vmem] * lanes,
        out_specs=pl.BlockSpec(memory_space=pl.ANY),
        scratch_shapes=[pltpu.SemaphoreType.DMA((lanes,))],
        compiler_params=pltpu.CompilerParams(vmem_limit_bytes=VMEM_BYTES),
        cost_estimate=NO_COST,
    )(my_lane.reshape(1), *pieces)


def lane_swap(array, bit):
    lanes = lax.axis_size("tensor")
    return lax.ppermute(array, "tensor", [(lane, lane ^ bit) for lane in range(lanes)])


def lane_pieces(pieces, bit):
    lanes = lax.axis_size("tensor")
    while bit:
        pieces = {**pieces, **{at | bit: lane_swap(item, bit) for at, item in pieces.items()}}
        bit //= 2
    return [pieces[at] for at in range(lanes)]


def swap(array, bit):
    ranks = lax.axis_size("dp")
    return lax.ppermute(array, "dp", [(rank, rank ^ bit) for rank in range(ranks)])


def spread(array):
    found = [array, swap(array, 1)]
    others = [swap(array, step) for step in range(2, lax.axis_size("dp"), 2)]
    for other in others:
        found += [other, swap(other, 1)]
    return found


def added(left, right):
    return left.astype(jnp.float32) + right.astype(jnp.float32)


def chip_sum(keep, received):
    count = lax.axis_size("dp") // 2
    rows = keep.shape[0] // count
    total = [
        added(keep[at * rows : (at + 1) * rows], received[at * rows : (at + 1) * rows])
        for at in range(count)
    ]
    return total[0], [item.astype(keep.dtype) for item in total[1:]]


def exchange(sends):
    return [swap(item, 2 * at + 2) for at, item in enumerate(sends)]


def final_kernel(count, rotary, outs, *refs):
    total = refs[0][...].astype(jnp.float32)
    for ref in refs[1 : 1 + count]:
        total = total + ref[...].astype(jnp.float32)
    if rotary:
        total = total * refs[1 + count][...] - pltpu.roll(total, HD // 2, 1) * refs[2 + count][...]
    for at in outs:
        refs[at][...] = total.astype(refs[at].dtype)


def final_sum(keep, received, tables, after, thru=(), copies=1):
    vmem = pl.BlockSpec(memory_space=pltpu.VMEM)
    hbm = pl.BlockSpec(memory_space=pl.ANY)
    parts = [keep, *received, *tables]
    inputs = len(parts) + len(after) + len(thru)
    results = pl.pallas_call(
        partial(
            final_kernel, len(received), len(tables) > 0, range(inputs, inputs + copies)
        ),
        out_shape=[jax.ShapeDtypeStruct(keep.shape, jnp.bfloat16)] * copies
        + [jax.ShapeDtypeStruct(item.shape, item.dtype) for item in thru],
        in_specs=[vmem] * len(parts) + [hbm] * (len(after) + len(thru)),
        out_specs=[vmem] * copies + [hbm] * len(thru),
        input_output_aliases={inputs - len(thru) + at: copies + at for at in range(len(thru))},
        compiler_params=pltpu.CompilerParams(vmem_limit_bytes=VMEM_BYTES),
        cost_estimate=NO_COST,
    )(*parts, *after, *thru)
    return results


def prepare_kernel(
    rows_ref, weight_ref, query_ref, cos_ref, sin_ref, *refs
):
    up_ref, up_t_ref, turned_ref = refs[-3:]
    total = jnp.dot(rows_ref[...], weight_ref[...], preferred_element_type=jnp.float32)
    up_ref[...] = total.astype(up_ref.dtype)
    up_t_ref[...] = total.T.astype(up_t_ref.dtype)
    for at in range(0, query_ref.shape[1], HD):
        raw = query_ref[:, at : at + HD].astype(jnp.float32)
        turned = raw * cos_ref[...] + pltpu.roll(raw, HD // 2, 1) * sin_ref[...]
        turned_ref[:, at : at + HD] = turned.astype(turned_ref.dtype)


def prepare(rows, weight, query, cosine, sine, after):
    height, depth = rows.shape
    width = weight.shape[1]
    steps = 4
    tall = height // steps
    across = lambda columns: pl.BlockSpec((tall, columns), lambda step: (step, 0))
    return pl.pallas_call(
        prepare_kernel,
        grid=(steps,),
        out_shape=[
            jax.ShapeDtypeStruct((height, width), jnp.bfloat16),
            jax.ShapeDtypeStruct((width, height), jnp.bfloat16),
            jax.ShapeDtypeStruct(query.shape, jnp.bfloat16),
        ],
        in_specs=[
            across(depth),
            pl.BlockSpec(weight.shape, lambda step: (0, 0)),
            across(width),
            across(HD),
            across(HD),
        ]
        + [pl.BlockSpec(memory_space=pl.ANY)] * len(after),
        out_specs=[
            across(width),
            pl.BlockSpec((width, tall), lambda step: (0, step)),
            across(width),
        ],
        compiler_params=pltpu.CompilerParams(vmem_limit_bytes=VMEM_BYTES),
        cost_estimate=pl.CostEstimate(
            flops=2 * height * weight.size, bytes_accessed=2 * rows.size, transcendentals=0
        ),
    )(rows, weight, query, cosine, sine, *after)


def turn_back_kernel(grad_ref, cos_ref, sin_ref, *refs):
    out_ref = refs[-1]
    scale = 1.0 / math.sqrt(HD)
    for at in range(0, grad_ref.shape[0], HD):
        grad = grad_ref[at : at + HD, :].T * scale
        back = grad * cos_ref[...] - pltpu.roll(grad, HD // 2, 1) * sin_ref[...]
        out_ref[:, at : at + HD] = back.astype(out_ref.dtype)


def turn_back(grad_t, cosine, sine, after):
    width, height = grad_t.shape
    steps = 4
    tall = height // steps
    return pl.pallas_call(
        turn_back_kernel,
        grid=(steps,),
        out_shape=jax.ShapeDtypeStruct((height, width), jnp.bfloat16),
        in_specs=[
            pl.BlockSpec((width, tall), lambda step: (0, step)),
            pl.BlockSpec((tall, HD), lambda step: (step, 0)),
            pl.BlockSpec((tall, HD), lambda step: (step, 0)),
        ]
        + [pl.BlockSpec(memory_space=pl.ANY)] * len(after),
        out_specs=pl.BlockSpec((tall, width), lambda step: (step, 0)),
        compiler_params=pltpu.CompilerParams(vmem_limit_bytes=VMEM_BYTES),
        cost_estimate=NO_COST,
    )(grad_t, cosine, sine, *after)


def hold_kernel(*refs):
    pass


def hold(array, after):
    hbm = pl.BlockSpec(memory_space=pl.ANY)
    return pl.pallas_call(
        hold_kernel,
        out_shape=jax.ShapeDtypeStruct(array.shape, array.dtype),
        in_specs=[hbm] * (1 + len(after)),
        out_specs=hbm,
        input_output_aliases={0: 0},
        cost_estimate=NO_COST,
    )(array, *after)


def product_kernel(my_ref, left_ref, right_ref, *refs):
    keep_ref, send_ref = refs[-3:-1]
    half = keep_ref.shape[1]
    total = jnp.dot(left_ref[...], right_ref[...], preferred_element_type=jnp.float32)
    total = total.astype(keep_ref.dtype).T
    odd = my_ref[1]

    @pl.when(odd == 0)
    def even_core():
        keep_ref[0] = total[:half]
        send_ref[0] = total[half:]

    @pl.when(odd == 1)
    def odd_core():
        keep_ref[0] = total[half:]
        send_ref[0] = total[:half]


def product(my_rank, left, right, thru, after):
    count = lax.axis_size("dp") // 2
    width, depth = left.shape
    cols = right.shape[1] // count
    mine, odd = my_rank // 2, my_rank & 1
    if cols % 128:
        total = jnp.dot(left, right, preferred_element_type=jnp.float32).astype(jnp.bfloat16)
        pieces = total.T.reshape(count, 2, cols // 2, width)
        pieces = jnp.take(pieces, jnp.arange(count, dtype=jnp.int32) ^ mine, axis=0)
        low, high = pieces[:, 0], pieces[:, 1]
        return jnp.where(odd > 0, high, low), jnp.where(odd > 0, low, high), thru
    hbm = pl.BlockSpec(memory_space=pl.ANY)
    stacked = pl.BlockSpec((1, cols // 2, width), lambda step, my_ref: (step, 0, 0))
    stack = jax.ShapeDtypeStruct((count, cols // 2, width), jnp.bfloat16)
    inputs = [jnp.stack([mine, odd]), left, right, *after, thru]
    return pl.pallas_call(
        product_kernel,
        grid_spec=pltpu.PrefetchScalarGridSpec(
            num_scalar_prefetch=1,
            grid=(count,),
            in_specs=[
                pl.BlockSpec(left.shape, lambda step, my_ref: (0, 0)),
                pl.BlockSpec((depth, cols), lambda step, my_ref: (0, step ^ my_ref[0])),
            ]
            + [hbm] * (len(after) + 1),
            out_specs=[stacked, stacked, hbm],
        ),
        out_shape=[stack, stack, jax.ShapeDtypeStruct(thru.shape, thru.dtype)],
        input_output_aliases={len(inputs) - 1: 2},
        compiler_params=pltpu.CompilerParams(vmem_limit_bytes=VMEM_BYTES),
        cost_estimate=NO_COST,
    )(*inputs)


def weight_final_kernel(count, factor, *refs):
    total = refs[0][0].astype(jnp.float32)
    for ref in refs[1 : 1 + count]:
        total = total + ref[0].astype(jnp.float32)
    refs[-1][...] = total * factor


def weight_final(keep, received, factor, after):
    vmem = pl.BlockSpec(memory_space=pltpu.VMEM)
    hbm = pl.BlockSpec(memory_space=pl.ANY)
    return pl.pallas_call(
        partial(weight_final_kernel, len(received), factor),
        out_shape=jax.ShapeDtypeStruct(keep.shape[1:], jnp.float32),
        in_specs=[vmem] * (1 + len(received)) + [hbm] * len(after),
        out_specs=vmem,
        compiler_params=pltpu.CompilerParams(vmem_limit_bytes=VMEM_BYTES),
        cost_estimate=NO_COST,
    )(keep, *received, *after)


def local(query, key, value, grad_out, out_weight, plan, segments):
    rank_count = lax.axis_size("dp")
    my_rank = lax.axis_index("dp")
    my_lane = lax.axis_index("tensor")
    row_count = query.shape[0]
    block_count = row_count // ROWBLK
    local_heads = query.shape[1] // HD
    group = HEADS // KV
    bits = [1 << at for at in range(rank_count.bit_length() - 1)]
    kv_head = my_lane * local_heads // group
    own_value = lax.dynamic_slice_in_dim(value, kv_head * HD, HD, 1)
    own_places = positions_of(segments).reshape(1, block_count, ROWBLK)
    places_all = lax.all_to_all(
        jnp.broadcast_to(own_places, (rank_count, block_count, ROWBLK)),
        "dp",
        split_axis=0,
        concat_axis=0,
        tiled=True,
    ).reshape(-1, ROWBLK)
    values = spread(own_value)

    mine = my_rank * block_count + jnp.arange(block_count, dtype=jnp.int32)
    hit = plan[None, :] == mine[:, None]
    dest = jnp.sum(
        jnp.where(hit, jnp.arange(plan.shape[0], dtype=jnp.int32)[None, :], 0), axis=1
    )
    run = dest // RUN_BLOCKS
    slot = dest % RUN_BLOCKS
    cosine, sine, rot_key, places = rope(kv_head, dest, places_all, key)
    need = slot - (slot * ROWBLK - places[:, 0]) // ROWBLK + 1
    keys = spread(rot_key)
    up, up_t, turned = prepare(grad_out, out_weight, query, cosine, sine, [rot_key])

    distance = (plan // block_count) ^ my_rank
    within = plan % block_count
    half_place = (distance & 1) * (rank_count // 2) + distance // 2
    tables = (
        half_place * block_count + within,
        distance * block_count + within,
        run,
        slot,
        need,
    )
    grad_query_t, attn_t, gkey_keep, gkey_send, gvalue_keep, gvalue_send = attend(
        tables, turned, up, up_t, places, keys, values
    )
    value_keep, value_sends = chip_sum(gvalue_keep, swap(gvalue_send, 1))
    value_received = exchange(value_sends)
    key_keep, key_sends = chip_sum(gkey_keep, swap(gkey_send, 1))
    key_received = exchange(key_sends)
    weight_keep, weight_send, value_keep = product(
        my_rank, attn_t, grad_out, value_keep, [value_sends[0], key_sends[0]]
    )
    far = lax.axis_size("tensor") // 2
    value_partial, value_near, weight_send = final_sum(
        value_keep, value_received, (), (), thru=[weight_send], copies=2
    )
    value_far = lane_swap(value_partial, far)
    weight_keep, weight_sends = chip_sum(weight_keep, swap(weight_send, 1))
    weight_received = exchange(weight_sends)
    value_near = hold(value_near, weight_sends[:1])
    value_far = hold(value_far, weight_sends[:1])
    value_pieces = lane_pieces({0: value_near, far: value_far}, far // 2)
    value_all = assemble(my_lane, value_pieces)
    (key_partial,) = final_sum(
        key_keep, key_received, (cosine, sine), [value_far, value_pieces[1]]
    )
    grad_query = turn_back(grad_query_t, cosine, sine, [key_partial])
    key_far = hold(lane_swap(key_partial, far), [*weight_received, grad_query])
    key_all = assemble(my_lane, lane_pieces({0: key_partial, far: key_far}, far // 2))
    weight_grad = weight_final(
        weight_keep, weight_received, 1.0 / rank_count, [key_far, value_all]
    )
    lanes_per_key = group // local_heads

    def combine(gathered):
        if lanes_per_key == 1:
            return gathered
        merged = (
            gathered.astype(jnp.float32).reshape(row_count, KV, lanes_per_key, HD).sum(axis=2)
        )
        return merged.astype(jnp.bfloat16).reshape(row_count, KV * HD)

    return (grad_query, combine(key_all), combine(value_all), weight_grad)


def solution(mesh):
    in_specs = (
        P("dp", "tensor"),
        P("dp", None),
        P("dp", None),
        P("dp", None),
        P(None, "tensor"),
        P(),
        P("dp"),
    )
    out_specs = (P("dp", "tensor"), P("dp", None), P("dp", None), P("dp", "tensor"))
    return jax.shard_map(local, mesh=mesh, in_specs=in_specs, out_specs=out_specs, check_vma=False)
```
